32 devices in a mesh: dp: 8 (over y, x, core), band: 4 (over z).
Axes of the slice: x: 2, y: 2, z: 4, core: 2. Of those that a mesh axis runs over, the one named last changes fastest.
Arguments:
- patches: bfloat16 [128, 64, 128, 256], P('dp', None, 'band'), may hold values from -6 to 6
- bias_token: bfloat16 [128], replicated, may hold values from -6 to 6
- gen_attn: bfloat16 [4, 128, 128], replicated, may hold values from -2 to 2
- gen_gain: bfloat16 [2, 128], replicated, may hold values from 0.5 to 1.5
- gen_ff_in: bfloat16 [128, 2048], replicated, may hold values from -0.5 to 0.5
- gen_ff_out: bfloat16 [2048, 128], replicated, may hold values from -0.125 to 0.125
- gen_kernel: bfloat16 [128, 196608], P(None, ('dp', 'band')), may hold values from -0.0029296875 to 0.0029296875
- gen_bias: bfloat16 [128, 768], replicated, may hold values from -0.4375 to 0.4375
- pos_table: bfloat16 [196, 768], replicated, may hold values from -6 to 6
- norm_gain: bfloat16 [2, 768], replicated, may hold values from 0.5 to 1.5
- norm_bias: bfloat16 [2, 768], replicated, may hold values from -4 to 4
- w_qkv: bfloat16 [768, 2304], P(('dp', 'band')), may hold values from -0.21875 to 0.21875
- w_out: bfloat16 [768, 768], P(('dp', 'band')), may hold values from -1.5 to 1.5
- w_fc1: bfloat16 [768, 3072], P(('dp', 'band')), may hold values from -0.21875 to 0.21875
- bias_in: bfloat16 [3072], replicated, may hold values from -4 to 4
- w_fc2: bfloat16 [3072, 768], P(('dp', 'band')), may hold values from -0.109375 to 0.109375
- wavelengths: int32 [128], replicated, may hold values from 400 to 2499
- kept: int32 [128, 64], P(('dp', 'band')), may hold values from 0 to 195, as said below
- counts: int32 [128], P(('dp', 'band')), may hold values from 34 to 64, as said below
- cotangent: bfloat16 [128, 64, 768], P(('dp', 'band')), may hold values from -6 to 6
Outputs:
- output: bfloat16 [128, 64, 768], P(('dp', 'band'))
- grad_patches: bfloat16 [128, 64, 128, 256], P('dp', None, 'band')
- grad_bias_token: float32 [128], replicated
- grad_gen_attn: float32 [4, 128, 128], replicated
- grad_gen_gain: float32 [2, 128], replicated
- grad_gen_ff_in: float32 [128, 2048], replicated
- grad_gen_ff_out: float32 [2048, 128], replicated
- grad_gen_kernel: float32 [128, 196608], P(None, ('dp', 'band'))
- grad_gen_bias: float32 [128, 768], replicated
- grad_pos_table: float32 [196, 768], replicated
- grad_norm_gain: float32 [2, 768], replicated
- grad_norm_bias: float32 [2, 768], replicated
- grad_w_qkv: float32 [768, 2304], P(('dp', 'band'))
- grad_w_out: float32 [768, 768], P(('dp', 'band'))
- grad_w_fc1: float32 [768, 3072], P(('dp', 'band'))
- grad_bias_in: float32 [3072], replicated
- grad_w_fc2: float32 [3072, 768], P(('dp', 'band'))
The draws below stay inside these ranges and needn't reach their ends.
Inputs may be any that keep to these rules, and one draw needn't show every extreme that they name: `kept`: each row names 64 different patch positions; slots at or after the image's count hold positions that no output reads. `counts`: slots of an image at or after its count are padding; in every draw some image keeps 64 patches.
All inputs are finite; a program needn't handle non-finite values.
Results may differ from the reference program's by a relative error of at most 0.03.
Values may be sent and summed in bfloat16 or wider, within the bound.
No kernel may reach another device: no remote copies, remote signals or barrier semaphores. Data moves between devices by JAX's collectives and lax.ppermute only.
A program may use at most 256 MiB of HBM per device.

```python
import math
from functools import partial
import jax
import jax.numpy as jnp
from jax import lax

D = 768
HEADS = 12
HDIM = 64
FF = 3072
GW = 128
GEN_HEADS = 4
GEN_FF = 2048
P2 = 256
POS = 196
BANDS = 128
CAP = 64
IMAGES = 128
N_DP = 8


def choose_row(single_key):
    return jax.random.permutation(single_key, POS)[:CAP]


def draw_kept(key, part):
    key = jax.random.fold_in(key, 11)
    row_keys = jax.random.split(key, IMAGES)
    return jax.vmap(choose_row)(row_keys).astype(jnp.int32)


def draw_counts(key, part):
    key = jax.random.fold_in(key, 23)
    base_key, pick_key = jax.random.split(key)
    drawn = jax.random.randint(base_key, (IMAGES,), CAP // 2 + 2, CAP + 1)
    chosen = jax.random.randint(pick_key, (), 0, IMAGES)
    return jnp.where(jnp.arange(IMAGES) == chosen, CAP, drawn).astype(jnp.int32)


def with_ends(array, stream_key, least, largest):
    shape = array.shape
    spot = [jax.random.randint(jax.random.fold_in(stream_key, axis), (), 0, shape[axis]) for axis in range(len(shape))]
    array = array.at[tuple(spot)].set(least)
    longest = shape.index(max(shape))
    spot[longest] = (spot[longest] + 1) % shape[longest]
    return array.at[tuple(spot)].set(largest)


def with_spikes(values, stream_key, source, target, blocks, factor):
    owner, partner = [(jnp.arange(values.shape[axis_at]) // (values.shape[axis_at] // blocks)).reshape([-1 if axis == axis_at else 1 for axis in range(values.ndim)]) for axis_at in (source, target)]
    chosen = jax.random.permutation(stream_key, blocks)[partner]
    strong = (owner == chosen) | (owner == (partner + blocks // 2) % blocks)
    return jnp.where(strong, factor * values, values)


def steps_of(own_key, dims, shards, smallest, high):
    def one(axis_at, shards_of):
        draws = jax.random.uniform(jax.random.fold_in(jax.random.fold_in(own_key, 6), axis_at), (shards_of,), jnp.float32, smallest / len(shards), high / len(shards))
        return jnp.repeat(jnp.exp(draws), dims[axis_at] // shards_of).reshape((-1,) + (1,) * (len(dims) - axis_at - 1))

    level = one(*shards[0])
    for cut in shards[1:]:
        level = level * one(*cut)
    return level


def normal_values(rng, shape, scale, most, shards=(), kind=jnp.bfloat16):
    entries = scale * jax.random.normal(rng, shape, jnp.float32)
    if shards:
        entries = entries * steps_of(rng, shape, shards, -0.22, 0.18)
    return jnp.clip(entries, -most, most).astype(kind)


def heavy_noise(rng, dims, deviation, limit, shards, heavy, dtype=jnp.bfloat16):
    entries = deviation * jax.random.normal(rng, dims, jnp.float32)
    if shards:
        entries = entries * steps_of(rng, dims, shards, -0.22, 0.18)
    return jnp.clip(with_spikes(entries, jax.random.fold_in(rng, 3), *heavy), -limit, limit).astype(dtype)


def setup_inputs(seed: int = 0) -> dict:
    seeds = jax.random.split(jax.random.key(seed), 21)
    patches = heavy_noise(seeds[0], (IMAGES, CAP, BANDS, P2), 1.0, 6.0, ((0, 8), (2, 4)), (2, 0, 8, 2.0))
    bias_token = normal_values(seeds[1], (GW,), 1.0, 6.0)
    gen_attn = normal_values(seeds[2], (4, GW, GW), 0.15, 2.0)
    gen_gain = jnp.clip(1.0 + 0.1 * jax.random.normal(seeds[3], (2, GW), jnp.float32), 0.5, 1.5).astype(jnp.bfloat16)
    gen_ff_in = normal_values(seeds[4], (GW, GEN_FF), GW ** -0.5, 0.5)
    gen_ff_out = normal_values(seeds[5], (GEN_FF, GW), GEN_FF ** -0.5, 0.125)
    gen_kernel = normal_values(seeds[6], (GW, P2 * D), (GW * BANDS * P2) ** -0.5, 0.0029296875, ((1, 32),))
    gen_bias = normal_values(seeds[7], (GW, D), 0.03, 0.4375)
    pos_table = normal_values(seeds[8], (POS, D), 0.5, 6.0)
    norm_gain = jnp.clip(1.0 + 0.1 * jax.random.normal(seeds[9], (2, D), jnp.float32), 0.5, 1.5).astype(jnp.bfloat16)
    norm_bias = normal_values(seeds[10], (2, D), 0.3, 4.0)
    w_qkv = normal_values(seeds[11], (D, 3 * D), D ** -0.5, 0.21875, ((0, 32),))
    w_out = normal_values(seeds[12], (D, D), (D // 48) ** -0.5, 1.5, ((0, 32),))
    w_fc1 = normal_values(seeds[13], (D, FF), D ** -0.5, 0.21875, ((0, 32),))
    bias_in = normal_values(seeds[14], (FF,), 0.3, 4.0)
    w_fc2 = normal_values(seeds[15], (FF, D), FF ** -0.5, 0.109375, ((0, 32),))
    wavelengths = with_ends(jax.random.randint(seeds[16], (BANDS,), 400, 2500), jax.random.fold_in(seeds[16], 1), 400, 2499).astype(jnp.int32)
    kept = draw_kept(jax.random.fold_in(seeds[20], 71), 0)
    counts = draw_counts(jax.random.fold_in(seeds[20], 71), 0)
    cotangent = normal_values(seeds[19], (IMAGES, CAP, D), 1.0, 6.0, ((0, 32),))
    return {"patches": patches, "bias_token": bias_token, "gen_attn": gen_attn, "gen_gain": gen_gain, "gen_ff_in": gen_ff_in, "gen_ff_out": gen_ff_out, "gen_kernel": gen_kernel, "gen_bias": gen_bias, "pos_table": pos_table, "norm_gain": norm_gain, "norm_bias": norm_bias, "w_qkv": w_qkv, "w_out": w_out, "w_fc1": w_fc1, "bias_in": bias_in, "w_fc2": w_fc2, "wavelengths": wavelengths, "kept": kept, "counts": counts, "cotangent": cotangent}


@jax.custom_vjp
def low(v):
    return lax.optimization_barrier(v.astype(jnp.bfloat16)).astype(jnp.float32)

@jax.custom_vjp
def low_back(v):
    return v

def low_keep(v):
    return (low(v), None)

def low_pass(kept, grad):
    return (grad,)

def back_keep(v):
    return (v, None)

def back_low(kept, grad):
    return (low(grad),)
low.defvjp(low_keep, low_pass)
low_back.defvjp(back_keep, back_low)

def matmul(left_arr, right_arr):
    return jnp.dot(left_arr, right_arr, precision=lax.Precision.HIGHEST, preferred_element_type=jnp.float32)

def layer_norm(values, gain_vec, shift_vec):
    center = values - lax.optimization_barrier(jnp.mean(values, axis=-1, keepdims=True))
    spread = lax.optimization_barrier(jnp.mean(center * center, axis=-1, keepdims=True))
    return center * lax.rsqrt(spread + 1e-06) * gain_vec + shift_vec

def wave_embed(wavelengths, embed_width):
    half_width = embed_width // 2
    steps_arr = jnp.arange(half_width).astype(jnp.float32)
    frequency = jnp.exp(steps_arr * (-math.log(10000.0) / half_width))
    angles = wavelengths.astype(jnp.float32)[:, None] * frequency[None, :]
    return jnp.concatenate([jnp.sin(angles), jnp.cos(angles)], axis=1)

def generate(wavelengths, bias_token, gen_attn, gen_gain, gen_ff_in, gen_ff_out):
    embed_width = bias_token.shape[0]
    head_size = embed_width // GEN_HEADS
    sequence = jnp.concatenate([bias_token[None, :], wave_embed(wavelengths, embed_width)], axis=0)
    queries = matmul(sequence, gen_attn[0])
    keys_arr = matmul(sequence, gen_attn[1])
    values_arr = matmul(sequence, gen_attn[2])
    head_outs = []
    for head in range(GEN_HEADS):
        first_col = head * head_size
        query_head = queries[:, first_col:first_col + head_size]
        key_head = keys_arr[:, first_col:first_col + head_size]
        value_head = values_arr[:, first_col:first_col + head_size]
        scores = matmul(query_head, key_head.T) * (1.0 / math.sqrt(head_size))
        weights = jax.nn.softmax(scores, axis=-1)
        head_outs.append(matmul(weights, value_head))
    mixed_heads = jnp.concatenate(head_outs, axis=1)
    zero_shift = jnp.zeros_like(bias_token)
    first_out = layer_norm(sequence + matmul(mixed_heads, gen_attn[3]), gen_gain[0], zero_shift)
    hidden = jax.nn.gelu(matmul(first_out, gen_ff_in), approximate=False)
    return layer_norm(first_out + matmul(hidden, gen_ff_out), gen_gain[1], zero_shift)

def attend(qkv_rows, valid_mask, images_count):
    shaped = qkv_rows.reshape(images_count, CAP, 3, HEADS, HDIM)
    queries = shaped[:, :, 0]
    keys_arr = shaped[:, :, 1]
    values_arr = shaped[:, :, 2]
    scores = low_back(jnp.einsum('gqhd,gkhd->ghqk', queries, keys_arr, precision=lax.Precision.HIGHEST) * HDIM ** (-0.5))
    scores = jnp.where(valid_mask[:, None, None, :], scores, -1e+30)
    weights = low(jax.nn.softmax(scores, axis=-1))
    mixed_heads = jnp.einsum('ghqk,gkhd->gqhd', weights, values_arr, precision=lax.Precision.HIGHEST)
    return mixed_heads.reshape(images_count * CAP, D)

def group_forward(kernel_mat, embed_bias, pos_table, norm_gain, norm_bias, w_qkv, w_out, w_fc1, bias_in, w_fc2, block_in):
    patch_group, kept_group, count_group = block_in
    images_count = patch_group.shape[0]
    row_count = images_count * CAP
    valid_mask = jnp.arange(CAP)[None, :] < count_group[:, None]
    keep_col = valid_mask.reshape(row_count, 1).astype(jnp.float32)
    embedded = matmul(patch_group.reshape(row_count, BANDS * P2), kernel_mat)
    start_rows = low_back(embedded) + embed_bias[None, :] + pos_table[kept_group.reshape(row_count)]
    normed = low(layer_norm(start_rows, norm_gain[0], norm_bias[0]))
    qkv_rows = low_back(low(matmul(normed, w_qkv)))
    mixed_rows = low_back(low(attend(qkv_rows, valid_mask, images_count)))
    middle = start_rows + low_back(matmul(mixed_rows, w_out))
    normed_two = low(layer_norm(middle, norm_gain[1], norm_bias[1]))
    pre_act = low_back(matmul(normed_two, w_fc1) + bias_in[None, :])
    activation = low(jax.nn.gelu(pre_act, approximate=False))
    final_rows = middle + low_back(matmul(activation, w_fc2))
    return (final_rows * keep_col).reshape(images_count, CAP, D)

def forward(wavelengths, kept, counts, float_args):
    patches, bias_token, gen_attn, gen_gain, gen_ff_in, gen_ff_out, gen_kernel, gen_bias, pos_table, norm_gain, norm_bias, w_qkv, w_out, w_fc1, bias_in, w_fc2 = float_args
    states = generate(wavelengths, bias_token, gen_attn, gen_gain, gen_ff_in, gen_ff_out)
    embed_bias = matmul(states[0:1], gen_bias)[0]
    kernel = low_back(low(matmul(low(states[1:]), gen_kernel)))
    kernel_mat = kernel.reshape(BANDS * P2, D)
    group_size = IMAGES // N_DP
    blocks_in = (patches.reshape(N_DP, group_size, CAP, BANDS, P2), kept.reshape(N_DP, group_size, CAP), counts.reshape(N_DP, group_size))
    step_fn = jax.checkpoint(partial(group_forward, kernel_mat, embed_bias, pos_table, norm_gain, norm_bias, w_qkv, w_out, w_fc1, bias_in, w_fc2))
    return lax.map(step_fn, blocks_in).reshape(IMAGES, CAP, D)

def reference(patches, bias_token, gen_attn, gen_gain, gen_ff_in, gen_ff_out, gen_kernel, gen_bias, pos_table, norm_gain, norm_bias, w_qkv, w_out, w_fc1, bias_in, w_fc2, wavelengths, kept, counts, cotangent):
    float_args = tuple((single.astype(jnp.float32) for single in (patches, bias_token, gen_attn, gen_gain, gen_ff_in, gen_ff_out, gen_kernel, gen_bias, pos_table, norm_gain, norm_bias, w_qkv, w_out, w_fc1, bias_in, w_fc2)))
    result, backward = jax.vjp(partial(forward, wavelengths, kept, counts), float_args)
    grads, = backward(cotangent.astype(jnp.float32))
    return (result.astype(jnp.bfloat16), grads[0].astype(jnp.bfloat16), grads[1], grads[2], grads[3], grads[4], grads[5], grads[6], grads[7], grads[8], grads[9], grads[10], grads[11], grads[12], grads[13], grads[14], grads[15])
```

```python
from functools import partial
import math

import jax
import jax.numpy as jnp
from jax import lax
from jax.sharding import PartitionSpec as P

HEADS = 12
HDIM = 64
GEN_HEADS = 4


def matmul(left_arr, right_arr):
    return jnp.dot(
        left_arr, right_arr, precision=lax.Precision.HIGHEST, preferred_element_type=jnp.float32
    )


def layer_norm(values, gain_vec, shift_vec):
    center = values - jnp.mean(values, axis=-1, keepdims=True)
    spread = jnp.mean(center * center, axis=-1, keepdims=True)
    return center * lax.rsqrt(spread + 1e-06) * gain_vec + shift_vec


def wave_embed(wavelengths, embed_width):
    half_width = embed_width // 2
    steps_arr = jnp.arange(half_width).astype(jnp.float32)
    frequency = jnp.exp(steps_arr * (-math.log(10000.0) / half_width))
    angles = wavelengths.astype(jnp.float32)[:, None] * frequency[None, :]
    return jnp.concatenate([jnp.sin(angles), jnp.cos(angles)], axis=1)


def generate(wavelengths, bias_token, gen_attn, gen_gain, gen_ff_in, gen_ff_out):
    embed_width = bias_token.shape[0]
    head_size = embed_width // GEN_HEADS
    sequence = jnp.concatenate([bias_token[None, :], wave_embed(wavelengths, embed_width)], axis=0)
    queries = matmul(sequence, gen_attn[0])
    keys_arr = matmul(sequence, gen_attn[1])
    values_arr = matmul(sequence, gen_attn[2])
    head_outs = []
    for head in range(GEN_HEADS):
        first_col = head * head_size
        query_head = queries[:, first_col : first_col + head_size]
        key_head = keys_arr[:, first_col : first_col + head_size]
        value_head = values_arr[:, first_col : first_col + head_size]
        scores = matmul(query_head, key_head.T) * (1.0 / math.sqrt(head_size))
        weights = jax.nn.softmax(scores, axis=-1)
        head_outs.append(matmul(weights, value_head))
    mixed_heads = jnp.concatenate(head_outs, axis=1)
    zero_shift = jnp.zeros_like(bias_token)
    first_out = layer_norm(sequence + matmul(mixed_heads, gen_attn[3]), gen_gain[0], zero_shift)
    hidden = jax.nn.gelu(matmul(first_out, gen_ff_in), approximate=False)
    return layer_norm(first_out + matmul(hidden, gen_ff_out), gen_gain[1], zero_shift)


def inner(left_arr, right_arr):
    return lax.dot_general(
        left_arr, right_arr, (((0,), (0,)), ((), ())), preferred_element_type=jnp.float32
    )


def times_transpose(left_arr, right_arr):
    return lax.dot_general(
        left_arr, right_arr, (((1,), (1,)), ((), ())), preferred_element_type=jnp.float32
    )


def masked_scores(queries, keys_arr, valid_mask):
    raw_scores = jnp.einsum(
        "gqhd,gkhd->ghqk", queries, keys_arr, preferred_element_type=jnp.float32
    ) * HDIM ** (-0.5)
    return jnp.where(valid_mask[:, None, None, :], raw_scores, -1e30)


def bit_steps(size):
    steps = []
    step = 1
    while step < size:
        steps.append(step)
        step *= 2
    return steps


def swap(values, axis, step):
    size = lax.axis_size(axis)
    return lax.ppermute(values, axis, [(spot, spot ^ step) for spot in range(size)])


def turn(items, by):
    by = by % max(len(items), 1)
    return items[by:] + items[:by]


def gather_dp(piece, by):
    steps = bit_steps(lax.axis_size("dp"))
    held = piece[None]
    keys = [0]
    blocks = [(keys, held)]
    for step in turn(steps[1:], by):
        got = swap(held, "dp", step)
        got_keys = [key ^ step for key in keys]
        blocks.append((got_keys, got))
        held = jnp.concatenate([held, got], axis=0)
        keys = keys + got_keys
    if steps:
        blocks += [([key ^ 1 for key in some], swap(block, "dp", 1)) for some, block in blocks]
    return blocks


def swap_band(values, at):
    spot = lax.axis_index("band")
    blocks = []
    for step in range(lax.axis_size("band")):
        block = lax.dynamic_index_in_dim(values, spot ^ step, at, keepdims=False)
        blocks.append(([step], (swap(block, "band", step) if step else block)[None]))
    return blocks


def gather_band(piece):
    return [
        ([step], (swap(piece, "band", step) if step else piece)[None])
        for step in range(lax.axis_size("band"))
    ]


def place(blocks, axis, at):
    spot = lax.axis_index(axis)
    first = blocks[0][1]
    count = sum(len(keys) for keys, _ in blocks)
    shape = first.shape[1 : at + 1] + (count,) + first.shape[at + 1 :]
    whole = jnp.zeros(shape, first.dtype)
    for keys, block in blocks:
        for number, key in enumerate(keys):
            whole = lax.dynamic_update_index_in_dim(whole, block[number], spot ^ key, at)
    return whole


def add_low(left_arr, right_arr):
    return (left_arr.astype(jnp.float32) + right_arr.astype(jnp.float32)).astype(left_arr.dtype)


def scatter_dp(values, at, by):
    size = lax.axis_size("dp")
    spot = lax.axis_index("dp")
    steps = bit_steps(size)
    shape = values.shape
    values = values.reshape(shape[:at] + (2,) * len(steps) + shape[at + 1 :])
    left = list(reversed(steps))
    for step in steps[:1] + turn(steps[1:], by):
        dim = at + left.index(step)
        bit = (spot // step) % 2
        send = lax.dynamic_index_in_dim(values, 1 - bit, dim, keepdims=False)
        keep = lax.dynamic_index_in_dim(values, bit, dim, keepdims=False)
        values = add_low(keep, swap(send, "dp", step))
        left.remove(step)
    return values


def scatter_band(values, at):
    total = 0.0
    for _, block in swap_band(values, at):
        total = total + block[0].astype(jnp.float32)
    return total


def sum_rows(rows_arr):
    dp_size = lax.axis_size("dp")
    band_size = lax.axis_size("band")
    row_count, width = rows_arr.shape
    share = -(-row_count // (dp_size * band_size))
    padded = jnp.pad(rows_arr, ((0, share * dp_size * band_size - row_count), (0, 0)))
    own = scatter_band(scatter_dp(padded.reshape(dp_size, band_size, share, width), 0, 0), 0)
    whole = place(gather_dp(place(gather_band(own), "band", 0), 1), "dp", 0)
    return whole.reshape(-1, width)[:row_count]


def psum_small(values):
    for axis in ("dp", "band"):
        for step in bit_steps(lax.axis_size(axis)):
            values = values + swap(values, axis, step)
    return values


def column_blocks(matrix, width):
    return [matrix[:, spot : spot + width] for spot in range(0, matrix.shape[1], width)]


def shards(
    patches,
    bias_token,
    gen_attn,
    gen_gain,
    gen_ff_in,
    gen_ff_out,
    gen_kernel,
    gen_bias,
    pos_table,
    norm_gain,
    norm_bias,
    w_qkv,
    w_out,
    w_fc1,
    bias_in,
    w_fc2,
    wavelengths,
    kept,
    counts,
    cotangent,
):
    group_size, slot_count, bands_dev, pixel_count = patches.shape
    local_images = group_size // lax.axis_size("band")
    model_width = w_out.shape[1]
    row_total = local_images * slot_count
    gen_params = (
        bias_token.astype(jnp.float32),
        gen_attn.astype(jnp.float32),
        gen_gain.astype(jnp.float32),
        gen_ff_in.astype(jnp.float32),
        gen_ff_out.astype(jnp.float32),
    )
    states, gen_backward = jax.vjp(partial(generate, wavelengths), *gen_params)
    bias_matrix = gen_bias.astype(jnp.float32)
    embed_bias = matmul(states[0:1], bias_matrix)[0]
    band_states = states[1:].astype(jnp.bfloat16)
    dp_size = lax.axis_size("dp")
    band_size = lax.axis_size("band")
    device_count = dp_size * band_size
    own_pixels = pixel_count // device_count
    groups = 2
    group_bands = bands_dev // groups
    band_total = bands_dev * band_size
    weight_parts = (
        column_blocks(w_qkv, model_width)
        + [w_out]
        + column_blocks(w_fc1, model_width)
        + [w_fc2]
    )
    weight_spots = [0]
    for block in weight_parts:
        weight_spots.append(weight_spots[-1] + block.shape[0])
    weights = lax.all_gather(jnp.concatenate(weight_parts, axis=0), ("dp", "band"), axis=0)
    blocks = [
        weights[:, first:last].reshape(-1, model_width)
        for first, last in zip(weight_spots[:-1], weight_spots[1:])
    ]
    qkv_full = jnp.concatenate(blocks[:3], axis=1)
    out_full = blocks[3]
    fc_in_full = jnp.concatenate(blocks[4:-1], axis=1)
    fc_out_full = blocks[-1]
    shard_cube = gen_kernel.reshape(gen_kernel.shape[0], own_pixels, model_width)
    own_kernel = (
        jnp.einsum("rg,gpc->rpc", band_states, shard_cube, preferred_element_type=jnp.float32)
        .astype(jnp.bfloat16)
        .reshape(band_size, groups, group_bands, own_pixels, model_width)
    )
    patch_cube = patches.reshape(group_size * slot_count, bands_dev, pixel_count)
    patch_parts = []
    kernel_parts = []
    product = jnp.zeros((group_size * slot_count, model_width), jnp.float32)
    for part in range(groups):
        piece = place(swap_band(own_kernel[:, part], 0), "band", 1)
        piece = piece.reshape(group_bands, band_size * own_pixels, model_width)
        kernel_part = place(gather_dp(piece, part), "dp", 1).reshape(-1, model_width)
        taken = patch_cube[:, part * group_bands : (part + 1) * group_bands].reshape(
            group_size * slot_count, group_bands * pixel_count
        )
        product = product + jnp.dot(taken, kernel_part, preferred_element_type=jnp.float32)
        patch_parts.append(taken)
        kernel_parts.append(kernel_part)
    embedded = scatter_band(
        product.astype(jnp.bfloat16).reshape(band_size, row_total, model_width), 0
    )
    valid_mask = jnp.arange(slot_count)[None, :] < counts[:, None]
    keep_col = valid_mask.reshape(row_total, 1).astype(jnp.float32)
    kept_flat = kept.reshape(row_total)
    pos_rows = jnp.take(pos_table, kept_flat, axis=0).astype(jnp.float32)
    start_rows = embedded.reshape(row_total, model_width) + embed_bias[None, :] + pos_rows
    gains = norm_gain.astype(jnp.float32)
    shifts = norm_bias.astype(jnp.float32)
    normed_full, norm_one_back = jax.vjp(layer_norm, start_rows, gains[0], shifts[0])
    normed = normed_full.astype(jnp.bfloat16)
    qkv_rows = jnp.dot(normed, qkv_full, preferred_element_type=jnp.float32).astype(jnp.bfloat16)
    shaped = qkv_rows.reshape(local_images, slot_count, 3, HEADS, HDIM)
    queries = shaped[:, :, 0]
    keys_arr = shaped[:, :, 1]
    values_arr = shaped[:, :, 2]
    scores = masked_scores(queries, keys_arr, valid_mask)
    row_peak = jnp.max(scores, axis=-1, keepdims=True)
    exponent = jnp.exp(scores - row_peak)
    row_total_sum = jnp.sum(exponent, axis=-1, keepdims=True)
    probs_low = (exponent / row_total_sum).astype(jnp.bfloat16)
    mixed_rows = jnp.einsum(
        "ghqk,gkhd->gqhd", probs_low, values_arr, preferred_element_type=jnp.float32
    )
    mixed_rows = mixed_rows.reshape(row_total, model_width).astype(jnp.bfloat16)
    middle = start_rows + jnp.dot(mixed_rows, out_full, preferred_element_type=jnp.float32)
    normed_two_full, norm_two_back = jax.vjp(layer_norm, middle, gains[1], shifts[1])
    normed_two = normed_two_full.astype(jnp.bfloat16)
    pre_act = (
        jnp.dot(normed_two, fc_in_full, preferred_element_type=jnp.float32)
        + bias_in.astype(jnp.float32)[None, :]
    )
    activ_full, gelu_back = jax.vjp(partial(jax.nn.gelu, approximate=False), pre_act)
    activation = activ_full.astype(jnp.bfloat16)
    final_rows = middle + jnp.dot(activation, fc_out_full, preferred_element_type=jnp.float32)
    result = (
        (final_rows * keep_col).astype(jnp.bfloat16).reshape(local_images, slot_count, model_width)
    )
    grad_final = cotangent.reshape(row_total, model_width).astype(jnp.float32) * keep_col
    grad_branch_two = grad_final.astype(jnp.bfloat16)
    grad_fc_out = inner(activation, grad_branch_two)
    (grad_pre_full,) = gelu_back(times_transpose(grad_branch_two, fc_out_full))
    grad_pre = grad_pre_full.astype(jnp.bfloat16)
    grad_bias_in = jnp.sum(grad_pre.astype(jnp.float32), axis=0)
    grad_fc_in = inner(normed_two, grad_pre)
    grad_mid_norm, grad_gain_two, grad_shift_two = norm_two_back(
        times_transpose(grad_pre, fc_in_full)
    )
    grad_middle = grad_final + grad_mid_norm
    grad_branch = grad_middle.astype(jnp.bfloat16)
    grad_out_w = inner(mixed_rows, grad_branch)
    grad_mixed = times_transpose(grad_branch, out_full).astype(jnp.bfloat16)
    grad_mixed = grad_mixed.reshape(local_images, slot_count, HEADS, HDIM)
    scores_again = masked_scores(queries, keys_arr, valid_mask)
    probs_again = jnp.exp(scores_again - row_peak) / row_total_sum
    grad_values = jnp.einsum(
        "ghqk,gqhd->gkhd",
        probs_again.astype(jnp.bfloat16),
        grad_mixed,
        preferred_element_type=jnp.float32,
    )
    grad_probs = jnp.einsum(
        "gqhd,gkhd->ghqk", grad_mixed, values_arr, preferred_element_type=jnp.float32
    )
    grad_scores = probs_again * (
        grad_probs - jnp.sum(grad_probs * probs_again, axis=-1, keepdims=True)
    )
    grad_scores = grad_scores.astype(jnp.bfloat16)
    grad_queries = jnp.einsum(
        "ghqk,gkhd->gqhd", grad_scores, keys_arr, preferred_element_type=jnp.float32
    ) * HDIM ** (-0.5)
    grad_keys = jnp.einsum(
        "ghqk,gqhd->gkhd", grad_scores, queries, preferred_element_type=jnp.float32
    ) * HDIM ** (-0.5)
    grad_qkv = jnp.stack([grad_queries, grad_keys, grad_values], axis=2)
    grad_qkv = grad_qkv.reshape(row_total, 3 * model_width).astype(jnp.bfloat16)
    grad_qkv_w = inner(normed, grad_qkv)
    grad_start_norm, grad_gain_one, grad_shift_one = norm_one_back(
        times_transpose(grad_qkv, qkv_full)
    )
    grad_start = grad_middle + grad_start_norm
    one_hot = (kept_flat[:, None] == jnp.arange(pos_table.shape[0])[None, :]).astype(jnp.float32)
    grad_pos = lax.dot_general(
        one_hot,
        grad_start,
        (((0,), (0,)), ((), ())),
        precision=lax.Precision.HIGHEST,
        preferred_element_type=jnp.float32,
    )
    grad_embed_bias = jnp.sum(grad_start, axis=0)
    grad_embed = grad_start.astype(jnp.bfloat16)
    flat_piece = place(gather_band(grad_embed), "band", 0).reshape(-1, model_width)
    weight_grads = [
        block.astype(jnp.bfloat16).reshape(device_count, -1, model_width)
        for block in (
            column_blocks(grad_qkv_w, model_width)
            + [grad_out_w]
            + column_blocks(grad_fc_in, model_width)
            + [grad_fc_out]
        )
    ]
    own_grads = lax.psum_scatter(
        jnp.concatenate(weight_grads, axis=1), ("dp", "band"), scatter_dimension=0
    ).astype(jnp.float32)
    own_blocks = [
        own_grads[first:last] for first, last in zip(weight_spots[:-1], weight_spots[1:])
    ]
    grad_qkv_own = jnp.concatenate(own_blocks[:3], axis=1)
    grad_out_own = own_blocks[3]
    grad_fc_in_own = jnp.concatenate(own_blocks[4:-1], axis=1)
    grad_fc_out_own = own_blocks[-1]
    small = sum_rows(
        jnp.concatenate(
            [
                grad_embed_bias[None],
                grad_gain_one[None],
                grad_gain_two[None],
                grad_shift_one[None],
                grad_shift_two[None],
                grad_bias_in.reshape(-1, model_width),
                grad_pos,
            ],
            axis=0,
        )
    )
    grad_bias_embed = small[0]
    grad_gains = small[1:3]
    grad_shifts = small[3:5]
    bias_rows = bias_in.shape[0] // model_width
    grad_bias_all = small[5 : 5 + bias_rows].reshape(-1)
    grad_pos_all = small[5 + bias_rows :]
    grad_groups = 2 * groups
    grad_bands = bands_dev // grad_groups
    received = []
    for part in range(grad_groups):
        first = (part % 2) * grad_bands * pixel_count
        taken = patch_parts[part // 2][:, first : first + grad_bands * pixel_count]
        grad_part = inner(taken, flat_piece).astype(jnp.bfloat16)
        grad_part = grad_part.reshape(grad_bands, dp_size, -1, model_width)
        own_part = scatter_dp(grad_part, 1, part)
        own_part = own_part.reshape(grad_bands, band_size, own_pixels, model_width)
        received.append(place(swap_band(own_part, 1), "band", 0))
    kernel_grads = jnp.stack(received, axis=1).reshape(band_total, own_pixels * model_width)
    update = jnp.concatenate(
        [
            times_transpose(flat_piece, kernel_part)
            .astype(jnp.bfloat16)
            .reshape(group_size, slot_count, group_bands, pixel_count)
            for kernel_part in kernel_parts
        ],
        axis=2,
    )
    grad_gen_kernel = inner(band_states, kernel_grads)
    grad_states_all = psum_small(times_transpose(kernel_grads, gen_kernel))
    grad_gen_bias = states[0][:, None] * grad_bias_embed[None, :]
    grad_bias_state = matmul(grad_bias_embed[None, :], bias_matrix.T)
    grad_sequence = jnp.concatenate([grad_bias_state, grad_states_all], axis=0)
    grad_token, grad_attn, grad_gain_gen, grad_ff_first, grad_ff_second = gen_backward(
        grad_sequence
    )
    grad_patches = update
    return (
        result,
        grad_patches,
        grad_token,
        grad_attn,
        grad_gain_gen,
        grad_ff_first,
        grad_ff_second,
        grad_gen_kernel,
        grad_gen_bias,
        grad_pos_all,
        grad_gains,
        grad_shifts,
        grad_qkv_own,
        grad_out_own,
        grad_fc_in_own,
        grad_bias_all,
        grad_fc_out_own,
    )


def solution(mesh):
    placed = (
        P("dp", None, "band", None),
        P(),
        P(),
        P(),
        P(),
        P(),
        P(None, ("dp", "band")),
        P(),
        P(),
        P(),
        P(),
        P(("dp", "band"), None),
        P(("dp", "band"), None),
        P(("dp", "band"), None),
        P(),
        P(("dp", "band"), None),
        P(),
        P(("dp", "band"), None),
        P(("dp", "band")),
        P(("dp", "band"), None, None),
    )
    return jax.shard_map(
        shards,
        mesh=mesh,
        in_specs=placed,
        out_specs=(
            P(("dp", "band"), None, None),
            P("dp", None, "band", None),
            P(),
            P(),
            P(),
            P(),
            P(),
            P(None, ("dp", "band")),
            P(),
            P(),
            P(),
            P(),
            P(("dp", "band"), None),
            P(("dp", "band"), None),
            P(("dp", "band"), None),
            P(),
            P(("dp", "band"), None),
        ),
        check_vma=False,
    )
```

```python
from functools import partial
import math

import jax
import jax.numpy as jnp
from jax import lax
from jax.experimental import pallas as pl
from jax.experimental.pallas import tpu as pltpu
from jax.sharding import PartitionSpec as P

HEADS = 12
HDIM = 64
GEN_HEADS = 4


def inner(left_arr, right_arr):
    return lax.dot_general(
        left_arr, right_arr, (((0,), (0,)), ((), ())), preferred_element_type=jnp.float32
    )


def times_transpose(left_arr, right_arr):
    return lax.dot_general(
        left_arr, right_arr, (((1,), (1,)), ((), ())), preferred_element_type=jnp.float32
    )


def bit_steps(size):
    steps = []
    step = 1
    while step < size:
        steps.append(step)
        step *= 2
    return steps


def swap(values, axis, step):
    size = lax.axis_size(axis)
    return lax.ppermute(values, axis, [(spot, spot ^ step) for spot in range(size)])


def turn(items, by):
    by = by % max(len(items), 1)
    return items[by:] + items[:by]


def gather_core(blocks):
    return [([key ^ 1 for key in keys], swap(block, "dp", 1)) for keys, block in blocks]


def place(blocks, axis, at):
    spot = lax.axis_index(axis)
    first = blocks[0][1]
    count = sum(len(keys) for keys, _ in blocks)
    shape = first.shape[1 : at + 1] + (count,) + first.shape[at + 1 :]
    whole = jnp.zeros(shape, first.dtype)
    for keys, block in blocks:
        for number, key in enumerate(keys):
            whole = lax.dynamic_update_index_in_dim(whole, block[number], spot ^ key, at)
    return whole


def add_low(left_arr, right_arr):
    return (left_arr.astype(jnp.float32) + right_arr.astype(jnp.float32)).astype(left_arr.dtype)


def split_half(values, at, step, left):
    left = sorted(left, reverse=True)
    shape = values.shape
    values = values.reshape(shape[:at] + (2,) * len(left) + shape[at + 1 :])
    dim = at + left.index(step)
    bit = (lax.axis_index("dp") // step) % 2
    rest = shape[:at] + (-1,) + shape[at + 1 :]
    send = lax.dynamic_index_in_dim(values, 1 - bit, dim, keepdims=False)
    keep = lax.dynamic_index_in_dim(values, bit, dim, keepdims=False)
    return send.reshape(rest), keep.reshape(rest)


def together(*arrays):
    return lax.optimization_barrier(arrays)


def column_blocks(matrix, width):
    return [matrix[:, spot : spot + width] for spot in range(0, matrix.shape[1], width)]


def run_kernel(body, args, in_specs, after=(), **options):
    count = len(after)

    def whole(*refs):
        body(*refs[count:])

    return pl.pallas_call(
        whole,
        in_specs=[pl.BlockSpec(memory_space=pl.ANY)] * count + in_specs,
        compiler_params=pltpu.CompilerParams(vmem_limit_bytes=60 * 1024 * 1024),
        cost_estimate=pl.CostEstimate(flops=1000, bytes_accessed=1000, transcendentals=0),
        **options,
    )(*after, *args)


def dot_nn(left_arr, right_arr):
    return lax.dot_general(
        left_arr, right_arr, (((1,), (0,)), ((), ())), preferred_element_type=jnp.float32
    )


def norm_stats(values):
    center = values - jnp.mean(values, axis=-1, keepdims=True)
    spread = jnp.mean(center * center, axis=-1, keepdims=True)
    scale = lax.rsqrt(spread + 1e-06)
    return center * scale, scale


def norm_back(unit, scale, gain, grad):
    weighted = grad * gain
    first = jnp.mean(weighted, axis=-1, keepdims=True)
    second = jnp.mean(weighted * unit, axis=-1, keepdims=True)
    grad_values = (weighted - first - unit * second) * scale
    grad_gain = jnp.sum(grad * unit, axis=0, keepdims=True)
    grad_shift = jnp.sum(grad, axis=0, keepdims=True)
    return grad_values, grad_gain, grad_shift


def block_body(part_count, tile_rows, ff_step, keys_lists, *refs):
    part_refs = refs[:part_count]
    weight_count = sum(len(keys_list) for keys_list in keys_lists)
    weight_refs = refs[part_count : part_count + weight_count]
    (
        spot_ref,
        base_ref,
        cot_ref,
        keep_ref,
        mask_ref,
        gain_ref,
        shift_ref,
        bias_ref,
        result_ref,
        start_grad_ref,
        embed_grad_ref,
        normed_ref,
        qkv_grad_ref,
        mixed_ref,
        branch_ref,
        normed_two_ref,
        pre_grad_ref,
        act_ref,
        sums_ref,
        bias_grad_ref,
        qkv_w,
        out_w,
        fc_in_w,
        fc_out_w,
        qkv_ref,
        probs_ref,
        total_ref,
        back_ref,
        mixed_grad_ref,
        sems,
    ) = refs[part_count + weight_count :]
    bf16 = jnp.bfloat16
    f32 = jnp.float32
    width = base_ref.shape[1]
    share = width // sum(len(keys) for keys in keys_lists[0])
    hidden = fc_in_w.shape[1]
    targets = (
        [(qkv_w, column, share) for column in range(3)]
        + [(out_w, 0, share)]
        + [(fc_in_w, column, share) for column in range(hidden // width)]
        + [(fc_out_w, 0, share * hidden // width)]
    )
    copies = {}
    for number, (target_ref, column, rows) in enumerate(targets):
        half, first = (0, number * share) if number < 6 else (1, (number - 6) * share)
        half_refs = weight_refs[: len(keys_lists[0])] if half == 0 else weight_refs[len(keys_lists[0]) :]
        for keys, weight_ref in zip(keys_lists[half], half_refs):
            for index, key in enumerate(keys):
                at = pl.multiple_of(jnp.bitwise_xor(spot_ref[0], key) * rows, rows)
                copy = pltpu.make_async_copy(
                    weight_ref.at[index, pl.ds(first, rows), :],
                    target_ref.at[pl.ds(at, rows), pl.ds(column * width, width)],
                    sems.at[sum(len(some) for some in copies.values())],
                )
                copy.start()
                copies.setdefault(id(target_ref), []).append(copy)

    def arrive(target_ref):
        for copy in copies[id(target_ref)]:
            copy.wait()

    row_total, width = base_ref.shape
    tiles = row_total // tile_rows
    head_pairs = HEADS // 2
    lanes = 2 * HDIM

    start = base_ref[...]
    for part_ref in part_refs:
        start = start + part_ref[...].astype(f32)
    unit_one, scale_one = norm_stats(start)
    normed = (unit_one * gain_ref[0:1] + shift_ref[0:1]).astype(bf16)
    normed_ref[...] = normed
    arrive(qkv_w)
    for spot in range(3):
        cols = slice(spot * width, (spot + 1) * width)
        qkv_ref[:, cols] = dot_nn(normed, qkv_w[:, cols]).astype(bf16)

    low_lanes = lax.broadcasted_iota(jnp.int32, (tile_rows, lanes), 1) < HDIM

    def half(values, odd):
        keep = jnp.logical_not(low_lanes) if odd else low_lanes
        return jnp.where(keep, values, jnp.zeros_like(values))

    def head_slices(pair, tile):
        rows = pl.ds(tile * tile_rows, tile_rows)
        cols = [
            pl.ds(pl.multiple_of(which * width + pair * lanes, lanes), lanes) for which in range(3)
        ]
        return rows, cols

    def attend(pair, carry):
        for tile in range(tiles):
            rows, cols = head_slices(pair, tile)
            queries, keys_arr, values_arr = [qkv_ref[rows, col] for col in cols]
            mixed = jnp.zeros((tile_rows, lanes), f32)
            for odd in range(2):
                scores = times_transpose(half(queries, odd), keys_arr) * HDIM ** (-0.5)
                scores = scores + mask_ref[tile]
                exponent = jnp.exp(scores - jnp.max(scores, axis=-1, keepdims=True))
                probs = exponent * (1.0 / jnp.sum(exponent, axis=-1, keepdims=True))
                probs_ref[(pair * 2 + odd) * tiles + tile] = probs
                mixed = mixed + dot_nn(probs.astype(bf16), half(values_arr, odd))
            mixed_ref[rows, cols[0]] = mixed.astype(bf16)
        return carry

    lax.fori_loop(0, head_pairs, attend, 0)
    arrive(out_w)
    middle = start + dot_nn(mixed_ref[...], out_w[...])
    unit_two, scale_two = norm_stats(middle)
    normed_two = (unit_two * gain_ref[1:2] + shift_ref[1:2]).astype(bf16)
    normed_two_ref[...] = normed_two
    total_ref[...] = middle
    back_ref[...] = jnp.zeros_like(back_ref)
    arrive(fc_in_w)
    arrive(fc_out_w)

    def feed(step, carry):
        cols = pl.ds(pl.multiple_of(step * ff_step, ff_step), ff_step)
        pre = dot_nn(normed_two_ref[...], fc_in_w[:, cols]) + bias_ref[:, cols]
        cdf = 0.5 * (1.0 + lax.erf(pre * 0.5**0.5))
        act = (pre * cdf).astype(bf16)
        act_ref[:, cols] = act
        slope = cdf + pre * (jnp.exp(-0.5 * pre * pre) * (2.0 * math.pi) ** (-0.5))
        pre_grad = slope * times_transpose(cot_ref[...], fc_out_w[cols, :])
        pre_grad = pre_grad.astype(bf16)
        pre_grad_ref[:, cols] = pre_grad
        bias_grad_ref[:, cols] = jnp.sum(pre_grad.astype(f32), axis=0, keepdims=True)
        total_ref[...] += dot_nn(act, fc_out_w[cols, :])
        back_ref[...] += times_transpose(pre_grad, fc_in_w[:, cols])
        return carry

    lax.fori_loop(0, fc_in_w.shape[1] // ff_step, feed, 0)
    result_ref[...] = (total_ref[...] * keep_ref[...]).astype(bf16)
    grad_norm, gain_two, shift_two = norm_back(unit_two, scale_two, gain_ref[1:2], back_ref[...])
    grad_middle = cot_ref[...].astype(f32) + grad_norm
    grad_branch = grad_middle.astype(bf16)
    branch_ref[...] = grad_branch
    mixed_grad_ref[...] = times_transpose(grad_branch, out_w[...]).astype(bf16)

    def attend_back(pair, carry):
        for tile in range(tiles):
            rows, cols = head_slices(pair, tile)
            queries, keys_arr, values_arr = [qkv_ref[rows, col] for col in cols]
            grad_mixed = mixed_grad_ref[rows, cols[0]]
            grads = [jnp.zeros((tile_rows, lanes), f32) for _ in range(3)]
            for odd in range(2):
                probs = probs_ref[(pair * 2 + odd) * tiles + tile]
                own_grad = half(grad_mixed, odd)
                grad_probs = times_transpose(own_grad, values_arr)
                grad_scores = probs * (
                    grad_probs - jnp.sum(grad_probs * probs, axis=-1, keepdims=True)
                )
                grad_scores = grad_scores.astype(bf16)
                grads[0] = grads[0] + dot_nn(grad_scores, half(keys_arr, odd))
                grads[1] = grads[1] + inner(grad_scores, half(queries, odd))
                grads[2] = grads[2] + inner(probs.astype(bf16), own_grad)
            for which, factor in enumerate((HDIM ** (-0.5), HDIM ** (-0.5), 1.0)):
                qkv_grad_ref[rows, cols[which]] = (grads[which] * factor).astype(bf16)
        return carry

    lax.fori_loop(0, head_pairs, attend_back, 0)
    back = jnp.zeros((row_total, width), f32)
    for spot in range(3):
        cols = slice(spot * width, (spot + 1) * width)
        back = back + times_transpose(qkv_grad_ref[:, cols], qkv_w[:, cols])
    grad_norm, gain_one, shift_one = norm_back(unit_one, scale_one, gain_ref[0:1], back)
    grad_start = grad_middle + grad_norm
    start_grad_ref[...] = grad_start
    embed_grad_ref[...] = grad_start.astype(bf16)
    sums_ref[...] = jnp.concatenate(
        [jnp.sum(grad_start, axis=0, keepdims=True), gain_one, gain_two, shift_one, shift_two]
        + [jnp.zeros((3, width), f32)],
        axis=0,
    )


def block(parts, weight_halves, spots, base, cot, keep, mask, gains, shifts, bias):
    row_total, width = base.shape
    tile_rows = mask.shape[1]
    hidden = bias.shape[1]
    bf16 = jnp.bfloat16
    f32 = jnp.float32
    keys_lists = [[keys for keys, _ in blocks] for blocks in weight_halves]
    weight_args = [block for blocks in weight_halves for _, block in blocks]
    pieces = sum(len(keys) for keys in keys_lists[0])
    inside = pl.BlockSpec(memory_space=pltpu.VMEM)
    outside = pl.BlockSpec(memory_space=pl.ANY)
    rows = (row_total, width)
    shapes = [
        (rows, bf16),
        (rows, f32),
        (rows, bf16),
        (rows, bf16),
        ((row_total, 3 * width), bf16),
        (rows, bf16),
        (rows, bf16),
        (rows, bf16),
        ((row_total, hidden), bf16),
        ((row_total, hidden), bf16),
        ((8, width), f32),
        ((1, hidden), f32),
    ]
    return run_kernel(
        partial(block_body, len(parts), tile_rows, 512, keys_lists),
        (*parts, *weight_args, spots, base, cot, keep, mask, gains, shifts, bias),
        [inside] * len(parts)
        + [outside] * len(weight_args)
        + [pl.BlockSpec(memory_space=pltpu.SMEM)]
        + [inside] * 7,
        out_shape=[jax.ShapeDtypeStruct(shape, kind) for shape, kind in shapes],
        out_specs=[inside] * len(shapes),
        scratch_shapes=[
            pltpu.VMEM((width, 3 * width), bf16),
            pltpu.VMEM((width, width), bf16),
            pltpu.VMEM((width, hidden), bf16),
            pltpu.VMEM((hidden, width), bf16),
            pltpu.VMEM((row_total, 3 * width), bf16),
            pltpu.VMEM((HEADS * row_total // tile_rows, tile_rows, tile_rows), f32),
            pltpu.VMEM(rows, f32),
            pltpu.VMEM(rows, f32),
            pltpu.VMEM(rows, bf16),
            pltpu.SemaphoreType.DMA(((5 + hidden // width) * pieces,)),
        ],
    )


def dot_full(left_arr, right_arr, left_dim=1, right_dim=0):
    return lax.dot_general(
        left_arr,
        right_arr,
        (((left_dim,), (right_dim,)), ((), ())),
        precision=lax.Precision.HIGHEST,
        preferred_element_type=jnp.float32,
    )


def head_part(values, head):
    size = values.shape[1] // GEN_HEADS
    lane = lax.broadcasted_iota(jnp.int32, values.shape, 1)
    inside = jnp.logical_and(lane >= head * size, lane < (head + 1) * size)
    return jnp.where(inside, values, 0.0)


def generate_body(
    waves_ref,
    token_ref,
    attn_hbm,
    gain_hbm,
    ff_in_hbm,
    ff_out_hbm,
    bias_w_hbm,
    columns_hbm,
    kernel_ref,
    embed_bias_ref,
    low_ref,
    states_ref,
    rows_ref,
    weights_ref,
    pre_ref,
    scales_ref,
    attn_ref,
    gain_ref,
    ff_in_ref,
    ff_out_ref,
    bias_w_ref,
    columns_ref,
    sems,
):
    f32 = jnp.float32
    copies = [
        pltpu.make_async_copy(source, target, sems.at[number])
        for number, (source, target) in enumerate(
            (
                (attn_hbm, attn_ref),
                (gain_hbm, gain_ref),
                (ff_in_hbm, ff_in_ref),
                (ff_out_hbm, ff_out_ref),
                (columns_hbm, columns_ref),
                (bias_w_hbm, bias_w_ref),
            )
        )
    ]
    for copy in copies:
        copy.start()
    bands = waves_ref.shape[1]
    width = token_ref.shape[1]
    padded = rows_ref.shape[1]
    square = (bands, bands)
    diagonal = lax.broadcasted_iota(jnp.int32, square, 0) == lax.broadcasted_iota(
        jnp.int32, square, 1
    )
    waves = jnp.broadcast_to(waves_ref[...].astype(f32), square)
    column = jnp.sum(jnp.where(diagonal, waves, 0.0), axis=1, keepdims=True)
    lane = lax.broadcasted_iota(jnp.int32, (bands, width), 1)
    half_width = width // 2
    number = jnp.where(lane < half_width, lane, lane - half_width).astype(f32)
    angles = column * jnp.exp(number * (-math.log(10000.0) / half_width))
    wave = jnp.where(lane < half_width, jnp.sin(angles), jnp.cos(angles))
    sequence = jnp.concatenate(
        [wave, token_ref[...].astype(f32), jnp.zeros((padded - bands - 1, width), f32)], axis=0
    )
    rows_ref[0] = sequence
    copies[0].wait()
    copies[1].wait()
    for which in range(3):
        rows_ref[1 + which] = dot_full(sequence, attn_ref[which].astype(f32))
    queries = rows_ref[1]
    keys_arr = rows_ref[2]
    values_arr = rows_ref[3]
    key_spot = lax.broadcasted_iota(jnp.int32, (padded, padded), 1)
    mixed = jnp.zeros((padded, width), f32)
    for head in range(GEN_HEADS):
        scores = dot_full(head_part(queries, head), keys_arr, 1, 1)
        scores = scores * (1.0 / math.sqrt(width // GEN_HEADS))
        scores = jnp.where(key_spot <= bands, scores, -1e30)
        exponent = jnp.exp(scores - jnp.max(scores, axis=-1, keepdims=True))
        weights = exponent / jnp.sum(exponent, axis=-1, keepdims=True)
        weights_ref[head] = weights
        mixed = mixed + dot_full(weights, head_part(values_arr, head))
    rows_ref[4] = mixed
    unit_one, scale_one = norm_stats(sequence + dot_full(mixed, attn_ref[3].astype(f32)))
    rows_ref[5] = unit_one
    first = unit_one * gain_ref[0:1].astype(f32)
    copies[2].wait()
    pre = dot_full(first, ff_in_ref[...].astype(f32))
    pre_ref[...] = pre
    hidden = pre * (0.5 * (1.0 + lax.erf(pre * 0.5**0.5)))
    copies[3].wait()
    unit_two, scale_two = norm_stats(first + dot_full(hidden, ff_out_ref[...].astype(f32)))
    rows_ref[6] = unit_two
    states = unit_two * gain_ref[1:2].astype(f32)
    states_ref[...] = states
    scales_ref[0] = jnp.broadcast_to(scale_one, (padded, width))
    scales_ref[1] = jnp.broadcast_to(scale_two, (padded, width))
    low = states[:bands].astype(jnp.bfloat16)
    low_ref[...] = low
    features = kernel_ref.shape[2]
    copies[4].wait()
    for pixel in range(kernel_ref.shape[0]):
        cols = slice(pixel * features, (pixel + 1) * features)
        kernel_ref[pixel] = dot_nn(low, columns_ref[:, cols]).astype(jnp.bfloat16)
    copies[5].wait()
    token_state = states[bands : bands + 8]
    embed_bias_ref[...] = dot_full(token_state, bias_w_ref[...].astype(f32))


def generate_fast(wavelengths, token, gen_attn, gen_gain, ff_in, ff_out, gen_bias, columns):
    f32 = jnp.float32
    bf16 = jnp.bfloat16
    bands = wavelengths.shape[0]
    width = token.shape[0]
    padded = -(-(bands + 1) // 8) * 8
    features = gen_bias.shape[1]
    shapes = [
        ((columns.shape[1] // features, bands, features), bf16),
        ((8, features), f32),
        ((bands, width), bf16),
        ((padded, width), f32),
        ((7, padded, width), f32),
        ((GEN_HEADS, padded, padded), f32),
        ((padded, ff_in.shape[1]), f32),
        ((2, padded, width), f32),
    ]
    inside = pl.BlockSpec(memory_space=pltpu.VMEM)
    outside = pl.BlockSpec(memory_space=pl.ANY)
    weights = (gen_attn, gen_gain, ff_in, ff_out, gen_bias, columns)
    return run_kernel(
        generate_body,
        (wavelengths[None], token[None], *weights),
        out_shape=[jax.ShapeDtypeStruct(shape, kind) for shape, kind in shapes],
        in_specs=[inside] * 2 + [outside] * 6,
        out_specs=[inside] * len(shapes),
        scratch_shapes=[pltpu.VMEM(weight.shape, bf16) for weight in weights]
        + [pltpu.SemaphoreType.DMA((6,))],
    )


def generate_back_body(
    grad_ref,
    grad_bias_ref,
    attn_ref,
    gain_ref,
    ff_in_ref,
    ff_out_ref,
    bias_w_ref,
    states_ref,
    rows_ref,
    weights_ref,
    pre_ref,
    scales_ref,
    token_out,
    attn_out,
    gain_out,
    ff_in_out,
    ff_out_out,
    bias_out,
):
    f32 = jnp.float32
    bands, width = grad_ref.shape
    padded = rows_ref.shape[1]
    head_scale = 1.0 / math.sqrt(width // GEN_HEADS)
    bias_grad = grad_bias_ref[...]
    row_spot = lax.broadcasted_iota(jnp.int32, (padded - bands, width), 0)
    token_grad = dot_full(bias_grad, bias_w_ref[...].astype(f32), 1, 1)
    token_grad = jnp.where(row_spot == 0, token_grad[0:1], 0.0)
    grad_states = jnp.concatenate([grad_ref[...], token_grad], axis=0)
    token_state = states_ref[bands : bands + 8]
    first_row = lax.broadcasted_iota(jnp.int32, token_state.shape, 0) == 0
    bias_out[...] = dot_full(jnp.where(first_row, token_state, 0.0), bias_grad, 0, 0)
    unit_one = rows_ref[5]
    gain_one = gain_ref[0:1].astype(f32)
    gain_two = gain_ref[1:2].astype(f32)
    grad_two, gain_two_grad, _ = norm_back(rows_ref[6], scales_ref[1], gain_two, grad_states)
    pre = pre_ref[...]
    cdf = 0.5 * (1.0 + lax.erf(pre * 0.5**0.5))
    ff_out_out[...] = dot_full(pre * cdf, grad_two, 0, 0)
    slope = cdf + pre * (jnp.exp(-0.5 * pre * pre) * (2.0 * math.pi) ** (-0.5))
    grad_pre = slope * dot_full(grad_two, ff_out_ref[...].astype(f32), 1, 1)
    ff_in_out[...] = dot_full(unit_one * gain_one, grad_pre, 0, 0)
    grad_first = grad_two + dot_full(grad_pre, ff_in_ref[...].astype(f32), 1, 1)
    grad_one, gain_one_grad, _ = norm_back(unit_one, scales_ref[0], gain_one, grad_first)
    gain_out[...] = jnp.concatenate([gain_one_grad, gain_two_grad], axis=0)
    attn_out[3] = dot_full(rows_ref[4], grad_one, 0, 0)
    grad_mixed = dot_full(grad_one, attn_ref[3].astype(f32), 1, 1)
    sequence = rows_ref[0]
    queries = rows_ref[1]
    keys_arr = rows_ref[2]
    values_arr = rows_ref[3]
    grads = [jnp.zeros((padded, width), f32) for _ in range(3)]
    for head in range(GEN_HEADS):
        weights = weights_ref[head]
        own_grad = head_part(grad_mixed, head)
        grad_weights = dot_full(own_grad, values_arr, 1, 1)
        grad_scores = weights * (
            grad_weights - jnp.sum(grad_weights * weights, axis=-1, keepdims=True)
        )
        grad_scores = grad_scores * head_scale
        grads[0] = grads[0] + dot_full(grad_scores, head_part(keys_arr, head))
        grads[1] = grads[1] + dot_full(grad_scores, head_part(queries, head), 0, 0)
        grads[2] = grads[2] + dot_full(weights, own_grad, 0, 0)
    grad_sequence = grad_one
    for which in range(3):
        attn_out[which] = dot_full(sequence, grads[which], 0, 0)
        grad_sequence = grad_sequence + dot_full(
            grads[which], attn_ref[which].astype(f32), 1, 1
        )
    token_out[...] = grad_sequence[bands : bands + 1]


def generate_back(grad_states, grad_bias, gen_attn, gen_gain, ff_in, ff_out, gen_bias, kept_arrs):
    f32 = jnp.float32
    width = gen_gain.shape[1]
    shapes = [
        (1, width),
        gen_attn.shape,
        gen_gain.shape,
        ff_in.shape,
        ff_out.shape,
        gen_bias.shape,
    ]
    inside = pl.BlockSpec(memory_space=pltpu.VMEM)
    return run_kernel(
        generate_back_body,
        (grad_states, grad_bias, gen_attn, gen_gain, ff_in, ff_out, gen_bias, *kept_arrs),
        out_shape=[jax.ShapeDtypeStruct(shape, f32) for shape in shapes],
        in_specs=[inside] * (7 + len(kept_arrs)),
        out_specs=[inside] * len(shapes),
    )


def fill_kernel(keys_lists, piece_refs, spot, mat_ref, bands, pixels):
    for keys, piece_ref in zip(keys_lists, piece_refs):
        for number, key in enumerate(keys):
            share = piece_ref.shape[2]
            first = jnp.bitwise_xor(spot, key) * share
            for band in range(bands):
                rows = pl.ds(pl.multiple_of(band * pixels + first, share), share)
                mat_ref[rows, :] = piece_ref[number, band]


def fill_step(keys_lists, piece_refs, spot, mat_ref, band_step, group_steps):
    pixels = mat_ref.shape[0] // band_step
    step = pl.program_id(0)
    used = 0
    for group, keys_list in enumerate(keys_lists):
        group_refs = piece_refs[used : used + len(keys_list)]
        used += len(keys_list)

        @pl.when(step // group_steps == group)
        def _(keys_list=keys_list, group_refs=group_refs):
            fill_kernel(keys_list, group_refs, spot, mat_ref, band_step, pixels)


def embed_body(keys_lists, group_steps, band_step, *refs):
    spot_ref, patch_ref = refs[:2]
    count = sum(len(keys_list) for keys_list in keys_lists)
    piece_refs = refs[2 : 2 + count]
    *out_refs, mat_ref, total_ref = refs[2 + count :]
    step = pl.program_id(0)
    fill_step(keys_lists, piece_refs, spot_ref[0], mat_ref, band_step, group_steps)

    @pl.when(step == 0)
    def _():
        total_ref[...] = jnp.zeros_like(total_ref)

    total_ref[...] += dot_nn(patch_ref[...], mat_ref[...])

    @pl.when(step == pl.num_programs(0) - 1)
    def _():
        for key, out_ref in enumerate(out_refs):
            rows = out_ref.shape[0]
            first = pl.multiple_of(jnp.bitwise_xor(spot_ref[1], key) * rows, rows)
            out_ref[...] = total_ref[pl.ds(first, rows), :].astype(out_ref.dtype)


def piece_specs(kernel_groups, band_step):
    group_steps = kernel_groups[0][0][1].shape[1] // band_step
    specs = []
    arrays = []
    for group, blocks in enumerate(kernel_groups):
        for keys, block in blocks:
            specs.append(
                pl.BlockSpec(
                    (len(keys), band_step) + block.shape[2:],
                    lambda step, group=group: (
                        0,
                        jnp.clip(step - group * group_steps, 0, group_steps - 1),
                        0,
                        0,
                    ),
                )
            )
            arrays.append(block)
    keys_lists = [[keys for keys, _ in blocks] for blocks in kernel_groups]
    return specs, arrays, keys_lists, group_steps


def embed_share(spots, patch_rows, kernel_groups, owners):
    row_total = patch_rows.shape[0]
    blocks = kernel_groups[0]
    group_bands = blocks[0][1].shape[1]
    width = blocks[0][1].shape[3]
    pixels = sum(len(keys) for keys, _ in blocks) * blocks[0][1].shape[2]
    band_step = min(4, group_bands)
    depth = band_step * pixels
    specs, arrays, keys_lists, group_steps = piece_specs(kernel_groups, band_step)
    rows = row_total // owners
    return run_kernel(
        partial(embed_body, keys_lists, group_steps, band_step),
        [spots, patch_rows, *arrays],
        [
            pl.BlockSpec(memory_space=pltpu.SMEM),
            pl.BlockSpec((row_total, depth), lambda step: (0, step)),
        ]
        + specs,
        grid=(group_steps * len(kernel_groups),),
        out_shape=[jax.ShapeDtypeStruct((rows, width), jnp.bfloat16)] * owners,
        out_specs=[pl.BlockSpec((rows, width), lambda step: (0, 0))] * owners,
        scratch_shapes=[
            pltpu.VMEM((depth, width), jnp.bfloat16),
            pltpu.VMEM((row_total, width), jnp.float32),
        ],
    )


def kernel_grad_body(dp_size, band_step, *refs):
    spot_ref, patch_ref = refs[:2]
    *grad_refs, send_ref, keep_ref, hold_ref = refs[2:]
    rows = grad_refs[0].shape[0]
    total = 0.0
    for key, grad_ref in enumerate(grad_refs):
        first = pl.multiple_of(jnp.bitwise_xor(spot_ref[1], key) * rows, rows)
        total = total + inner(patch_ref[pl.ds(first, rows), :], grad_ref[...])
    hold_ref[...] = total.astype(hold_ref.dtype)
    pixels = hold_ref.shape[0] // band_step
    share = pixels // dp_size
    core = lax.rem(spot_ref[0], 2)
    for band in range(band_step):
        for chip in range(dp_size // 2):
            base = band * pixels + chip * 2 * share
            kept = pl.multiple_of(base + core * share, share)
            sent = pl.multiple_of(base + (1 - core) * share, share)
            keep_ref[band, chip] = hold_ref[pl.ds(kept, share), :]
            send_ref[band, chip] = hold_ref[pl.ds(sent, share), :]


def kernel_grad_part(spots, patch_rows, grads, first_band, group_bands, bands_dev, dp_size, after):
    row_total = patch_rows.shape[0]
    width = grads[0].shape[1]
    band_step = min(2, group_bands)
    pixels = patch_rows.shape[1] // bands_dev
    depth = band_step * pixels
    offset = first_band // band_step
    share = pixels // dp_size
    half = (group_bands, dp_size // 2, share, width)
    half_spec = pl.BlockSpec((band_step,) + half[1:], lambda step: (step, 0, 0, 0))
    return run_kernel(
        partial(kernel_grad_body, dp_size, band_step),
        (spots, patch_rows, *grads),
        after=after,
        grid=(group_bands // band_step,),
        out_shape=[jax.ShapeDtypeStruct(half, jnp.bfloat16)] * 2,
        in_specs=[
            pl.BlockSpec(memory_space=pltpu.SMEM),
            pl.BlockSpec((row_total, depth), lambda step: (0, offset + step)),
        ]
        + [pl.BlockSpec(grad.shape, lambda step: (0, 0)) for grad in grads],
        out_specs=[half_spec, half_spec],
        scratch_shapes=[pltpu.VMEM((depth, width), jnp.bfloat16)],
    )


def patch_grad_body(keys_lists, grad_count, group_steps, band_step, *refs):
    spot_ref = refs[0]
    grad_refs = refs[1 : 1 + grad_count]
    out_ref, mat_ref = refs[-2:]
    piece_refs = refs[1 + grad_count : -2]
    fill_step(keys_lists, piece_refs, spot_ref[0], mat_ref, band_step, group_steps)
    for key, grad_ref in enumerate(grad_refs):
        rows = grad_ref.shape[0]
        first = pl.multiple_of(jnp.bitwise_xor(spot_ref[1], key) * rows, rows)
        out_ref[pl.ds(first, rows), :] = times_transpose(grad_ref[...], mat_ref[...]).astype(
            out_ref.dtype
        )


def patch_grad(spots, grads, kernel_groups, pixels, after):
    rows, width = grads[0].shape
    row_total = rows * len(grads)
    band_step = min(4, kernel_groups[0][0][1].shape[1])
    depth = band_step * pixels
    specs, arrays, keys_lists, group_steps = piece_specs(kernel_groups, band_step)
    steps = group_steps * len(kernel_groups)
    return run_kernel(
        partial(patch_grad_body, keys_lists, len(grads), group_steps, band_step),
        [spots, *grads, *arrays],
        [pl.BlockSpec(memory_space=pltpu.SMEM)]
        + [pl.BlockSpec(grad.shape, lambda step: (0, 0)) for grad in grads]
        + specs,
        after=after,
        grid=(steps,),
        out_shape=jax.ShapeDtypeStruct((row_total, steps * depth), jnp.bfloat16),
        out_specs=pl.BlockSpec((row_total, depth), lambda step: (0, step)),
        scratch_shapes=[pltpu.VMEM((depth, width), jnp.bfloat16)],
    )


def states_grad_body(batches, low_ref, columns_ref, *refs):
    *piece_refs, spot_ref, grad_ref, part_ref, hold_ref = refs
    pixels, bands, width = piece_refs[0].shape
    for number, piece_ref in enumerate(piece_refs):
        key, batch = divmod(number, batches)
        first = (jnp.bitwise_xor(spot_ref[1], key) * batches + batch) * bands
        hold_ref[:, pl.ds(pl.multiple_of(first, bands), bands), :] = piece_ref[...]
    total = 0.0
    for pixel in range(pixels):
        cols = slice(pixel * width, (pixel + 1) * width)
        grads = hold_ref[pixel]
        grad_ref[:, cols] = inner(low_ref[...], grads)
        total = total + times_transpose(grads, columns_ref[:, cols])
    part_ref[...] = total


def states_grad(spots, low, columns, pieces):
    batch_lists = pieces
    pieces = [piece for batch_list in batch_lists for piece in batch_list]
    pixels, bands, width = pieces[0].shape
    if bands % 16:
        blocks = [([key], piece[None]) for key, piece in enumerate(pieces)]
        whole = place(blocks, "band", 1).reshape(pixels, -1, width)
        grads = whole.transpose(1, 0, 2).reshape(low.shape[0], -1)
        return inner(low, grads), times_transpose(grads, columns)
    inside = pl.BlockSpec(memory_space=pltpu.VMEM)
    return run_kernel(
        partial(states_grad_body, len(batch_lists[0])),
        (low, columns, *pieces, spots),
        out_shape=[
            jax.ShapeDtypeStruct(columns.shape, jnp.float32),
            jax.ShapeDtypeStruct(low.shape, jnp.float32),
        ],
        in_specs=[inside] * (2 + len(pieces)) + [pl.BlockSpec(memory_space=pltpu.SMEM)],
        out_specs=[inside, inside],
        scratch_shapes=[pltpu.VMEM((pixels, bands * len(pieces), width), jnp.bfloat16)],
    )


def flatten_body(in_ref, out_ref):
    out_ref[...] = in_ref[...].reshape(out_ref.shape)


def flatten_rows(cube, after):
    rows, bands, pixels = cube.shape
    step_rows = 64
    return run_kernel(
        flatten_body,
        (cube,),
        [pl.BlockSpec((step_rows, bands, pixels), lambda step: (step, 0, 0))],
        after=after,
        grid=(rows // step_rows,),
        out_shape=jax.ShapeDtypeStruct((rows, bands * pixels), cube.dtype),
        out_specs=pl.BlockSpec((step_rows, bands * pixels), lambda step: (step, 0)),
    )


def unflatten_rows(flat, bands, after):
    rows, depth = flat.shape
    step_rows = 64
    return run_kernel(
        flatten_body,
        (flat,),
        [pl.BlockSpec((step_rows, depth), lambda step: (step, 0))],
        after=after,
        grid=(rows // step_rows,),
        out_shape=jax.ShapeDtypeStruct((rows, bands, depth // bands), flat.dtype),
        out_specs=pl.BlockSpec((step_rows, bands, depth // bands), lambda step: (step, 0, 0)),
    )


def stack_body(*refs):
    *part_refs, out_ref, hold_ref = refs
    width = out_ref.shape[1]
    first = 0
    for part_ref in part_refs:
        rows = part_ref.shape[0]
        for spot in range(0, part_ref.shape[1], width):
            hold_ref[pl.ds(first, rows), :] = part_ref[:, spot : spot + width].astype(jnp.float32)
            first += rows
    out_ref[...] = hold_ref[...].astype(out_ref.dtype)


def stack_weights(shards_in):
    width = shards_in[-1].shape[1]
    if any(shard.shape[0] % 8 for shard in shards_in):
        return jnp.concatenate(
            [part for shard in shards_in for part in column_blocks(shard, width)], axis=0
        )
    row_total = sum(shard.size for shard in shards_in) // width
    inside = pl.BlockSpec(memory_space=pltpu.VMEM)
    return run_kernel(
        stack_body,
        shards_in,
        [inside] * len(shards_in),
        out_shape=jax.ShapeDtypeStruct((row_total, width), shards_in[0].dtype),
        out_specs=inside,
        scratch_shapes=[pltpu.VMEM((row_total, width), jnp.float32)],
    )


def plane_body(block_rows, spot_ref, *refs):
    *stack_refs, first_ref, last_ref, hold_ref = refs
    band_size = len(stack_refs)
    for key, stack_ref in enumerate(stack_refs):
        owner = jnp.bitwise_xor(spot_ref[1], key)
        values = stack_ref[...].astype(jnp.float32)
        done = 0
        for rows in block_rows:
            at = pl.multiple_of(done * band_size + owner * rows, 8)
            hold_ref[pl.ds(at, rows), :] = values[done : done + rows]
            done += rows
    half = first_ref.shape[0]
    first_ref[...] = hold_ref[:half, :].astype(first_ref.dtype)
    last_ref[...] = hold_ref[half:, :].astype(last_ref.dtype)


def plane_weights(spots, stacks, block_rows):
    row_total, width = stacks[0].shape
    band_size = len(stacks)
    half = row_total * band_size // 2
    if any(rows % 8 for rows in block_rows):
        whole = place([([key], stack[None]) for key, stack in enumerate(stacks)], "band", 0)
        parts = []
        done = 0
        for rows in block_rows:
            parts.append(whole[:, done : done + rows].reshape(-1, width))
            done += rows
        merged = jnp.concatenate(parts, axis=0)
        return merged[:half], merged[half:]
    inside = pl.BlockSpec(memory_space=pltpu.VMEM)
    return run_kernel(
        partial(plane_body, block_rows),
        (spots, *stacks),
        [pl.BlockSpec(memory_space=pltpu.SMEM)] + [inside] * band_size,
        out_shape=[jax.ShapeDtypeStruct((half, width), stacks[0].dtype)] * 2,
        out_specs=[inside] * 2,
        scratch_shapes=[pltpu.VMEM((row_total * band_size, width), jnp.float32)],
    )


def weight_grad_body(dp_size, spot_ref, *refs):
    (
        normed_ref,
        qkv_grad_ref,
        mixed_ref,
        branch_ref,
        normed_two_ref,
        pre_grad_ref,
        act_ref,
        cot_ref,
        *out_refs,
        hold_ref,
        feed_ref,
        sems,
    ) = refs
    width = normed_ref.shape[1]
    share = width // dp_size
    hidden = act_ref.shape[1]
    core = lax.rem(spot_ref[0], 2)
    copies = []

    def send(source_ref, rows, half, first):
        for chip in range(dp_size // 2):
            for other in range(2):
                owner = chip * 2 + (core if other == 0 else 1 - core)
                copy = pltpu.make_async_copy(
                    source_ref.at[pl.ds(pl.multiple_of(owner * rows, rows), rows), :],
                    out_refs[half * 2 + other].at[chip, pl.ds(first, rows), :],
                    sems.at[len(copies)],
                )
                copy.start()
                copies.append(copy)

    makers = (
        [(normed_ref, qkv_grad_ref, column) for column in range(3)]
        + [(mixed_ref, branch_ref, 0)]
        + [(normed_two_ref, pre_grad_ref, column) for column in range(hidden // width)]
    )
    for number, (left_ref, right_ref, column) in enumerate(makers):
        cols = slice(column * width, (column + 1) * width)
        hold_ref[number] = inner(left_ref[...], right_ref[:, cols]).astype(hold_ref.dtype)
        send(hold_ref.at[number], share, number // 6, number % 6 * share)
    for column in range(hidden // width):
        cols = slice(column * width, (column + 1) * width)
        feed_ref[cols, :] = inner(act_ref[:, cols], cot_ref[...]).astype(feed_ref.dtype)
    send(feed_ref, hidden // dp_size, 1, 2 * share)
    for copy in copies:
        copy.wait()


def weight_grad(spots, dp_size, pairs, after):
    width = pairs[0][0].shape[1]
    hidden = pairs[3][0].shape[1]
    bf16 = jnp.bfloat16
    half = (dp_size // 2, 6 * width // dp_size, width)
    inside = pl.BlockSpec(memory_space=pltpu.VMEM)
    outside = pl.BlockSpec(memory_space=pl.ANY)
    return run_kernel(
        partial(weight_grad_body, dp_size),
        [spots] + [single for pair in pairs for single in pair],
        [pl.BlockSpec(memory_space=pltpu.SMEM)] + [inside] * 8,
        after=after,
        out_shape=[jax.ShapeDtypeStruct(half, bf16)] * 4,
        out_specs=[outside] * 4,
        scratch_shapes=[
            pltpu.VMEM((4 + hidden // width, width, width), bf16),
            pltpu.VMEM((hidden, width), bf16),
            pltpu.SemaphoreType.DMA(((5 + hidden // width) * dp_size,)),
        ],
    )


def shards(
    patches,
    bias_token,
    gen_attn,
    gen_gain,
    gen_ff_in,
    gen_ff_out,
    gen_kernel,
    gen_bias,
    pos_table,
    norm_gain,
    norm_bias,
    w_qkv,
    w_out,
    w_fc1,
    bias_in,
    w_fc2,
    wavelengths,
    kept,
    counts,
    cotangent,
):
    group_size, slot_count, bands_dev, pixel_count = patches.shape
    dp_size = lax.axis_size("dp")
    band_size = lax.axis_size("band")
    device_count = dp_size * band_size
    local_images = group_size // band_size
    model_width = w_out.shape[1]
    row_total = local_images * slot_count
    own_pixels = pixel_count // device_count
    share = own_pixels * band_size
    groups = 2
    group_bands = bands_dev // groups
    band_total = bands_dev * band_size
    gen_width = bias_token.shape[0]
    f32 = jnp.float32
    bf16 = jnp.bfloat16
    spot = lax.axis_index("band")
    spots = jnp.stack([lax.axis_index("dp"), spot]).astype(jnp.int32)

    own_kernel, embed_bias, band_states, *gen_kept = generate_fast(
        wavelengths,
        bias_token,
        gen_attn,
        gen_gain,
        gen_ff_in,
        gen_ff_out,
        gen_bias,
        gen_kernel,
    )
    hidden = w_fc1.shape[1]
    weight_rows = [w_qkv.shape[0]] * (4 + hidden // model_width) + [w_fc2.shape[0]]
    stack = stack_weights((w_qkv, w_out, w_fc1, w_fc2))
    patch_rows = flatten_rows(
        patches.reshape(group_size * slot_count, bands_dev, pixel_count), (own_kernel,)
    )
    own_kernel = own_kernel.reshape(own_pixels, band_size, bands_dev, model_width)
    other_bands = range(1, band_size)
    dp_steps = bit_steps(dp_size)[1:]
    orders = [turn(dp_steps, group) for group in range(groups)]

    sent = [
        lax.dynamic_index_in_dim(own_kernel, spot ^ key, 1, keepdims=False).transpose(1, 0, 2)
        for key in range(band_size)
    ]
    got = [swap(sent[key], "band", key) for key in other_bands]
    *got, patch_rows, stack = together(*got, patch_rows, stack)
    piece = place(
        [([key], block[None]) for key, block in enumerate([sent[0]] + got)], "band", 1
    ).reshape(bands_dev, share, model_width)

    held = [
        piece[group * group_bands : (group + 1) * group_bands][None] for group in range(groups)
    ]
    held_keys = [[0] for _ in range(groups)]
    stacks = [stack]
    stack_keys = list(other_bands)
    for stage in range(len(dp_steps)):
        last = stage == len(dp_steps) - 1
        now_keys = stack_keys if last else stack_keys[:2]
        stack_keys = stack_keys[len(now_keys) :]
        got = [swap(held[group], "dp", orders[group][stage]) for group in range(groups)]
        got += [swap(held[group], "dp", 1) for group in range(groups) if last]
        got += [swap(stack, "band", key) for key in now_keys]
        stack, *got = together(stack, *got)
        stacks += got[len(got) - len(now_keys) :]
        if not last:
            for group in range(groups):
                held[group] = jnp.concatenate([held[group], got[group]], axis=0)
                held_keys[group] += [key ^ orders[group][stage] for key in held_keys[group]]
    kernel_groups = []
    for group in range(groups):
        late_keys = [key ^ orders[group][-1] for key in held_keys[group]]
        blocks = [(held_keys[group], held[group]), (late_keys, got[group])]
        blocks.append(([key ^ 1 for key in held_keys[group]], got[groups + group]))
        blocks += gather_core([(late_keys, got[group])])
        kernel_groups.append(blocks)

    planes = plane_weights(spots, stacks, weight_rows)
    got = [swap(plane, "dp", orders[half][0]) for half, plane in enumerate(planes)]
    embedded = embed_share(spots, patch_rows, kernel_groups, band_size)
    *embedded, first_got, last_got = together(*embedded, *got)
    held = [
        jnp.concatenate([plane[None], got[None]], axis=0)
        for plane, got in zip(planes, (first_got, last_got))
    ]
    held_keys = [[0, orders[half][0]] for half in range(2)]
    for stage in range(1, len(dp_steps) - 1):
        for half in range(2):
            step = orders[half][stage]
            held[half] = jnp.concatenate([held[half], swap(held[half], "dp", step)], axis=0)
            held_keys[half] = held_keys[half] + [key ^ step for key in held_keys[half]]
    got = [swap(held[half], "dp", orders[half][-1]) for half in range(2)]
    parts = [embedded[0]] + [swap(embedded[key], "band", key) for key in other_bands]
    held[0], held[1], got[0], got[1], *parts = together(*held, *got, *parts)
    weight_halves = []
    for half in range(2):
        blocks = [(held_keys[half], held[half])]
        blocks.append(([key ^ orders[half][-1] for key in held_keys[half]], got[half]))
        weight_halves.append(blocks + gather_core(blocks))

    valid_mask = jnp.arange(slot_count)[None, :] < counts[:, None]
    keep_col = valid_mask.reshape(row_total, 1)
    kept_flat = kept.reshape(row_total)
    pos_rows = jnp.take(pos_table, kept_flat, axis=0).astype(f32)
    base = embed_bias[0:1] + pos_rows
    tile_images = 2 if local_images % 2 == 0 else 1
    tile_rows = tile_images * slot_count
    image_spot = jnp.arange(tile_rows) // slot_count
    same_image = image_spot[:, None] == image_spot[None, :]
    mask = jnp.where(same_image[None] & valid_mask.reshape(-1, 1, tile_rows), 0.0, -1e30)
    cot = jnp.where(keep_col, cotangent.reshape(row_total, model_width), 0)
    (
        result,
        grad_start,
        grad_embed,
        normed,
        grad_qkv,
        mixed_rows,
        grad_branch,
        normed_two,
        grad_pre,
        activation,
        sums,
        grad_bias_in,
    ) = block(
        parts,
        weight_halves,
        spots,
        base,
        cot,
        keep_col.astype(f32),
        mask.astype(f32),
        norm_gain.astype(f32),
        norm_bias.astype(f32),
        bias_in.astype(f32)[None],
    )

    halves = weight_grad(
        spots,
        dp_size,
        (
            (normed, grad_qkv),
            (mixed_rows, grad_branch),
            (normed_two, grad_pre),
            (activation, cot),
        ),
        (),
    )
    grad_embed, *halves = together(grad_embed, *halves)
    grads = [grad_embed] + [swap(grad_embed, "band", key) for key in other_bands]
    got = [swap(halves[2 * half + 1], "dp", 1) for half in range(2)]
    weight_sums = [add_low(halves[2 * half], got[half]) for half in range(2)]
    weight_split = [
        split_half(weight_sums[half], 0, orders[half][0], dp_steps) for half in range(2)
    ]
    weight_got = [swap(weight_split[half][0], "dp", orders[half][0]) for half in range(2)]
    one_hot = (kept_flat[:, None] == jnp.arange(pos_table.shape[0])[None, :]).astype(f32)
    grad_pos = lax.dot_general(
        one_hot,
        grad_start,
        (((0,), (0,)), ((), ())),
        precision=lax.Precision.HIGHEST,
        preferred_element_type=f32,
    )
    small_rows = jnp.concatenate(
        [sums[1:5], grad_bias_in.reshape(-1, model_width), grad_pos], axis=0
    ).astype(bf16)
    small_steps = [("band", step) for step in bit_steps(band_size)]
    small_steps += [("dp", step) for step in bit_steps(dp_size)]
    small_rows, *grads = together(small_rows, *grads)

    kernel_split = []
    for group in range(groups):
        kernel_split += kernel_grad_part(
            spots,
            patch_rows,
            grads,
            group * group_bands,
            group_bands,
            bands_dev,
            dp_size,
            tuple(weight_sums),
        )
    weight_got[0], weight_got[1], *kernel_split = together(*weight_got, *kernel_split)

    got = [swap(kernel_split[2 * group], "dp", 1) for group in range(groups)]
    weight_sums = [add_low(weight_split[half][1], weight_got[half]) for half in range(2)]
    for stage in range(1, len(dp_steps)):
        for half in range(2):
            send, keep = split_half(
                weight_sums[half], 0, orders[half][stage], orders[half][stage:]
            )
            weight_sums[half] = add_low(keep, swap(send, "dp", orders[half][stage]))
    small_rows = small_rows + swap(small_rows, *small_steps[0])
    update = patch_grad(spots, grads, kernel_groups, pixel_count, ())
    got[0], got[1], weight_sums[0], weight_sums[1], small_rows, update = together(
        *got, *weight_sums, small_rows, update
    )
    kernel_sums = [add_low(kernel_split[2 * group + 1], got[group]) for group in range(groups)]

    by_band = []
    done = 0
    weight_sum = jnp.concatenate([values.reshape(-1, model_width) for values in weight_sums], axis=0)
    for rows in weight_rows:
        block_sum = weight_sum[done * band_size : (done + rows) * band_size]
        by_band.append(block_sum.reshape(band_size, rows, model_width))
        done += rows
    by_band = jnp.concatenate(by_band, axis=1)
    sent = [
        lax.dynamic_index_in_dim(by_band, spot ^ key, 0, keepdims=False)
        for key in range(band_size)
    ]
    weight_got = [sent[0]] + [swap(sent[key], "band", key) for key in other_bands]
    grad_patches = unflatten_rows(update, bands_dev, tuple(kernel_sums))
    for stage in range(len(dp_steps)):
        split = [
            split_half(kernel_sums[group], 1, orders[group][stage], orders[group][stage:])
            for group in range(groups)
        ]
        got = [swap(split[group][0], "dp", orders[group][stage]) for group in range(groups)]
        if stage == 0:
            got[0], got[1], grad_patches, *weight_got = together(*got, grad_patches, *weight_got)
        else:
            small_got = swap(small_rows, *small_steps[stage])
            got[0], got[1], small_got = together(*got, small_got)
            small_rows = small_rows + small_got
        kernel_sums = [add_low(split[group][1], got[group]) for group in range(groups)]

    own_part = jnp.concatenate(kernel_sums, axis=0)
    own_part = own_part.reshape(bands_dev, band_size, own_pixels, model_width)
    own_part = own_part.transpose(1, 2, 0, 3)
    sent = [
        lax.dynamic_index_in_dim(own_part, spot ^ key, 0, keepdims=False)
        for key in range(band_size)
    ]
    pieces = [sent[0]] + [swap(sent[key], "band", key) for key in other_bands]
    small_got = swap(small_rows, *small_steps[len(dp_steps)])
    small_got, *pieces = together(small_got, *pieces)
    small_rows = small_rows + small_got
    grad_gen_kernel, states_part = states_grad(
        spots, band_states, gen_kernel, [[block] for block in pieces]
    )
    for axis, step in small_steps[len(dp_steps) + 1 :]:
        small_rows = small_rows + swap(small_rows, axis, step)
    tail = jnp.concatenate([states_part, sums[0].reshape(-1, gen_width)], axis=0)
    for axis, step in small_steps:
        tail = tail + swap(tail, axis, step)
    own_grads = sum(got.astype(f32) for got in weight_got)
    own_blocks = []
    done = 0
    for rows in weight_rows:
        own_blocks.append(own_grads[done : done + rows])
        done += rows
    grad_qkv_own = jnp.concatenate(own_blocks[:3], axis=1)
    grad_out_own = own_blocks[3]
    grad_fc_in_own = jnp.concatenate(own_blocks[4:-1], axis=1)
    grad_fc_out_own = own_blocks[-1]
    grad_bias_embed = jnp.pad(tail[band_total:].reshape(1, model_width), ((0, 7), (0, 0)))
    grad_token, grad_attn, grad_gain_gen, grad_ff_first, grad_ff_second, grad_gen_bias = (
        generate_back(
            tail[:band_total],
            grad_bias_embed,
            gen_attn,
            gen_gain,
            gen_ff_in,
            gen_ff_out,
            gen_bias,
            gen_kept,
        )
    )

    small = small_rows.astype(f32)
    grad_gains = small[0:2]
    grad_shifts = small[2:4]
    bias_rows = bias_in.shape[0] // model_width
    grad_bias_all = small[4 : 4 + bias_rows].reshape(-1)
    grad_pos_all = small[4 + bias_rows :]
    grad_patches = grad_patches.reshape(group_size, slot_count, bands_dev, pixel_count)
    return (
        result.reshape(local_images, slot_count, model_width),
        grad_patches,
        grad_token[0],
        grad_attn,
        grad_gain_gen,
        grad_ff_first,
        grad_ff_second,
        grad_gen_kernel,
        grad_gen_bias,
        grad_pos_all,
        grad_gains,
        grad_shifts,
        grad_qkv_own,
        grad_out_own,
        grad_fc_in_own,
        grad_bias_all,
        grad_fc_out_own,
    )


def solution(mesh):
    placed = (
        P("dp", None, "band", None),
        P(),
        P(),
        P(),
        P(),
        P(),
        P(None, ("dp", "band")),
        P(),
        P(),
        P(),
        P(),
        P(("dp", "band"), None),
        P(("dp", "band"), None),
        P(("dp", "band"), None),
        P(),
        P(("dp", "band"), None),
        P(),
        P(("dp", "band"), None),
        P(("dp", "band")),
        P(("dp", "band"), None, None),
    )
    return jax.shard_map(
        shards,
        mesh=mesh,
        in_specs=placed,
        out_specs=(
            P(("dp", "band"), None, None),
            P("dp", None, "band", None),
            P(),
            P(),
            P(),
            P(),
            P(),
            P(None, ("dp", "band")),
            P(),
            P(),
            P(),
            P(),
            P(("dp", "band"), None),
            P(("dp", "band"), None),
            P(("dp", "band"), None),
            P(),
            P(("dp", "band"), None),
        ),
        check_vma=False,
    )
```

```python
from functools import partial
import math

import jax
import jax.numpy as jnp
from jax import lax
from jax.experimental import pallas as pl
from jax.experimental.pallas import tpu as pltpu
from jax.sharding import PartitionSpec as P

HEADS = 12
HDIM = 64
GEN_HEADS = 4


def inner(left_arr, right_arr):
    return lax.dot_general(
        left_arr, right_arr, (((0,), (0,)), ((), ())), preferred_element_type=jnp.float32
    )


def times_transpose(left_arr, right_arr):
    return lax.dot_general(
        left_arr, right_arr, (((1,), (1,)), ((), ())), preferred_element_type=jnp.float32
    )


def bit_steps(size):
    steps = []
    step = 1
    while step < size:
        steps.append(step)
        step *= 2
    return steps


def swap(values, axis, step):
    size = lax.axis_size(axis)
    return lax.ppermute(values, axis, [(spot, spot ^ step) for spot in range(size)])


def turn(items, by):
    by = by % max(len(items), 1)
    return items[by:] + items[:by]


def gather_core(blocks):
    return [([key ^ 1 for key in keys], swap(block, "dp", 1)) for keys, block in blocks]


def place(blocks, axis, at):
    spot = lax.axis_index(axis)
    first = blocks[0][1]
    count = sum(len(keys) for keys, _ in blocks)
    shape = first.shape[1 : at + 1] + (count,) + first.shape[at + 1 :]
    whole = jnp.zeros(shape, first.dtype)
    for keys, block in blocks:
        for number, key in enumerate(keys):
            whole = lax.dynamic_update_index_in_dim(whole, block[number], spot ^ key, at)
    return whole


def add_low(left_arr, right_arr):
    return (left_arr.astype(jnp.float32) + right_arr.astype(jnp.float32)).astype(left_arr.dtype)


def split_half(values, at, step, left):
    left = sorted(left, reverse=True)
    shape = values.shape
    values = values.reshape(shape[:at] + (2,) * len(left) + shape[at + 1 :])
    dim = at + left.index(step)
    bit = (lax.axis_index("dp") // step) % 2
    rest = shape[:at] + (-1,) + shape[at + 1 :]
    send = lax.dynamic_index_in_dim(values, 1 - bit, dim, keepdims=False)
    keep = lax.dynamic_index_in_dim(values, bit, dim, keepdims=False)
    return send.reshape(rest), keep.reshape(rest)


def together(*arrays):
    return lax.optimization_barrier(arrays)


def column_blocks(matrix, width):
    return [matrix[:, spot : spot + width] for spot in range(0, matrix.shape[1], width)]


def run_kernel(body, args, in_specs, after=(), **options):
    count = len(after)

    def whole(*refs):
        body(*refs[count:])

    return pl.pallas_call(
        whole,
        in_specs=[pl.BlockSpec(memory_space=pl.ANY)] * count + in_specs,
        compiler_params=pltpu.CompilerParams(vmem_limit_bytes=60 * 1024 * 1024),
        cost_estimate=pl.CostEstimate(flops=1000, bytes_accessed=1000, transcendentals=0),
        **options,
    )(*after, *args)


def dot_nn(left_arr, right_arr):
    return lax.dot_general(
        left_arr, right_arr, (((1,), (0,)), ((), ())), preferred_element_type=jnp.float32
    )


def norm_stats(values):
    center = values - jnp.mean(values, axis=-1, keepdims=True)
    spread = jnp.mean(center * center, axis=-1, keepdims=True)
    scale = lax.rsqrt(spread + 1e-06)
    return center * scale, scale


def norm_back(unit, scale, gain, grad):
    weighted = grad * gain
    first = jnp.mean(weighted, axis=-1, keepdims=True)
    second = jnp.mean(weighted * unit, axis=-1, keepdims=True)
    grad_values = (weighted - first - unit * second) * scale
    grad_gain = jnp.sum(grad * unit, axis=0, keepdims=True)
    grad_shift = jnp.sum(grad, axis=0, keepdims=True)
    return grad_values, grad_gain, grad_shift


def stash_spans(width, hidden):
    sizes = {
        "normed": width,
        "mixed": width,
        "normed_two": width,
        "act": hidden,
        "qkv_grad": 3 * width,
        "branch": width,
        "pre_grad": hidden,
        "cot": width,
        "small": width,
    }
    spans = {}
    first = 0
    for name, size in sizes.items():
        spans[name] = (first, size)
        first += size
    return spans


def block_body(part_count, tile_rows, ff_step, keys_lists, *refs):
    part_refs = refs[:part_count]
    weight_count = sum(len(keys_list) for keys_list in keys_lists)
    weight_refs = refs[part_count : part_count + weight_count]
    (
        spot_ref,
        base_ref,
        cot_ref,
        keep_ref,
        mask_ref,
        gain_ref,
        shift_ref,
        bias_ref,
        kept_ref,
        result_ref,
        embed_grad_ref,
        stash_ref,
        sums_ref,
        qkv_w,
        out_w,
        fc_in_w,
        fc_out_w,
        qkv_ref,
        probs_ref,
        total_ref,
        back_ref,
        mixed_grad_ref,
        bias_grad_ref,
        sems,
    ) = refs[part_count + weight_count :]
    bf16 = jnp.bfloat16
    f32 = jnp.float32
    width = base_ref.shape[1]
    hidden = fc_in_w.shape[1]
    spans = stash_spans(width, hidden)
    views = {name: stash_ref.at[:, pl.ds(first, size)] for name, (first, size) in spans.items()}
    normed_ref = views["normed"]
    mixed_ref = views["mixed"]
    normed_two_ref = views["normed_two"]
    act_ref = views["act"]
    qkv_grad_ref = views["qkv_grad"]
    branch_ref = views["branch"]
    pre_grad_ref = views["pre_grad"]
    views["cot"][...] = cot_ref[...]
    share = width // sum(len(keys) for keys in keys_lists[0])
    targets = (
        [(qkv_w, column, share) for column in range(3)]
        + [(out_w, 0, share)]
        + [(fc_in_w, column, share) for column in range(hidden // width)]
        + [(fc_out_w, 0, share * hidden // width)]
    )
    copies = {}
    for number, (target_ref, column, rows) in enumerate(targets):
        half, first = (0, number * share) if number < 6 else (1, (number - 6) * share)
        half_refs = weight_refs[: len(keys_lists[0])] if half == 0 else weight_refs[len(keys_lists[0]) :]
        for keys, weight_ref in zip(keys_lists[half], half_refs):
            for index, key in enumerate(keys):
                at = pl.multiple_of(jnp.bitwise_xor(spot_ref[0], key) * rows, rows)
                copy = pltpu.make_async_copy(
                    weight_ref.at[index, pl.ds(first, rows), :],
                    target_ref.at[pl.ds(at, rows), pl.ds(column * width, width)],
                    sems.at[sum(len(some) for some in copies.values())],
                )
                copy.start()
                copies.setdefault(id(target_ref), []).append(copy)

    def arrive(target_ref):
        for copy in copies[id(target_ref)]:
            copy.wait()

    row_total, width = base_ref.shape
    tiles = row_total // tile_rows
    head_pairs = HEADS // 2
    lanes = 2 * HDIM

    start = base_ref[...]
    for part_ref in part_refs:
        start = start + part_ref[...].astype(f32)
    unit_one, scale_one = norm_stats(start)
    normed = (unit_one * gain_ref[0:1] + shift_ref[0:1]).astype(bf16)
    normed_ref[...] = normed
    arrive(qkv_w)
    for spot in range(3):
        cols = slice(spot * width, (spot + 1) * width)
        qkv_ref[:, cols] = dot_nn(normed, qkv_w[:, cols]).astype(bf16)

    low_lanes = lax.broadcasted_iota(jnp.int32, (tile_rows, lanes), 1) < HDIM

    def half(values, odd):
        keep = jnp.logical_not(low_lanes) if odd else low_lanes
        return jnp.where(keep, values, jnp.zeros_like(values))

    def head_slices(pair, tile):
        rows = pl.ds(tile * tile_rows, tile_rows)
        cols = [
            pl.ds(pl.multiple_of(which * width + pair * lanes, lanes), lanes) for which in range(3)
        ]
        return rows, cols

    def attend(pair, carry):
        for tile in range(tiles):
            rows, cols = head_slices(pair, tile)
            queries, keys_arr, values_arr = [qkv_ref[rows, col] for col in cols]
            mixed = jnp.zeros((tile_rows, lanes), f32)
            for odd in range(2):
                scores = times_transpose(half(queries, odd), keys_arr) * HDIM ** (-0.5)
                scores = scores + mask_ref[tile]
                exponent = jnp.exp(scores - jnp.max(scores, axis=-1, keepdims=True))
                probs = exponent * (1.0 / jnp.sum(exponent, axis=-1, keepdims=True))
                probs_ref[(pair * 2 + odd) * tiles + tile] = probs
                mixed = mixed + dot_nn(probs.astype(bf16), half(values_arr, odd))
            mixed_ref[rows, cols[0]] = mixed.astype(bf16)
        return carry

    lax.fori_loop(0, head_pairs, attend, 0)
    arrive(out_w)
    middle = start + dot_nn(mixed_ref[...], out_w[...])
    unit_two, scale_two = norm_stats(middle)
    normed_two = (unit_two * gain_ref[1:2] + shift_ref[1:2]).astype(bf16)
    normed_two_ref[...] = normed_two
    total_ref[...] = middle
    back_ref[...] = jnp.zeros_like(back_ref)
    arrive(fc_in_w)
    arrive(fc_out_w)

    def feed(step, carry):
        cols = pl.ds(pl.multiple_of(step * ff_step, ff_step), ff_step)
        pre = dot_nn(normed_two_ref[...], fc_in_w[:, cols]) + bias_ref[:, cols]
        cdf = 0.5 * (1.0 + lax.erf(pre * 0.5**0.5))
        act = (pre * cdf).astype(bf16)
        act_ref[:, cols] = act
        slope = cdf + pre * (jnp.exp(-0.5 * pre * pre) * (2.0 * math.pi) ** (-0.5))
        pre_grad = slope * times_transpose(cot_ref[...], fc_out_w[cols, :])
        pre_grad = pre_grad.astype(bf16)
        pre_grad_ref[:, cols] = pre_grad
        bias_grad_ref[:, cols] = jnp.sum(pre_grad.astype(f32), axis=0, keepdims=True)
        total_ref[...] += dot_nn(act, fc_out_w[cols, :])
        back_ref[...] += times_transpose(pre_grad, fc_in_w[:, cols])
        return carry

    lax.fori_loop(0, fc_in_w.shape[1] // ff_step, feed, 0)
    result_ref[...] = (total_ref[...] * keep_ref[...]).astype(bf16)
    grad_norm, gain_two, shift_two = norm_back(unit_two, scale_two, gain_ref[1:2], back_ref[...])
    grad_middle = cot_ref[...].astype(f32) + grad_norm
    grad_branch = grad_middle.astype(bf16)
    branch_ref[...] = grad_branch
    mixed_grad_ref[...] = times_transpose(grad_branch, out_w[...]).astype(bf16)

    def attend_back(pair, carry):
        for tile in range(tiles):
            rows, cols = head_slices(pair, tile)
            queries, keys_arr, values_arr = [qkv_ref[rows, col] for col in cols]
            grad_mixed = mixed_grad_ref[rows, cols[0]]
            grads = [jnp.zeros((tile_rows, lanes), f32) for _ in range(3)]
            for odd in range(2):
                probs = probs_ref[(pair * 2 + odd) * tiles + tile]
                own_grad = half(grad_mixed, odd)
                grad_probs = times_transpose(own_grad, values_arr)
                grad_scores = probs * (
                    grad_probs - jnp.sum(grad_probs * probs, axis=-1, keepdims=True)
                )
                grad_scores = grad_scores.astype(bf16)
                grads[0] = grads[0] + dot_nn(grad_scores, half(keys_arr, odd))
                grads[1] = grads[1] + inner(grad_scores, half(queries, odd))
                grads[2] = grads[2] + inner(probs.astype(bf16), own_grad)
            for which, factor in enumerate((HDIM ** (-0.5), HDIM ** (-0.5), 1.0)):
                qkv_grad_ref[rows, cols[which]] = (grads[which] * factor).astype(bf16)
        return carry

    lax.fori_loop(0, head_pairs, attend_back, 0)
    back = jnp.zeros((row_total, width), f32)
    for spot in range(3):
        cols = slice(spot * width, (spot + 1) * width)
        back = back + times_transpose(qkv_grad_ref[:, cols], qkv_w[:, cols])
    grad_norm, gain_one, shift_one = norm_back(unit_one, scale_one, gain_ref[0:1], back)
    grad_start = grad_middle + grad_norm
    embed_grad_ref[...] = grad_start.astype(bf16)
    sums = jnp.concatenate(
        [jnp.sum(grad_start, axis=0, keepdims=True), gain_one, gain_two, shift_one, shift_two]
        + [jnp.zeros((3, width), f32)],
        axis=0,
    )
    sums_ref[...] = sums
    small_ref = views["small"]
    positions = small_ref.shape[0] - 16
    spots_at = lax.broadcasted_iota(jnp.int32, (positions, row_total), 0)
    one_hot = jnp.where(spots_at == kept_ref[...], 1.0, 0.0)
    by_position = lax.dot_general(
        one_hot,
        grad_start,
        (((1,), (0,)), ((), ())),
        precision=lax.Precision.HIGHEST,
        preferred_element_type=f32,
    )
    cuts = [bias_grad_ref[:, spot : spot + width] for spot in range(0, hidden, width)]
    cuts.append(jnp.zeros((8 - len(cuts), width), f32))
    small_ref[...] = jnp.concatenate([by_position, sums, *cuts], axis=0).astype(bf16)


def block(parts, weight_halves, spots, base, cot, keep, mask, gains, shifts, bias, kept):
    row_total, width = base.shape
    tile_rows = mask.shape[1]
    hidden = bias.shape[1]
    bf16 = jnp.bfloat16
    f32 = jnp.float32
    keys_lists = [[keys for keys, _ in blocks] for blocks in weight_halves]
    weight_args = [block for blocks in weight_halves for _, block in blocks]
    pieces = sum(len(keys) for keys in keys_lists[0])
    inside = pl.BlockSpec(memory_space=pltpu.VMEM)
    outside = pl.BlockSpec(memory_space=pl.ANY)
    rows = (row_total, width)
    shapes = [
        (rows, bf16),
        (rows, bf16),
        ((row_total, sum(stash_spans(width, hidden)["small"])), bf16),
        ((8, width), f32),
    ]
    return run_kernel(
        partial(block_body, len(parts), tile_rows, 512, keys_lists),
        (*parts, *weight_args, spots, base, cot, keep, mask, gains, shifts, bias, kept),
        [inside] * len(parts)
        + [outside] * len(weight_args)
        + [pl.BlockSpec(memory_space=pltpu.SMEM)]
        + [inside] * 8,
        out_shape=[jax.ShapeDtypeStruct(shape, kind) for shape, kind in shapes],
        out_specs=[inside] * len(shapes),
        scratch_shapes=[
            pltpu.VMEM((width, 3 * width), bf16),
            pltpu.VMEM((width, width), bf16),
            pltpu.VMEM((width, hidden), bf16),
            pltpu.VMEM((hidden, width), bf16),
            pltpu.VMEM((row_total, 3 * width), bf16),
            pltpu.VMEM((HEADS * row_total // tile_rows, tile_rows, tile_rows), f32),
            pltpu.VMEM(rows, f32),
            pltpu.VMEM(rows, f32),
            pltpu.VMEM(rows, bf16),
            pltpu.VMEM((1, hidden), f32),
            pltpu.SemaphoreType.DMA(((5 + hidden // width) * pieces,)),
        ],
    )


def dot_full(left_arr, right_arr, left_dim=1, right_dim=0):
    return lax.dot_general(
        left_arr,
        right_arr,
        (((left_dim,), (right_dim,)), ((), ())),
        precision=lax.Precision.HIGHEST,
        preferred_element_type=jnp.float32,
    )


def head_part(values, head):
    size = values.shape[1] // GEN_HEADS
    lane = lax.broadcasted_iota(jnp.int32, values.shape, 1)
    inside = jnp.logical_and(lane >= head * size, lane < (head + 1) * size)
    return jnp.where(inside, values, 0.0)


def generate_body(
    waves_ref,
    token_ref,
    attn_hbm,
    gain_hbm,
    ff_in_hbm,
    ff_out_hbm,
    bias_w_hbm,
    columns_hbm,
    kernel_ref,
    embed_bias_ref,
    low_ref,
    states_ref,
    rows_ref,
    weights_ref,
    pre_ref,
    scales_ref,
    attn_ref,
    gain_ref,
    ff_in_ref,
    ff_out_ref,
    bias_w_ref,
    columns_ref,
    sems,
):
    f32 = jnp.float32
    copies = [
        pltpu.make_async_copy(source, target, sems.at[number])
        for number, (source, target) in enumerate(
            (
                (attn_hbm, attn_ref),
                (gain_hbm, gain_ref),
                (ff_in_hbm, ff_in_ref),
                (ff_out_hbm, ff_out_ref),
                (columns_hbm, columns_ref),
                (bias_w_hbm, bias_w_ref),
            )
        )
    ]
    for copy in copies:
        copy.start()
    bands = waves_ref.shape[1]
    width = token_ref.shape[1]
    padded = rows_ref.shape[1]
    square = (bands, bands)
    diagonal = lax.broadcasted_iota(jnp.int32, square, 0) == lax.broadcasted_iota(
        jnp.int32, square, 1
    )
    waves = jnp.broadcast_to(waves_ref[...].astype(f32), square)
    column = jnp.sum(jnp.where(diagonal, waves, 0.0), axis=1, keepdims=True)
    lane = lax.broadcasted_iota(jnp.int32, (bands, width), 1)
    half_width = width // 2
    number = jnp.where(lane < half_width, lane, lane - half_width).astype(f32)
    angles = column * jnp.exp(number * (-math.log(10000.0) / half_width))
    wave = jnp.where(lane < half_width, jnp.sin(angles), jnp.cos(angles))
    sequence = jnp.concatenate(
        [wave, token_ref[...].astype(f32), jnp.zeros((padded - bands - 1, width), f32)], axis=0
    )
    rows_ref[0] = sequence
    copies[0].wait()
    copies[1].wait()
    for which in range(3):
        rows_ref[1 + which] = dot_full(sequence, attn_ref[which].astype(f32))
    queries = rows_ref[1]
    keys_arr = rows_ref[2]
    values_arr = rows_ref[3]
    key_spot = lax.broadcasted_iota(jnp.int32, (padded, padded), 1)
    mixed = jnp.zeros((padded, width), f32)
    for head in range(GEN_HEADS):
        scores = dot_full(head_part(queries, head), keys_arr, 1, 1)
        scores = scores * (1.0 / math.sqrt(width // GEN_HEADS))
        scores = jnp.where(key_spot <= bands, scores, -1e30)
        exponent = jnp.exp(scores - jnp.max(scores, axis=-1, keepdims=True))
        weights = exponent / jnp.sum(exponent, axis=-1, keepdims=True)
        weights_ref[head] = weights
        mixed = mixed + dot_full(weights, head_part(values_arr, head))
    rows_ref[4] = mixed
    unit_one, scale_one = norm_stats(sequence + dot_full(mixed, attn_ref[3].astype(f32)))
    rows_ref[5] = unit_one
    first = unit_one * gain_ref[0:1].astype(f32)
    copies[2].wait()
    pre = dot_full(first, ff_in_ref[...].astype(f32))
    pre_ref[...] = pre
    hidden = pre * (0.5 * (1.0 + lax.erf(pre * 0.5**0.5)))
    copies[3].wait()
    unit_two, scale_two = norm_stats(first + dot_full(hidden, ff_out_ref[...].astype(f32)))
    rows_ref[6] = unit_two
    states = unit_two * gain_ref[1:2].astype(f32)
    states_ref[...] = states
    scales_ref[0] = jnp.broadcast_to(scale_one, (padded, width))
    scales_ref[1] = jnp.broadcast_to(scale_two, (padded, width))
    low = states[:bands].astype(jnp.bfloat16)
    low_ref[...] = low
    features = kernel_ref.shape[2]
    copies[4].wait()
    for pixel in range(kernel_ref.shape[0]):
        cols = slice(pixel * features, (pixel + 1) * features)
        kernel_ref[pixel] = dot_nn(low, columns_ref[:, cols]).astype(jnp.bfloat16)
    copies[5].wait()
    token_state = states[bands : bands + 8]
    embed_bias_ref[...] = dot_full(token_state, bias_w_ref[...].astype(f32))


def generate_fast(wavelengths, token, gen_attn, gen_gain, ff_in, ff_out, gen_bias, columns):
    f32 = jnp.float32
    bf16 = jnp.bfloat16
    bands = wavelengths.shape[0]
    width = token.shape[0]
    padded = -(-(bands + 1) // 8) * 8
    features = gen_bias.shape[1]
    shapes = [
        ((columns.shape[1] // features, bands, features), bf16),
        ((8, features), f32),
        ((bands, width), bf16),
        ((padded, width), f32),
        ((7, padded, width), f32),
        ((GEN_HEADS, padded, padded), f32),
        ((padded, ff_in.shape[1]), f32),
        ((2, padded, width), f32),
    ]
    inside = pl.BlockSpec(memory_space=pltpu.VMEM)
    outside = pl.BlockSpec(memory_space=pl.ANY)
    weights = (gen_attn, gen_gain, ff_in, ff_out, gen_bias, columns)
    return run_kernel(
        generate_body,
        (wavelengths[None], token[None], *weights),
        out_shape=[jax.ShapeDtypeStruct(shape, kind) for shape, kind in shapes],
        in_specs=[inside] * 2 + [outside] * 6,
        out_specs=[inside] * len(shapes),
        scratch_shapes=[pltpu.VMEM(weight.shape, bf16) for weight in weights]
        + [pltpu.SemaphoreType.DMA((6,))],
    )


def generate_back_body(
    tail_ref,
    attn_ref,
    gain_ref,
    ff_in_ref,
    ff_out_ref,
    bias_w_ref,
    states_ref,
    rows_ref,
    weights_ref,
    pre_ref,
    scales_ref,
    token_out,
    attn_out,
    gain_out,
    ff_in_out,
    ff_out_out,
    bias_out,
):
    f32 = jnp.float32
    padded, width = states_ref.shape
    features = bias_w_ref.shape[1]
    bands = padded - 8
    head_scale = 1.0 / math.sqrt(width // GEN_HEADS)
    cuts = [tail_ref[bands + spot : bands + spot + 1, :] for spot in range(features // width)]
    bias_grad = jnp.concatenate(cuts, axis=1)
    bias_grad = jnp.concatenate([bias_grad, jnp.zeros((7, features), f32)], axis=0)
    row_spot = lax.broadcasted_iota(jnp.int32, (padded - bands, width), 0)
    token_grad = dot_full(bias_grad, bias_w_ref[...].astype(f32), 1, 1)
    token_grad = jnp.where(row_spot == 0, token_grad[0:1], 0.0)
    grad_states = jnp.concatenate([tail_ref[:bands, :], token_grad], axis=0)
    token_state = states_ref[bands : bands + 8]
    first_row = lax.broadcasted_iota(jnp.int32, token_state.shape, 0) == 0
    bias_out[...] = dot_full(jnp.where(first_row, token_state, 0.0), bias_grad, 0, 0)
    unit_one = rows_ref[5]
    gain_one = gain_ref[0:1].astype(f32)
    gain_two = gain_ref[1:2].astype(f32)
    grad_two, gain_two_grad, _ = norm_back(rows_ref[6], scales_ref[1], gain_two, grad_states)
    pre = pre_ref[...]
    cdf = 0.5 * (1.0 + lax.erf(pre * 0.5**0.5))
    ff_out_out[...] = dot_full(pre * cdf, grad_two, 0, 0)
    slope = cdf + pre * (jnp.exp(-0.5 * pre * pre) * (2.0 * math.pi) ** (-0.5))
    grad_pre = slope * dot_full(grad_two, ff_out_ref[...].astype(f32), 1, 1)
    ff_in_out[...] = dot_full(unit_one * gain_one, grad_pre, 0, 0)
    grad_first = grad_two + dot_full(grad_pre, ff_in_ref[...].astype(f32), 1, 1)
    grad_one, gain_one_grad, _ = norm_back(unit_one, scales_ref[0], gain_one, grad_first)
    gain_out[...] = jnp.concatenate([gain_one_grad, gain_two_grad], axis=0)
    attn_out[3] = dot_full(rows_ref[4], grad_one, 0, 0)
    grad_mixed = dot_full(grad_one, attn_ref[3].astype(f32), 1, 1)
    sequence = rows_ref[0]
    queries = rows_ref[1]
    keys_arr = rows_ref[2]
    values_arr = rows_ref[3]
    grads = [jnp.zeros((padded, width), f32) for _ in range(3)]
    for head in range(GEN_HEADS):
        weights = weights_ref[head]
        own_grad = head_part(grad_mixed, head)
        grad_weights = dot_full(own_grad, values_arr, 1, 1)
        grad_scores = weights * (
            grad_weights - jnp.sum(grad_weights * weights, axis=-1, keepdims=True)
        )
        grad_scores = grad_scores * head_scale
        grads[0] = grads[0] + dot_full(grad_scores, head_part(keys_arr, head))
        grads[1] = grads[1] + dot_full(grad_scores, head_part(queries, head), 0, 0)
        grads[2] = grads[2] + dot_full(weights, own_grad, 0, 0)
    grad_sequence = grad_one
    for which in range(3):
        attn_out[which] = dot_full(sequence, grads[which], 0, 0)
        grad_sequence = grad_sequence + dot_full(
            grads[which], attn_ref[which].astype(f32), 1, 1
        )
    token_out[...] = grad_sequence[bands : bands + 1]


def generate_back(tail, gen_attn, gen_gain, ff_in, ff_out, gen_bias, kept_arrs):
    f32 = jnp.float32
    width = gen_gain.shape[1]
    shapes = [
        (1, width),
        gen_attn.shape,
        gen_gain.shape,
        ff_in.shape,
        ff_out.shape,
        gen_bias.shape,
    ]
    inside = pl.BlockSpec(memory_space=pltpu.VMEM)
    return run_kernel(
        generate_back_body,
        (tail, gen_attn, gen_gain, ff_in, ff_out, gen_bias, *kept_arrs),
        out_shape=[jax.ShapeDtypeStruct(shape, f32) for shape in shapes],
        in_specs=[inside] * (6 + len(kept_arrs)),
        out_specs=[inside] * len(shapes),
    )


def fill_kernel(keys_lists, piece_refs, spot, mat_ref, bands, pixels):
    for keys, piece_ref in zip(keys_lists, piece_refs):
        for number, key in enumerate(keys):
            share = piece_ref.shape[2]
            first = jnp.bitwise_xor(spot, key) * share
            for band in range(bands):
                rows = pl.ds(pl.multiple_of(band * pixels + first, share), share)
                mat_ref[rows, :] = piece_ref[number, band]


def fill_step(keys_lists, piece_refs, spot, mat_ref, band_step, group_steps):
    pixels = mat_ref.shape[0] // band_step
    step = pl.program_id(0)
    used = 0
    for group, keys_list in enumerate(keys_lists):
        group_refs = piece_refs[used : used + len(keys_list)]
        used += len(keys_list)

        @pl.when(step // group_steps == group)
        def _(keys_list=keys_list, group_refs=group_refs):
            fill_kernel(keys_list, group_refs, spot, mat_ref, band_step, pixels)


def embed_body(keys_lists, group_steps, band_step, *refs):
    spot_ref, patch_ref = refs[:2]
    count = sum(len(keys_list) for keys_list in keys_lists)
    piece_refs = refs[2 : 2 + count]
    *out_refs, mat_ref, total_ref = refs[2 + count :]
    step = pl.program_id(0)
    fill_step(keys_lists, piece_refs, spot_ref[0], mat_ref, band_step, group_steps)

    @pl.when(step == 0)
    def _():
        total_ref[...] = jnp.zeros_like(total_ref)

    total_ref[...] += dot_nn(patch_ref[...], mat_ref[...])

    @pl.when(step == pl.num_programs(0) - 1)
    def _():
        for key, out_ref in enumerate(out_refs):
            rows = out_ref.shape[0]
            first = pl.multiple_of(jnp.bitwise_xor(spot_ref[1], key) * rows, rows)
            out_ref[...] = total_ref[pl.ds(first, rows), :].astype(out_ref.dtype)


def group_band_count(kernel_groups):
    return min(block.shape[1] for blocks in kernel_groups for _, block in blocks)


def piece_specs(kernel_groups, band_step):
    group_steps = group_band_count(kernel_groups) // band_step
    specs = []
    arrays = []
    for group, blocks in enumerate(kernel_groups):
        for keys, block in blocks:
            whole = block.shape[1] > group_steps * band_step
            first = group * group_steps

            def pick(step, first=first, whole=whole):
                here = jnp.clip(step - first, 0, group_steps - 1)
                return (0, here + first if whole else here, 0, 0)

            specs.append(pl.BlockSpec((len(keys), band_step) + block.shape[2:], pick))
            arrays.append(block)
    keys_lists = [[keys for keys, _ in blocks] for blocks in kernel_groups]
    return specs, arrays, keys_lists, group_steps


def embed_share(spots, patch_rows, kernel_groups, owners):
    row_total = patch_rows.shape[0]
    blocks = kernel_groups[0]
    group_bands = group_band_count(kernel_groups)
    width = blocks[0][1].shape[3]
    pixels = sum(len(keys) for keys, _ in blocks) * blocks[0][1].shape[2]
    band_step = min(4, group_bands)
    depth = band_step * pixels
    specs, arrays, keys_lists, group_steps = piece_specs(kernel_groups, band_step)
    rows = row_total // owners
    return run_kernel(
        partial(embed_body, keys_lists, group_steps, band_step),
        [spots, patch_rows, *arrays],
        [
            pl.BlockSpec(memory_space=pltpu.SMEM),
            pl.BlockSpec((row_total, depth), lambda step: (0, step)),
        ]
        + specs,
        grid=(group_steps * len(kernel_groups),),
        out_shape=[jax.ShapeDtypeStruct((rows, width), jnp.bfloat16)] * owners,
        out_specs=[pl.BlockSpec((rows, width), lambda step: (0, 0))] * owners,
        scratch_shapes=[
            pltpu.VMEM((depth, width), jnp.bfloat16),
            pltpu.VMEM((row_total, width), jnp.float32),
        ],
    )


def kernel_grad_body(dp_size, band_step, *refs):
    spot_ref, patch_ref = refs[:2]
    *grad_refs, first_ref, last_ref, keep_ref, hold_ref = refs[2:]
    rows = grad_refs[0].shape[0]
    total = 0.0
    for key, grad_ref in enumerate(grad_refs):
        first = pl.multiple_of(jnp.bitwise_xor(spot_ref[1], key) * rows, rows)
        total = total + inner(patch_ref[pl.ds(first, rows), :], grad_ref[...])
    hold_ref[...] = total.astype(hold_ref.dtype)
    pixels = hold_ref.shape[0] // band_step
    share = pixels // dp_size
    core = lax.rem(spot_ref[0], 2)
    for band in range(band_step):
        for chip in range(dp_size // 2):
            base = band * pixels + chip * 2 * share
            kept = pl.multiple_of(base + core * share, share)
            keep_ref[band, chip] = hold_ref[pl.ds(kept, share), :]

    half = pl.num_programs(0) // 2
    for number, send_ref in enumerate((first_ref, last_ref)):

        @pl.when(pl.program_id(0) // half == number)
        def _(send_ref=send_ref):
            for band in range(band_step):
                for chip in range(dp_size // 2):
                    base = band * pixels + chip * 2 * share
                    sent = pl.multiple_of(base + (1 - core) * share, share)
                    send_ref[band, chip] = hold_ref[pl.ds(sent, share), :]


def kernel_grad_part(spots, patch_rows, grads, first_band, group_bands, bands_dev, dp_size, after):
    row_total = patch_rows.shape[0]
    width = grads[0].shape[1]
    band_step = min(2, group_bands // 2)
    pixels = patch_rows.shape[1] // bands_dev
    depth = band_step * pixels
    offset = first_band // band_step
    share = pixels // dp_size
    chips = (dp_size // 2, share, width)
    steps = group_bands // band_step
    block = (band_step,) + chips
    return run_kernel(
        partial(kernel_grad_body, dp_size, band_step),
        (spots, patch_rows, *grads),
        after=after,
        grid=(steps,),
        out_shape=[
            jax.ShapeDtypeStruct((bands,) + chips, jnp.bfloat16)
            for bands in (group_bands // 2, group_bands // 2, group_bands)
        ],
        in_specs=[
            pl.BlockSpec(memory_space=pltpu.SMEM),
            pl.BlockSpec((row_total, depth), lambda step: (0, offset + step)),
        ]
        + [pl.BlockSpec(grad.shape, lambda step: (0, 0)) for grad in grads],
        out_specs=[
            pl.BlockSpec(block, lambda step: (jnp.minimum(step, steps // 2 - 1), 0, 0, 0)),
            pl.BlockSpec(block, lambda step: (jnp.maximum(step - steps // 2, 0), 0, 0, 0)),
            pl.BlockSpec(block, lambda step: (step, 0, 0, 0)),
        ],
        scratch_shapes=[pltpu.VMEM((depth, width), jnp.bfloat16)],
    )


def patch_grad_body(keys_lists, grad_count, group_steps, band_step, *refs):
    spot_ref = refs[0]
    grad_refs = refs[1 : 1 + grad_count]
    out_ref, mat_ref = refs[-2:]
    piece_refs = refs[1 + grad_count : -2]
    fill_step(keys_lists, piece_refs, spot_ref[0], mat_ref, band_step, group_steps)
    for key, grad_ref in enumerate(grad_refs):
        rows = grad_ref.shape[0]
        first = pl.multiple_of(jnp.bitwise_xor(spot_ref[1], key) * rows, rows)
        out_ref[pl.ds(first, rows), :] = times_transpose(grad_ref[...], mat_ref[...]).astype(
            out_ref.dtype
        )


def patch_grad(spots, grads, kernel_groups, pixels, after):
    rows, width = grads[0].shape
    row_total = rows * len(grads)
    band_step = min(4, group_band_count(kernel_groups))
    depth = band_step * pixels
    specs, arrays, keys_lists, group_steps = piece_specs(kernel_groups, band_step)
    steps = group_steps * len(kernel_groups)
    return run_kernel(
        partial(patch_grad_body, keys_lists, len(grads), group_steps, band_step),
        [spots, *grads, *arrays],
        [pl.BlockSpec(memory_space=pltpu.SMEM)]
        + [pl.BlockSpec(grad.shape, lambda step: (0, 0)) for grad in grads]
        + specs,
        after=after,
        grid=(steps,),
        out_shape=jax.ShapeDtypeStruct((row_total, steps * depth), jnp.bfloat16),
        out_specs=pl.BlockSpec((row_total, depth), lambda step: (0, step)),
        scratch_shapes=[pltpu.VMEM((depth, width), jnp.bfloat16)],
    )


def states_grad_body(batches, low_ref, columns_ref, *refs):
    *piece_refs, sums_ref, spot_ref, grad_ref, part_ref, hold_ref = refs
    pixels, bands, width = piece_refs[0].shape
    for number, piece_ref in enumerate(piece_refs):
        key, batch = divmod(number, batches)
        first = (jnp.bitwise_xor(spot_ref[1], key) * batches + batch) * bands
        hold_ref[:, pl.ds(pl.multiple_of(first, bands), bands), :] = piece_ref[...]
    total = 0.0
    for pixel in range(pixels):
        cols = slice(pixel * width, (pixel + 1) * width)
        grads = hold_ref[pixel]
        grad_ref[:, cols] = inner(low_ref[...], grads)
        total = total + times_transpose(grads, columns_ref[:, cols])
    bands, states = total.shape
    part_ref[:bands, :] = total
    rows = [sums_ref[0:1, spot : spot + states] for spot in range(0, width, states)]
    rows.append(jnp.zeros((part_ref.shape[0] - bands - len(rows), states), jnp.float32))
    part_ref[bands:, :] = jnp.concatenate(rows, axis=0)


def states_grad(spots, low, columns, pieces, sums):
    pixels, bands, width = pieces[0].shape
    tail_rows = low.shape[0] + -(-width // low.shape[1] // 8) * 8
    if bands % 16:
        blocks = [([key], piece[None]) for key, piece in enumerate(pieces)]
        whole = place(blocks, "band", 1).reshape(pixels, -1, width)
        grads = whole.transpose(1, 0, 2).reshape(low.shape[0], -1)
        rows = [times_transpose(grads, columns), sums[0].reshape(-1, low.shape[1])]
        tail = jnp.concatenate(rows, axis=0)
        tail = jnp.pad(tail, ((0, tail_rows - tail.shape[0]), (0, 0)))
        return inner(low, grads), tail
    inside = pl.BlockSpec(memory_space=pltpu.VMEM)
    return run_kernel(
        partial(states_grad_body, 1),
        (low, columns, *pieces, sums, spots),
        out_shape=[
            jax.ShapeDtypeStruct(columns.shape, jnp.float32),
            jax.ShapeDtypeStruct((tail_rows, low.shape[1]), jnp.float32),
        ],
        in_specs=[inside] * (3 + len(pieces)) + [pl.BlockSpec(memory_space=pltpu.SMEM)],
        out_specs=[inside, inside],
        scratch_shapes=[pltpu.VMEM((pixels, bands * len(pieces), width), jnp.bfloat16)],
    )


def flatten_body(in_ref, out_ref):
    out_ref[...] = in_ref[...].reshape(out_ref.shape)


def flatten_rows(cube, after):
    rows, bands, pixels = cube.shape
    step_rows = 64
    return run_kernel(
        flatten_body,
        (cube,),
        [pl.BlockSpec((step_rows, bands, pixels), lambda step: (step, 0, 0))],
        after=after,
        grid=(rows // step_rows,),
        out_shape=jax.ShapeDtypeStruct((rows, bands * pixels), cube.dtype),
        out_specs=pl.BlockSpec((step_rows, bands * pixels), lambda step: (step, 0)),
    )


def unflatten_rows(flat, bands, after):
    rows, depth = flat.shape
    step_rows = 64
    return run_kernel(
        flatten_body,
        (flat,),
        [pl.BlockSpec((step_rows, depth), lambda step: (step, 0))],
        after=after,
        grid=(rows // step_rows,),
        out_shape=jax.ShapeDtypeStruct((rows, bands, depth // bands), flat.dtype),
        out_specs=pl.BlockSpec((step_rows, bands, depth // bands), lambda step: (step, 0, 0)),
    )


def stack_body(*refs):
    *part_refs, out_ref, hold_ref = refs
    width = out_ref.shape[1]
    first = 0
    for part_ref in part_refs:
        rows = part_ref.shape[0]
        for spot in range(0, part_ref.shape[1], width):
            hold_ref[pl.ds(first, rows), :] = part_ref[:, spot : spot + width].astype(jnp.float32)
            first += rows
    out_ref[...] = hold_ref[...].astype(out_ref.dtype)


def stack_weights(shards_in):
    width = shards_in[-1].shape[1]
    if any(shard.shape[0] % 8 for shard in shards_in):
        return jnp.concatenate(
            [part for shard in shards_in for part in column_blocks(shard, width)], axis=0
        )
    row_total = sum(shard.size for shard in shards_in) // width
    inside = pl.BlockSpec(memory_space=pltpu.VMEM)
    return run_kernel(
        stack_body,
        shards_in,
        [inside] * len(shards_in),
        out_shape=jax.ShapeDtypeStruct((row_total, width), shards_in[0].dtype),
        out_specs=inside,
        scratch_shapes=[pltpu.VMEM((row_total, width), jnp.float32)],
    )


def plane_body(block_rows, spot_ref, *refs):
    *stack_refs, first_ref, last_ref, hold_ref = refs
    band_size = len(stack_refs)
    for key, stack_ref in enumerate(stack_refs):
        owner = jnp.bitwise_xor(spot_ref[1], key)
        values = stack_ref[...].astype(jnp.float32)
        done = 0
        for rows in block_rows:
            at = pl.multiple_of(done * band_size + owner * rows, 8)
            hold_ref[pl.ds(at, rows), :] = values[done : done + rows]
            done += rows
    half = first_ref.shape[0]
    first_ref[...] = hold_ref[:half, :].astype(first_ref.dtype)
    last_ref[...] = hold_ref[half:, :].astype(last_ref.dtype)


def plane_weights(spots, stacks, block_rows):
    row_total, width = stacks[0].shape
    band_size = len(stacks)
    half = row_total * band_size // 2
    if any(rows % 8 for rows in block_rows):
        whole = place([([key], stack[None]) for key, stack in enumerate(stacks)], "band", 0)
        parts = []
        done = 0
        for rows in block_rows:
            parts.append(whole[:, done : done + rows].reshape(-1, width))
            done += rows
        merged = jnp.concatenate(parts, axis=0)
        return merged[:half], merged[half:]
    inside = pl.BlockSpec(memory_space=pltpu.VMEM)
    return run_kernel(
        partial(plane_body, block_rows),
        (spots, *stacks),
        [pl.BlockSpec(memory_space=pltpu.SMEM)] + [inside] * band_size,
        out_shape=[jax.ShapeDtypeStruct((half, width), stacks[0].dtype)] * 2,
        out_specs=[inside] * 2,
        scratch_shapes=[pltpu.VMEM((row_total * band_size, width), jnp.float32)],
    )


def weight_grad_body(dp_size, first_steps, hidden, spot_ref, own_ref, other_ref, *refs):
    *out_refs, turned_ref, hold_ref, feed_ref, small_ref, sems = refs
    width = hold_ref.shape[2]
    row_total = own_ref.shape[0]
    spans = stash_spans(width, hidden)
    share = width // dp_size
    chips = dp_size // 2
    core = lax.rem(spot_ref[0], 2)
    copies = []

    def view(name, column=0, size=None):
        first, whole = spans[name]
        first = first + column * width
        return [ref[:, first : first + (size or whole)] for ref in (own_ref, other_ref)]

    def turn_rows(name, at):
        first, size = spans[name]
        for spot in range(0, size, width):
            for number, ref in enumerate((own_ref, other_ref)):
                cols = slice(number * row_total, (number + 1) * row_total)
                turned = ref[:, first + spot : first + spot + width].T
                turned_ref[at + spot : at + spot + width, cols] = turned

    def pick(at, rows):
        parts = []
        for chip in range(chips):
            first = at + (chip * 2 + core) * rows
            parts.append(turned_ref[pl.ds(pl.multiple_of(first, 16), rows), :])
        return jnp.concatenate(parts, axis=0)

    def send(source_ref, rows, half, first, stride=None):
        step = first_steps[half] // 2
        bit = lax.rem(lax.div(spot_ref[0], first_steps[half]), 2)
        for index in range(chips // 2):
            for which in range(2):
                own_bit = bit if which == 0 else 1 - bit
                chip = index // step * 2 * step + own_bit * step + index % step
                at = chip * (stride or rows)
                copy = pltpu.make_async_copy(
                    source_ref.at[pl.ds(pl.multiple_of(at, 16), rows), :],
                    out_refs[half * 2 + which].at[index, pl.ds(first, rows), :],
                    sems.at[len(copies)],
                )
                copy.start()
                copies.append(copy)

    def product(left, names, column):
        right = view(names, column, width)
        total = dot_nn(left[:, :row_total], right[0])
        return total + dot_nn(left[:, row_total:], right[1])

    blocks = (
        [("normed", "qkv_grad", column) for column in range(3)]
        + [("mixed", "branch", 0)]
        + [("normed_two", "pre_grad", column) for column in range(hidden // width)]
    )
    turned_at = {"normed": 0, "mixed": width, "normed_two": 2 * width, "act": 3 * width}
    picked = {}
    for number, (left, right, column) in enumerate(blocks):
        if left not in picked:
            turn_rows(left, turned_at[left])
            picked = {left: pick(turned_at[left], share)}
        hold_ref[number] = product(picked[left], right, column).astype(hold_ref.dtype)
        send(hold_ref.at[number], share, number // 6, number % 6 * share)
    small = sum(part.astype(jnp.float32) for part in view("small"))
    small_ref[...] = small.astype(small_ref.dtype)
    small_share = row_total // dp_size
    turn_rows("act", turned_at["act"])
    feed_rows = hidden // dp_size
    for chip in range(chips):
        at = turned_at["act"] + (chip * 2 + core) * feed_rows
        left = turned_ref[pl.ds(pl.multiple_of(at, 16), feed_rows), :]
        feed_ref[chip * feed_rows : (chip + 1) * feed_rows, :] = product(left, "cot", 0).astype(
            feed_ref.dtype
        )
    send(feed_ref, feed_rows, 1, (len(blocks) - 6) * share)
    own_small = small_ref.at[pl.ds(pl.multiple_of(core * small_share, 16), (dp_size - 1) * small_share), :]
    send(own_small, small_share, 0, 6 * share, 2 * small_share)
    for copy in copies:
        copy.wait()


def weight_grad(spots, dp_size, first_steps, hidden, own, other):
    row_total, columns = own.shape
    width = (columns - 2 * hidden) // 9
    bf16 = jnp.bfloat16
    blocks = 4 + hidden // width
    chips = dp_size // 2
    share = width // dp_size
    rows = [6 * share + row_total // dp_size, (blocks - 6) * share + hidden // dp_size]
    inside = pl.BlockSpec(memory_space=pltpu.VMEM)
    outside = pl.BlockSpec(memory_space=pl.ANY)
    return run_kernel(
        partial(weight_grad_body, dp_size, first_steps, hidden),
        (spots, own, other),
        [pl.BlockSpec(memory_space=pltpu.SMEM), inside, inside],
        out_shape=[
            jax.ShapeDtypeStruct((chips // 2, rows[half], width), bf16)
            for half in range(2)
            for _ in range(2)
        ],
        out_specs=[outside] * 4,
        scratch_shapes=[
            pltpu.VMEM((3 * width + hidden, 2 * row_total), bf16),
            pltpu.VMEM((blocks, chips * share, width), bf16),
            pltpu.VMEM((hidden // 2, width), bf16),
            pltpu.VMEM((row_total, width), bf16),
            pltpu.SemaphoreType.DMA(((blocks + 2) * chips,)),
        ],
    )


def add_split_body(step, part_steps, spot_ref, keep_ref, *refs):
    *got_refs, send_ref, held_ref = refs
    bit = lax.rem(lax.div(spot_ref[0], step), 2)
    for number, got_ref in enumerate(got_refs):

        @pl.when(pl.program_id(0) // part_steps == number)
        def _(got_ref=got_ref):
            for out_ref, which in ((send_ref, 1 - bit), (held_ref, bit)):
                values = keep_ref[:, which].astype(jnp.float32)
                values = values + got_ref[:, which].astype(jnp.float32)
                out_ref[...] = values.astype(out_ref.dtype)


def add_split(spots, keep, gots, at, step, left):
    left = sorted(left, reverse=True)
    place_of = left.index(step)
    shape = keep.shape
    width = shape[-1]
    outer = math.prod(shape[:at]) * 2**place_of
    part_outer = outer // len(gots)
    inner_rows = keep.size // (outer * 2 * width)
    rows_step = inner_rows
    while rows_step > 320 and rows_step % 32 == 0:
        rows_step //= 2
    outer_step = 1
    while part_outer % (2 * outer_step) == 0 and 2 * outer_step * rows_step <= 320:
        outer_step *= 2
    part_steps = part_outer // outer_step
    block_in = (outer_step, 2, rows_step, width)
    block_out = pl.BlockSpec((outer_step, rows_step, width), lambda first, rows: (first, rows, 0))

    def part_spec(number):
        def pick(first, rows):
            return (jnp.clip(first - number * part_steps, 0, part_steps - 1), 0, rows, 0)

        return pl.BlockSpec(block_in, pick)

    outs = run_kernel(
        partial(add_split_body, step, part_steps),
        (spots, keep.reshape((outer, 2, inner_rows, width)))
        + tuple(got.reshape((part_outer, 2, inner_rows, width)) for got in gots),
        [
            pl.BlockSpec(memory_space=pltpu.SMEM),
            pl.BlockSpec(block_in, lambda first, rows: (first, 0, rows, 0)),
        ]
        + [part_spec(number) for number in range(len(gots))],
        grid=(outer // outer_step, inner_rows // rows_step),
        out_shape=[jax.ShapeDtypeStruct((outer, inner_rows, width), keep.dtype)] * 2,
        out_specs=[block_out] * 2,
    )
    rest = shape[:at] + (-1,) + shape[at + 1 :]
    return outs[0].reshape(rest), outs[1].reshape(rest)


def shards(
    patches,
    bias_token,
    gen_attn,
    gen_gain,
    gen_ff_in,
    gen_ff_out,
    gen_kernel,
    gen_bias,
    pos_table,
    norm_gain,
    norm_bias,
    w_qkv,
    w_out,
    w_fc1,
    bias_in,
    w_fc2,
    wavelengths,
    kept,
    counts,
    cotangent,
):
    group_size, slot_count, bands_dev, pixel_count = patches.shape
    dp_size = lax.axis_size("dp")
    band_size = lax.axis_size("band")
    device_count = dp_size * band_size
    local_images = group_size // band_size
    model_width = w_out.shape[1]
    row_total = local_images * slot_count
    own_pixels = pixel_count // device_count
    share = own_pixels * band_size
    groups = 2
    group_bands = bands_dev // groups
    f32 = jnp.float32
    bf16 = jnp.bfloat16
    spot = lax.axis_index("band")
    spots = jnp.stack([lax.axis_index("dp"), spot]).astype(jnp.int32)

    own_kernel, embed_bias, band_states, *gen_kept = generate_fast(
        wavelengths,
        bias_token,
        gen_attn,
        gen_gain,
        gen_ff_in,
        gen_ff_out,
        gen_bias,
        gen_kernel,
    )
    hidden = w_fc1.shape[1]
    weight_rows = [w_qkv.shape[0]] * (4 + hidden // model_width) + [w_fc2.shape[0]]
    stack = stack_weights((w_qkv, w_out, w_fc1, w_fc2))
    patch_rows = flatten_rows(
        patches.reshape(group_size * slot_count, bands_dev, pixel_count), (own_kernel,)
    )
    own_kernel = own_kernel.reshape(own_pixels, band_size, bands_dev, model_width)
    other_bands = range(1, band_size)
    dp_steps = bit_steps(dp_size)[1:]
    orders = [turn(dp_steps, group) for group in range(groups)]

    sent = [
        lax.dynamic_index_in_dim(own_kernel, spot ^ key, 1, keepdims=False).transpose(1, 0, 2)
        for key in range(band_size)
    ]
    got = [swap(sent[key], "band", key) for key in other_bands]
    *got, patch_rows, stack = together(*got, patch_rows, stack)
    piece = place(
        [([key], block[None]) for key, block in enumerate([sent[0]] + got)], "band", 1
    ).reshape(bands_dev, share, model_width)

    own_pieces = [piece[group * group_bands : (group + 1) * group_bands] for group in range(groups)]
    held = [own_piece[None] for own_piece in own_pieces]
    held_keys = [[0] for _ in range(groups)]
    kernel_groups = [[([0], piece[None])] for _ in range(groups)]
    waiting = []
    stacks = {0: stack}
    stack_keys = [band_size // 2] + [key for key in other_bands if key != band_size // 2]
    for stage in range(len(dp_steps)):
        last = stage == len(dp_steps) - 1
        now_keys = stack_keys if last else stack_keys[:1]
        stack_keys = stack_keys[len(now_keys) :]
        got = [swap(held[group], "dp", orders[group][stage]) for group in range(groups)]
        if stage == 0:
            core_got = swap(piece, "dp", 1)
        elif waiting:
            core_got = swap(waiting[0][2], "dp", 1)
        stack_got = [swap(stack, "band", key) for key in now_keys]
        got[0], got[1], core_got, stack, *stack_got = together(*got, core_got, stack, *stack_got)
        stacks.update(zip(now_keys, stack_got))
        if stage == 0:
            for blocks in kernel_groups:
                blocks.append(([1], core_got[None]))
        elif waiting:
            group, keys, _ = waiting.pop(0)
            kernel_groups[group].append(([key ^ 1 for key in keys], core_got))
        for group in range(groups):
            keys = [key ^ orders[group][stage] for key in held_keys[group]]
            kernel_groups[group].append((keys, got[group]))
            waiting.append((group, keys, got[group]))
            if not last:
                held[group] = jnp.concatenate([held[group], got[group]], axis=0)
                held_keys[group] = held_keys[group] + keys
    for group, keys, last_got in waiting:
        kernel_groups[group].append(([key ^ 1 for key in keys], swap(last_got, "dp", 1)))

    planes = plane_weights(spots, [stacks[key] for key in range(band_size)], weight_rows)
    got = [swap(plane, "dp", orders[half][0]) for half, plane in enumerate(planes)]
    embedded = embed_share(spots, patch_rows, kernel_groups, band_size)
    *embedded, first_got, last_got = together(*embedded, *got)
    held = [
        jnp.concatenate([plane[None], got[None]], axis=0)
        for plane, got in zip(planes, (first_got, last_got))
    ]
    held_keys = [[0, orders[half][0]] for half in range(2)]
    for stage in range(1, len(dp_steps) - 1):
        for half in range(2):
            step = orders[half][stage]
            held[half] = jnp.concatenate([held[half], swap(held[half], "dp", step)], axis=0)
            held_keys[half] = held_keys[half] + [key ^ step for key in held_keys[half]]
    got = [swap(held[half], "dp", orders[half][-1]) for half in range(2)]
    parts = [embedded[0]] + [swap(embedded[key], "band", key) for key in other_bands]
    held[0], held[1], got[0], got[1], *parts = together(*held, *got, *parts)
    weight_halves = []
    for half in range(2):
        blocks = [(held_keys[half], held[half])]
        blocks.append(([key ^ orders[half][-1] for key in held_keys[half]], got[half]))
        weight_halves.append(blocks + gather_core(blocks))

    valid_mask = jnp.arange(slot_count)[None, :] < counts[:, None]
    keep_col = valid_mask.reshape(row_total, 1)
    kept_flat = kept.reshape(row_total)
    pos_rows = jnp.take(pos_table, kept_flat, axis=0).astype(f32)
    base = embed_bias[0:1] + pos_rows
    tile_images = 2 if local_images % 2 == 0 else 1
    tile_rows = tile_images * slot_count
    image_spot = jnp.arange(tile_rows) // slot_count
    same_image = image_spot[:, None] == image_spot[None, :]
    mask = jnp.where(same_image[None] & valid_mask.reshape(-1, 1, tile_rows), 0.0, -1e30)
    cot = jnp.where(keep_col, cotangent.reshape(row_total, model_width), 0)
    (
        result,
        grad_embed,
        stash,
        sums,
    ) = block(
        parts,
        weight_halves,
        spots,
        base,
        cot,
        keep_col.astype(f32),
        mask.astype(f32),
        norm_gain.astype(f32),
        norm_bias.astype(f32),
        bias_in.astype(f32)[None],
        kept_flat[None],
    )

    grads = [grad_embed] + [swap(grad_embed, "band", key) for key in other_bands]
    first_steps = [order[0] for order in orders]
    weight_split = weight_grad(
        spots, dp_size, first_steps, hidden, stash, swap(stash, "dp", 1)
    )
    mixed = together(*grads, *weight_split)
    grads, weight_split = list(mixed[:band_size]), mixed[band_size:]

    weight_got = [
        swap(weight_split[2 * half + 1], "dp", first_steps[half]) for half in range(2)
    ]
    kernel_split = []
    for group in range(groups):
        *sends, keep = kernel_grad_part(
            spots,
            patch_rows,
            grads,
            group * group_bands,
            group_bands,
            bands_dev,
            dp_size,
            (),
        )
        core_got = [swap(send, "dp", 1) for send in sends]
        kernel_split += add_split(spots, keep, core_got, 1, orders[group][0], dp_steps)
    weight_got[0], weight_got[1], *kernel_split = together(*weight_got, *kernel_split)
    weight_sums = [add_low(weight_split[2 * half], weight_got[half]) for half in range(2)]
    small_share = row_total // device_count
    half_rows = [weight_rows[:6] + [small_share], weight_rows[6:]]
    early_blocks = [0, 1, 2, 3, 6]
    late_blocks = [4, 5]

    def cut_blocks(values, rows_list, numbers):
        lead = values.shape[0]
        parts = []
        for number in numbers:
            rows = rows_list[number]
            first = sum(rows_list[:number]) * band_size
            part = values[:, first : first + rows * band_size]
            parts.append(part.reshape(lead, band_size, rows, model_width))
        return parts

    def over_band(by_band):
        sent = [
            lax.dynamic_index_in_dim(by_band, spot ^ key, 1, keepdims=False)
            for key in range(band_size)
        ]
        return [sent[0]] + [swap(sent[key], "band", key) for key in other_bands]

    def total(blocks):
        return sum(block_sum.astype(f32) for block_sum in blocks)

    def over_chips(values, order, first=0):
        for stage in range(first, len(order)):
            send, keep = split_half(values, 0, order[stage], order[stage:])
            values = add_low(keep, swap(send, "dp", order[stage]))
        return values

    update = patch_grad(spots, grads, kernel_groups, pixel_count, ())
    for stage in range(len(dp_steps)):
        last = stage == len(dp_steps) - 1
        got = [swap(kernel_split[2 * group], "dp", orders[group][stage]) for group in range(groups)]
        if stage == 0:
            early = cut_blocks(weight_sums[0], half_rows[0], early_blocks)
            part_got = over_band(jnp.concatenate(early, axis=2))
            got[0], got[1], update, weight_sums[1], *part_got = together(
                *got, update, weight_sums[1], *part_got
            )
            early = total(part_got).astype(bf16)
            early_rows = early.shape[1]
            late = cut_blocks(weight_sums[0], half_rows[0], late_blocks)
            late = [part.reshape(part.shape[0], -1, model_width) for part in late]
            weight_sums[0] = jnp.concatenate([early, *late], axis=1)
        else:
            got[0], got[1], weight_sums[0] = together(*got, weight_sums[0])
        if not last:
            kernel_split = [
                part
                for group in range(groups)
                for part in add_split(
                    spots,
                    kernel_split[2 * group + 1],
                    [got[group]],
                    1,
                    orders[group][stage + 1],
                    orders[group][stage + 1 :],
                )
            ]
    kernel_sums = [add_low(kernel_split[2 * group + 1], got[group]) for group in range(groups)]

    own_part = jnp.concatenate(kernel_sums, axis=0)
    own_part = own_part.reshape(bands_dev, band_size, own_pixels, model_width)
    own_part = own_part.transpose(1, 2, 0, 3)
    sent = [
        lax.dynamic_index_in_dim(own_part, spot ^ key, 0, keepdims=False)
        for key in range(band_size)
    ]
    pieces = [sent[0]] + [swap(sent[key], "band", key) for key in other_bands]
    weight_sums = [over_chips(weight_sums[half], orders[half], 1) for half in range(2)]
    grad_patches = unflatten_rows(update, bands_dev, (sent[0],))
    weight_sums[0], weight_sums[1], grad_patches, *pieces = together(
        *weight_sums, grad_patches, *pieces
    )
    grad_gen_kernel, tail = states_grad(spots, band_states, gen_kernel, pieces, sums)
    weight_sums[0], weight_sums[1], tail = together(*weight_sums, tail)

    small = weight_sums[0][:, early_rows - small_share : early_rows]
    small_steps = [("band", step) for step in bit_steps(band_size)]
    small_steps += [("dp", step) for step in turn(bit_steps(dp_size), 1)]

    def widen(values, number):
        return jnp.concatenate([values, swap(values, *small_steps[number])], axis=0)

    tail = total([tail] + [swap(tail, "band", key) for key in other_bands])
    small = widen(small, 0)
    tail, small, weight_sums[0], weight_sums[1] = together(tail, small, *weight_sums)
    late_rows = [half_rows[0][number] for number in late_blocks]
    late = cut_blocks(weight_sums[0][:, early_rows:], late_rows, range(len(late_rows)))
    late += cut_blocks(weight_sums[1], half_rows[1], range(len(half_rows[1])))
    last_sum = total(over_band(jnp.concatenate(late, axis=2)))
    for number, step in enumerate(turn(bit_steps(dp_size), 1)):
        got = swap(tail, "dp", step)
        if number + 1 < len(small_steps):
            small = widen(small, number + 1)
        got, small = together(got, small)
        tail = tail + got
    for number in range(len(bit_steps(dp_size)) + 1, len(small_steps)):
        small = widen(small, number)
    own_grads = jnp.concatenate(
        [weight_sums[0][0, : early_rows - small_share].astype(f32), last_sum[0]], axis=0
    )
    small_order = (jnp.arange(dp_size) ^ spots[0])[:, None] * band_size
    small_order = (small_order + (jnp.arange(band_size) ^ spots[1])[None, :]).reshape(-1)
    small = small.reshape(2, dp_size // 2, band_size, small_share, model_width)
    small = small.transpose(1, 0, 2, 3, 4).reshape(-1, small_share, model_width)
    small = jnp.take(small, small_order, axis=0).reshape(row_total, model_width)
    own_blocks = []
    done = 0
    for rows in weight_rows:
        own_blocks.append(own_grads[done : done + rows])
        done += rows
    grad_qkv_own = jnp.concatenate(own_blocks[:3], axis=1)
    grad_out_own = own_blocks[3]
    grad_fc_in_own = jnp.concatenate(own_blocks[4:-1], axis=1)
    grad_fc_out_own = own_blocks[-1]
    grad_token, grad_attn, grad_gain_gen, grad_ff_first, grad_ff_second, grad_gen_bias = (
        generate_back(
            tail,
            gen_attn,
            gen_gain,
            gen_ff_in,
            gen_ff_out,
            gen_bias,
            gen_kept,
        )
    )

    small = small.astype(f32)
    sums_at = small.shape[0] - 16
    grad_pos_all = small[: pos_table.shape[0]]
    grad_gains = small[sums_at + 1 : sums_at + 3]
    grad_shifts = small[sums_at + 3 : sums_at + 5]
    grad_bias_all = small[sums_at + 8 : sums_at + 8 + hidden // model_width].reshape(-1)
    grad_patches = grad_patches.reshape(group_size, slot_count, bands_dev, pixel_count)
    return (
        result.reshape(local_images, slot_count, model_width),
        grad_patches,
        grad_token[0],
        grad_attn,
        grad_gain_gen,
        grad_ff_first,
        grad_ff_second,
        grad_gen_kernel,
        grad_gen_bias,
        grad_pos_all,
        grad_gains,
        grad_shifts,
        grad_qkv_own,
        grad_out_own,
        grad_fc_in_own,
        grad_bias_all,
        grad_fc_out_own,
    )


def solution(mesh):
    placed = (
        P("dp", None, "band", None),
        P(),
        P(),
        P(),
        P(),
        P(),
        P(None, ("dp", "band")),
        P(),
        P(),
        P(),
        P(),
        P(("dp", "band"), None),
        P(("dp", "band"), None),
        P(("dp", "band"), None),
        P(),
        P(("dp", "band"), None),
        P(),
        P(("dp", "band"), None),
        P(("dp", "band")),
        P(("dp", "band"), None, None),
    )
    return jax.shard_map(
        shards,
        mesh=mesh,
        in_specs=placed,
        out_specs=(
            P(("dp", "band"), None, None),
            P("dp", None, "band", None),
            P(),
            P(),
            P(),
            P(),
            P(),
            P(None, ("dp", "band")),
            P(),
            P(),
            P(),
            P(),
            P(("dp", "band"), None),
            P(("dp", "band"), None),
            P(("dp", "band"), None),
            P(),
            P(("dp", "band"), None),
        ),
        check_vma=False,
    )
```

```python
from functools import partial
import math

import jax
import jax.numpy as jnp
from jax import lax
from jax.experimental import pallas as pl
from jax.experimental.pallas import tpu as pltpu
from jax.sharding import PartitionSpec as P

HEADS = 12
HDIM = 64
GEN_HEADS = 4


def inner(left_arr, right_arr):
    return lax.dot_general(
        left_arr, right_arr, (((0,), (0,)), ((), ())), preferred_element_type=jnp.float32
    )


def times_transpose(left_arr, right_arr):
    return lax.dot_general(
        left_arr, right_arr, (((1,), (1,)), ((), ())), preferred_element_type=jnp.float32
    )


def bit_steps(size):
    steps = []
    step = 1
    while step < size:
        steps.append(step)
        step *= 2
    return steps


def swap(values, axis, step):
    size = lax.axis_size(axis)
    return lax.ppermute(values, axis, [(spot, spot ^ step) for spot in range(size)])


def turn(items, by):
    by = by % max(len(items), 1)
    return items[by:] + items[:by]


def gather_core(blocks):
    return [([key ^ 1 for key in keys], swap(block, "dp", 1)) for keys, block in blocks]


def place(blocks, axis, at):
    spot = lax.axis_index(axis)
    first = blocks[0][1]
    count = sum(len(keys) for keys, _ in blocks)
    shape = first.shape[1 : at + 1] + (count,) + first.shape[at + 1 :]
    whole = jnp.zeros(shape, first.dtype)
    for keys, block in blocks:
        for number, key in enumerate(keys):
            whole = lax.dynamic_update_index_in_dim(whole, block[number], spot ^ key, at)
    return whole


def add_low(left_arr, right_arr):
    return (left_arr.astype(jnp.float32) + right_arr.astype(jnp.float32)).astype(left_arr.dtype)


def split_half(values, at, step, left):
    left = sorted(left, reverse=True)
    shape = values.shape
    values = values.reshape(shape[:at] + (2,) * len(left) + shape[at + 1 :])
    dim = at + left.index(step)
    bit = (lax.axis_index("dp") // step) % 2
    rest = shape[:at] + (-1,) + shape[at + 1 :]
    send = lax.dynamic_index_in_dim(values, 1 - bit, dim, keepdims=False)
    keep = lax.dynamic_index_in_dim(values, bit, dim, keepdims=False)
    return send.reshape(rest), keep.reshape(rest)


def together(*arrays):
    return lax.optimization_barrier(arrays)


def column_blocks(matrix, width):
    return [matrix[:, spot : spot + width] for spot in range(0, matrix.shape[1], width)]


def run_kernel(body, args, in_specs, after=(), **options):
    count = len(after)

    def whole(*refs):
        body(*refs[count:])

    return pl.pallas_call(
        whole,
        in_specs=[pl.BlockSpec(memory_space=pl.ANY)] * count + in_specs,
        compiler_params=pltpu.CompilerParams(vmem_limit_bytes=60 * 1024 * 1024),
        cost_estimate=pl.CostEstimate(flops=1000, bytes_accessed=1000, transcendentals=0),
        **options,
    )(*after, *args)


def dot_nn(left_arr, right_arr):
    return lax.dot_general(
        left_arr, right_arr, (((1,), (0,)), ((), ())), preferred_element_type=jnp.float32
    )


def norm_stats(values):
    center = values - jnp.mean(values, axis=-1, keepdims=True)
    spread = jnp.mean(center * center, axis=-1, keepdims=True)
    scale = lax.rsqrt(spread + 1e-06)
    return center * scale, scale


def norm_back(unit, scale, gain, grad):
    weighted = grad * gain
    first = jnp.mean(weighted, axis=-1, keepdims=True)
    second = jnp.mean(weighted * unit, axis=-1, keepdims=True)
    grad_values = (weighted - first - unit * second) * scale
    grad_gain = jnp.sum(grad * unit, axis=0, keepdims=True)
    grad_shift = jnp.sum(grad, axis=0, keepdims=True)
    return grad_values, grad_gain, grad_shift


def stash_spans(width, hidden):
    sizes = {
        "normed": width,
        "mixed": width,
        "normed_two": width,
        "act": hidden,
        "qkv_grad": 3 * width,
        "branch": width,
        "pre_grad": hidden,
        "cot": width,
        "small": width,
    }
    spans = {}
    first = 0
    for name, size in sizes.items():
        spans[name] = (first, size)
        first += size
    return spans


def block_body(part_count, tile_rows, ff_step, keys_lists, *refs):
    part_refs = refs[:part_count]
    weight_count = sum(len(keys_list) for keys_list in keys_lists)
    weight_refs = refs[part_count : part_count + weight_count]
    (
        spot_ref,
        base_ref,
        cot_ref,
        keep_ref,
        mask_ref,
        gain_ref,
        shift_ref,
        bias_ref,
        kept_ref,
        result_ref,
        embed_grad_ref,
        stash_ref,
        sums_ref,
        qkv_w,
        out_w,
        fc_in_w,
        fc_out_w,
        qkv_ref,
        probs_ref,
        total_ref,
        back_ref,
        mixed_grad_ref,
        bias_grad_ref,
        sems,
    ) = refs[part_count + weight_count :]
    bf16 = jnp.bfloat16
    f32 = jnp.float32
    width = base_ref.shape[1]
    hidden = fc_in_w.shape[1]
    spans = stash_spans(width, hidden)
    views = {name: stash_ref.at[:, pl.ds(first, size)] for name, (first, size) in spans.items()}
    normed_ref = views["normed"]
    mixed_ref = views["mixed"]
    normed_two_ref = views["normed_two"]
    act_ref = views["act"]
    qkv_grad_ref = views["qkv_grad"]
    branch_ref = views["branch"]
    pre_grad_ref = views["pre_grad"]
    views["cot"][...] = cot_ref[...]
    share = width // sum(len(keys) for keys in keys_lists[0])
    targets = (
        [(qkv_w, column, share) for column in range(3)]
        + [(out_w, 0, share)]
        + [(fc_in_w, column, share) for column in range(hidden // width)]
        + [(fc_out_w, 0, share * hidden // width)]
    )
    copies = {}
    for number, (target_ref, column, rows) in enumerate(targets):
        half, first = (0, number * share) if number < 6 else (1, (number - 6) * share)
        half_refs = weight_refs[: len(keys_lists[0])] if half == 0 else weight_refs[len(keys_lists[0]) :]
        for keys, weight_ref in zip(keys_lists[half], half_refs):
            for index, key in enumerate(keys):
                at = pl.multiple_of(jnp.bitwise_xor(spot_ref[0], key) * rows, rows)
                copy = pltpu.make_async_copy(
                    weight_ref.at[index, pl.ds(first, rows), :],
                    target_ref.at[pl.ds(at, rows), pl.ds(column * width, width)],
                    sems.at[sum(len(some) for some in copies.values())],
                )
                copy.start()
                copies.setdefault(id(target_ref), []).append(copy)

    def arrive(target_ref):
        for copy in copies[id(target_ref)]:
            copy.wait()

    row_total, width = base_ref.shape
    tiles = row_total // tile_rows
    head_pairs = HEADS // 2
    lanes = 2 * HDIM

    start = base_ref[...]
    for part_ref in part_refs:
        start = start + part_ref[...].astype(f32)
    unit_one, scale_one = norm_stats(start)
    normed = (unit_one * gain_ref[0:1] + shift_ref[0:1]).astype(bf16)
    normed_ref[...] = normed
    arrive(qkv_w)
    for spot in range(3):
        cols = slice(spot * width, (spot + 1) * width)
        qkv_ref[:, cols] = dot_nn(normed, qkv_w[:, cols]).astype(bf16)

    low_lanes = lax.broadcasted_iota(jnp.int32, (tile_rows, lanes), 1) < HDIM

    def half(values, odd):
        keep = jnp.logical_not(low_lanes) if odd else low_lanes
        return jnp.where(keep, values, jnp.zeros_like(values))

    def head_slices(pair, tile):
        rows = pl.ds(tile * tile_rows, tile_rows)
        cols = [
            pl.ds(pl.multiple_of(which * width + pair * lanes, lanes), lanes) for which in range(3)
        ]
        return rows, cols

    def attend(pair, carry):
        for tile in range(tiles):
            rows, cols = head_slices(pair, tile)
            queries, keys_arr, values_arr = [qkv_ref[rows, col] for col in cols]
            mixed = jnp.zeros((tile_rows, lanes), f32)
            for odd in range(2):
                scores = times_transpose(half(queries, odd), keys_arr) * HDIM ** (-0.5)
                scores = scores + mask_ref[tile]
                exponent = jnp.exp(scores - jnp.max(scores, axis=-1, keepdims=True))
                probs = exponent * (1.0 / jnp.sum(exponent, axis=-1, keepdims=True))
                probs_ref[(pair * 2 + odd) * tiles + tile] = probs
                mixed = mixed + dot_nn(probs.astype(bf16), half(values_arr, odd))
            mixed_ref[rows, cols[0]] = mixed.astype(bf16)
        return carry

    lax.fori_loop(0, head_pairs, attend, 0)
    arrive(out_w)
    middle = start + dot_nn(mixed_ref[...], out_w[...])
    unit_two, scale_two = norm_stats(middle)
    normed_two = (unit_two * gain_ref[1:2] + shift_ref[1:2]).astype(bf16)
    normed_two_ref[...] = normed_two
    total_ref[...] = middle
    back_ref[...] = jnp.zeros_like(back_ref)
    arrive(fc_in_w)
    arrive(fc_out_w)

    def feed(step, carry):
        cols = pl.ds(pl.multiple_of(step * ff_step, ff_step), ff_step)
        pre = dot_nn(normed_two_ref[...], fc_in_w[:, cols]) + bias_ref[:, cols]
        cdf = 0.5 * (1.0 + lax.erf(pre * 0.5**0.5))
        act = (pre * cdf).astype(bf16)
        act_ref[:, cols] = act
        slope = cdf + pre * (jnp.exp(-0.5 * pre * pre) * (2.0 * math.pi) ** (-0.5))
        pre_grad = slope * times_transpose(cot_ref[...], fc_out_w[cols, :])
        pre_grad = pre_grad.astype(bf16)
        pre_grad_ref[:, cols] = pre_grad
        bias_grad_ref[:, cols] = jnp.sum(pre_grad.astype(f32), axis=0, keepdims=True)
        total_ref[...] += dot_nn(act, fc_out_w[cols, :])
        back_ref[...] += times_transpose(pre_grad, fc_in_w[:, cols])
        return carry

    lax.fori_loop(0, fc_in_w.shape[1] // ff_step, feed, 0)
    result_ref[...] = (total_ref[...] * keep_ref[...]).astype(bf16)
    grad_norm, gain_two, shift_two = norm_back(unit_two, scale_two, gain_ref[1:2], back_ref[...])
    grad_middle = cot_ref[...].astype(f32) + grad_norm
    grad_branch = grad_middle.astype(bf16)
    branch_ref[...] = grad_branch
    mixed_grad_ref[...] = times_transpose(grad_branch, out_w[...]).astype(bf16)

    def attend_back(pair, carry):
        for tile in range(tiles):
            rows, cols = head_slices(pair, tile)
            queries, keys_arr, values_arr = [qkv_ref[rows, col] for col in cols]
            grad_mixed = mixed_grad_ref[rows, cols[0]]
            grads = [jnp.zeros((tile_rows, lanes), f32) for _ in range(3)]
            for odd in range(2):
                probs = probs_ref[(pair * 2 + odd) * tiles + tile]
                own_grad = half(grad_mixed, odd)
                grad_probs = times_transpose(own_grad, values_arr)
                grad_scores = probs * (
                    grad_probs - jnp.sum(grad_probs * probs, axis=-1, keepdims=True)
                )
                grad_scores = grad_scores.astype(bf16)
                grads[0] = grads[0] + dot_nn(grad_scores, half(keys_arr, odd))
                grads[1] = grads[1] + inner(grad_scores, half(queries, odd))
                grads[2] = grads[2] + inner(probs.astype(bf16), own_grad)
            for which, factor in enumerate((HDIM ** (-0.5), HDIM ** (-0.5), 1.0)):
                qkv_grad_ref[rows, cols[which]] = (grads[which] * factor).astype(bf16)
        return carry

    lax.fori_loop(0, head_pairs, attend_back, 0)
    back = jnp.zeros((row_total, width), f32)
    for spot in range(3):
        cols = slice(spot * width, (spot + 1) * width)
        back = back + times_transpose(qkv_grad_ref[:, cols], qkv_w[:, cols])
    grad_norm, gain_one, shift_one = norm_back(unit_one, scale_one, gain_ref[0:1], back)
    grad_start = grad_middle + grad_norm
    embed_grad_ref[...] = grad_start.astype(bf16)
    sums = jnp.concatenate(
        [jnp.sum(grad_start, axis=0, keepdims=True), gain_one, gain_two, shift_one, shift_two]
        + [jnp.zeros((3, width), f32)],
        axis=0,
    )
    sums_ref[...] = sums
    small_ref = views["small"]
    positions = small_ref.shape[0] - 16
    spots_at = lax.broadcasted_iota(jnp.int32, (positions, row_total), 0)
    one_hot = jnp.where(spots_at == kept_ref[...], 1.0, 0.0).astype(bf16)
    by_position = dot_nn(one_hot, grad_start.astype(bf16))
    cuts = [bias_grad_ref[:, spot : spot + width] for spot in range(0, hidden, width)]
    cuts.append(jnp.zeros((8 - len(cuts), width), f32))
    small_ref[...] = jnp.concatenate([by_position, sums, *cuts], axis=0).astype(bf16)


def block(parts, weight_halves, spots, base, cot, keep, mask, gains, shifts, bias, kept):
    row_total, width = base.shape
    tile_rows = mask.shape[1]
    hidden = bias.shape[1]
    bf16 = jnp.bfloat16
    f32 = jnp.float32
    keys_lists = [[keys for keys, _ in blocks] for blocks in weight_halves]
    weight_args = [block for blocks in weight_halves for _, block in blocks]
    pieces = sum(len(keys) for keys in keys_lists[0])
    inside = pl.BlockSpec(memory_space=pltpu.VMEM)
    outside = pl.BlockSpec(memory_space=pl.ANY)
    rows = (row_total, width)
    shapes = [
        (rows, bf16),
        (rows, bf16),
        ((row_total, sum(stash_spans(width, hidden)["small"])), bf16),
        ((8, width), f32),
    ]
    return run_kernel(
        partial(block_body, len(parts), tile_rows, 512, keys_lists),
        (*parts, *weight_args, spots, base, cot, keep, mask, gains, shifts, bias, kept),
        [inside] * len(parts)
        + [outside] * len(weight_args)
        + [pl.BlockSpec(memory_space=pltpu.SMEM)]
        + [inside] * 8,
        out_shape=[jax.ShapeDtypeStruct(shape, kind) for shape, kind in shapes],
        out_specs=[inside] * len(shapes),
        scratch_shapes=[
            pltpu.VMEM((width, 3 * width), bf16),
            pltpu.VMEM((width, width), bf16),
            pltpu.VMEM((width, hidden), bf16),
            pltpu.VMEM((hidden, width), bf16),
            pltpu.VMEM((row_total, 3 * width), bf16),
            pltpu.VMEM((HEADS * row_total // tile_rows, tile_rows, tile_rows), f32),
            pltpu.VMEM(rows, f32),
            pltpu.VMEM(rows, f32),
            pltpu.VMEM(rows, bf16),
            pltpu.VMEM((1, hidden), f32),
            pltpu.SemaphoreType.DMA(((5 + hidden // width) * pieces,)),
        ],
    )


def dot_full(left_arr, right_arr, left_dim=1, right_dim=0):
    return lax.dot_general(
        left_arr,
        right_arr,
        (((left_dim,), (right_dim,)), ((), ())),
        precision=lax.Precision.HIGH,
        preferred_element_type=jnp.float32,
    )


def head_part(values, head):
    size = values.shape[1] // GEN_HEADS
    lane = lax.broadcasted_iota(jnp.int32, values.shape, 1)
    inside = jnp.logical_and(lane >= head * size, lane < (head + 1) * size)
    return jnp.where(inside, values, 0.0)


def generate_body(
    waves_ref,
    token_ref,
    attn_hbm,
    gain_hbm,
    ff_in_hbm,
    ff_out_hbm,
    bias_w_hbm,
    columns_hbm,
    kernel_ref,
    embed_bias_ref,
    low_ref,
    states_ref,
    rows_ref,
    weights_ref,
    pre_ref,
    scales_ref,
    attn_ref,
    gain_ref,
    ff_in_ref,
    ff_out_ref,
    bias_w_ref,
    columns_ref,
    sems,
):
    f32 = jnp.float32
    copies = [
        pltpu.make_async_copy(source, target, sems.at[number])
        for number, (source, target) in enumerate(
            (
                (attn_hbm, attn_ref),
                (gain_hbm, gain_ref),
                (ff_in_hbm, ff_in_ref),
                (ff_out_hbm, ff_out_ref),
                (columns_hbm, columns_ref),
                (bias_w_hbm, bias_w_ref),
            )
        )
    ]
    for copy in copies:
        copy.start()
    bands = waves_ref.shape[1]
    width = token_ref.shape[1]
    padded = rows_ref.shape[1]
    square = (bands, bands)
    diagonal = lax.broadcasted_iota(jnp.int32, square, 0) == lax.broadcasted_iota(
        jnp.int32, square, 1
    )
    waves = jnp.broadcast_to(waves_ref[...].astype(f32), square)
    column = jnp.sum(jnp.where(diagonal, waves, 0.0), axis=1, keepdims=True)
    lane = lax.broadcasted_iota(jnp.int32, (bands, width), 1)
    half_width = width // 2
    number = jnp.where(lane < half_width, lane, lane - half_width).astype(f32)
    angles = column * jnp.exp(number * (-math.log(10000.0) / half_width))
    wave = jnp.where(lane < half_width, jnp.sin(angles), jnp.cos(angles))
    sequence = jnp.concatenate(
        [wave, token_ref[...].astype(f32), jnp.zeros((padded - bands - 1, width), f32)], axis=0
    )
    rows_ref[0] = sequence
    copies[0].wait()
    copies[1].wait()
    for which in range(3):
        rows_ref[1 + which] = dot_full(sequence, attn_ref[which].astype(f32))
    queries = rows_ref[1]
    keys_arr = rows_ref[2]
    values_arr = rows_ref[3]
    key_spot = lax.broadcasted_iota(jnp.int32, (padded, padded), 1)
    mixed = jnp.zeros((padded, width), f32)
    for head in range(GEN_HEADS):
        scores = dot_full(head_part(queries, head), keys_arr, 1, 1)
        scores = scores * (1.0 / math.sqrt(width // GEN_HEADS))
        scores = jnp.where(key_spot <= bands, scores, -1e30)
        exponent = jnp.exp(scores - jnp.max(scores, axis=-1, keepdims=True))
        weights = exponent / jnp.sum(exponent, axis=-1, keepdims=True)
        weights_ref[head] = weights
        mixed = mixed + dot_full(weights, head_part(values_arr, head))
    rows_ref[4] = mixed
    unit_one, scale_one = norm_stats(sequence + dot_full(mixed, attn_ref[3].astype(f32)))
    rows_ref[5] = unit_one
    first = unit_one * gain_ref[0:1].astype(f32)
    copies[2].wait()
    pre = dot_full(first, ff_in_ref[...].astype(f32))
    pre_ref[...] = pre
    hidden = pre * (0.5 * (1.0 + lax.erf(pre * 0.5**0.5)))
    copies[3].wait()
    unit_two, scale_two = norm_stats(first + dot_full(hidden, ff_out_ref[...].astype(f32)))
    rows_ref[6] = unit_two
    states = unit_two * gain_ref[1:2].astype(f32)
    states_ref[...] = states
    scales_ref[0] = jnp.broadcast_to(scale_one, (padded, width))
    scales_ref[1] = jnp.broadcast_to(scale_two, (padded, width))
    low = states[:bands].astype(jnp.bfloat16)
    low_ref[...] = low
    features = kernel_ref.shape[2]
    copies[4].wait()
    for pixel in range(kernel_ref.shape[0]):
        cols = slice(pixel * features, (pixel + 1) * features)
        kernel_ref[pixel] = dot_nn(low, columns_ref[:, cols]).astype(jnp.bfloat16)
    copies[5].wait()
    token_state = states[bands : bands + 8]
    embed_bias_ref[...] = dot_full(token_state, bias_w_ref[...].astype(f32))


def generate_fast(wavelengths, token, gen_attn, gen_gain, ff_in, ff_out, gen_bias, columns):
    f32 = jnp.float32
    bf16 = jnp.bfloat16
    bands = wavelengths.shape[0]
    width = token.shape[0]
    padded = -(-(bands + 1) // 8) * 8
    features = gen_bias.shape[1]
    shapes = [
        ((columns.shape[1] // features, bands, features), bf16),
        ((8, features), f32),
        ((bands, width), bf16),
        ((padded, width), f32),
        ((7, padded, width), f32),
        ((GEN_HEADS, padded, padded), f32),
        ((padded, ff_in.shape[1]), f32),
        ((2, padded, width), f32),
    ]
    inside = pl.BlockSpec(memory_space=pltpu.VMEM)
    outside = pl.BlockSpec(memory_space=pl.ANY)
    weights = (gen_attn, gen_gain, ff_in, ff_out, gen_bias, columns)
    return run_kernel(
        generate_body,
        (wavelengths[None], token[None], *weights),
        out_shape=[jax.ShapeDtypeStruct(shape, kind) for shape, kind in shapes],
        in_specs=[inside] * 2 + [outside] * 6,
        out_specs=[inside] * len(shapes),
        scratch_shapes=[pltpu.VMEM(weight.shape, bf16) for weight in weights]
        + [pltpu.SemaphoreType.DMA((6,))],
    )


def generate_back_body(
    tail_ref,
    attn_ref,
    gain_ref,
    ff_in_ref,
    ff_out_ref,
    bias_w_ref,
    states_ref,
    rows_ref,
    weights_ref,
    pre_ref,
    scales_ref,
    token_out,
    attn_out,
    gain_out,
    ff_in_out,
    ff_out_out,
    bias_out,
):
    f32 = jnp.float32
    padded, width = states_ref.shape
    features = bias_w_ref.shape[1]
    bands = padded - 8
    head_scale = 1.0 / math.sqrt(width // GEN_HEADS)
    cuts = [tail_ref[bands + spot : bands + spot + 1, :] for spot in range(features // width)]
    bias_grad = jnp.concatenate(cuts, axis=1)
    bias_grad = jnp.concatenate([bias_grad, jnp.zeros((7, features), f32)], axis=0)
    row_spot = lax.broadcasted_iota(jnp.int32, (padded - bands, width), 0)
    token_grad = dot_full(bias_grad, bias_w_ref[...].astype(f32), 1, 1)
    token_grad = jnp.where(row_spot == 0, token_grad[0:1], 0.0)
    grad_states = jnp.concatenate([tail_ref[:bands, :], token_grad], axis=0)
    token_state = states_ref[bands : bands + 8]
    first_row = lax.broadcasted_iota(jnp.int32, token_state.shape, 0) == 0
    bias_out[...] = dot_full(jnp.where(first_row, token_state, 0.0), bias_grad, 0, 0)
    unit_one = rows_ref[5]
    gain_one = gain_ref[0:1].astype(f32)
    gain_two = gain_ref[1:2].astype(f32)
    grad_two, gain_two_grad, _ = norm_back(rows_ref[6], scales_ref[1], gain_two, grad_states)
    pre = pre_ref[...]
    cdf = 0.5 * (1.0 + lax.erf(pre * 0.5**0.5))
    ff_out_out[...] = dot_full(pre * cdf, grad_two, 0, 0)
    slope = cdf + pre * (jnp.exp(-0.5 * pre * pre) * (2.0 * math.pi) ** (-0.5))
    grad_pre = slope * dot_full(grad_two, ff_out_ref[...].astype(f32), 1, 1)
    ff_in_out[...] = dot_full(unit_one * gain_one, grad_pre, 0, 0)
    grad_first = grad_two + dot_full(grad_pre, ff_in_ref[...].astype(f32), 1, 1)
    grad_one, gain_one_grad, _ = norm_back(unit_one, scales_ref[0], gain_one, grad_first)
    gain_out[...] = jnp.concatenate([gain_one_grad, gain_two_grad], axis=0)
    attn_out[3] = dot_full(rows_ref[4], grad_one, 0, 0)
    grad_mixed = dot_full(grad_one, attn_ref[3].astype(f32), 1, 1)
    sequence = rows_ref[0]
    queries = rows_ref[1]
    keys_arr = rows_ref[2]
    values_arr = rows_ref[3]
    grads = [jnp.zeros((padded, width), f32) for _ in range(3)]
    for head in range(GEN_HEADS):
        weights = weights_ref[head]
        own_grad = head_part(grad_mixed, head)
        grad_weights = dot_full(own_grad, values_arr, 1, 1)
        grad_scores = weights * (
            grad_weights - jnp.sum(grad_weights * weights, axis=-1, keepdims=True)
        )
        grad_scores = grad_scores * head_scale
        grads[0] = grads[0] + dot_full(grad_scores, head_part(keys_arr, head))
        grads[1] = grads[1] + dot_full(grad_scores, head_part(queries, head), 0, 0)
        grads[2] = grads[2] + dot_full(weights, own_grad, 0, 0)
    grad_sequence = grad_one
    for which in range(3):
        attn_out[which] = dot_full(sequence, grads[which], 0, 0)
        grad_sequence = grad_sequence + dot_full(
            grads[which], attn_ref[which].astype(f32), 1, 1
        )
    token_out[...] = grad_sequence[bands : bands + 1]


def generate_back(tail, gen_attn, gen_gain, ff_in, ff_out, gen_bias, kept_arrs):
    f32 = jnp.float32
    width = gen_gain.shape[1]
    shapes = [
        (1, width),
        gen_attn.shape,
        gen_gain.shape,
        ff_in.shape,
        ff_out.shape,
        gen_bias.shape,
    ]
    inside = pl.BlockSpec(memory_space=pltpu.VMEM)
    return run_kernel(
        generate_back_body,
        (tail, gen_attn, gen_gain, ff_in, ff_out, gen_bias, *kept_arrs),
        out_shape=[jax.ShapeDtypeStruct(shape, f32) for shape in shapes],
        in_specs=[inside] * (6 + len(kept_arrs)),
        out_specs=[inside] * len(shapes),
    )


def fill_kernel(keys_lists, piece_refs, spot, mat_ref, bands, pixels):
    for keys, piece_ref in zip(keys_lists, piece_refs):
        for number, key in enumerate(keys):
            share = piece_ref.shape[2]
            first = jnp.bitwise_xor(spot, key) * share
            for band in range(bands):
                rows = pl.ds(pl.multiple_of(band * pixels + first, share), share)
                mat_ref[rows, :] = piece_ref[number, band]


def fill_step(keys_lists, piece_refs, spot, mat_ref, band_step, group_steps):
    pixels = mat_ref.shape[0] // band_step
    step = pl.program_id(0)
    used = 0
    for group, keys_list in enumerate(keys_lists):
        group_refs = piece_refs[used : used + len(keys_list)]
        used += len(keys_list)

        @pl.when(step // group_steps == group)
        def _(keys_list=keys_list, group_refs=group_refs):
            fill_kernel(keys_list, group_refs, spot, mat_ref, band_step, pixels)


def embed_body(keys_lists, group_steps, band_step, *refs):
    spot_ref, patch_ref = refs[:2]
    count = sum(len(keys_list) for keys_list in keys_lists)
    piece_refs = refs[2 : 2 + count]
    *out_refs, mat_ref, total_ref = refs[2 + count :]
    step = pl.program_id(0)
    fill_step(keys_lists, piece_refs, spot_ref[0], mat_ref, band_step, group_steps)

    @pl.when(step == 0)
    def _():
        total_ref[...] = jnp.zeros_like(total_ref)

    total_ref[...] += dot_nn(patch_ref[...], mat_ref[...])

    @pl.when(step == pl.num_programs(0) - 1)
    def _():
        for key, out_ref in enumerate(out_refs):
            rows = out_ref.shape[0]
            first = pl.multiple_of(jnp.bitwise_xor(spot_ref[1], key) * rows, rows)
            out_ref[...] = total_ref[pl.ds(first, rows), :].astype(out_ref.dtype)


def group_band_count(kernel_groups):
    return min(block.shape[1] for blocks in kernel_groups for _, block in blocks)


def piece_specs(kernel_groups, band_step, first_group=0):
    group_steps = group_band_count(kernel_groups) // band_step
    specs = []
    arrays = []
    for group, blocks in enumerate(kernel_groups):
        for keys, block in blocks:
            whole = block.shape[1] > group_steps * band_step
            first = group * group_steps
            skip = first_group * group_steps

            def pick(step, first=first, whole=whole):
                here = jnp.clip(step - first, 0, group_steps - 1)
                return (0, here + first + skip if whole else here, 0, 0)

            specs.append(pl.BlockSpec((len(keys), band_step) + block.shape[2:], pick))
            arrays.append(block)
    keys_lists = [[keys for keys, _ in blocks] for blocks in kernel_groups]
    return specs, arrays, keys_lists, group_steps


def embed_share(spots, patch_rows, kernel_groups, owners):
    row_total = patch_rows.shape[0]
    blocks = kernel_groups[0]
    group_bands = group_band_count(kernel_groups)
    width = blocks[0][1].shape[3]
    pixels = sum(len(keys) for keys, _ in blocks) * blocks[0][1].shape[2]
    band_step = min(4, group_bands)
    depth = band_step * pixels
    specs, arrays, keys_lists, group_steps = piece_specs(kernel_groups, band_step)
    rows = row_total // owners
    return run_kernel(
        partial(embed_body, keys_lists, group_steps, band_step),
        [spots, patch_rows, *arrays],
        [
            pl.BlockSpec(memory_space=pltpu.SMEM),
            pl.BlockSpec((row_total, depth), lambda step: (0, step)),
        ]
        + specs,
        grid=(group_steps * len(kernel_groups),),
        out_shape=[jax.ShapeDtypeStruct((rows, width), jnp.bfloat16)] * owners,
        out_specs=[pl.BlockSpec((rows, width), lambda step: (0, 0))] * owners,
        scratch_shapes=[
            pltpu.VMEM((depth, width), jnp.bfloat16),
            pltpu.VMEM((row_total, width), jnp.float32),
        ],
    )


def kernel_grad_body(dp_size, band_step, *refs):
    spot_ref, patch_ref = refs[:2]
    *grad_refs, first_ref, last_ref, keep_ref, hold_ref = refs[2:]
    rows = grad_refs[0].shape[0]
    total = 0.0
    for key, grad_ref in enumerate(grad_refs):
        first = pl.multiple_of(jnp.bitwise_xor(spot_ref[1], key) * rows, rows)
        total = total + inner(patch_ref[pl.ds(first, rows), :], grad_ref[...])
    hold_ref[...] = total.astype(hold_ref.dtype)
    pixels = hold_ref.shape[0] // band_step
    share = pixels // dp_size
    core = lax.rem(spot_ref[0], 2)
    for band in range(band_step):
        for chip in range(dp_size // 2):
            base = band * pixels + chip * 2 * share
            kept = pl.multiple_of(base + core * share, share)
            keep_ref[band, chip] = hold_ref[pl.ds(kept, share), :]

    half = pl.num_programs(0) // 2
    for number, send_ref in enumerate((first_ref, last_ref)):

        @pl.when(pl.program_id(0) // half == number)
        def _(send_ref=send_ref):
            for band in range(band_step):
                for chip in range(dp_size // 2):
                    base = band * pixels + chip * 2 * share
                    sent = pl.multiple_of(base + (1 - core) * share, share)
                    send_ref[band, chip] = hold_ref[pl.ds(sent, share), :]


def kernel_grad_part(spots, patch_rows, grads, first_band, group_bands, bands_dev, dp_size, after):
    row_total = patch_rows.shape[0]
    width = grads[0].shape[1]
    band_step = min(4, group_bands // 2)
    pixels = patch_rows.shape[1] // bands_dev
    depth = band_step * pixels
    offset = first_band // band_step
    share = pixels // dp_size
    chips = (dp_size // 2, share, width)
    steps = group_bands // band_step
    block = (band_step,) + chips
    return run_kernel(
        partial(kernel_grad_body, dp_size, band_step),
        (spots, patch_rows, *grads),
        after=after,
        grid=(steps,),
        out_shape=[
            jax.ShapeDtypeStruct((bands,) + chips, jnp.bfloat16)
            for bands in (group_bands // 2, group_bands // 2, group_bands)
        ],
        in_specs=[
            pl.BlockSpec(memory_space=pltpu.SMEM),
            pl.BlockSpec((row_total, depth), lambda step: (0, offset + step)),
        ]
        + [pl.BlockSpec(grad.shape, lambda step: (0, 0)) for grad in grads],
        out_specs=[
            pl.BlockSpec(block, lambda step: (jnp.minimum(step, steps // 2 - 1), 0, 0, 0)),
            pl.BlockSpec(block, lambda step: (jnp.maximum(step - steps // 2, 0), 0, 0, 0)),
            pl.BlockSpec(block, lambda step: (step, 0, 0, 0)),
        ],
        scratch_shapes=[pltpu.VMEM((depth, width), jnp.bfloat16)],
    )


def patch_grad_body(keys_lists, grad_count, group_steps, band_step, *refs):
    spot_ref = refs[0]
    grad_refs = refs[1 : 1 + grad_count]
    out_ref, mat_ref = refs[-2:]
    piece_refs = refs[1 + grad_count : -2]
    fill_step(keys_lists, piece_refs, spot_ref[0], mat_ref, band_step, group_steps)
    for key, grad_ref in enumerate(grad_refs):
        rows = grad_ref.shape[0]
        first = pl.multiple_of(jnp.bitwise_xor(spot_ref[1], key) * rows, rows)
        out_ref[pl.ds(first, rows), :] = times_transpose(grad_ref[...], mat_ref[...]).astype(
            out_ref.dtype
        )


def patch_grad(spots, grads, kernel_groups, pixels, first_group, after):
    rows, width = grads[0].shape
    row_total = rows * len(grads)
    band_step = min(4, group_band_count(kernel_groups))
    depth = band_step * pixels
    specs, arrays, keys_lists, group_steps = piece_specs(kernel_groups, band_step, first_group)
    steps = group_steps * len(kernel_groups)
    return run_kernel(
        partial(patch_grad_body, keys_lists, len(grads), group_steps, band_step),
        [spots, *grads, *arrays],
        [pl.BlockSpec(memory_space=pltpu.SMEM)]
        + [pl.BlockSpec(grad.shape, lambda step: (0, 0)) for grad in grads]
        + specs,
        after=after,
        grid=(steps,),
        out_shape=jax.ShapeDtypeStruct((row_total, steps * depth), jnp.bfloat16),
        out_specs=pl.BlockSpec((row_total, depth), lambda step: (0, step)),
        scratch_shapes=[pltpu.VMEM((depth, width), jnp.bfloat16)],
    )


def states_grad_body(batches, low_ref, columns_ref, *refs):
    *piece_refs, sums_ref, spot_ref, grad_ref, part_ref, hold_ref = refs
    pixels, bands, width = piece_refs[0].shape
    for number, piece_ref in enumerate(piece_refs):
        key, batch = divmod(number, batches)
        first = (jnp.bitwise_xor(spot_ref[1], key) * batches + batch) * bands
        hold_ref[:, pl.ds(pl.multiple_of(first, bands), bands), :] = piece_ref[...]
    total = 0.0
    for pixel in range(pixels):
        cols = slice(pixel * width, (pixel + 1) * width)
        grads = hold_ref[pixel]
        grad_ref[:, cols] = inner(low_ref[...], grads)
        total = total + times_transpose(grads, columns_ref[:, cols])
    bands, states = total.shape
    part_ref[:bands, :] = total
    rows = [sums_ref[0:1, spot : spot + states] for spot in range(0, width, states)]
    rows.append(jnp.zeros((part_ref.shape[0] - bands - len(rows), states), jnp.float32))
    part_ref[bands:, :] = jnp.concatenate(rows, axis=0)


def states_grad(spots, low, columns, pieces, sums):
    pixels, bands, width = pieces[0].shape
    tail_rows = low.shape[0] + -(-width // low.shape[1] // 8) * 8
    if bands % 16:
        blocks = [([key], piece[None]) for key, piece in enumerate(pieces)]
        whole = place(blocks, "band", 1).reshape(pixels, -1, width)
        grads = whole.transpose(1, 0, 2).reshape(low.shape[0], -1)
        rows = [times_transpose(grads, columns), sums[0].reshape(-1, low.shape[1])]
        tail = jnp.concatenate(rows, axis=0)
        tail = jnp.pad(tail, ((0, tail_rows - tail.shape[0]), (0, 0)))
        return inner(low, grads), tail
    inside = pl.BlockSpec(memory_space=pltpu.VMEM)
    return run_kernel(
        partial(states_grad_body, 1),
        (low, columns, *pieces, sums, spots),
        out_shape=[
            jax.ShapeDtypeStruct(columns.shape, jnp.float32),
            jax.ShapeDtypeStruct((tail_rows, low.shape[1]), jnp.float32),
        ],
        in_specs=[inside] * (3 + len(pieces)) + [pl.BlockSpec(memory_space=pltpu.SMEM)],
        out_specs=[inside, inside],
        scratch_shapes=[pltpu.VMEM((pixels, bands * len(pieces), width), jnp.bfloat16)],
    )


def flatten_body(in_ref, out_ref):
    out_ref[...] = in_ref[...].reshape(out_ref.shape)


def unflatten_body(*refs):
    *in_refs, out_ref = refs
    done = 0
    for in_ref in in_refs:
        part = in_ref[...]
        bands = part.shape[1] // out_ref.shape[2]
        out_ref[:, done : done + bands, :] = part.reshape(-1, bands, out_ref.shape[2])
        done += bands


def flatten_rows(cube, after):
    rows, bands, pixels = cube.shape
    step_rows = 64
    return run_kernel(
        flatten_body,
        (cube,),
        [pl.BlockSpec((step_rows, bands, pixels), lambda step: (step, 0, 0))],
        after=after,
        grid=(rows // step_rows,),
        out_shape=jax.ShapeDtypeStruct((rows, bands * pixels), cube.dtype),
        out_specs=pl.BlockSpec((step_rows, bands * pixels), lambda step: (step, 0)),
    )


def unflatten_rows(flats, bands, after):
    rows = flats[0].shape[0]
    pixels = sum(flat.shape[1] for flat in flats) // bands
    step_rows = 64
    return run_kernel(
        unflatten_body,
        flats,
        [pl.BlockSpec((step_rows, flat.shape[1]), lambda step: (step, 0)) for flat in flats],
        after=after,
        grid=(rows // step_rows,),
        out_shape=jax.ShapeDtypeStruct((rows, bands, pixels), flats[0].dtype),
        out_specs=pl.BlockSpec((step_rows, bands, pixels), lambda step: (step, 0, 0)),
    )


def stack_body(*refs):
    *part_refs, out_ref, hold_ref = refs
    width = out_ref.shape[1]
    first = 0
    for part_ref in part_refs:
        rows = part_ref.shape[0]
        for spot in range(0, part_ref.shape[1], width):
            hold_ref[pl.ds(first, rows), :] = part_ref[:, spot : spot + width].astype(jnp.float32)
            first += rows
    out_ref[...] = hold_ref[...].astype(out_ref.dtype)


def stack_weights(shards_in):
    width = shards_in[-1].shape[1]
    if any(shard.shape[0] % 8 for shard in shards_in):
        return jnp.concatenate(
            [part for shard in shards_in for part in column_blocks(shard, width)], axis=0
        )
    row_total = sum(shard.size for shard in shards_in) // width
    inside = pl.BlockSpec(memory_space=pltpu.VMEM)
    return run_kernel(
        stack_body,
        shards_in,
        [inside] * len(shards_in),
        out_shape=jax.ShapeDtypeStruct((row_total, width), shards_in[0].dtype),
        out_specs=inside,
        scratch_shapes=[pltpu.VMEM((row_total, width), jnp.float32)],
    )


def plane_body(block_rows, spot_ref, *refs):
    *stack_refs, first_ref, last_ref, hold_ref = refs
    band_size = len(stack_refs)
    for key, stack_ref in enumerate(stack_refs):
        owner = jnp.bitwise_xor(spot_ref[1], key)
        values = stack_ref[...].astype(jnp.float32)
        done = 0
        for rows in block_rows:
            at = pl.multiple_of(done * band_size + owner * rows, 8)
            hold_ref[pl.ds(at, rows), :] = values[done : done + rows]
            done += rows
    half = first_ref.shape[0]
    first_ref[...] = hold_ref[:half, :].astype(first_ref.dtype)
    last_ref[...] = hold_ref[half:, :].astype(last_ref.dtype)


def plane_weights(spots, stacks, block_rows):
    row_total, width = stacks[0].shape
    band_size = len(stacks)
    half = row_total * band_size // 2
    if any(rows % 8 for rows in block_rows):
        whole = place([([key], stack[None]) for key, stack in enumerate(stacks)], "band", 0)
        parts = []
        done = 0
        for rows in block_rows:
            parts.append(whole[:, done : done + rows].reshape(-1, width))
            done += rows
        merged = jnp.concatenate(parts, axis=0)
        return merged[:half], merged[half:]
    inside = pl.BlockSpec(memory_space=pltpu.VMEM)
    return run_kernel(
        partial(plane_body, block_rows),
        (spots, *stacks),
        [pl.BlockSpec(memory_space=pltpu.SMEM)] + [inside] * band_size,
        out_shape=[jax.ShapeDtypeStruct((half, width), stacks[0].dtype)] * 2,
        out_specs=[inside] * 2,
        scratch_shapes=[pltpu.VMEM((row_total * band_size, width), jnp.float32)],
    )


def weight_grad_body(dp_size, parts, hidden, spot_ref, own_ref, other_ref, *refs):
    *out_refs, turned_ref, hold_ref, feed_ref, small_ref, sems = refs
    width = hold_ref.shape[2]
    row_total = own_ref.shape[0]
    spans = stash_spans(width, hidden)
    share = width // dp_size
    chips = dp_size // 2
    core = lax.rem(spot_ref[0], 2)
    copies = []

    def view(name, column=0, size=None):
        first, whole = spans[name]
        first = first + column * width
        return [ref[:, first : first + (size or whole)] for ref in (own_ref, other_ref)]

    def turn_rows(name, at):
        first, size = spans[name]
        for spot in range(0, size, width):
            for number, ref in enumerate((own_ref, other_ref)):
                cols = slice(number * row_total, (number + 1) * row_total)
                turned = ref[:, first + spot : first + spot + width].T
                turned_ref[at + spot : at + spot + width, cols] = turned

    def pick(at, rows):
        parts = []
        for chip in range(chips):
            first = at + (chip * 2 + core) * rows
            parts.append(turned_ref[pl.ds(pl.multiple_of(first, 16), rows), :])
        return jnp.concatenate(parts, axis=0)

    def send(source_ref, rows, number, stride=None):
        part = [number in numbers for _, numbers in parts].index(True)
        first_step, numbers = parts[part]
        first = share * numbers.index(number)
        step = first_step // 2
        bit = lax.rem(lax.div(spot_ref[0], first_step), 2)
        for index in range(chips // 2):
            for which in range(2):
                own_bit = bit if which == 0 else 1 - bit
                chip = index // step * 2 * step + own_bit * step + index % step
                at = chip * (stride or rows)
                copy = pltpu.make_async_copy(
                    source_ref.at[pl.ds(pl.multiple_of(at, 16), rows), :],
                    out_refs[part * 2 + which].at[index, pl.ds(first, rows), :],
                    sems.at[len(copies)],
                )
                copy.start()
                copies.append(copy)

    def product(left, names, column):
        right = view(names, column, width)
        total = dot_nn(left[:, :row_total], right[0])
        return total + dot_nn(left[:, row_total:], right[1])

    blocks = (
        [("normed", "qkv_grad", column) for column in range(3)]
        + [("mixed", "branch", 0)]
        + [("normed_two", "pre_grad", column) for column in range(hidden // width)]
    )
    turned_at = {"normed": 0, "mixed": width, "normed_two": 2 * width, "act": 3 * width}
    picked = {}
    for number, (left, right, column) in enumerate(blocks):
        if left not in picked:
            turn_rows(left, turned_at[left])
            picked = {left: pick(turned_at[left], share)}
        hold_ref[number] = product(picked[left], right, column).astype(hold_ref.dtype)
        send(hold_ref.at[number], share, number)
    small = sum(part.astype(jnp.float32) for part in view("small"))
    small_ref[...] = small.astype(small_ref.dtype)
    small_share = row_total // dp_size
    turn_rows("act", turned_at["act"])
    feed_rows = hidden // dp_size
    for chip in range(chips):
        at = turned_at["act"] + (chip * 2 + core) * feed_rows
        left = turned_ref[pl.ds(pl.multiple_of(at, 16), feed_rows), :]
        feed_ref[chip * feed_rows : (chip + 1) * feed_rows, :] = product(left, "cot", 0).astype(
            feed_ref.dtype
        )
    send(feed_ref, feed_rows, len(blocks))
    own_small = small_ref.at[pl.ds(pl.multiple_of(core * small_share, 16), (dp_size - 1) * small_share), :]
    send(own_small, small_share, len(blocks) + 1, 2 * small_share)
    for copy in copies:
        copy.wait()


def weight_grad(spots, dp_size, parts, hidden, own, other):
    row_total, columns = own.shape
    width = (columns - 2 * hidden) // 9
    bf16 = jnp.bfloat16
    blocks = 4 + hidden // width
    chips = dp_size // 2
    share = width // dp_size
    block_rows = [share] * blocks + [hidden // dp_size, row_total // dp_size]
    rows = [sum(block_rows[number] for number in numbers) for _, numbers in parts]
    inside = pl.BlockSpec(memory_space=pltpu.VMEM)
    outside = pl.BlockSpec(memory_space=pl.ANY)
    return run_kernel(
        partial(weight_grad_body, dp_size, parts, hidden),
        (spots, own, other),
        [pl.BlockSpec(memory_space=pltpu.SMEM), inside, inside],
        out_shape=[
            jax.ShapeDtypeStruct((chips // 2, part_rows, width), bf16)
            for part_rows in rows
            for _ in range(2)
        ],
        out_specs=[outside] * (2 * len(parts)),
        scratch_shapes=[
            pltpu.VMEM((3 * width + hidden, 2 * row_total), bf16),
            pltpu.VMEM((blocks, chips * share, width), bf16),
            pltpu.VMEM((hidden // 2, width), bf16),
            pltpu.VMEM((row_total, width), bf16),
            pltpu.SemaphoreType.DMA(((blocks + 2) * chips,)),
        ],
    )


def add_split_body(step, part_steps, spot_ref, keep_ref, *refs):
    *got_refs, send_ref, held_ref = refs
    bit = lax.rem(lax.div(spot_ref[0], step), 2)
    for number, got_ref in enumerate(got_refs):

        @pl.when(pl.program_id(0) // part_steps == number)
        def _(got_ref=got_ref):
            for out_ref, which in ((send_ref, 1 - bit), (held_ref, bit)):
                values = keep_ref[:, which].astype(jnp.float32)
                values = values + got_ref[:, which].astype(jnp.float32)
                out_ref[...] = values.astype(out_ref.dtype)


def add_split(spots, keep, gots, at, step, left):
    left = sorted(left, reverse=True)
    place_of = left.index(step)
    shape = keep.shape
    width = shape[-1]
    outer = math.prod(shape[:at]) * 2**place_of
    part_outer = outer // len(gots)
    inner_rows = keep.size // (outer * 2 * width)
    rows_step = inner_rows
    while rows_step > 512 and rows_step % 32 == 0:
        rows_step //= 2
    outer_step = 1
    while part_outer % (2 * outer_step) == 0 and 2 * outer_step * rows_step <= 512:
        outer_step *= 2
    part_steps = part_outer // outer_step
    block_in = (outer_step, 2, rows_step, width)
    block_out = pl.BlockSpec((outer_step, rows_step, width), lambda first, rows: (first, rows, 0))

    def part_spec(number):
        def pick(first, rows):
            return (jnp.clip(first - number * part_steps, 0, part_steps - 1), 0, rows, 0)

        return pl.BlockSpec(block_in, pick)

    outs = run_kernel(
        partial(add_split_body, step, part_steps),
        (spots, keep.reshape((outer, 2, inner_rows, width)))
        + tuple(got.reshape((part_outer, 2, inner_rows, width)) for got in gots),
        [
            pl.BlockSpec(memory_space=pltpu.SMEM),
            pl.BlockSpec(block_in, lambda first, rows: (first, 0, rows, 0)),
        ]
        + [part_spec(number) for number in range(len(gots))],
        grid=(outer // outer_step, inner_rows // rows_step),
        out_shape=[jax.ShapeDtypeStruct((outer, inner_rows, width), keep.dtype)] * 2,
        out_specs=[block_out] * 2,
    )
    rest = shape[:at] + (-1,) + shape[at + 1 :]
    return outs[0].reshape(rest), outs[1].reshape(rest)


def shards(
    patches,
    bias_token,
    gen_attn,
    gen_gain,
    gen_ff_in,
    gen_ff_out,
    gen_kernel,
    gen_bias,
    pos_table,
    norm_gain,
    norm_bias,
    w_qkv,
    w_out,
    w_fc1,
    bias_in,
    w_fc2,
    wavelengths,
    kept,
    counts,
    cotangent,
):
    group_size, slot_count, bands_dev, pixel_count = patches.shape
    dp_size = lax.axis_size("dp")
    band_size = lax.axis_size("band")
    device_count = dp_size * band_size
    local_images = group_size // band_size
    model_width = w_out.shape[1]
    row_total = local_images * slot_count
    own_pixels = pixel_count // device_count
    share = own_pixels * band_size
    groups = 2
    group_bands = bands_dev // groups
    f32 = jnp.float32
    bf16 = jnp.bfloat16
    spot = lax.axis_index("band")
    spots = jnp.stack([lax.axis_index("dp"), spot]).astype(jnp.int32)

    own_kernel, embed_bias, band_states, *gen_kept = generate_fast(
        wavelengths,
        bias_token,
        gen_attn,
        gen_gain,
        gen_ff_in,
        gen_ff_out,
        gen_bias,
        gen_kernel,
    )
    hidden = w_fc1.shape[1]
    weight_rows = [w_qkv.shape[0]] * (4 + hidden // model_width) + [w_fc2.shape[0]]
    stack = stack_weights((w_qkv, w_out, w_fc1, w_fc2))
    patch_rows = flatten_rows(
        patches.reshape(group_size * slot_count, bands_dev, pixel_count), (own_kernel,)
    )
    own_kernel = own_kernel.reshape(own_pixels, band_size, bands_dev, model_width)
    other_bands = range(1, band_size)
    dp_steps = bit_steps(dp_size)[1:]
    orders = [turn(dp_steps, group) for group in range(groups)]

    sent = [
        lax.dynamic_index_in_dim(own_kernel, spot ^ key, 1, keepdims=False).transpose(1, 0, 2)
        for key in range(band_size)
    ]
    got = [swap(sent[key], "band", key) for key in other_bands]
    *got, patch_rows, stack = together(*got, patch_rows, stack)
    piece = place(
        [([key], block[None]) for key, block in enumerate([sent[0]] + got)], "band", 1
    ).reshape(bands_dev, share, model_width)

    own_pieces = [piece[group * group_bands : (group + 1) * group_bands] for group in range(groups)]
    held = [own_piece[None] for own_piece in own_pieces]
    held_keys = [[0] for _ in range(groups)]
    kernel_groups = [[([0], piece[None])] for _ in range(groups)]
    waiting = []
    stacks = {0: stack}
    stack_keys = [band_size // 2] + [key for key in other_bands if key != band_size // 2]
    for stage in range(len(dp_steps)):
        last = stage == len(dp_steps) - 1
        now_keys = stack_keys if last else stack_keys[:1]
        stack_keys = stack_keys[len(now_keys) :]
        got = [swap(held[group], "dp", orders[group][stage]) for group in range(groups)]
        if stage == 0:
            core_got = swap(piece, "dp", 1)
        elif waiting:
            core_got = swap(waiting[0][2], "dp", 1)
        stack_got = [swap(stack, "band", key) for key in now_keys]
        got[0], got[1], core_got, stack, *stack_got = together(*got, core_got, stack, *stack_got)
        stacks.update(zip(now_keys, stack_got))
        if stage == 0:
            for blocks in kernel_groups:
                blocks.append(([1], core_got[None]))
        elif waiting:
            group, keys, _ = waiting.pop(0)
            kernel_groups[group].append(([key ^ 1 for key in keys], core_got))
        for group in range(groups):
            keys = [key ^ orders[group][stage] for key in held_keys[group]]
            kernel_groups[group].append((keys, got[group]))
            waiting.append((group, keys, got[group]))
            if not last:
                held[group] = jnp.concatenate([held[group], got[group]], axis=0)
                held_keys[group] = held_keys[group] + keys
    for group, keys, last_got in waiting:
        kernel_groups[group].append(([key ^ 1 for key in keys], swap(last_got, "dp", 1)))

    planes = plane_weights(spots, [stacks[key] for key in range(band_size)], weight_rows)
    got = [swap(plane, "dp", orders[half][0]) for half, plane in enumerate(planes)]
    embedded = embed_share(spots, patch_rows, kernel_groups, band_size)
    *embedded, first_got, last_got = together(*embedded, *got)
    held = [
        jnp.concatenate([plane[None], got[None]], axis=0)
        for plane, got in zip(planes, (first_got, last_got))
    ]
    held_keys = [[0, orders[half][0]] for half in range(2)]
    for stage in range(1, len(dp_steps) - 1):
        for half in range(2):
            step = orders[half][stage]
            held[half] = jnp.concatenate([held[half], swap(held[half], "dp", step)], axis=0)
            held_keys[half] = held_keys[half] + [key ^ step for key in held_keys[half]]
    got = [swap(held[half], "dp", orders[half][-1]) for half in range(2)]
    parts = [embedded[0]] + [swap(embedded[key], "band", key) for key in other_bands]
    held[0], held[1], got[0], got[1], *parts = together(*held, *got, *parts)
    weight_halves = []
    for half in range(2):
        blocks = [(held_keys[half], held[half])]
        blocks.append(([key ^ orders[half][-1] for key in held_keys[half]], got[half]))
        weight_halves.append(blocks + gather_core(blocks))

    valid_mask = jnp.arange(slot_count)[None, :] < counts[:, None]
    keep_col = valid_mask.reshape(row_total, 1)
    kept_flat = kept.reshape(row_total)
    pos_rows = jnp.take(pos_table, kept_flat, axis=0).astype(f32)
    base = embed_bias[0:1] + pos_rows
    tile_images = 2 if local_images % 2 == 0 else 1
    tile_rows = tile_images * slot_count
    image_spot = jnp.arange(tile_rows) // slot_count
    same_image = image_spot[:, None] == image_spot[None, :]
    mask = jnp.where(same_image[None] & valid_mask.reshape(-1, 1, tile_rows), 0.0, -1e30)
    cot = jnp.where(keep_col, cotangent.reshape(row_total, model_width), 0)
    (
        result,
        grad_embed,
        stash,
        sums,
    ) = block(
        parts,
        weight_halves,
        spots,
        base,
        cot,
        keep_col.astype(f32),
        mask.astype(f32),
        norm_gain.astype(f32),
        norm_bias.astype(f32),
        bias_in.astype(f32)[None],
        kept_flat[None],
    )

    small_share = row_total // device_count
    block_rows = weight_rows + [small_share]
    part_blocks = [[0, 1, 9], [2, 3], [4, 5, 6, 7], [8]]
    part_orders = [orders[0], orders[1], orders[0], orders[1]]
    weight_parts = [(order[0], numbers) for order, numbers in zip(part_orders, part_blocks)]
    grads = [grad_embed] + [swap(grad_embed, "band", key) for key in other_bands]
    weight_split = weight_grad(
        spots, dp_size, weight_parts, hidden, stash, swap(stash, "dp", 1)
    )
    mixed = together(*grads, *weight_split)
    grads, weight_split = list(mixed[:band_size]), mixed[band_size:]
    weight_keep, weight_send = list(weight_split[0::2]), list(weight_split[1::2])

    weight_got = [swap(weight_send[part], "dp", part_orders[part][0]) for part in range(2)]
    kernel_split = []
    for group in range(groups):
        *sends, keep = kernel_grad_part(
            spots,
            patch_rows,
            grads,
            group * group_bands,
            group_bands,
            bands_dev,
            dp_size,
            (),
        )
        core_got = [swap(send, "dp", 1) for send in sends]
        kernel_split += add_split(spots, keep, core_got, 1, orders[group][0], dp_steps)
    weight_got[0], weight_got[1], *kernel_split = together(*weight_got, *kernel_split)

    def cut_blocks(values, numbers):
        lead = values.shape[0]
        cuts = []
        first = 0
        for number in numbers:
            rows = block_rows[number]
            cut = values[:, first : first + rows * band_size]
            cuts.append(cut.reshape(lead, band_size, rows, model_width))
            first += rows * band_size
        return jnp.concatenate(cuts, axis=2)

    def over_band(by_band):
        sent = [
            lax.dynamic_index_in_dim(by_band, spot ^ key, 1, keepdims=False)
            for key in range(band_size)
        ]
        return [sent[0]] + [swap(sent[key], "band", key) for key in other_bands]

    def total(blocks):
        return sum(block_sum.astype(f32) for block_sum in blocks)

    def over_chips(sums):
        cut = [
            values if isinstance(values, tuple) else split_half(values, 0, order[0], order)
            for values, order in sums
        ]
        got = [None] * len(sums)
        for step in sorted({order[0] for _, order in sums}):
            here = [number for number, (_, order) in enumerate(sums) if order[0] == step]
            flat = [cut[number][0].reshape(-1, model_width) for number in here]
            moved = swap(jnp.concatenate(flat, axis=0) if len(flat) > 1 else flat[0], "dp", step)
            first = 0
            for number, rows in zip(here, flat):
                part = moved[first : first + rows.shape[0]]
                got[number] = part.reshape(cut[number][0].shape)
                first += rows.shape[0]
        return [
            (add_low(cut[number][1], got[number]), order[1:])
            for number, (_, order) in enumerate(sums)
        ]

    update = patch_grad(spots, grads, kernel_groups, pixel_count, 0, ())
    for stage in range(len(dp_steps)):
        last = stage == len(dp_steps) - 1
        got = [swap(kernel_split[2 * group], "dp", orders[group][stage]) for group in range(groups)]
        if stage == 0:
            cuts = [
                cut_blocks(add_low(weight_keep[part], weight_got[part]), part_blocks[part])
                for part in range(2)
            ]
            part_got = over_band(jnp.concatenate(cuts, axis=2))
            got[0], got[1], update, *part_got = together(*got, update, *part_got)
            early = total(part_got).astype(bf16)
            early_rows = cuts[0].shape[2]
            early = [early[:, :early_rows], early[:, early_rows:]]
        else:
            got[0], got[1], early[0], early[1] = together(*got, *early)
        if not last:
            kernel_split = [
                part
                for group in range(groups)
                for part in add_split(
                    spots,
                    kernel_split[2 * group + 1],
                    [got[group]],
                    1,
                    orders[group][stage + 1],
                    orders[group][stage + 1 :],
                )
            ]
    kernel_sums = [add_low(kernel_split[2 * group + 1], got[group]) for group in range(groups)]

    own_part = jnp.concatenate(kernel_sums, axis=0)
    own_part = own_part.reshape(bands_dev, band_size, own_pixels, model_width)
    own_part = own_part.transpose(1, 2, 0, 3)
    sent = [
        lax.dynamic_index_in_dim(own_part, spot ^ key, 0, keepdims=False)
        for key in range(band_size)
    ]
    pieces = [sent[0]] + [swap(sent[key], "band", key) for key in other_bands]
    sums_left = over_chips(
        [(early[part], part_orders[part][1:]) for part in range(2)]
        + [
            ((weight_send[part], weight_keep[part]), part_orders[part])
            for part in range(2, 4)
        ]
    )
    while any(order for _, order in sums_left[:2]):
        moved = over_chips([one for one in sums_left[:2] if one[1]])
        sums_left[:2] = [moved.pop(0) if one[1] else one for one in sums_left[:2]]
    weight_sums = [values for values, _ in sums_left]
    grad_patches = unflatten_rows([update], bands_dev, (sent[0],))
    mixed = together(*weight_sums, grad_patches, *pieces)
    weight_sums, grad_patches, pieces = list(mixed[:4]), mixed[4], mixed[5:]
    grad_gen_kernel, tail = states_grad(spots, band_states, gen_kernel, pieces, sums)
    mixed = together(*weight_sums, tail)
    weight_sums, tail = list(mixed[:-1]), mixed[-1]

    small = weight_sums[0][:, -small_share:]
    late = [(weight_sums[part], part_orders[part][1:]) for part in range(2, 4)]
    small_steps = [("band", step) for step in bit_steps(band_size)]
    small_steps += [("dp", step) for step in turn(bit_steps(dp_size), 1)]

    def widen(values, number):
        return jnp.concatenate([values, swap(values, *small_steps[number])], axis=0)

    while any(order for _, order in late):
        late = over_chips(late)
    late = [values for values, _ in late]
    tail = total([tail] + [swap(tail, "band", key) for key in other_bands])
    small = widen(small, 0)
    tail, small, late[0], late[1] = together(tail, small, *late)
    cuts = [cut_blocks(late[part - 2], part_blocks[part]) for part in range(2, 4)]
    last_sum = total(over_band(jnp.concatenate(cuts, axis=2)))
    for number, step in enumerate(turn(bit_steps(dp_size), 1)):
        got = swap(tail, "dp", step)
        if number + 1 < len(small_steps):
            small = widen(small, number + 1)
        got, small = together(got, small)
        tail = tail + got
    for number in range(len(bit_steps(dp_size)) + 1, len(small_steps)):
        small = widen(small, number)
    own_grads = jnp.concatenate(
        [
            weight_sums[0][0, :-small_share].astype(f32),
            weight_sums[1][0].astype(f32),
            last_sum[0],
        ],
        axis=0,
    )
    small_order = (jnp.arange(dp_size) ^ spots[0])[:, None] * band_size
    small_order = (small_order + (jnp.arange(band_size) ^ spots[1])[None, :]).reshape(-1)
    small = small.reshape(2, dp_size // 2, band_size, small_share, model_width)
    small = small.transpose(1, 0, 2, 3, 4).reshape(-1, small_share, model_width)
    small = jnp.take(small, small_order, axis=0).reshape(row_total, model_width)
    own_blocks = []
    done = 0
    for rows in weight_rows:
        own_blocks.append(own_grads[done : done + rows])
        done += rows
    grad_qkv_own = jnp.concatenate(own_blocks[:3], axis=1)
    grad_out_own = own_blocks[3]
    grad_fc_in_own = jnp.concatenate(own_blocks[4:-1], axis=1)
    grad_fc_out_own = own_blocks[-1]
    grad_token, grad_attn, grad_gain_gen, grad_ff_first, grad_ff_second, grad_gen_bias = (
        generate_back(
            tail,
            gen_attn,
            gen_gain,
            gen_ff_in,
            gen_ff_out,
            gen_bias,
            gen_kept,
        )
    )

    small = small.astype(f32)
    sums_at = small.shape[0] - 16
    grad_pos_all = small[: pos_table.shape[0]]
    grad_gains = small[sums_at + 1 : sums_at + 3]
    grad_shifts = small[sums_at + 3 : sums_at + 5]
    grad_bias_all = small[sums_at + 8 : sums_at + 8 + hidden // model_width].reshape(-1)
    grad_patches = grad_patches.reshape(group_size, slot_count, bands_dev, pixel_count)
    return (
        result.reshape(local_images, slot_count, model_width),
        grad_patches,
        grad_token[0],
        grad_attn,
        grad_gain_gen,
        grad_ff_first,
        grad_ff_second,
        grad_gen_kernel,
        grad_gen_bias,
        grad_pos_all,
        grad_gains,
        grad_shifts,
        grad_qkv_own,
        grad_out_own,
        grad_fc_in_own,
        grad_bias_all,
        grad_fc_out_own,
    )


def solution(mesh):
    placed = (
        P("dp", None, "band", None),
        P(),
        P(),
        P(),
        P(),
        P(),
        P(None, ("dp", "band")),
        P(),
        P(),
        P(),
        P(),
        P(("dp", "band"), None),
        P(("dp", "band"), None),
        P(("dp", "band"), None),
        P(),
        P(("dp", "band"), None),
        P(),
        P(("dp", "band"), None),
        P(("dp", "band")),
        P(("dp", "band"), None, None),
    )
    return jax.shard_map(
        shards,
        mesh=mesh,
        in_specs=placed,
        out_specs=(
            P(("dp", "band"), None, None),
            P("dp", None, "band", None),
            P(),
            P(),
            P(),
            P(),
            P(),
            P(None, ("dp", "band")),
            P(),
            P(),
            P(),
            P(),
            P(("dp", "band"), None),
            P(("dp", "band"), None),
            P(("dp", "band"), None),
            P(),
            P(("dp", "band"), None),
        ),
        check_vma=False,
    )
```

```python
from functools import partial
import math

import jax
import jax.numpy as jnp
from jax import lax
from jax.experimental import pallas as pl
from jax.experimental.pallas import tpu as pltpu
from jax.sharding import PartitionSpec as P

HEADS = 12
HDIM = 64
GEN_HEADS = 4


def inner(left_arr, right_arr):
    return lax.dot_general(
        left_arr, right_arr, (((0,), (0,)), ((), ())), preferred_element_type=jnp.float32
    )


def times_transpose(left_arr, right_arr):
    return lax.dot_general(
        left_arr, right_arr, (((1,), (1,)), ((), ())), preferred_element_type=jnp.float32
    )


def bit_steps(size):
    steps = []
    step = 1
    while step < size:
        steps.append(step)
        step *= 2
    return steps


def swap(values, axis, step):
    size = lax.axis_size(axis)
    return lax.ppermute(values, axis, [(spot, spot ^ step) for spot in range(size)])


def turn(items, by):
    by = by % max(len(items), 1)
    return items[by:] + items[:by]


def gather_core(blocks):
    return [([key ^ 1 for key in keys], swap(block, "dp", 1)) for keys, block in blocks]


def place(blocks, axis, at):
    spot = lax.axis_index(axis)
    first = blocks[0][1]
    count = sum(len(keys) for keys, _ in blocks)
    shape = first.shape[1 : at + 1] + (count,) + first.shape[at + 1 :]
    whole = jnp.zeros(shape, first.dtype)
    for keys, block in blocks:
        for number, key in enumerate(keys):
            whole = lax.dynamic_update_index_in_dim(whole, block[number], spot ^ key, at)
    return whole


def add_low(left_arr, right_arr):
    return (left_arr.astype(jnp.float32) + right_arr.astype(jnp.float32)).astype(left_arr.dtype)


def split_half(values, at, step, left):
    left = sorted(left, reverse=True)
    shape = values.shape
    values = values.reshape(shape[:at] + (2,) * len(left) + shape[at + 1 :])
    dim = at + left.index(step)
    bit = (lax.axis_index("dp") // step) % 2
    rest = shape[:at] + (-1,) + shape[at + 1 :]
    send = lax.dynamic_index_in_dim(values, 1 - bit, dim, keepdims=False)
    keep = lax.dynamic_index_in_dim(values, bit, dim, keepdims=False)
    return send.reshape(rest), keep.reshape(rest)


def together(*arrays):
    return lax.optimization_barrier(arrays)


def column_blocks(matrix, width):
    return [matrix[:, spot : spot + width] for spot in range(0, matrix.shape[1], width)]


def run_kernel(body, args, in_specs, after=(), **options):
    count = len(after)

    def whole(*refs):
        body(*refs[count:])

    return pl.pallas_call(
        whole,
        in_specs=[pl.BlockSpec(memory_space=pl.ANY)] * count + in_specs,
        compiler_params=pltpu.CompilerParams(vmem_limit_bytes=60 * 1024 * 1024),
        cost_estimate=pl.CostEstimate(flops=1000, bytes_accessed=1000, transcendentals=0),
        **options,
    )(*after, *args)


def dot_nn(left_arr, right_arr):
    return lax.dot_general(
        left_arr, right_arr, (((1,), (0,)), ((), ())), preferred_element_type=jnp.float32
    )


def norm_stats(values):
    center = values - jnp.mean(values, axis=-1, keepdims=True)
    spread = jnp.mean(center * center, axis=-1, keepdims=True)
    scale = lax.rsqrt(spread + 1e-06)
    return center * scale, scale


def norm_back(unit, scale, gain, grad):
    weighted = grad * gain
    first = jnp.mean(weighted, axis=-1, keepdims=True)
    second = jnp.mean(weighted * unit, axis=-1, keepdims=True)
    grad_values = (weighted - first - unit * second) * scale
    grad_gain = jnp.sum(grad * unit, axis=0, keepdims=True)
    grad_shift = jnp.sum(grad, axis=0, keepdims=True)
    return grad_values, grad_gain, grad_shift


def stash_spans(width, hidden):
    sizes = {
        "normed": width,
        "mixed": width,
        "normed_two": width,
        "act": hidden,
        "qkv_grad": 3 * width,
        "branch": width,
        "pre_grad": hidden,
        "cot": width,
        "small": width,
    }
    spans = {}
    first = 0
    for name, size in sizes.items():
        spans[name] = (first, size)
        first += size
    return spans


def block_body(part_count, tile_rows, ff_step, keys_lists, *refs):
    part_refs = refs[:part_count]
    weight_count = sum(len(keys_list) for keys_list in keys_lists)
    weight_refs = refs[part_count : part_count + weight_count]
    (
        spot_ref,
        base_ref,
        cot_ref,
        keep_ref,
        mask_ref,
        gain_ref,
        shift_ref,
        bias_ref,
        kept_ref,
        result_ref,
        embed_grad_ref,
        stash_ref,
        sums_ref,
        qkv_w,
        out_w,
        fc_in_w,
        fc_out_w,
        qkv_ref,
        probs_ref,
        total_ref,
        back_ref,
        mixed_grad_ref,
        bias_grad_ref,
        sems,
    ) = refs[part_count + weight_count :]
    bf16 = jnp.bfloat16
    f32 = jnp.float32
    width = base_ref.shape[1]
    hidden = fc_in_w.shape[1]
    spans = stash_spans(width, hidden)
    views = {name: stash_ref.at[:, pl.ds(first, size)] for name, (first, size) in spans.items()}
    normed_ref = views["normed"]
    mixed_ref = views["mixed"]
    normed_two_ref = views["normed_two"]
    act_ref = views["act"]
    qkv_grad_ref = views["qkv_grad"]
    branch_ref = views["branch"]
    pre_grad_ref = views["pre_grad"]
    views["cot"][...] = cot_ref[...]
    share = width // sum(len(keys) for keys in keys_lists[0])
    targets = (
        [(qkv_w, column, share) for column in range(3)]
        + [(out_w, 0, share)]
        + [(fc_in_w, column, share) for column in range(hidden // width)]
        + [(fc_out_w, 0, share * hidden // width)]
    )
    copies = {}
    for number, (target_ref, column, rows) in enumerate(targets):
        half, first = (0, number * share) if number < 6 else (1, (number - 6) * share)
        half_refs = weight_refs[: len(keys_lists[0])] if half == 0 else weight_refs[len(keys_lists[0]) :]
        for keys, weight_ref in zip(keys_lists[half], half_refs):
            for index, key in enumerate(keys):
                at = pl.multiple_of(jnp.bitwise_xor(spot_ref[0], key) * rows, rows)
                copy = pltpu.make_async_copy(
                    weight_ref.at[index, pl.ds(first, rows), :],
                    target_ref.at[pl.ds(at, rows), pl.ds(column * width, width)],
                    sems.at[sum(len(some) for some in copies.values())],
                )
                copy.start()
                copies.setdefault(id(target_ref), []).append(copy)

    def arrive(target_ref):
        for copy in copies[id(target_ref)]:
            copy.wait()

    row_total, width = base_ref.shape
    tiles = row_total // tile_rows
    head_pairs = HEADS // 2
    lanes = 2 * HDIM

    start = base_ref[...]
    for part_ref in part_refs:
        start = start + part_ref[...].astype(f32)
    unit_one, scale_one = norm_stats(start)
    normed = (unit_one * gain_ref[0:1] + shift_ref[0:1]).astype(bf16)
    normed_ref[...] = normed
    arrive(qkv_w)
    for spot in range(3):
        cols = slice(spot * width, (spot + 1) * width)
        qkv_ref[:, cols] = dot_nn(normed, qkv_w[:, cols]).astype(bf16)

    low_lanes = lax.broadcasted_iota(jnp.int32, (tile_rows, lanes), 1) < HDIM

    def half(values, odd):
        keep = jnp.logical_not(low_lanes) if odd else low_lanes
        return jnp.where(keep, values, jnp.zeros_like(values))

    def head_slices(pair, tile):
        rows = pl.ds(tile * tile_rows, tile_rows)
        cols = [
            pl.ds(pl.multiple_of(which * width + pair * lanes, lanes), lanes) for which in range(3)
        ]
        return rows, cols

    def attend(pair, carry):
        for tile in range(tiles):
            rows, cols = head_slices(pair, tile)
            queries, keys_arr, values_arr = [qkv_ref[rows, col] for col in cols]
            mixed = jnp.zeros((tile_rows, lanes), f32)
            for odd in range(2):
                scores = times_transpose(half(queries, odd), keys_arr) * HDIM ** (-0.5)
                scores = scores + mask_ref[tile]
                exponent = jnp.exp(scores - jnp.max(scores, axis=-1, keepdims=True))
                probs = exponent * (1.0 / jnp.sum(exponent, axis=-1, keepdims=True))
                probs_ref[(pair * 2 + odd) * tiles + tile] = probs
                mixed = mixed + dot_nn(probs.astype(bf16), half(values_arr, odd))
            mixed_ref[rows, cols[0]] = mixed.astype(bf16)
        return carry

    lax.fori_loop(0, head_pairs, attend, 0)
    arrive(out_w)
    middle = start + dot_nn(mixed_ref[...], out_w[...])
    unit_two, scale_two = norm_stats(middle)
    normed_two = (unit_two * gain_ref[1:2] + shift_ref[1:2]).astype(bf16)
    normed_two_ref[...] = normed_two
    total_ref[...] = middle
    back_ref[...] = jnp.zeros_like(back_ref)
    arrive(fc_in_w)
    arrive(fc_out_w)

    def feed(step, carry):
        cols = pl.ds(pl.multiple_of(step * ff_step, ff_step), ff_step)
        pre = dot_nn(normed_two_ref[...], fc_in_w[:, cols]) + bias_ref[:, cols]
        cdf = 0.5 * (1.0 + lax.erf(pre * 0.5**0.5))
        act = (pre * cdf).astype(bf16)
        act_ref[:, cols] = act
        slope = cdf + pre * (jnp.exp(-0.5 * pre * pre) * (2.0 * math.pi) ** (-0.5))
        pre_grad = slope * times_transpose(cot_ref[...], fc_out_w[cols, :])
        pre_grad = pre_grad.astype(bf16)
        pre_grad_ref[:, cols] = pre_grad
        bias_grad_ref[:, cols] = jnp.sum(pre_grad.astype(f32), axis=0, keepdims=True)
        total_ref[...] += dot_nn(act, fc_out_w[cols, :])
        back_ref[...] += times_transpose(pre_grad, fc_in_w[:, cols])
        return carry

    lax.fori_loop(0, fc_in_w.shape[1] // ff_step, feed, 0)
    result_ref[...] = (total_ref[...] * keep_ref[...]).astype(bf16)
    grad_norm, gain_two, shift_two = norm_back(unit_two, scale_two, gain_ref[1:2], back_ref[...])
    grad_middle = cot_ref[...].astype(f32) + grad_norm
    grad_branch = grad_middle.astype(bf16)
    branch_ref[...] = grad_branch
    mixed_grad_ref[...] = times_transpose(grad_branch, out_w[...]).astype(bf16)

    def attend_back(pair, carry):
        for tile in range(tiles):
            rows, cols = head_slices(pair, tile)
            queries, keys_arr, values_arr = [qkv_ref[rows, col] for col in cols]
            grad_mixed = mixed_grad_ref[rows, cols[0]]
            grads = [jnp.zeros((tile_rows, lanes), f32) for _ in range(3)]
            for odd in range(2):
                probs = probs_ref[(pair * 2 + odd) * tiles + tile]
                own_grad = half(grad_mixed, odd)
                grad_probs = times_transpose(own_grad, values_arr)
                grad_scores = probs * (
                    grad_probs - jnp.sum(grad_probs * probs, axis=-1, keepdims=True)
                )
                grad_scores = grad_scores.astype(bf16)
                grads[0] = grads[0] + dot_nn(grad_scores, half(keys_arr, odd))
                grads[1] = grads[1] + inner(grad_scores, half(queries, odd))
                grads[2] = grads[2] + inner(probs.astype(bf16), own_grad)
            for which, factor in enumerate((HDIM ** (-0.5), HDIM ** (-0.5), 1.0)):
                qkv_grad_ref[rows, cols[which]] = (grads[which] * factor).astype(bf16)
        return carry

    lax.fori_loop(0, head_pairs, attend_back, 0)
    back = jnp.zeros((row_total, width), f32)
    for spot in range(3):
        cols = slice(spot * width, (spot + 1) * width)
        back = back + times_transpose(qkv_grad_ref[:, cols], qkv_w[:, cols])
    grad_norm, gain_one, shift_one = norm_back(unit_one, scale_one, gain_ref[0:1], back)
    grad_start = grad_middle + grad_norm
    embed_grad_ref[...] = grad_start.astype(bf16)
    sums = jnp.concatenate(
        [jnp.sum(grad_start, axis=0, keepdims=True), gain_one, gain_two, shift_one, shift_two]
        + [jnp.zeros((3, width), f32)],
        axis=0,
    )
    sums_ref[...] = sums
    small_ref = views["small"]
    positions = small_ref.shape[0] - 16
    spots_at = lax.broadcasted_iota(jnp.int32, (positions, row_total), 0)
    one_hot = jnp.where(spots_at == kept_ref[...], 1.0, 0.0).astype(bf16)
    by_position = dot_nn(one_hot, grad_start.astype(bf16))
    cuts = [bias_grad_ref[:, spot : spot + width] for spot in range(0, hidden, width)]
    cuts.append(jnp.zeros((8 - len(cuts), width), f32))
    small_ref[...] = jnp.concatenate([by_position, sums, *cuts], axis=0).astype(bf16)


def block(parts, weight_halves, spots, base, cot, keep, mask, gains, shifts, bias, kept):
    row_total, width = base.shape
    tile_rows = mask.shape[1]
    hidden = bias.shape[1]
    bf16 = jnp.bfloat16
    f32 = jnp.float32
    keys_lists = [[keys for keys, _ in blocks] for blocks in weight_halves]
    weight_args = [block for blocks in weight_halves for _, block in blocks]
    pieces = sum(len(keys) for keys in keys_lists[0])
    inside = pl.BlockSpec(memory_space=pltpu.VMEM)
    outside = pl.BlockSpec(memory_space=pl.ANY)
    rows = (row_total, width)
    shapes = [
        (rows, bf16),
        (rows, bf16),
        ((row_total, sum(stash_spans(width, hidden)["small"])), bf16),
        ((8, width), f32),
    ]
    return run_kernel(
        partial(block_body, len(parts), tile_rows, 512, keys_lists),
        (*parts, *weight_args, spots, base, cot, keep, mask, gains, shifts, bias, kept),
        [inside] * len(parts)
        + [outside] * len(weight_args)
        + [pl.BlockSpec(memory_space=pltpu.SMEM)]
        + [inside] * 8,
        out_shape=[jax.ShapeDtypeStruct(shape, kind) for shape, kind in shapes],
        out_specs=[inside] * len(shapes),
        scratch_shapes=[
            pltpu.VMEM((width, 3 * width), bf16),
            pltpu.VMEM((width, width), bf16),
            pltpu.VMEM((width, hidden), bf16),
            pltpu.VMEM((hidden, width), bf16),
            pltpu.VMEM((row_total, 3 * width), bf16),
            pltpu.VMEM((HEADS * row_total // tile_rows, tile_rows, tile_rows), f32),
            pltpu.VMEM(rows, f32),
            pltpu.VMEM(rows, f32),
            pltpu.VMEM(rows, bf16),
            pltpu.VMEM((1, hidden), f32),
            pltpu.SemaphoreType.DMA(((5 + hidden // width) * pieces,)),
        ],
    )


def dot_full(left_arr, right_arr, left_dim=1, right_dim=0):
    return lax.dot_general(
        left_arr,
        right_arr,
        (((left_dim,), (right_dim,)), ((), ())),
        precision=lax.Precision.HIGH,
        preferred_element_type=jnp.float32,
    )


def head_part(values, head):
    size = values.shape[1] // GEN_HEADS
    lane = lax.broadcasted_iota(jnp.int32, values.shape, 1)
    inside = jnp.logical_and(lane >= head * size, lane < (head + 1) * size)
    return jnp.where(inside, values, 0.0)


def generate_body(
    waves_ref,
    token_ref,
    attn_hbm,
    gain_hbm,
    ff_in_hbm,
    ff_out_hbm,
    bias_w_hbm,
    columns_hbm,
    kernel_ref,
    embed_bias_ref,
    low_ref,
    states_ref,
    rows_ref,
    weights_ref,
    pre_ref,
    scales_ref,
    attn_ref,
    gain_ref,
    ff_in_ref,
    ff_out_ref,
    bias_w_ref,
    columns_ref,
    sems,
):
    f32 = jnp.float32
    copies = [
        pltpu.make_async_copy(source, target, sems.at[number])
        for number, (source, target) in enumerate(
            (
                (attn_hbm, attn_ref),
                (gain_hbm, gain_ref),
                (ff_in_hbm, ff_in_ref),
                (ff_out_hbm, ff_out_ref),
                (columns_hbm, columns_ref),
                (bias_w_hbm, bias_w_ref),
            )
        )
    ]
    for copy in copies:
        copy.start()
    bands = waves_ref.shape[1]
    width = token_ref.shape[1]
    padded = rows_ref.shape[1]
    square = (bands, bands)
    diagonal = lax.broadcasted_iota(jnp.int32, square, 0) == lax.broadcasted_iota(
        jnp.int32, square, 1
    )
    waves = jnp.broadcast_to(waves_ref[...].astype(f32), square)
    column = jnp.sum(jnp.where(diagonal, waves, 0.0), axis=1, keepdims=True)
    lane = lax.broadcasted_iota(jnp.int32, (bands, width), 1)
    half_width = width // 2
    number = jnp.where(lane < half_width, lane, lane - half_width).astype(f32)
    angles = column * jnp.exp(number * (-math.log(10000.0) / half_width))
    wave = jnp.where(lane < half_width, jnp.sin(angles), jnp.cos(angles))
    sequence = jnp.concatenate(
        [wave, token_ref[...].astype(f32), jnp.zeros((padded - bands - 1, width), f32)], axis=0
    )
    rows_ref[0] = sequence
    copies[0].wait()
    copies[1].wait()
    for which in range(3):
        rows_ref[1 + which] = dot_full(sequence, attn_ref[which].astype(f32))
    queries = rows_ref[1]
    keys_arr = rows_ref[2]
    values_arr = rows_ref[3]
    key_spot = lax.broadcasted_iota(jnp.int32, (padded, padded), 1)
    mixed = jnp.zeros((padded, width), f32)
    for head in range(GEN_HEADS):
        scores = dot_full(head_part(queries, head), keys_arr, 1, 1)
        scores = scores * (1.0 / math.sqrt(width // GEN_HEADS))
        scores = jnp.where(key_spot <= bands, scores, -1e30)
        exponent = jnp.exp(scores - jnp.max(scores, axis=-1, keepdims=True))
        weights = exponent / jnp.sum(exponent, axis=-1, keepdims=True)
        weights_ref[head] = weights
        mixed = mixed + dot_full(weights, head_part(values_arr, head))
    rows_ref[4] = mixed
    unit_one, scale_one = norm_stats(sequence + dot_full(mixed, attn_ref[3].astype(f32)))
    rows_ref[5] = unit_one
    first = unit_one * gain_ref[0:1].astype(f32)
    copies[2].wait()
    pre = dot_full(first, ff_in_ref[...].astype(f32))
    pre_ref[...] = pre
    hidden = pre * (0.5 * (1.0 + lax.erf(pre * 0.5**0.5)))
    copies[3].wait()
    unit_two, scale_two = norm_stats(first + dot_full(hidden, ff_out_ref[...].astype(f32)))
    rows_ref[6] = unit_two
    states = unit_two * gain_ref[1:2].astype(f32)
    states_ref[...] = states
    scales_ref[0] = jnp.broadcast_to(scale_one, (padded, width))
    scales_ref[1] = jnp.broadcast_to(scale_two, (padded, width))
    low = states[:bands].astype(jnp.bfloat16)
    low_ref[...] = low
    features = kernel_ref.shape[2]
    copies[4].wait()
    for pixel in range(kernel_ref.shape[0]):
        cols = slice(pixel * features, (pixel + 1) * features)
        kernel_ref[pixel] = dot_nn(low, columns_ref[:, cols]).astype(jnp.bfloat16)
    copies[5].wait()
    token_state = states[bands : bands + 8]
    embed_bias_ref[...] = dot_full(token_state, bias_w_ref[...].astype(f32))


def generate_fast(wavelengths, token, gen_attn, gen_gain, ff_in, ff_out, gen_bias, columns):
    f32 = jnp.float32
    bf16 = jnp.bfloat16
    bands = wavelengths.shape[0]
    width = token.shape[0]
    padded = -(-(bands + 1) // 8) * 8
    features = gen_bias.shape[1]
    shapes = [
        ((columns.shape[1] // features, bands, features), bf16),
        ((8, features), f32),
        ((bands, width), bf16),
        ((padded, width), f32),
        ((7, padded, width), f32),
        ((GEN_HEADS, padded, padded), f32),
        ((padded, ff_in.shape[1]), f32),
        ((2, padded, width), f32),
    ]
    inside = pl.BlockSpec(memory_space=pltpu.VMEM)
    outside = pl.BlockSpec(memory_space=pl.ANY)
    weights = (gen_attn, gen_gain, ff_in, ff_out, gen_bias, columns)
    return run_kernel(
        generate_body,
        (wavelengths[None], token[None], *weights),
        out_shape=[jax.ShapeDtypeStruct(shape, kind) for shape, kind in shapes],
        in_specs=[inside] * 2 + [outside] * 6,
        out_specs=[inside] * len(shapes),
        scratch_shapes=[pltpu.VMEM(weight.shape, bf16) for weight in weights]
        + [pltpu.SemaphoreType.DMA((6,))],
    )


def generate_back_body(
    tail_ref,
    attn_ref,
    gain_ref,
    ff_in_ref,
    ff_out_ref,
    bias_w_ref,
    states_ref,
    rows_ref,
    weights_ref,
    pre_ref,
    scales_ref,
    token_out,
    attn_out,
    gain_out,
    ff_in_out,
    ff_out_out,
    bias_out,
):
    f32 = jnp.float32
    padded, width = states_ref.shape
    features = bias_w_ref.shape[1]
    bands = padded - 8
    head_scale = 1.0 / math.sqrt(width // GEN_HEADS)
    cuts = [tail_ref[bands + spot : bands + spot + 1, :] for spot in range(features // width)]
    bias_grad = jnp.concatenate(cuts, axis=1)
    bias_grad = jnp.concatenate([bias_grad, jnp.zeros((7, features), f32)], axis=0)
    row_spot = lax.broadcasted_iota(jnp.int32, (padded - bands, width), 0)
    token_grad = dot_full(bias_grad, bias_w_ref[...].astype(f32), 1, 1)
    token_grad = jnp.where(row_spot == 0, token_grad[0:1], 0.0)
    grad_states = jnp.concatenate([tail_ref[:bands, :], token_grad], axis=0)
    token_state = states_ref[bands : bands + 8]
    first_row = lax.broadcasted_iota(jnp.int32, token_state.shape, 0) == 0
    bias_out[...] = dot_full(jnp.where(first_row, token_state, 0.0), bias_grad, 0, 0)
    unit_one = rows_ref[5]
    gain_one = gain_ref[0:1].astype(f32)
    gain_two = gain_ref[1:2].astype(f32)
    grad_two, gain_two_grad, _ = norm_back(rows_ref[6], scales_ref[1], gain_two, grad_states)
    pre = pre_ref[...]
    cdf = 0.5 * (1.0 + lax.erf(pre * 0.5**0.5))
    ff_out_out[...] = dot_full(pre * cdf, grad_two, 0, 0)
    slope = cdf + pre * (jnp.exp(-0.5 * pre * pre) * (2.0 * math.pi) ** (-0.5))
    grad_pre = slope * dot_full(grad_two, ff_out_ref[...].astype(f32), 1, 1)
    ff_in_out[...] = dot_full(unit_one * gain_one, grad_pre, 0, 0)
    grad_first = grad_two + dot_full(grad_pre, ff_in_ref[...].astype(f32), 1, 1)
    grad_one, gain_one_grad, _ = norm_back(unit_one, scales_ref[0], gain_one, grad_first)
    gain_out[...] = jnp.concatenate([gain_one_grad, gain_two_grad], axis=0)
    attn_out[3] = dot_full(rows_ref[4], grad_one, 0, 0)
    grad_mixed = dot_full(grad_one, attn_ref[3].astype(f32), 1, 1)
    sequence = rows_ref[0]
    queries = rows_ref[1]
    keys_arr = rows_ref[2]
    values_arr = rows_ref[3]
    grads = [jnp.zeros((padded, width), f32) for _ in range(3)]
    for head in range(GEN_HEADS):
        weights = weights_ref[head]
        own_grad = head_part(grad_mixed, head)
        grad_weights = dot_full(own_grad, values_arr, 1, 1)
        grad_scores = weights * (
            grad_weights - jnp.sum(grad_weights * weights, axis=-1, keepdims=True)
        )
        grad_scores = grad_scores * head_scale
        grads[0] = grads[0] + dot_full(grad_scores, head_part(keys_arr, head))
        grads[1] = grads[1] + dot_full(grad_scores, head_part(queries, head), 0, 0)
        grads[2] = grads[2] + dot_full(weights, own_grad, 0, 0)
    grad_sequence = grad_one
    for which in range(3):
        attn_out[which] = dot_full(sequence, grads[which], 0, 0)
        grad_sequence = grad_sequence + dot_full(
            grads[which], attn_ref[which].astype(f32), 1, 1
        )
    token_out[...] = grad_sequence[bands : bands + 1]


def generate_back(tail, gen_attn, gen_gain, ff_in, ff_out, gen_bias, kept_arrs):
    f32 = jnp.float32
    width = gen_gain.shape[1]
    shapes = [
        (1, width),
        gen_attn.shape,
        gen_gain.shape,
        ff_in.shape,
        ff_out.shape,
        gen_bias.shape,
    ]
    inside = pl.BlockSpec(memory_space=pltpu.VMEM)
    return run_kernel(
        generate_back_body,
        (tail, gen_attn, gen_gain, ff_in, ff_out, gen_bias, *kept_arrs),
        out_shape=[jax.ShapeDtypeStruct(shape, f32) for shape in shapes],
        in_specs=[inside] * (6 + len(kept_arrs)),
        out_specs=[inside] * len(shapes),
    )


def fill_kernel(keys_lists, piece_refs, spot, mat_ref, bands, pixels):
    for keys, piece_ref in zip(keys_lists, piece_refs):
        for number, key in enumerate(keys):
            share = piece_ref.shape[2]
            first = jnp.bitwise_xor(spot, key) * share
            for band in range(bands):
                rows = pl.ds(pl.multiple_of(band * pixels + first, share), share)
                mat_ref[rows, :] = piece_ref[number, band]


def fill_step(keys_lists, piece_refs, spot, mat_ref, band_step, group_steps):
    pixels = mat_ref.shape[0] // band_step
    step = pl.program_id(0)
    used = 0
    for group, keys_list in enumerate(keys_lists):
        group_refs = piece_refs[used : used + len(keys_list)]
        used += len(keys_list)

        @pl.when(step // group_steps == group)
        def _(keys_list=keys_list, group_refs=group_refs):
            fill_kernel(keys_list, group_refs, spot, mat_ref, band_step, pixels)


def embed_body(keys_lists, group_steps, band_step, *refs):
    spot_ref, patch_ref = refs[:2]
    count = sum(len(keys_list) for keys_list in keys_lists)
    piece_refs = refs[2 : 2 + count]
    *out_refs, mat_ref, total_ref = refs[2 + count :]
    step = pl.program_id(0)
    fill_step(keys_lists, piece_refs, spot_ref[0], mat_ref, band_step, group_steps)

    @pl.when(step == 0)
    def _():
        total_ref[...] = jnp.zeros_like(total_ref)

    total_ref[...] += dot_nn(patch_ref[...], mat_ref[...])

    @pl.when(step == pl.num_programs(0) - 1)
    def _():
        for key, out_ref in enumerate(out_refs):
            rows = out_ref.shape[0]
            first = pl.multiple_of(jnp.bitwise_xor(spot_ref[1], key) * rows, rows)
            out_ref[...] = total_ref[pl.ds(first, rows), :].astype(out_ref.dtype)


def group_band_count(kernel_groups):
    return min(block.shape[1] for blocks in kernel_groups for _, block in blocks)


def piece_specs(kernel_groups, band_step, first_group=0):
    group_steps = group_band_count(kernel_groups) // band_step
    specs = []
    arrays = []
    for group, blocks in enumerate(kernel_groups):
        for keys, block in blocks:
            whole = block.shape[1] > group_steps * band_step
            first = group * group_steps
            skip = first_group * group_steps

            def pick(step, first=first, whole=whole):
                here = jnp.clip(step - first, 0, group_steps - 1)
                return (0, here + first + skip if whole else here, 0, 0)

            specs.append(pl.BlockSpec((len(keys), band_step) + block.shape[2:], pick))
            arrays.append(block)
    keys_lists = [[keys for keys, _ in blocks] for blocks in kernel_groups]
    return specs, arrays, keys_lists, group_steps


def embed_share(spots, patch_rows, kernel_groups, owners):
    row_total = patch_rows.shape[0]
    blocks = kernel_groups[0]
    group_bands = group_band_count(kernel_groups)
    width = blocks[0][1].shape[3]
    pixels = sum(len(keys) for keys, _ in blocks) * blocks[0][1].shape[2]
    band_step = min(4, group_bands)
    depth = band_step * pixels
    specs, arrays, keys_lists, group_steps = piece_specs(kernel_groups, band_step)
    rows = row_total // owners
    return run_kernel(
        partial(embed_body, keys_lists, group_steps, band_step),
        [spots, patch_rows, *arrays],
        [
            pl.BlockSpec(memory_space=pltpu.SMEM),
            pl.BlockSpec((row_total, depth), lambda step: (0, step)),
        ]
        + specs,
        grid=(group_steps * len(kernel_groups),),
        out_shape=[jax.ShapeDtypeStruct((rows, width), jnp.bfloat16)] * owners,
        out_specs=[pl.BlockSpec((rows, width), lambda step: (0, 0))] * owners,
        scratch_shapes=[
            pltpu.VMEM((depth, width), jnp.bfloat16),
            pltpu.VMEM((row_total, width), jnp.float32),
        ],
    )


def kernel_grad_body(dp_size, band_step, *refs):
    spot_ref, patch_ref = refs[:2]
    *grad_refs, first_ref, last_ref, keep_ref, hold_ref = refs[2:]
    rows = grad_refs[0].shape[0]
    total = 0.0
    for key, grad_ref in enumerate(grad_refs):
        first = pl.multiple_of(jnp.bitwise_xor(spot_ref[1], key) * rows, rows)
        total = total + inner(patch_ref[pl.ds(first, rows), :], grad_ref[...])
    hold_ref[...] = total.astype(hold_ref.dtype)
    pixels = hold_ref.shape[0] // band_step
    share = pixels // dp_size
    core = lax.rem(spot_ref[0], 2)
    for band in range(band_step):
        for chip in range(dp_size // 2):
            base = band * pixels + chip * 2 * share
            kept = pl.multiple_of(base + core * share, share)
            keep_ref[band, chip] = hold_ref[pl.ds(kept, share), :]

    half = pl.num_programs(0) // 2
    for number, send_ref in enumerate((first_ref, last_ref)):

        @pl.when(pl.program_id(0) // half == number)
        def _(send_ref=send_ref):
            for band in range(band_step):
                for chip in range(dp_size // 2):
                    base = band * pixels + chip * 2 * share
                    sent = pl.multiple_of(base + (1 - core) * share, share)
                    send_ref[band, chip] = hold_ref[pl.ds(sent, share), :]


def kernel_grad_part(spots, patch_rows, grads, first_band, group_bands, bands_dev, dp_size, after):
    row_total = patch_rows.shape[0]
    width = grads[0].shape[1]
    band_step = min(4, group_bands // 2)
    pixels = patch_rows.shape[1] // bands_dev
    depth = band_step * pixels
    offset = first_band // band_step
    share = pixels // dp_size
    chips = (dp_size // 2, share, width)
    steps = group_bands // band_step
    block = (band_step,) + chips
    return run_kernel(
        partial(kernel_grad_body, dp_size, band_step),
        (spots, patch_rows, *grads),
        after=after,
        grid=(steps,),
        out_shape=[
            jax.ShapeDtypeStruct((bands,) + chips, jnp.bfloat16)
            for bands in (group_bands // 2, group_bands // 2, group_bands)
        ],
        in_specs=[
            pl.BlockSpec(memory_space=pltpu.SMEM),
            pl.BlockSpec((row_total, depth), lambda step: (0, offset + step)),
        ]
        + [pl.BlockSpec(grad.shape, lambda step: (0, 0)) for grad in grads],
        out_specs=[
            pl.BlockSpec(block, lambda step: (jnp.minimum(step, steps // 2 - 1), 0, 0, 0)),
            pl.BlockSpec(block, lambda step: (jnp.maximum(step - steps // 2, 0), 0, 0, 0)),
            pl.BlockSpec(block, lambda step: (step, 0, 0, 0)),
        ],
        scratch_shapes=[pltpu.VMEM((depth, width), jnp.bfloat16)],
    )


def patch_grad_body(keys_lists, grad_count, group_steps, band_step, *refs):
    spot_ref = refs[0]
    grad_refs = refs[1 : 1 + grad_count]
    out_ref, mat_ref = refs[-2:]
    piece_refs = refs[1 + grad_count : -2]
    fill_step(keys_lists, piece_refs, spot_ref[0], mat_ref, band_step, group_steps)
    for key, grad_ref in enumerate(grad_refs):
        rows = grad_ref.shape[0]
        first = pl.multiple_of(jnp.bitwise_xor(spot_ref[1], key) * rows, rows)
        out_ref[pl.ds(first, rows), :] = times_transpose(grad_ref[...], mat_ref[...]).astype(
            out_ref.dtype
        )


def patch_grad(spots, grads, kernel_groups, pixels, first_group, after):
    rows, width = grads[0].shape
    row_total = rows * len(grads)
    band_step = min(4, group_band_count(kernel_groups))
    depth = band_step * pixels
    specs, arrays, keys_lists, group_steps = piece_specs(kernel_groups, band_step, first_group)
    steps = group_steps * len(kernel_groups)
    return run_kernel(
        partial(patch_grad_body, keys_lists, len(grads), group_steps, band_step),
        [spots, *grads, *arrays],
        [pl.BlockSpec(memory_space=pltpu.SMEM)]
        + [pl.BlockSpec(grad.shape, lambda step: (0, 0)) for grad in grads]
        + specs,
        after=after,
        grid=(steps,),
        out_shape=jax.ShapeDtypeStruct((row_total, steps * depth), jnp.bfloat16),
        out_specs=pl.BlockSpec((row_total, depth), lambda step: (0, step)),
        scratch_shapes=[pltpu.VMEM((depth, width), jnp.bfloat16)],
    )


def states_grad_body(batches, low_ref, columns_ref, *refs):
    *piece_refs, sums_ref, spot_ref, grad_ref, part_ref, hold_ref = refs
    pixels, bands, width = piece_refs[0].shape
    for number, piece_ref in enumerate(piece_refs):
        key, batch = divmod(number, batches)
        first = (jnp.bitwise_xor(spot_ref[1], key) * batches + batch) * bands
        hold_ref[:, pl.ds(pl.multiple_of(first, bands), bands), :] = piece_ref[...]
    total = 0.0
    for pixel in range(pixels):
        cols = slice(pixel * width, (pixel + 1) * width)
        grads = hold_ref[pixel]
        grad_ref[:, cols] = inner(low_ref[...], grads)
        total = total + times_transpose(grads, columns_ref[:, cols])
    bands, states = total.shape
    part_ref[:bands, :] = total
    rows = [sums_ref[0:1, spot : spot + states] for spot in range(0, width, states)]
    rows.append(jnp.zeros((part_ref.shape[0] - bands - len(rows), states), jnp.float32))
    part_ref[bands:, :] = jnp.concatenate(rows, axis=0)


def states_grad(spots, low, columns, pieces, sums):
    pixels, bands, width = pieces[0].shape
    tail_rows = low.shape[0] + -(-width // low.shape[1] // 8) * 8
    if bands % 16:
        blocks = [([key], piece[None]) for key, piece in enumerate(pieces)]
        whole = place(blocks, "band", 1).reshape(pixels, -1, width)
        grads = whole.transpose(1, 0, 2).reshape(low.shape[0], -1)
        rows = [times_transpose(grads, columns), sums[0].reshape(-1, low.shape[1])]
        tail = jnp.concatenate(rows, axis=0)
        tail = jnp.pad(tail, ((0, tail_rows - tail.shape[0]), (0, 0)))
        return inner(low, grads), tail
    inside = pl.BlockSpec(memory_space=pltpu.VMEM)
    return run_kernel(
        partial(states_grad_body, 1),
        (low, columns, *pieces, sums, spots),
        out_shape=[
            jax.ShapeDtypeStruct(columns.shape, jnp.float32),
            jax.ShapeDtypeStruct((tail_rows, low.shape[1]), jnp.float32),
        ],
        in_specs=[inside] * (3 + len(pieces)) + [pl.BlockSpec(memory_space=pltpu.SMEM)],
        out_specs=[inside, inside],
        scratch_shapes=[pltpu.VMEM((pixels, bands * len(pieces), width), jnp.bfloat16)],
    )


def flatten_body(in_ref, out_ref):
    out_ref[...] = in_ref[...].reshape(out_ref.shape)


def unflatten_body(*refs):
    *in_refs, out_ref = refs
    done = 0
    for in_ref in in_refs:
        part = in_ref[...]
        bands = part.shape[1] // out_ref.shape[2]
        out_ref[:, done : done + bands, :] = part.reshape(-1, bands, out_ref.shape[2])
        done += bands


def flatten_rows(cube, after):
    rows, bands, pixels = cube.shape
    step_rows = 64
    return run_kernel(
        flatten_body,
        (cube,),
        [pl.BlockSpec((step_rows, bands, pixels), lambda step: (step, 0, 0))],
        after=after,
        grid=(rows // step_rows,),
        out_shape=jax.ShapeDtypeStruct((rows, bands * pixels), cube.dtype),
        out_specs=pl.BlockSpec((step_rows, bands * pixels), lambda step: (step, 0)),
    )


def unflatten_rows(flats, bands, after):
    rows = flats[0].shape[0]
    pixels = sum(flat.shape[1] for flat in flats) // bands
    step_rows = 64
    return run_kernel(
        unflatten_body,
        flats,
        [pl.BlockSpec((step_rows, flat.shape[1]), lambda step: (step, 0)) for flat in flats],
        after=after,
        grid=(rows // step_rows,),
        out_shape=jax.ShapeDtypeStruct((rows, bands, pixels), flats[0].dtype),
        out_specs=pl.BlockSpec((step_rows, bands, pixels), lambda step: (step, 0, 0)),
    )


def stack_body(*refs):
    *part_refs, out_ref, hold_ref = refs
    width = out_ref.shape[1]
    first = 0
    for part_ref in part_refs:
        rows = part_ref.shape[0]
        for spot in range(0, part_ref.shape[1], width):
            hold_ref[pl.ds(first, rows), :] = part_ref[:, spot : spot + width].astype(jnp.float32)
            first += rows
    out_ref[...] = hold_ref[...].astype(out_ref.dtype)


def stack_weights(shards_in):
    width = shards_in[-1].shape[1]
    if any(shard.shape[0] % 8 for shard in shards_in):
        return jnp.concatenate(
            [part for shard in shards_in for part in column_blocks(shard, width)], axis=0
        )
    row_total = sum(shard.size for shard in shards_in) // width
    inside = pl.BlockSpec(memory_space=pltpu.VMEM)
    return run_kernel(
        stack_body,
        shards_in,
        [inside] * len(shards_in),
        out_shape=jax.ShapeDtypeStruct((row_total, width), shards_in[0].dtype),
        out_specs=inside,
        scratch_shapes=[pltpu.VMEM((row_total, width), jnp.float32)],
    )


def plane_body(block_rows, spot_ref, *refs):
    *stack_refs, first_ref, last_ref, hold_ref = refs
    band_size = len(stack_refs)
    for key, stack_ref in enumerate(stack_refs):
        owner = jnp.bitwise_xor(spot_ref[1], key)
        values = stack_ref[...].astype(jnp.float32)
        done = 0
        for rows in block_rows:
            at = pl.multiple_of(done * band_size + owner * rows, 8)
            hold_ref[pl.ds(at, rows), :] = values[done : done + rows]
            done += rows
    half = first_ref.shape[0]
    first_ref[...] = hold_ref[:half, :].astype(first_ref.dtype)
    last_ref[...] = hold_ref[half:, :].astype(last_ref.dtype)


def plane_weights(spots, stacks, block_rows):
    row_total, width = stacks[0].shape
    band_size = len(stacks)
    half = row_total * band_size // 2
    if any(rows % 8 for rows in block_rows):
        whole = place([([key], stack[None]) for key, stack in enumerate(stacks)], "band", 0)
        parts = []
        done = 0
        for rows in block_rows:
            parts.append(whole[:, done : done + rows].reshape(-1, width))
            done += rows
        merged = jnp.concatenate(parts, axis=0)
        return merged[:half], merged[half:]
    inside = pl.BlockSpec(memory_space=pltpu.VMEM)
    return run_kernel(
        partial(plane_body, block_rows),
        (spots, *stacks),
        [pl.BlockSpec(memory_space=pltpu.SMEM)] + [inside] * band_size,
        out_shape=[jax.ShapeDtypeStruct((half, width), stacks[0].dtype)] * 2,
        out_specs=[inside] * 2,
        scratch_shapes=[pltpu.VMEM((row_total * band_size, width), jnp.float32)],
    )


def weight_grad_body(dp_size, parts, hidden, spot_ref, own_ref, other_ref, *refs):
    *out_refs, turned_ref, hold_ref, feed_ref, small_ref, sems = refs
    width = hold_ref.shape[2]
    row_total = own_ref.shape[0]
    spans = stash_spans(width, hidden)
    share = width // dp_size
    chips = dp_size // 2
    core = lax.rem(spot_ref[0], 2)
    copies = []

    def view(name, column=0, size=None):
        first, whole = spans[name]
        first = first + column * width
        return [ref[:, first : first + (size or whole)] for ref in (own_ref, other_ref)]

    def turn_rows(name, at):
        first, size = spans[name]
        for spot in range(0, size, width):
            for number, ref in enumerate((own_ref, other_ref)):
                cols = slice(number * row_total, (number + 1) * row_total)
                turned = ref[:, first + spot : first + spot + width].T
                turned_ref[at + spot : at + spot + width, cols] = turned

    def pick(at, rows):
        parts = []
        for chip in range(chips):
            first = at + (chip * 2 + core) * rows
            parts.append(turned_ref[pl.ds(pl.multiple_of(first, 16), rows), :])
        return jnp.concatenate(parts, axis=0)

    def send(source_ref, rows, number, stride=None):
        part = [number in numbers for _, numbers in parts].index(True)
        first_step, numbers = parts[part]
        first = share * numbers.index(number)
        step = first_step // 2
        bit = lax.rem(lax.div(spot_ref[0], first_step), 2)
        for index in range(chips // 2):
            for which in range(2):
                own_bit = bit if which == 0 else 1 - bit
                chip = index // step * 2 * step + own_bit * step + index % step
                at = chip * (stride or rows)
                copy = pltpu.make_async_copy(
                    source_ref.at[pl.ds(pl.multiple_of(at, 16), rows), :],
                    out_refs[part * 2 + which].at[index, pl.ds(first, rows), :],
                    sems.at[len(copies)],
                )
                copy.start()
                copies.append(copy)

    def product(left, names, column):
        right = view(names, column, width)
        total = dot_nn(left[:, :row_total], right[0])
        return total + dot_nn(left[:, row_total:], right[1])

    blocks = (
        [("normed", "qkv_grad", column) for column in range(3)]
        + [("mixed", "branch", 0)]
        + [("normed_two", "pre_grad", column) for column in range(hidden // width)]
    )
    turned_at = {"normed": 0, "mixed": width, "normed_two": 2 * width, "act": 3 * width}
    picked = {}
    for number, (left, right, column) in enumerate(blocks):
        if left not in picked:
            turn_rows(left, turned_at[left])
            picked = {left: pick(turned_at[left], share)}
        hold_ref[number] = product(picked[left], right, column).astype(hold_ref.dtype)
        send(hold_ref.at[number], share, number)
    small = sum(part.astype(jnp.float32) for part in view("small"))
    small_ref[...] = small.astype(small_ref.dtype)
    small_share = row_total // dp_size
    turn_rows("act", turned_at["act"])
    feed_rows = hidden // dp_size
    for chip in range(chips):
        at = turned_at["act"] + (chip * 2 + core) * feed_rows
        left = turned_ref[pl.ds(pl.multiple_of(at, 16), feed_rows), :]
        feed_ref[chip * feed_rows : (chip + 1) * feed_rows, :] = product(left, "cot", 0).astype(
            feed_ref.dtype
        )
    send(feed_ref, feed_rows, len(blocks))
    own_small = small_ref.at[pl.ds(pl.multiple_of(core * small_share, 16), (dp_size - 1) * small_share), :]
    send(own_small, small_share, len(blocks) + 1, 2 * small_share)
    for copy in copies:
        copy.wait()


def weight_grad(spots, dp_size, parts, hidden, own, other):
    row_total, columns = own.shape
    width = (columns - 2 * hidden) // 9
    bf16 = jnp.bfloat16
    blocks = 4 + hidden // width
    chips = dp_size // 2
    share = width // dp_size
    block_rows = [share] * blocks + [hidden // dp_size, row_total // dp_size]
    rows = [sum(block_rows[number] for number in numbers) for _, numbers in parts]
    inside = pl.BlockSpec(memory_space=pltpu.VMEM)
    outside = pl.BlockSpec(memory_space=pl.ANY)
    return run_kernel(
        partial(weight_grad_body, dp_size, parts, hidden),
        (spots, own, other),
        [pl.BlockSpec(memory_space=pltpu.SMEM), inside, inside],
        out_shape=[
            jax.ShapeDtypeStruct((chips // 2, part_rows, width), bf16)
            for part_rows in rows
            for _ in range(2)
        ],
        out_specs=[outside] * (2 * len(parts)),
        scratch_shapes=[
            pltpu.VMEM((3 * width + hidden, 2 * row_total), bf16),
            pltpu.VMEM((blocks, chips * share, width), bf16),
            pltpu.VMEM((hidden // 2, width), bf16),
            pltpu.VMEM((row_total, width), bf16),
            pltpu.SemaphoreType.DMA(((blocks + 2) * chips,)),
        ],
    )


def add_split_body(step, part_steps, spot_ref, keep_ref, *refs):
    *got_refs, send_ref, held_ref = refs
    bit = lax.rem(lax.div(spot_ref[0], step), 2)
    for number, got_ref in enumerate(got_refs):

        @pl.when(pl.program_id(0) // part_steps == number)
        def _(got_ref=got_ref):
            for out_ref, which in ((send_ref, 1 - bit), (held_ref, bit)):
                values = keep_ref[:, which].astype(jnp.float32)
                values = values + got_ref[:, which].astype(jnp.float32)
                out_ref[...] = values.astype(out_ref.dtype)


def add_split(spots, keep, gots, at, step, left):
    left = sorted(left, reverse=True)
    place_of = left.index(step)
    shape = keep.shape
    width = shape[-1]
    outer = math.prod(shape[:at]) * 2**place_of
    part_outer = outer // len(gots)
    inner_rows = keep.size // (outer * 2 * width)
    rows_step = inner_rows
    while rows_step > 512 and rows_step % 32 == 0:
        rows_step //= 2
    outer_step = 1
    while part_outer % (2 * outer_step) == 0 and 2 * outer_step * rows_step <= 512:
        outer_step *= 2
    part_steps = part_outer // outer_step
    block_in = (outer_step, 2, rows_step, width)
    block_out = pl.BlockSpec((outer_step, rows_step, width), lambda first, rows: (first, rows, 0))

    def part_spec(number):
        def pick(first, rows):
            return (jnp.clip(first - number * part_steps, 0, part_steps - 1), 0, rows, 0)

        return pl.BlockSpec(block_in, pick)

    outs = run_kernel(
        partial(add_split_body, step, part_steps),
        (spots, keep.reshape((outer, 2, inner_rows, width)))
        + tuple(got.reshape((part_outer, 2, inner_rows, width)) for got in gots),
        [
            pl.BlockSpec(memory_space=pltpu.SMEM),
            pl.BlockSpec(block_in, lambda first, rows: (first, 0, rows, 0)),
        ]
        + [part_spec(number) for number in range(len(gots))],
        grid=(outer // outer_step, inner_rows // rows_step),
        out_shape=[jax.ShapeDtypeStruct((outer, inner_rows, width), keep.dtype)] * 2,
        out_specs=[block_out] * 2,
    )
    rest = shape[:at] + (-1,) + shape[at + 1 :]
    return outs[0].reshape(rest), outs[1].reshape(rest)


def owners_body(groups, spot_ref, *refs):
    keep_refs = refs[:groups]
    got_refs = refs[groups : 2 * groups]
    *out_refs, hold_ref = refs[2 * groups :]
    pixels = out_refs[0].shape[0]
    for group, (keep_ref, got_ref) in enumerate(zip(keep_refs, got_refs)):
        bands = keep_ref.shape[0]
        hold_ref[...] = keep_ref[...].astype(jnp.float32) + got_ref[...].astype(jnp.float32)
        for key, out_ref in enumerate(out_refs):
            first = pl.multiple_of(jnp.bitwise_xor(spot_ref[1], key) * pixels, pixels)
            part = hold_ref[:, pl.ds(first, pixels), :]
            out_ref[:, group * bands : (group + 1) * bands, :] = jnp.swapaxes(part, 0, 1).astype(
                out_ref.dtype
            )


def by_owner(spots, keeps, gots, band_size):
    bands, share, width = keeps[0].shape
    pixels = share // band_size
    if pixels % 8:
        whole = jnp.concatenate([add_low(keep, got) for keep, got in zip(keeps, gots)], axis=0)
        whole = whole.reshape(-1, band_size, pixels, width).transpose(1, 2, 0, 3)
        return [
            lax.dynamic_index_in_dim(whole, spots[1] ^ key, 0, keepdims=False)
            for key in range(band_size)
        ]
    inside = pl.BlockSpec(memory_space=pltpu.VMEM)
    return run_kernel(
        partial(owners_body, len(keeps)),
        (spots, *keeps, *gots),
        [pl.BlockSpec(memory_space=pltpu.SMEM)] + [inside] * (2 * len(keeps)),
        out_shape=[
            jax.ShapeDtypeStruct((pixels, bands * len(keeps), width), keeps[0].dtype)
        ]
        * band_size,
        out_specs=[inside] * band_size,
        scratch_shapes=[pltpu.VMEM((bands, share, width), jnp.float32)],
    )


def shards(
    patches,
    bias_token,
    gen_attn,
    gen_gain,
    gen_ff_in,
    gen_ff_out,
    gen_kernel,
    gen_bias,
    pos_table,
    norm_gain,
    norm_bias,
    w_qkv,
    w_out,
    w_fc1,
    bias_in,
    w_fc2,
    wavelengths,
    kept,
    counts,
    cotangent,
):
    group_size, slot_count, bands_dev, pixel_count = patches.shape
    dp_size = lax.axis_size("dp")
    band_size = lax.axis_size("band")
    device_count = dp_size * band_size
    local_images = group_size // band_size
    model_width = w_out.shape[1]
    row_total = local_images * slot_count
    own_pixels = pixel_count // device_count
    share = own_pixels * band_size
    groups = 2
    group_bands = bands_dev // groups
    f32 = jnp.float32
    bf16 = jnp.bfloat16
    spot = lax.axis_index("band")
    spots = jnp.stack([lax.axis_index("dp"), spot]).astype(jnp.int32)

    own_kernel, embed_bias, band_states, *gen_kept = generate_fast(
        wavelengths,
        bias_token,
        gen_attn,
        gen_gain,
        gen_ff_in,
        gen_ff_out,
        gen_bias,
        gen_kernel,
    )
    hidden = w_fc1.shape[1]
    weight_rows = [w_qkv.shape[0]] * (4 + hidden // model_width) + [w_fc2.shape[0]]
    stack = stack_weights((w_qkv, w_out, w_fc1, w_fc2))
    patch_rows = flatten_rows(
        patches.reshape(group_size * slot_count, bands_dev, pixel_count), (own_kernel,)
    )
    own_kernel = own_kernel.reshape(own_pixels, band_size, bands_dev, model_width)
    other_bands = range(1, band_size)
    dp_steps = bit_steps(dp_size)[1:]
    orders = [turn(dp_steps, group) for group in range(groups)]

    sent = [
        lax.dynamic_index_in_dim(own_kernel, spot ^ key, 1, keepdims=False).transpose(1, 0, 2)
        for key in range(band_size)
    ]
    got = [swap(sent[key], "band", key) for key in other_bands]
    *got, patch_rows, stack = together(*got, patch_rows, stack)
    piece = place(
        [([key], block[None]) for key, block in enumerate([sent[0]] + got)], "band", 1
    ).reshape(bands_dev, share, model_width)

    own_pieces = [piece[group * group_bands : (group + 1) * group_bands] for group in range(groups)]
    held = [own_piece[None] for own_piece in own_pieces]
    held_keys = [[0] for _ in range(groups)]
    kernel_groups = [[([0], piece[None])] for _ in range(groups)]
    waiting = []
    stacks = {0: stack}
    stack_keys = [band_size // 2] + [key for key in other_bands if key != band_size // 2]
    for stage in range(len(dp_steps)):
        last = stage == len(dp_steps) - 1
        now_keys = stack_keys if last else stack_keys[:1]
        stack_keys = stack_keys[len(now_keys) :]
        got = [swap(held[group], "dp", orders[group][stage]) for group in range(groups)]
        if stage == 0:
            core_got = swap(piece, "dp", 1)
        elif waiting:
            core_got = swap(waiting[0][2], "dp", 1)
        stack_got = [swap(stack, "band", key) for key in now_keys]
        got[0], got[1], core_got, stack, *stack_got = together(*got, core_got, stack, *stack_got)
        stacks.update(zip(now_keys, stack_got))
        if stage == 0:
            for blocks in kernel_groups:
                blocks.append(([1], core_got[None]))
        elif waiting:
            group, keys, _ = waiting.pop(0)
            kernel_groups[group].append(([key ^ 1 for key in keys], core_got))
        for group in range(groups):
            keys = [key ^ orders[group][stage] for key in held_keys[group]]
            kernel_groups[group].append((keys, got[group]))
            waiting.append((group, keys, got[group]))
            if not last:
                held[group] = jnp.concatenate([held[group], got[group]], axis=0)
                held_keys[group] = held_keys[group] + keys
    for group, keys, last_got in waiting:
        kernel_groups[group].append(([key ^ 1 for key in keys], swap(last_got, "dp", 1)))

    planes = plane_weights(spots, [stacks[key] for key in range(band_size)], weight_rows)
    got = [swap(plane, "dp", orders[half][0]) for half, plane in enumerate(planes)]
    embedded = embed_share(spots, patch_rows, kernel_groups, band_size)
    *embedded, first_got, last_got = together(*embedded, *got)
    held = [
        jnp.concatenate([plane[None], got[None]], axis=0)
        for plane, got in zip(planes, (first_got, last_got))
    ]
    held_keys = [[0, orders[half][0]] for half in range(2)]
    for stage in range(1, len(dp_steps) - 1):
        for half in range(2):
            step = orders[half][stage]
            held[half] = jnp.concatenate([held[half], swap(held[half], "dp", step)], axis=0)
            held_keys[half] = held_keys[half] + [key ^ step for key in held_keys[half]]
    got = [swap(held[half], "dp", orders[half][-1]) for half in range(2)]
    parts = [embedded[0]] + [swap(embedded[key], "band", key) for key in other_bands]
    held[0], held[1], got[0], got[1], *parts = together(*held, *got, *parts)
    weight_halves = []
    for half in range(2):
        blocks = [(held_keys[half], held[half])]
        blocks.append(([key ^ orders[half][-1] for key in held_keys[half]], got[half]))
        weight_halves.append(blocks + gather_core(blocks))

    valid_mask = jnp.arange(slot_count)[None, :] < counts[:, None]
    keep_col = valid_mask.reshape(row_total, 1)
    kept_flat = kept.reshape(row_total)
    pos_rows = jnp.take(pos_table, kept_flat, axis=0).astype(f32)
    base = embed_bias[0:1] + pos_rows
    tile_images = 2 if local_images % 2 == 0 else 1
    tile_rows = tile_images * slot_count
    image_spot = jnp.arange(tile_rows) // slot_count
    same_image = image_spot[:, None] == image_spot[None, :]
    mask = jnp.where(same_image[None] & valid_mask.reshape(-1, 1, tile_rows), 0.0, -1e30)
    cot = jnp.where(keep_col, cotangent.reshape(row_total, model_width), 0)
    (
        result,
        grad_embed,
        stash,
        sums,
    ) = block(
        parts,
        weight_halves,
        spots,
        base,
        cot,
        keep_col.astype(f32),
        mask.astype(f32),
        norm_gain.astype(f32),
        norm_bias.astype(f32),
        bias_in.astype(f32)[None],
        kept_flat[None],
    )

    small_share = row_total // device_count
    block_rows = weight_rows + [small_share]
    part_blocks = [[0, 9], [1], [2], [3], [4, 5, 6, 7], [8]]
    part_orders = [orders[0], orders[1], orders[1], orders[0], orders[0], orders[1]]
    weight_parts = [(order[0], numbers) for order, numbers in zip(part_orders, part_blocks)]
    grads = [grad_embed] + [swap(grad_embed, "band", key) for key in other_bands]
    weight_split = weight_grad(
        spots, dp_size, weight_parts, hidden, stash, swap(stash, "dp", 1)
    )
    mixed = together(*grads, *weight_split)
    grads, weight_split = list(mixed[:band_size]), mixed[band_size:]
    weight_keep, weight_send = list(weight_split[0::2]), list(weight_split[1::2])

    weight_got = [swap(weight_send[part], "dp", part_orders[part][0]) for part in range(2)]
    kernel_split = []
    for group in range(groups):
        *sends, keep = kernel_grad_part(
            spots,
            patch_rows,
            grads,
            group * group_bands,
            group_bands,
            bands_dev,
            dp_size,
            (),
        )
        core_got = [swap(send, "dp", 1) for send in sends]
        kernel_split += add_split(spots, keep, core_got, 1, orders[group][0], dp_steps)
    weight_got[0], weight_got[1], *kernel_split = together(*weight_got, *kernel_split)

    def cut_blocks(values, numbers):
        lead = values.shape[0]
        cuts = []
        first = 0
        for number in numbers:
            rows = block_rows[number]
            cut = values[:, first : first + rows * band_size]
            cuts.append(cut.reshape(lead, band_size, rows, model_width))
            first += rows * band_size
        return jnp.concatenate(cuts, axis=2)

    def over_band(by_band):
        sent = [
            lax.dynamic_index_in_dim(by_band, spot ^ key, 1, keepdims=False)
            for key in range(band_size)
        ]
        return [sent[0]] + [swap(sent[key], "band", key) for key in other_bands]

    def total(blocks):
        return sum(block_sum.astype(f32) for block_sum in blocks)

    def over_chips(sums):
        cut = [
            values if isinstance(values, tuple) else split_half(values, 0, order[0], order)
            for values, order in sums
        ]
        got = [None] * len(sums)
        for step in sorted({order[0] for _, order in sums}):
            here = [number for number, (_, order) in enumerate(sums) if order[0] == step]
            flat = [cut[number][0].reshape(-1, model_width) for number in here]
            moved = swap(jnp.concatenate(flat, axis=0) if len(flat) > 1 else flat[0], "dp", step)
            first = 0
            for number, rows in zip(here, flat):
                part = moved[first : first + rows.shape[0]]
                got[number] = part.reshape(cut[number][0].shape)
                first += rows.shape[0]
        return [
            (add_low(cut[number][1], got[number]), order[1:])
            for number, (_, order) in enumerate(sums)
        ]

    update = patch_grad(spots, grads, kernel_groups, pixel_count, 0, ())
    for stage in range(len(dp_steps)):
        last = stage == len(dp_steps) - 1
        got = [swap(kernel_split[2 * group], "dp", orders[group][stage]) for group in range(groups)]
        part = 2 + stage
        cuts = [
            cut_blocks(weight_keep[part], part_blocks[part]),
            cut_blocks(weight_send[part], part_blocks[part]),
        ]
        if stage == 0:
            cuts += [
                cut_blocks(add_low(weight_keep[early], weight_got[early]), part_blocks[early])
                for early in range(2)
            ]
        part_got = [None]
        if stage < 2:
            part_got = over_band(jnp.concatenate(cuts, axis=2))
        if stage == 0:
            got[0], got[1], update, *part_got = together(*got, update, *part_got)
        else:
            got[0], got[1], *part_got = together(*got, *part_got)
        if stage < 2:
            summed = total(part_got).astype(bf16)
            rows = [cut.shape[2] for cut in cuts]
            spots_in = [sum(rows[:number]) for number in range(len(rows))]
            summed = [summed[:, first : first + size] for first, size in zip(spots_in, rows)]
            weight_keep[part], weight_send[part] = summed[:2]
            if stage == 0:
                early = summed[2:]
        if not last:
            kernel_split = [
                part
                for group in range(groups)
                for part in add_split(
                    spots,
                    kernel_split[2 * group + 1],
                    [got[group]],
                    1,
                    orders[group][stage + 1],
                    orders[group][stage + 1 :],
                )
            ]
    sent = by_owner(
        spots,
        [
            kernel_split[2 * group + 1].reshape(group_bands, share, model_width)
            for group in range(groups)
        ],
        [got[group].reshape(group_bands, share, model_width) for group in range(groups)],
        band_size,
    )
    pieces = [sent[0]] + [swap(sent[key], "band", key) for key in other_bands]
    sums_left = over_chips(
        [(early[part], part_orders[part][1:]) for part in range(2)]
        + [
            ((weight_send[part], weight_keep[part]), part_orders[part])
            for part in range(2, len(part_blocks))
        ]
    )
    while any(order for _, order in sums_left[:2]):
        moved = over_chips([one for one in sums_left[:2] if one[1]])
        sums_left[:2] = [moved.pop(0) if one[1] else one for one in sums_left[:2]]
    weight_sums = [values for values, _ in sums_left]
    grad_patches = unflatten_rows([update], bands_dev, (sent[0],))
    mixed = together(*weight_sums, grad_patches, *pieces)
    count = len(part_blocks)
    weight_sums, grad_patches, pieces = list(mixed[:count]), mixed[count], mixed[count + 1 :]
    grad_gen_kernel, tail = states_grad(spots, band_states, gen_kernel, pieces, sums)
    mixed = together(*weight_sums, tail)
    weight_sums, tail = list(mixed[:-1]), mixed[-1]

    small = weight_sums[0][:, -small_share:]
    late = [(weight_sums[part], part_orders[part][1:]) for part in range(2, count)]
    small_steps = [("band", step) for step in bit_steps(band_size)]
    small_steps += [("dp", step) for step in turn(bit_steps(dp_size), 1)]

    def widen(values, number):
        return jnp.concatenate([values, swap(values, *small_steps[number])], axis=0)

    while any(order for _, order in late):
        late = over_chips(late)
    late = [values for values, _ in late]
    tail = total([tail] + [swap(tail, "band", key) for key in other_bands])
    tail_steps = bit_steps(dp_size)
    tail = tail + swap(tail, "dp", tail_steps[0])
    tail, *late = together(tail, *late)
    cuts = [cut_blocks(late[part - 2], part_blocks[part]) for part in range(4, count)]
    last_sum = total(over_band(jnp.concatenate(cuts, axis=2)))
    small = widen(small, 0)
    for number, step in enumerate(tail_steps[1:]):
        got = swap(tail, "dp", step)
        small = widen(small, number + 1)
        got, small = together(got, small)
        tail = tail + got
    for number in range(len(tail_steps), len(small_steps)):
        small = widen(small, number)
    own_grads = jnp.concatenate(
        [
            weight_sums[0][0, :-small_share].astype(f32),
            weight_sums[1][0].astype(f32),
            late[0][0].astype(f32),
            late[1][0].astype(f32),
            last_sum[0],
        ],
        axis=0,
    )
    small_order = (jnp.arange(dp_size) ^ spots[0])[:, None] * band_size
    small_order = (small_order + (jnp.arange(band_size) ^ spots[1])[None, :]).reshape(-1)
    small = small.reshape(2, dp_size // 2, band_size, small_share, model_width)
    small = small.transpose(1, 0, 2, 3, 4).reshape(-1, small_share, model_width)
    small = jnp.take(small, small_order, axis=0).reshape(row_total, model_width)
    own_blocks = []
    done = 0
    for rows in weight_rows:
        own_blocks.append(own_grads[done : done + rows])
        done += rows
    grad_qkv_own = jnp.concatenate(own_blocks[:3], axis=1)
    grad_out_own = own_blocks[3]
    grad_fc_in_own = jnp.concatenate(own_blocks[4:-1], axis=1)
    grad_fc_out_own = own_blocks[-1]
    grad_token, grad_attn, grad_gain_gen, grad_ff_first, grad_ff_second, grad_gen_bias = (
        generate_back(
            tail,
            gen_attn,
            gen_gain,
            gen_ff_in,
            gen_ff_out,
            gen_bias,
            gen_kept,
        )
    )

    small = small.astype(f32)
    sums_at = small.shape[0] - 16
    grad_pos_all = small[: pos_table.shape[0]]
    grad_gains = small[sums_at + 1 : sums_at + 3]
    grad_shifts = small[sums_at + 3 : sums_at + 5]
    grad_bias_all = small[sums_at + 8 : sums_at + 8 + hidden // model_width].reshape(-1)
    grad_patches = grad_patches.reshape(group_size, slot_count, bands_dev, pixel_count)
    return (
        result.reshape(local_images, slot_count, model_width),
        grad_patches,
        grad_token[0],
        grad_attn,
        grad_gain_gen,
        grad_ff_first,
        grad_ff_second,
        grad_gen_kernel,
        grad_gen_bias,
        grad_pos_all,
        grad_gains,
        grad_shifts,
        grad_qkv_own,
        grad_out_own,
        grad_fc_in_own,
        grad_bias_all,
        grad_fc_out_own,
    )


def solution(mesh):
    placed = (
        P("dp", None, "band", None),
        P(),
        P(),
        P(),
        P(),
        P(),
        P(None, ("dp", "band")),
        P(),
        P(),
        P(),
        P(),
        P(("dp", "band"), None),
        P(("dp", "band"), None),
        P(("dp", "band"), None),
        P(),
        P(("dp", "band"), None),
        P(),
        P(("dp", "band"), None),
        P(("dp", "band")),
        P(("dp", "band"), None, None),
    )
    return jax.shard_map(
        shards,
        mesh=mesh,
        in_specs=placed,
        out_specs=(
            P(("dp", "band"), None, None),
            P("dp", None, "band", None),
            P(),
            P(),
            P(),
            P(),
            P(),
            P(None, ("dp", "band")),
            P(),
            P(),
            P(),
            P(),
            P(("dp", "band"), None),
            P(("dp", "band"), None),
            P(("dp", "band"), None),
            P(),
            P(("dp", "band"), None),
        ),
        check_vma=False,
    )
```

```python
from functools import partial
import math

import jax
import jax.numpy as jnp
from jax import lax
from jax.experimental import pallas as pl
from jax.experimental.pallas import tpu as pltpu
from jax.sharding import PartitionSpec as P

HEADS = 12
HDIM = 64
GEN_HEADS = 4


def inner(left_arr, right_arr):
    return lax.dot_general(
        left_arr, right_arr, (((0,), (0,)), ((), ())), preferred_element_type=jnp.float32
    )


def times_transpose(left_arr, right_arr):
    return lax.dot_general(
        left_arr, right_arr, (((1,), (1,)), ((), ())), preferred_element_type=jnp.float32
    )


def bit_steps(size):
    steps = []
    step = 1
    while step < size:
        steps.append(step)
        step *= 2
    return steps


def swap(values, axis, step):
    size = lax.axis_size(axis)
    return lax.ppermute(values, axis, [(spot, spot ^ step) for spot in range(size)])


def turn(items, by):
    by = by % max(len(items), 1)
    return items[by:] + items[:by]


def gather_core(blocks):
    return [([key ^ 1 for key in keys], swap(block, "dp", 1)) for keys, block in blocks]


def place(blocks, axis, at):
    spot = lax.axis_index(axis)
    first = blocks[0][1]
    count = sum(len(keys) for keys, _ in blocks)
    shape = first.shape[1 : at + 1] + (count,) + first.shape[at + 1 :]
    whole = jnp.zeros(shape, first.dtype)
    for keys, block in blocks:
        for number, key in enumerate(keys):
            whole = lax.dynamic_update_index_in_dim(whole, block[number], spot ^ key, at)
    return whole


def add_low(left_arr, right_arr):
    return (left_arr.astype(jnp.float32) + right_arr.astype(jnp.float32)).astype(left_arr.dtype)


def split_half(values, at, step, left):
    left = sorted(left, reverse=True)
    shape = values.shape
    values = values.reshape(shape[:at] + (2,) * len(left) + shape[at + 1 :])
    dim = at + left.index(step)
    bit = (lax.axis_index("dp") // step) % 2
    rest = shape[:at] + (-1,) + shape[at + 1 :]
    send = lax.dynamic_index_in_dim(values, 1 - bit, dim, keepdims=False)
    keep = lax.dynamic_index_in_dim(values, bit, dim, keepdims=False)
    return send.reshape(rest), keep.reshape(rest)


def together(*arrays):
    return lax.optimization_barrier(arrays)


def column_blocks(matrix, width):
    return [matrix[:, spot : spot + width] for spot in range(0, matrix.shape[1], width)]


def run_kernel(body, args, in_specs, after=(), limit=60, **options):
    count = len(after)

    def whole(*refs):
        body(*refs[count:])

    return pl.pallas_call(
        whole,
        in_specs=[pl.BlockSpec(memory_space=pl.ANY)] * count + in_specs,
        compiler_params=pltpu.CompilerParams(vmem_limit_bytes=limit * 1024 * 1024),
        cost_estimate=pl.CostEstimate(flops=1000, bytes_accessed=1000, transcendentals=0),
        **options,
    )(*after, *args)


def dot_nn(left_arr, right_arr):
    return lax.dot_general(
        left_arr, right_arr, (((1,), (0,)), ((), ())), preferred_element_type=jnp.float32
    )


def norm_stats(values):
    center = values - jnp.mean(values, axis=-1, keepdims=True)
    spread = jnp.mean(center * center, axis=-1, keepdims=True)
    scale = lax.rsqrt(spread + 1e-06)
    return center * scale, scale


def norm_back(unit, scale, gain, grad):
    weighted = grad * gain
    first = jnp.mean(weighted, axis=-1, keepdims=True)
    second = jnp.mean(weighted * unit, axis=-1, keepdims=True)
    grad_values = (weighted - first - unit * second) * scale
    grad_gain = jnp.sum(grad * unit, axis=0, keepdims=True)
    grad_shift = jnp.sum(grad, axis=0, keepdims=True)
    return grad_values, grad_gain, grad_shift


def stash_spans(width, hidden):
    sizes = {
        "normed": width,
        "mixed": width,
        "normed_two": width,
        "act": hidden,
        "qkv_grad": 3 * width,
        "branch": width,
        "pre_grad": hidden,
        "cot": width,
        "small": width,
    }
    spans = {}
    first = 0
    for name, size in sizes.items():
        spans[name] = (first, size)
        first += size
    return spans


def block_body(part_count, tile_rows, ff_step, keys_lists, *refs):
    part_refs = refs[:part_count]
    weight_count = sum(len(keys_list) for keys_list in keys_lists)
    weight_refs = refs[part_count : part_count + weight_count]
    (
        spot_ref,
        base_ref,
        cot_ref,
        keep_ref,
        mask_ref,
        gain_ref,
        shift_ref,
        bias_ref,
        kept_ref,
        result_ref,
        embed_grad_ref,
        stash_ref,
        sums_ref,
        qkv_w,
        out_w,
        fc_in_w,
        fc_out_w,
        qkv_ref,
        probs_ref,
        total_ref,
        back_ref,
        mixed_grad_ref,
        bias_grad_ref,
        sems,
    ) = refs[part_count + weight_count :]
    bf16 = jnp.bfloat16
    f32 = jnp.float32
    width = base_ref.shape[1]
    hidden = fc_in_w.shape[1]
    spans = stash_spans(width, hidden)
    views = {name: stash_ref.at[:, pl.ds(first, size)] for name, (first, size) in spans.items()}
    normed_ref = views["normed"]
    mixed_ref = views["mixed"]
    normed_two_ref = views["normed_two"]
    act_ref = views["act"]
    qkv_grad_ref = views["qkv_grad"]
    branch_ref = views["branch"]
    pre_grad_ref = views["pre_grad"]
    views["cot"][...] = cot_ref[...]
    share = width // sum(len(keys) for keys in keys_lists[0])
    targets = (
        [(qkv_w, column, share) for column in range(3)]
        + [(out_w, 0, share)]
        + [(fc_in_w, column, share) for column in range(hidden // width)]
        + [(fc_out_w, 0, share * hidden // width)]
    )
    copies = {}
    for number, (target_ref, column, rows) in enumerate(targets):
        half, first = (0, number * share) if number < 6 else (1, (number - 6) * share)
        half_refs = weight_refs[: len(keys_lists[0])] if half == 0 else weight_refs[len(keys_lists[0]) :]
        for keys, weight_ref in zip(keys_lists[half], half_refs):
            for index, key in enumerate(keys):
                at = pl.multiple_of(jnp.bitwise_xor(spot_ref[0], key) * rows, rows)
                copy = pltpu.make_async_copy(
                    weight_ref.at[index, pl.ds(first, rows), :],
                    target_ref.at[pl.ds(at, rows), pl.ds(column * width, width)],
                    sems.at[sum(len(some) for some in copies.values())],
                )
                copy.start()
                copies.setdefault(id(target_ref), []).append(copy)

    def arrive(target_ref):
        for copy in copies[id(target_ref)]:
            copy.wait()

    row_total, width = base_ref.shape
    tiles = row_total // tile_rows
    head_pairs = HEADS // 2
    lanes = 2 * HDIM

    start = base_ref[...]
    for part_ref in part_refs:
        start = start + part_ref[...].astype(f32)
    unit_one, scale_one = norm_stats(start)
    normed = (unit_one * gain_ref[0:1] + shift_ref[0:1]).astype(bf16)
    normed_ref[...] = normed
    arrive(qkv_w)
    for spot in range(3):
        cols = slice(spot * width, (spot + 1) * width)
        qkv_ref[:, cols] = dot_nn(normed, qkv_w[:, cols]).astype(bf16)

    low_lanes = lax.broadcasted_iota(jnp.int32, (tile_rows, lanes), 1) < HDIM

    def half(values, odd):
        keep = jnp.logical_not(low_lanes) if odd else low_lanes
        return jnp.where(keep, values, jnp.zeros_like(values))

    def head_slices(pair, tile):
        rows = pl.ds(tile * tile_rows, tile_rows)
        cols = [
            pl.ds(pl.multiple_of(which * width + pair * lanes, lanes), lanes) for which in range(3)
        ]
        return rows, cols

    def attend(pair, carry):
        for tile in range(tiles):
            rows, cols = head_slices(pair, tile)
            queries, keys_arr, values_arr = [qkv_ref[rows, col] for col in cols]
            mixed = jnp.zeros((tile_rows, lanes), f32)
            for odd in range(2):
                scores = times_transpose(half(queries, odd), keys_arr) * HDIM ** (-0.5)
                scores = scores + mask_ref[tile]
                exponent = jnp.exp(scores - jnp.max(scores, axis=-1, keepdims=True))
                probs = exponent * (1.0 / jnp.sum(exponent, axis=-1, keepdims=True))
                probs_ref[(pair * 2 + odd) * tiles + tile] = probs
                mixed = mixed + dot_nn(probs.astype(bf16), half(values_arr, odd))
            mixed_ref[rows, cols[0]] = mixed.astype(bf16)
        return carry

    lax.fori_loop(0, head_pairs, attend, 0)
    arrive(out_w)
    middle = start + dot_nn(mixed_ref[...], out_w[...])
    unit_two, scale_two = norm_stats(middle)
    normed_two = (unit_two * gain_ref[1:2] + shift_ref[1:2]).astype(bf16)
    normed_two_ref[...] = normed_two
    total_ref[...] = middle
    back_ref[...] = jnp.zeros_like(back_ref)
    arrive(fc_in_w)
    arrive(fc_out_w)

    def feed(step, carry):
        cols = pl.ds(pl.multiple_of(step * ff_step, ff_step), ff_step)
        pre = dot_nn(normed_two_ref[...], fc_in_w[:, cols]) + bias_ref[:, cols]
        cdf = 0.5 * (1.0 + lax.erf(pre * 0.5**0.5))
        act = (pre * cdf).astype(bf16)
        act_ref[:, cols] = act
        slope = cdf + pre * (jnp.exp(-0.5 * pre * pre) * (2.0 * math.pi) ** (-0.5))
        pre_grad = slope * times_transpose(cot_ref[...], fc_out_w[cols, :])
        pre_grad = pre_grad.astype(bf16)
        pre_grad_ref[:, cols] = pre_grad
        bias_grad_ref[:, cols] = jnp.sum(pre_grad.astype(f32), axis=0, keepdims=True)
        total_ref[...] += dot_nn(act, fc_out_w[cols, :])
        back_ref[...] += times_transpose(pre_grad, fc_in_w[:, cols])
        return carry

    lax.fori_loop(0, fc_in_w.shape[1] // ff_step, feed, 0)
    result_ref[...] = (total_ref[...] * keep_ref[...]).astype(bf16)
    grad_norm, gain_two, shift_two = norm_back(unit_two, scale_two, gain_ref[1:2], back_ref[...])
    grad_middle = cot_ref[...].astype(f32) + grad_norm
    grad_branch = grad_middle.astype(bf16)
    branch_ref[...] = grad_branch
    mixed_grad_ref[...] = times_transpose(grad_branch, out_w[...]).astype(bf16)

    def attend_back(pair, carry):
        for tile in range(tiles):
            rows, cols = head_slices(pair, tile)
            queries, keys_arr, values_arr = [qkv_ref[rows, col] for col in cols]
            grad_mixed = mixed_grad_ref[rows, cols[0]]
            grads = [jnp.zeros((tile_rows, lanes), f32) for _ in range(3)]
            for odd in range(2):
                probs = probs_ref[(pair * 2 + odd) * tiles + tile]
                own_grad = half(grad_mixed, odd)
                grad_probs = times_transpose(own_grad, values_arr)
                grad_scores = probs * (
                    grad_probs - jnp.sum(grad_probs * probs, axis=-1, keepdims=True)
                )
                grad_scores = grad_scores.astype(bf16)
                grads[0] = grads[0] + dot_nn(grad_scores, half(keys_arr, odd))
                grads[1] = grads[1] + inner(grad_scores, half(queries, odd))
                grads[2] = grads[2] + inner(probs.astype(bf16), own_grad)
            for which, factor in enumerate((HDIM ** (-0.5), HDIM ** (-0.5), 1.0)):
                qkv_grad_ref[rows, cols[which]] = (grads[which] * factor).astype(bf16)
        return carry

    lax.fori_loop(0, head_pairs, attend_back, 0)
    back = jnp.zeros((row_total, width), f32)
    for spot in range(3):
        cols = slice(spot * width, (spot + 1) * width)
        back = back + times_transpose(qkv_grad_ref[:, cols], qkv_w[:, cols])
    grad_norm, gain_one, shift_one = norm_back(unit_one, scale_one, gain_ref[0:1], back)
    grad_start = grad_middle + grad_norm
    embed_grad_ref[...] = grad_start.astype(bf16)
    sums = jnp.concatenate(
        [jnp.sum(grad_start, axis=0, keepdims=True), gain_one, gain_two, shift_one, shift_two]
        + [jnp.zeros((3, width), f32)],
        axis=0,
    )
    sums_ref[...] = sums
    small_ref = views["small"]
    positions = small_ref.shape[0] - 16
    spots_at = lax.broadcasted_iota(jnp.int32, (positions, row_total), 0)
    one_hot = jnp.where(spots_at == kept_ref[...], 1.0, 0.0).astype(bf16)
    by_position = dot_nn(one_hot, grad_start.astype(bf16))
    cuts = [bias_grad_ref[:, spot : spot + width] for spot in range(0, hidden, width)]
    cuts.append(jnp.zeros((8 - len(cuts), width), f32))
    small_ref[...] = jnp.concatenate([by_position, sums, *cuts], axis=0).astype(bf16)


def block(parts, weight_halves, spots, base, cot, keep, mask, gains, shifts, bias, kept):
    row_total, width = base.shape
    tile_rows = mask.shape[1]
    hidden = bias.shape[1]
    bf16 = jnp.bfloat16
    f32 = jnp.float32
    keys_lists = [[keys for keys, _ in blocks] for blocks in weight_halves]
    weight_args = [block for blocks in weight_halves for _, block in blocks]
    pieces = sum(len(keys) for keys in keys_lists[0])
    inside = pl.BlockSpec(memory_space=pltpu.VMEM)
    outside = pl.BlockSpec(memory_space=pl.ANY)
    rows = (row_total, width)
    shapes = [
        (rows, bf16),
        (rows, bf16),
        ((row_total, sum(stash_spans(width, hidden)["small"])), bf16),
        ((8, width), f32),
    ]
    return run_kernel(
        partial(block_body, len(parts), tile_rows, 512, keys_lists),
        (*parts, *weight_args, spots, base, cot, keep, mask, gains, shifts, bias, kept),
        [inside] * len(parts)
        + [outside] * len(weight_args)
        + [pl.BlockSpec(memory_space=pltpu.SMEM)]
        + [inside] * 8,
        out_shape=[jax.ShapeDtypeStruct(shape, kind) for shape, kind in shapes],
        out_specs=[inside] * len(shapes),
        scratch_shapes=[
            pltpu.VMEM((width, 3 * width), bf16),
            pltpu.VMEM((width, width), bf16),
            pltpu.VMEM((width, hidden), bf16),
            pltpu.VMEM((hidden, width), bf16),
            pltpu.VMEM((row_total, 3 * width), bf16),
            pltpu.VMEM((HEADS * row_total // tile_rows, tile_rows, tile_rows), f32),
            pltpu.VMEM(rows, f32),
            pltpu.VMEM(rows, f32),
            pltpu.VMEM(rows, bf16),
            pltpu.VMEM((1, hidden), f32),
            pltpu.SemaphoreType.DMA(((5 + hidden // width) * pieces,)),
        ],
    )


def dot_full(left_arr, right_arr, left_dim=1, right_dim=0):
    return lax.dot_general(
        left_arr,
        right_arr,
        (((left_dim,), (right_dim,)), ((), ())),
        precision=lax.Precision.HIGH,
        preferred_element_type=jnp.float32,
    )


def head_part(values, head):
    size = values.shape[1] // GEN_HEADS
    lane = lax.broadcasted_iota(jnp.int32, values.shape, 1)
    inside = jnp.logical_and(lane >= head * size, lane < (head + 1) * size)
    return jnp.where(inside, values, 0.0)


def generate_body(
    waves_ref,
    token_ref,
    attn_hbm,
    gain_hbm,
    ff_in_hbm,
    ff_out_hbm,
    bias_w_hbm,
    columns_hbm,
    kernel_ref,
    embed_bias_ref,
    low_ref,
    states_ref,
    rows_ref,
    weights_ref,
    pre_ref,
    scales_ref,
    attn_ref,
    gain_ref,
    ff_in_ref,
    ff_out_ref,
    bias_w_ref,
    columns_ref,
    sems,
):
    f32 = jnp.float32
    copies = [
        pltpu.make_async_copy(source, target, sems.at[number])
        for number, (source, target) in enumerate(
            (
                (attn_hbm, attn_ref),
                (gain_hbm, gain_ref),
                (ff_in_hbm, ff_in_ref),
                (ff_out_hbm, ff_out_ref),
                (columns_hbm, columns_ref),
                (bias_w_hbm, bias_w_ref),
            )
        )
    ]
    for copy in copies:
        copy.start()
    bands = waves_ref.shape[1]
    width = token_ref.shape[1]
    padded = rows_ref.shape[1]
    square = (bands, bands)
    diagonal = lax.broadcasted_iota(jnp.int32, square, 0) == lax.broadcasted_iota(
        jnp.int32, square, 1
    )
    waves = jnp.broadcast_to(waves_ref[...].astype(f32), square)
    column = jnp.sum(jnp.where(diagonal, waves, 0.0), axis=1, keepdims=True)
    lane = lax.broadcasted_iota(jnp.int32, (bands, width), 1)
    half_width = width // 2
    number = jnp.where(lane < half_width, lane, lane - half_width).astype(f32)
    angles = column * jnp.exp(number * (-math.log(10000.0) / half_width))
    wave = jnp.where(lane < half_width, jnp.sin(angles), jnp.cos(angles))
    sequence = jnp.concatenate(
        [wave, token_ref[...].astype(f32), jnp.zeros((padded - bands - 1, width), f32)], axis=0
    )
    rows_ref[0] = sequence
    copies[0].wait()
    copies[1].wait()
    for which in range(3):
        rows_ref[1 + which] = dot_full(sequence, attn_ref[which].astype(f32))
    queries = rows_ref[1]
    keys_arr = rows_ref[2]
    values_arr = rows_ref[3]
    key_spot = lax.broadcasted_iota(jnp.int32, (padded, padded), 1)
    mixed = jnp.zeros((padded, width), f32)
    for head in range(GEN_HEADS):
        scores = dot_full(head_part(queries, head), keys_arr, 1, 1)
        scores = scores * (1.0 / math.sqrt(width // GEN_HEADS))
        scores = jnp.where(key_spot <= bands, scores, -1e30)
        exponent = jnp.exp(scores - jnp.max(scores, axis=-1, keepdims=True))
        weights = exponent / jnp.sum(exponent, axis=-1, keepdims=True)
        weights_ref[head] = weights
        mixed = mixed + dot_full(weights, head_part(values_arr, head))
    rows_ref[4] = mixed
    unit_one, scale_one = norm_stats(sequence + dot_full(mixed, attn_ref[3].astype(f32)))
    rows_ref[5] = unit_one
    first = unit_one * gain_ref[0:1].astype(f32)
    copies[2].wait()
    pre = dot_full(first, ff_in_ref[...].astype(f32))
    pre_ref[...] = pre
    hidden = pre * (0.5 * (1.0 + lax.erf(pre * 0.5**0.5)))
    copies[3].wait()
    unit_two, scale_two = norm_stats(first + dot_full(hidden, ff_out_ref[...].astype(f32)))
    rows_ref[6] = unit_two
    states = unit_two * gain_ref[1:2].astype(f32)
    states_ref[...] = states
    scales_ref[0] = jnp.broadcast_to(scale_one, (padded, width))
    scales_ref[1] = jnp.broadcast_to(scale_two, (padded, width))
    low = states[:bands].astype(jnp.bfloat16)
    low_ref[...] = low
    features = kernel_ref.shape[2]
    copies[4].wait()
    for pixel in range(kernel_ref.shape[0]):
        cols = slice(pixel * features, (pixel + 1) * features)
        kernel_ref[pixel] = dot_nn(low, columns_ref[:, cols]).astype(jnp.bfloat16)
    copies[5].wait()
    token_state = states[bands : bands + 8]
    embed_bias_ref[...] = dot_full(token_state, bias_w_ref[...].astype(f32))


def generate_fast(wavelengths, token, gen_attn, gen_gain, ff_in, ff_out, gen_bias, columns):
    f32 = jnp.float32
    bf16 = jnp.bfloat16
    bands = wavelengths.shape[0]
    width = token.shape[0]
    padded = -(-(bands + 1) // 8) * 8
    features = gen_bias.shape[1]
    shapes = [
        ((columns.shape[1] // features, bands, features), bf16),
        ((8, features), f32),
        ((bands, width), bf16),
        ((padded, width), f32),
        ((7, padded, width), f32),
        ((GEN_HEADS, padded, padded), f32),
        ((padded, ff_in.shape[1]), f32),
        ((2, padded, width), f32),
    ]
    inside = pl.BlockSpec(memory_space=pltpu.VMEM)
    outside = pl.BlockSpec(memory_space=pl.ANY)
    weights = (gen_attn, gen_gain, ff_in, ff_out, gen_bias, columns)
    return run_kernel(
        generate_body,
        (wavelengths[None], token[None], *weights),
        out_shape=[jax.ShapeDtypeStruct(shape, kind) for shape, kind in shapes],
        in_specs=[inside] * 2 + [outside] * 6,
        out_specs=[inside] * len(shapes),
        scratch_shapes=[pltpu.VMEM(weight.shape, bf16) for weight in weights]
        + [pltpu.SemaphoreType.DMA((6,))],
    )


def generate_back_body(
    tail_ref,
    attn_ref,
    gain_ref,
    ff_in_ref,
    ff_out_ref,
    bias_w_ref,
    states_ref,
    rows_ref,
    weights_ref,
    pre_ref,
    scales_ref,
    token_out,
    attn_out,
    gain_out,
    ff_in_out,
    ff_out_out,
    bias_out,
):
    f32 = jnp.float32
    padded, width = states_ref.shape
    features = bias_w_ref.shape[1]
    bands = padded - 8
    head_scale = 1.0 / math.sqrt(width // GEN_HEADS)
    cuts = [tail_ref[bands + spot : bands + spot + 1, :] for spot in range(features // width)]
    bias_grad = jnp.concatenate(cuts, axis=1)
    bias_grad = jnp.concatenate([bias_grad, jnp.zeros((7, features), f32)], axis=0)
    row_spot = lax.broadcasted_iota(jnp.int32, (padded - bands, width), 0)
    token_grad = dot_full(bias_grad, bias_w_ref[...].astype(f32), 1, 1)
    token_grad = jnp.where(row_spot == 0, token_grad[0:1], 0.0)
    grad_states = jnp.concatenate([tail_ref[:bands, :], token_grad], axis=0)
    token_state = states_ref[bands : bands + 8]
    first_row = lax.broadcasted_iota(jnp.int32, token_state.shape, 0) == 0
    bias_out[...] = dot_full(jnp.where(first_row, token_state, 0.0), bias_grad, 0, 0)
    unit_one = rows_ref[5]
    gain_one = gain_ref[0:1].astype(f32)
    gain_two = gain_ref[1:2].astype(f32)
    grad_two, gain_two_grad, _ = norm_back(rows_ref[6], scales_ref[1], gain_two, grad_states)
    pre = pre_ref[...]
    cdf = 0.5 * (1.0 + lax.erf(pre * 0.5**0.5))
    ff_out_out[...] = dot_full(pre * cdf, grad_two, 0, 0)
    slope = cdf + pre * (jnp.exp(-0.5 * pre * pre) * (2.0 * math.pi) ** (-0.5))
    grad_pre = slope * dot_full(grad_two, ff_out_ref[...].astype(f32), 1, 1)
    ff_in_out[...] = dot_full(unit_one * gain_one, grad_pre, 0, 0)
    grad_first = grad_two + dot_full(grad_pre, ff_in_ref[...].astype(f32), 1, 1)
    grad_one, gain_one_grad, _ = norm_back(unit_one, scales_ref[0], gain_one, grad_first)
    gain_out[...] = jnp.concatenate([gain_one_grad, gain_two_grad], axis=0)
    attn_out[3] = dot_full(rows_ref[4], grad_one, 0, 0)
    grad_mixed = dot_full(grad_one, attn_ref[3].astype(f32), 1, 1)
    sequence = rows_ref[0]
    queries = rows_ref[1]
    keys_arr = rows_ref[2]
    values_arr = rows_ref[3]
    grads = [jnp.zeros((padded, width), f32) for _ in range(3)]
    for head in range(GEN_HEADS):
        weights = weights_ref[head]
        own_grad = head_part(grad_mixed, head)
        grad_weights = dot_full(own_grad, values_arr, 1, 1)
        grad_scores = weights * (
            grad_weights - jnp.sum(grad_weights * weights, axis=-1, keepdims=True)
        )
        grad_scores = grad_scores * head_scale
        grads[0] = grads[0] + dot_full(grad_scores, head_part(keys_arr, head))
        grads[1] = grads[1] + dot_full(grad_scores, head_part(queries, head), 0, 0)
        grads[2] = grads[2] + dot_full(weights, own_grad, 0, 0)
    grad_sequence = grad_one
    for which in range(3):
        attn_out[which] = dot_full(sequence, grads[which], 0, 0)
        grad_sequence = grad_sequence + dot_full(
            grads[which], attn_ref[which].astype(f32), 1, 1
        )
    token_out[...] = grad_sequence[bands : bands + 1]


def generate_back(tail, gen_attn, gen_gain, ff_in, ff_out, gen_bias, kept_arrs):
    f32 = jnp.float32
    width = gen_gain.shape[1]
    shapes = [
        (1, width),
        gen_attn.shape,
        gen_gain.shape,
        ff_in.shape,
        ff_out.shape,
        gen_bias.shape,
    ]
    inside = pl.BlockSpec(memory_space=pltpu.VMEM)
    return run_kernel(
        generate_back_body,
        (tail, gen_attn, gen_gain, ff_in, ff_out, gen_bias, *kept_arrs),
        out_shape=[jax.ShapeDtypeStruct(shape, f32) for shape in shapes],
        in_specs=[inside] * (6 + len(kept_arrs)),
        out_specs=[inside] * len(shapes),
    )


def fill_kernel(keys_lists, piece_refs, spot, mat_ref, bands, pixels):
    for keys, piece_ref in zip(keys_lists, piece_refs):
        for number, key in enumerate(keys):
            share = piece_ref.shape[2]
            first = jnp.bitwise_xor(spot, key) * share
            for band in range(bands):
                rows = pl.ds(pl.multiple_of(band * pixels + first, share), share)
                mat_ref[rows, :] = piece_ref[number, band]


def fill_step(keys_lists, piece_refs, spot, mat_ref, band_step, group_steps):
    pixels = mat_ref.shape[0] // band_step
    step = pl.program_id(0)
    used = 0
    for group, keys_list in enumerate(keys_lists):
        group_refs = piece_refs[used : used + len(keys_list)]
        used += len(keys_list)

        @pl.when(step // group_steps == group)
        def _(keys_list=keys_list, group_refs=group_refs):
            fill_kernel(keys_list, group_refs, spot, mat_ref, band_step, pixels)


def embed_body(keys_lists, group_steps, band_step, *refs):
    spot_ref, patch_ref = refs[:2]
    count = sum(len(keys_list) for keys_list in keys_lists)
    piece_refs = refs[2 : 2 + count]
    *out_refs, mat_ref, total_ref = refs[2 + count :]
    step = pl.program_id(0)
    fill_step(keys_lists, piece_refs, spot_ref[0], mat_ref, band_step, group_steps)

    @pl.when(step == 0)
    def _():
        total_ref[...] = jnp.zeros_like(total_ref)

    total_ref[...] += dot_nn(patch_ref[...], mat_ref[...])

    @pl.when(step == pl.num_programs(0) - 1)
    def _():
        for key, out_ref in enumerate(out_refs):
            rows = out_ref.shape[0]
            first = pl.multiple_of(jnp.bitwise_xor(spot_ref[1], key) * rows, rows)
            out_ref[...] = total_ref[pl.ds(first, rows), :].astype(out_ref.dtype)


def group_band_count(kernel_groups):
    return min(block.shape[1] for blocks in kernel_groups for _, block in blocks)


def piece_specs(kernel_groups, band_step, first_group=0):
    group_steps = group_band_count(kernel_groups) // band_step
    specs = []
    arrays = []
    for group, blocks in enumerate(kernel_groups):
        for keys, block in blocks:
            whole = block.shape[1] > group_steps * band_step
            first = group * group_steps
            skip = first_group * group_steps

            def pick(step, first=first, whole=whole):
                here = jnp.clip(step - first, 0, group_steps - 1)
                return (0, here + first + skip if whole else here, 0, 0)

            specs.append(pl.BlockSpec((len(keys), band_step) + block.shape[2:], pick))
            arrays.append(block)
    keys_lists = [[keys for keys, _ in blocks] for blocks in kernel_groups]
    return specs, arrays, keys_lists, group_steps


def embed_share(spots, patch_rows, kernel_groups, owners):
    row_total = patch_rows.shape[0]
    blocks = kernel_groups[0]
    group_bands = group_band_count(kernel_groups)
    width = blocks[0][1].shape[3]
    pixels = sum(len(keys) for keys, _ in blocks) * blocks[0][1].shape[2]
    band_step = min(4, group_bands)
    depth = band_step * pixels
    specs, arrays, keys_lists, group_steps = piece_specs(kernel_groups, band_step)
    rows = row_total // owners
    return run_kernel(
        partial(embed_body, keys_lists, group_steps, band_step),
        [spots, patch_rows, *arrays],
        [
            pl.BlockSpec(memory_space=pltpu.SMEM),
            pl.BlockSpec((row_total, depth), lambda step: (0, step)),
        ]
        + specs,
        grid=(group_steps * len(kernel_groups),),
        out_shape=[jax.ShapeDtypeStruct((rows, width), jnp.bfloat16)] * owners,
        out_specs=[pl.BlockSpec((rows, width), lambda step: (0, 0))] * owners,
        scratch_shapes=[
            pltpu.VMEM((depth, width), jnp.bfloat16),
            pltpu.VMEM((row_total, width), jnp.float32),
        ],
    )


def kernel_grad_body(dp_size, band_step, *refs):
    spot_ref, patch_ref = refs[:2]
    *grad_refs, send_ref, keep_ref, hold_ref = refs[2:]
    rows = grad_refs[0].shape[0]
    total = 0.0
    for key, grad_ref in enumerate(grad_refs):
        first = pl.multiple_of(jnp.bitwise_xor(spot_ref[1], key) * rows, rows)
        total = total + inner(patch_ref[pl.ds(first, rows), :], grad_ref[...])
    hold_ref[...] = total.astype(hold_ref.dtype)
    pixels = hold_ref.shape[0] // band_step
    share = pixels // dp_size
    core = lax.rem(spot_ref[0], 2)
    for band in range(band_step):
        for chip in range(dp_size // 2):
            base = band * pixels + chip * 2 * share
            kept = pl.multiple_of(base + core * share, share)
            keep_ref[band, chip] = hold_ref[pl.ds(kept, share), :]
            sent = pl.multiple_of(base + (1 - core) * share, share)
            send_ref[band, chip] = hold_ref[pl.ds(sent, share), :]


def kernel_grad_part(spots, patch_rows, grads, first_band, group_bands, bands_dev, dp_size, after):
    row_total = patch_rows.shape[0]
    width = grads[0].shape[1]
    band_step = min(4, group_bands)
    pixels = patch_rows.shape[1] // bands_dev
    depth = band_step * pixels
    offset = first_band // band_step
    share = pixels // dp_size
    chips = (dp_size // 2, share, width)
    steps = group_bands // band_step
    block = (band_step,) + chips
    return run_kernel(
        partial(kernel_grad_body, dp_size, band_step),
        (spots, patch_rows, *grads),
        after=after,
        limit=63,
        grid=(steps,),
        out_shape=[
            jax.ShapeDtypeStruct((bands,) + chips, jnp.bfloat16)
            for bands in (group_bands, group_bands)
        ],
        in_specs=[
            pl.BlockSpec(memory_space=pltpu.SMEM),
            pl.BlockSpec((row_total, depth), lambda step: (0, offset + step)),
        ]
        + [pl.BlockSpec(grad.shape, lambda step: (0, 0)) for grad in grads],
        out_specs=[
            pl.BlockSpec(block, lambda step: (step, 0, 0, 0)),
            pl.BlockSpec(block, lambda step: (step, 0, 0, 0)),
        ],
        scratch_shapes=[pltpu.VMEM((depth, width), jnp.bfloat16)],
    )


def patch_grad_body(keys_lists, grad_count, group_steps, band_step, *refs):
    spot_ref = refs[0]
    grad_refs = refs[1 : 1 + grad_count]
    out_ref, mat_ref = refs[-2:]
    piece_refs = refs[1 + grad_count : -2]
    fill_step(keys_lists, piece_refs, spot_ref[0], mat_ref, band_step, group_steps)
    for key, grad_ref in enumerate(grad_refs):
        rows = grad_ref.shape[0]
        first = pl.multiple_of(jnp.bitwise_xor(spot_ref[1], key) * rows, rows)
        out_ref[pl.ds(first, rows), :] = times_transpose(grad_ref[...], mat_ref[...]).astype(
            out_ref.dtype
        )


def patch_grad(spots, grads, kernel_groups, pixels, first_group, after):
    rows, width = grads[0].shape
    row_total = rows * len(grads)
    band_step = min(4, group_band_count(kernel_groups))
    depth = band_step * pixels
    specs, arrays, keys_lists, group_steps = piece_specs(kernel_groups, band_step, first_group)
    steps = group_steps * len(kernel_groups)
    return run_kernel(
        partial(patch_grad_body, keys_lists, len(grads), group_steps, band_step),
        [spots, *grads, *arrays],
        [pl.BlockSpec(memory_space=pltpu.SMEM)]
        + [pl.BlockSpec(grad.shape, lambda step: (0, 0)) for grad in grads]
        + specs,
        after=after,
        limit=63,
        grid=(steps,),
        out_shape=jax.ShapeDtypeStruct((row_total, steps * depth), jnp.bfloat16),
        out_specs=pl.BlockSpec((row_total, depth), lambda step: (0, step)),
        scratch_shapes=[pltpu.VMEM((depth, width), jnp.bfloat16)],
    )


def states_grad_body(batches, low_ref, columns_ref, *refs):
    *piece_refs, sums_ref, spot_ref, grad_ref, part_ref, hold_ref = refs
    pixels, bands, width = piece_refs[0].shape
    for number, piece_ref in enumerate(piece_refs):
        key, batch = divmod(number, batches)
        first = (jnp.bitwise_xor(spot_ref[1], key) * batches + batch) * bands
        hold_ref[:, pl.ds(pl.multiple_of(first, bands), bands), :] = piece_ref[...]
    total = 0.0
    for pixel in range(pixels):
        cols = slice(pixel * width, (pixel + 1) * width)
        grads = hold_ref[pixel]
        grad_ref[:, cols] = inner(low_ref[...], grads)
        total = total + times_transpose(grads, columns_ref[:, cols])
    bands, states = total.shape
    part_ref[:bands, :] = total
    rows = [sums_ref[0:1, spot : spot + states] for spot in range(0, width, states)]
    rows.append(jnp.zeros((part_ref.shape[0] - bands - len(rows), states), jnp.float32))
    part_ref[bands:, :] = jnp.concatenate(rows, axis=0)


def states_grad(spots, low, columns, pieces, sums):
    pixels, bands, width = pieces[0].shape
    tail_rows = low.shape[0] + -(-width // low.shape[1] // 8) * 8
    if bands % 16:
        blocks = [([key], piece[None]) for key, piece in enumerate(pieces)]
        whole = place(blocks, "band", 1).reshape(pixels, -1, width)
        grads = whole.transpose(1, 0, 2).reshape(low.shape[0], -1)
        rows = [times_transpose(grads, columns), sums[0].reshape(-1, low.shape[1])]
        tail = jnp.concatenate(rows, axis=0)
        tail = jnp.pad(tail, ((0, tail_rows - tail.shape[0]), (0, 0)))
        return inner(low, grads), tail
    inside = pl.BlockSpec(memory_space=pltpu.VMEM)
    return run_kernel(
        partial(states_grad_body, 1),
        (low, columns, *pieces, sums, spots),
        out_shape=[
            jax.ShapeDtypeStruct(columns.shape, jnp.float32),
            jax.ShapeDtypeStruct((tail_rows, low.shape[1]), jnp.float32),
        ],
        in_specs=[inside] * (3 + len(pieces)) + [pl.BlockSpec(memory_space=pltpu.SMEM)],
        out_specs=[inside, inside],
        scratch_shapes=[pltpu.VMEM((pixels, bands * len(pieces), width), jnp.bfloat16)],
    )


def flatten_body(in_ref, out_ref):
    out_ref[...] = in_ref[...].reshape(out_ref.shape)


def unflatten_body(*refs):
    *in_refs, out_ref = refs
    done = 0
    for in_ref in in_refs:
        part = in_ref[...]
        bands = part.shape[1] // out_ref.shape[2]
        out_ref[:, done : done + bands, :] = part.reshape(-1, bands, out_ref.shape[2])
        done += bands


def flatten_rows(cube, after):
    rows, bands, pixels = cube.shape
    step_rows = 64
    return run_kernel(
        flatten_body,
        (cube,),
        [pl.BlockSpec((step_rows, bands, pixels), lambda step: (step, 0, 0))],
        after=after,
        grid=(rows // step_rows,),
        out_shape=jax.ShapeDtypeStruct((rows, bands * pixels), cube.dtype),
        out_specs=pl.BlockSpec((step_rows, bands * pixels), lambda step: (step, 0)),
    )


def unflatten_rows(flats, bands, after):
    rows = flats[0].shape[0]
    pixels = sum(flat.shape[1] for flat in flats) // bands
    step_rows = 64
    return run_kernel(
        unflatten_body,
        flats,
        [pl.BlockSpec((step_rows, flat.shape[1]), lambda step: (step, 0)) for flat in flats],
        after=after,
        limit=63,
        grid=(rows // step_rows,),
        out_shape=jax.ShapeDtypeStruct((rows, bands, pixels), flats[0].dtype),
        out_specs=pl.BlockSpec((step_rows, bands, pixels), lambda step: (step, 0, 0)),
    )


def stack_body(*refs):
    *part_refs, out_ref, hold_ref = refs
    width = out_ref.shape[1]
    first = 0
    for part_ref in part_refs:
        rows = part_ref.shape[0]
        for spot in range(0, part_ref.shape[1], width):
            hold_ref[pl.ds(first, rows), :] = part_ref[:, spot : spot + width].astype(jnp.float32)
            first += rows
    out_ref[...] = hold_ref[...].astype(out_ref.dtype)


def stack_weights(shards_in):
    width = shards_in[-1].shape[1]
    if any(shard.shape[0] % 8 for shard in shards_in):
        return jnp.concatenate(
            [part for shard in shards_in for part in column_blocks(shard, width)], axis=0
        )
    row_total = sum(shard.size for shard in shards_in) // width
    inside = pl.BlockSpec(memory_space=pltpu.VMEM)
    return run_kernel(
        stack_body,
        shards_in,
        [inside] * len(shards_in),
        out_shape=jax.ShapeDtypeStruct((row_total, width), shards_in[0].dtype),
        out_specs=inside,
        scratch_shapes=[pltpu.VMEM((row_total, width), jnp.float32)],
    )


def plane_body(block_rows, spot_ref, *refs):
    *stack_refs, first_ref, last_ref, hold_ref = refs
    band_size = len(stack_refs)
    for key, stack_ref in enumerate(stack_refs):
        owner = jnp.bitwise_xor(spot_ref[1], key)
        values = stack_ref[...].astype(jnp.float32)
        done = 0
        for rows in block_rows:
            at = pl.multiple_of(done * band_size + owner * rows, 8)
            hold_ref[pl.ds(at, rows), :] = values[done : done + rows]
            done += rows
    half = first_ref.shape[0]
    first_ref[...] = hold_ref[:half, :].astype(first_ref.dtype)
    last_ref[...] = hold_ref[half:, :].astype(last_ref.dtype)


def plane_weights(spots, stacks, block_rows):
    row_total, width = stacks[0].shape
    band_size = len(stacks)
    half = row_total * band_size // 2
    if any(rows % 8 for rows in block_rows):
        whole = place([([key], stack[None]) for key, stack in enumerate(stacks)], "band", 0)
        parts = []
        done = 0
        for rows in block_rows:
            parts.append(whole[:, done : done + rows].reshape(-1, width))
            done += rows
        merged = jnp.concatenate(parts, axis=0)
        return merged[:half], merged[half:]
    inside = pl.BlockSpec(memory_space=pltpu.VMEM)
    return run_kernel(
        partial(plane_body, block_rows),
        (spots, *stacks),
        [pl.BlockSpec(memory_space=pltpu.SMEM)] + [inside] * band_size,
        out_shape=[jax.ShapeDtypeStruct((half, width), stacks[0].dtype)] * 2,
        out_specs=[inside] * 2,
        scratch_shapes=[pltpu.VMEM((row_total * band_size, width), jnp.float32)],
    )


def weight_grad_body(dp_size, parts, hidden, spot_ref, own_ref, other_ref, *refs):
    *out_refs, turned_ref, hold_ref, feed_ref, small_ref, sems = refs
    width = hold_ref.shape[2]
    row_total = own_ref.shape[0]
    spans = stash_spans(width, hidden)
    share = width // dp_size
    chips = dp_size // 2
    core = lax.rem(spot_ref[0], 2)
    copies = []

    def view(name, column=0, size=None):
        first, whole = spans[name]
        first = first + column * width
        return [ref[:, first : first + (size or whole)] for ref in (own_ref, other_ref)]

    def turn_rows(name, at):
        first, size = spans[name]
        for spot in range(0, size, width):
            for number, ref in enumerate((own_ref, other_ref)):
                cols = slice(number * row_total, (number + 1) * row_total)
                turned = ref[:, first + spot : first + spot + width].T
                turned_ref[at + spot : at + spot + width, cols] = turned

    def pick(at, rows):
        parts = []
        for chip in range(chips):
            first = at + (chip * 2 + core) * rows
            parts.append(turned_ref[pl.ds(pl.multiple_of(first, 16), rows), :])
        return jnp.concatenate(parts, axis=0)

    def send(source_ref, rows, number, stride=None):
        part = [number in numbers for _, numbers in parts].index(True)
        first_step, numbers = parts[part]
        first = share * numbers.index(number)
        step = first_step // 2
        bit = lax.rem(lax.div(spot_ref[0], first_step), 2)
        for index in range(chips // 2):
            for which in range(2):
                own_bit = bit if which == 0 else 1 - bit
                chip = index // step * 2 * step + own_bit * step + index % step
                at = chip * (stride or rows)
                copy = pltpu.make_async_copy(
                    source_ref.at[pl.ds(pl.multiple_of(at, 16), rows), :],
                    out_refs[part * 2 + which].at[index, pl.ds(first, rows), :],
                    sems.at[len(copies)],
                )
                copy.start()
                copies.append(copy)

    def product(left, names, column):
        right = view(names, column, width)
        total = dot_nn(left[:, :row_total], right[0])
        return total + dot_nn(left[:, row_total:], right[1])

    blocks = (
        [("normed", "qkv_grad", column) for column in range(3)]
        + [("mixed", "branch", 0)]
        + [("normed_two", "pre_grad", column) for column in range(hidden // width)]
    )
    turned_at = {"normed": 0, "mixed": width, "normed_two": 2 * width, "act": 3 * width}
    picked = {}
    for number, (left, right, column) in enumerate(blocks):
        if left not in picked:
            turn_rows(left, turned_at[left])
            picked = {left: pick(turned_at[left], share)}
        hold_ref[number] = product(picked[left], right, column).astype(hold_ref.dtype)
        send(hold_ref.at[number], share, number)
    small = sum(part.astype(jnp.float32) for part in view("small"))
    small_ref[...] = small.astype(small_ref.dtype)
    small_share = row_total // dp_size
    turn_rows("act", turned_at["act"])
    feed_rows = hidden // dp_size
    for chip in range(chips):
        at = turned_at["act"] + (chip * 2 + core) * feed_rows
        left = turned_ref[pl.ds(pl.multiple_of(at, 16), feed_rows), :]
        feed_ref[chip * feed_rows : (chip + 1) * feed_rows, :] = product(left, "cot", 0).astype(
            feed_ref.dtype
        )
    send(feed_ref, feed_rows, len(blocks))
    own_small = small_ref.at[pl.ds(pl.multiple_of(core * small_share, 16), (dp_size - 1) * small_share), :]
    send(own_small, small_share, len(blocks) + 1, 2 * small_share)
    for copy in copies:
        copy.wait()


def weight_grad(spots, dp_size, parts, hidden, own, other):
    row_total, columns = own.shape
    width = (columns - 2 * hidden) // 9
    bf16 = jnp.bfloat16
    blocks = 4 + hidden // width
    chips = dp_size // 2
    share = width // dp_size
    block_rows = [share] * blocks + [hidden // dp_size, row_total // dp_size]
    rows = [sum(block_rows[number] for number in numbers) for _, numbers in parts]
    inside = pl.BlockSpec(memory_space=pltpu.VMEM)
    outside = pl.BlockSpec(memory_space=pl.ANY)
    return run_kernel(
        partial(weight_grad_body, dp_size, parts, hidden),
        (spots, own, other),
        [pl.BlockSpec(memory_space=pltpu.SMEM), inside, inside],
        limit=63,
        out_shape=[
            jax.ShapeDtypeStruct((chips // 2, part_rows, width), bf16)
            for part_rows in rows
            for _ in range(2)
        ],
        out_specs=[outside] * (2 * len(parts)),
        scratch_shapes=[
            pltpu.VMEM((3 * width + hidden, 2 * row_total), bf16),
            pltpu.VMEM((blocks, chips * share, width), bf16),
            pltpu.VMEM((hidden // 2, width), bf16),
            pltpu.VMEM((row_total, width), bf16),
            pltpu.SemaphoreType.DMA(((blocks + 2) * chips,)),
        ],
    )


def add_split_body(step, part_steps, spot_ref, keep_ref, *refs):
    *got_refs, send_ref, held_ref = refs
    bit = lax.rem(lax.div(spot_ref[0], step), 2)
    for number, got_ref in enumerate(got_refs):

        @pl.when(pl.program_id(0) // part_steps == number)
        def _(got_ref=got_ref):
            for out_ref, which in ((send_ref, 1 - bit), (held_ref, bit)):
                values = keep_ref[:, which].astype(jnp.float32)
                values = values + got_ref[:, which].astype(jnp.float32)
                out_ref[...] = values.astype(out_ref.dtype)


def add_split(spots, keep, gots, at, step, left):
    left = sorted(left, reverse=True)
    place_of = left.index(step)
    shape = keep.shape
    width = shape[-1]
    outer = math.prod(shape[:at]) * 2**place_of
    part_outer = outer // len(gots)
    inner_rows = keep.size // (outer * 2 * width)
    rows_step = inner_rows
    while rows_step > 512 and rows_step % 32 == 0:
        rows_step //= 2
    outer_step = 1
    while part_outer % (2 * outer_step) == 0 and 2 * outer_step * rows_step <= 512:
        outer_step *= 2
    part_steps = part_outer // outer_step
    block_in = (outer_step, 2, rows_step, width)
    block_out = pl.BlockSpec((outer_step, rows_step, width), lambda first, rows: (first, rows, 0))

    def part_spec(number):
        def pick(first, rows):
            return (jnp.clip(first - number * part_steps, 0, part_steps - 1), 0, rows, 0)

        return pl.BlockSpec(block_in, pick)

    outs = run_kernel(
        partial(add_split_body, step, part_steps),
        (spots, keep.reshape((outer, 2, inner_rows, width)))
        + tuple(got.reshape((part_outer, 2, inner_rows, width)) for got in gots),
        [
            pl.BlockSpec(memory_space=pltpu.SMEM),
            pl.BlockSpec(block_in, lambda first, rows: (first, 0, rows, 0)),
        ]
        + [part_spec(number) for number in range(len(gots))],
        limit=63,
        grid=(outer // outer_step, inner_rows // rows_step),
        out_shape=[jax.ShapeDtypeStruct((outer, inner_rows, width), keep.dtype)] * 2,
        out_specs=[block_out] * 2,
    )
    rest = shape[:at] + (-1,) + shape[at + 1 :]
    return outs[0].reshape(rest), outs[1].reshape(rest)


def owners_body(groups, spot_ref, *refs):
    keep_refs = refs[:groups]
    got_refs = refs[groups : 2 * groups]
    *out_refs, hold_ref = refs[2 * groups :]
    pixels = out_refs[0].shape[0]
    for group, (keep_ref, got_ref) in enumerate(zip(keep_refs, got_refs)):
        bands = keep_ref.shape[0]
        hold_ref[...] = keep_ref[...].astype(jnp.float32) + got_ref[...].astype(jnp.float32)
        for key, out_ref in enumerate(out_refs):
            first = pl.multiple_of(jnp.bitwise_xor(spot_ref[1], key) * pixels, pixels)
            part = hold_ref[:, pl.ds(first, pixels), :]
            out_ref[:, group * bands : (group + 1) * bands, :] = jnp.swapaxes(part, 0, 1).astype(
                out_ref.dtype
            )


def by_owner(spots, keeps, gots, band_size):
    bands, share, width = keeps[0].shape
    pixels = share // band_size
    if pixels % 8:
        whole = jnp.concatenate([add_low(keep, got) for keep, got in zip(keeps, gots)], axis=0)
        whole = whole.reshape(-1, band_size, pixels, width).transpose(1, 2, 0, 3)
        return [
            lax.dynamic_index_in_dim(whole, spots[1] ^ key, 0, keepdims=False)
            for key in range(band_size)
        ]
    inside = pl.BlockSpec(memory_space=pltpu.VMEM)
    return run_kernel(
        partial(owners_body, len(keeps)),
        (spots, *keeps, *gots),
        [pl.BlockSpec(memory_space=pltpu.SMEM)] + [inside] * (2 * len(keeps)),
        limit=63,
        out_shape=[
            jax.ShapeDtypeStruct((pixels, bands * len(keeps), width), keeps[0].dtype)
        ]
        * band_size,
        out_specs=[inside] * band_size,
        scratch_shapes=[pltpu.VMEM((bands, share, width), jnp.float32)],
    )


def shards(
    patches,
    bias_token,
    gen_attn,
    gen_gain,
    gen_ff_in,
    gen_ff_out,
    gen_kernel,
    gen_bias,
    pos_table,
    norm_gain,
    norm_bias,
    w_qkv,
    w_out,
    w_fc1,
    bias_in,
    w_fc2,
    wavelengths,
    kept,
    counts,
    cotangent,
):
    group_size, slot_count, bands_dev, pixel_count = patches.shape
    dp_size = lax.axis_size("dp")
    band_size = lax.axis_size("band")
    device_count = dp_size * band_size
    local_images = group_size // band_size
    model_width = w_out.shape[1]
    row_total = local_images * slot_count
    own_pixels = pixel_count // device_count
    share = own_pixels * band_size
    groups = 2
    group_bands = bands_dev // groups
    f32 = jnp.float32
    bf16 = jnp.bfloat16
    spot = lax.axis_index("band")
    spots = jnp.stack([lax.axis_index("dp"), spot]).astype(jnp.int32)

    own_kernel, embed_bias, band_states, *gen_kept = generate_fast(
        wavelengths,
        bias_token,
        gen_attn,
        gen_gain,
        gen_ff_in,
        gen_ff_out,
        gen_bias,
        gen_kernel,
    )
    hidden = w_fc1.shape[1]
    weight_rows = [w_qkv.shape[0]] * (4 + hidden // model_width) + [w_fc2.shape[0]]
    stack = stack_weights((w_qkv, w_out, w_fc1, w_fc2))
    patch_rows = flatten_rows(
        patches.reshape(group_size * slot_count, bands_dev, pixel_count), (own_kernel,)
    )
    own_kernel = own_kernel.reshape(own_pixels, band_size, bands_dev, model_width)
    other_bands = range(1, band_size)
    dp_steps = bit_steps(dp_size)[1:]
    orders = [turn(dp_steps, group) for group in range(groups)]

    sent = [
        lax.dynamic_index_in_dim(own_kernel, spot ^ key, 1, keepdims=False).transpose(1, 0, 2)
        for key in range(band_size)
    ]
    got = [swap(sent[key], "band", key) for key in other_bands]
    *got, patch_rows, stack = together(*got, patch_rows, stack)
    piece = place(
        [([key], block[None]) for key, block in enumerate([sent[0]] + got)], "band", 1
    ).reshape(bands_dev, share, model_width)

    own_pieces = [piece[group * group_bands : (group + 1) * group_bands] for group in range(groups)]
    held = [own_piece[None] for own_piece in own_pieces]
    held_keys = [[0] for _ in range(groups)]
    kernel_groups = [[([0], piece[None])] for _ in range(groups)]
    waiting = []
    stacks = {0: stack}
    stack_keys = [band_size // 2] + [key for key in other_bands if key != band_size // 2]
    for stage in range(len(dp_steps)):
        last = stage == len(dp_steps) - 1
        now_keys = stack_keys if last else stack_keys[:1]
        stack_keys = stack_keys[len(now_keys) :]
        got = [swap(held[group], "dp", orders[group][stage]) for group in range(groups)]
        if stage == 0:
            core_got = swap(piece, "dp", 1)
        elif waiting:
            core_got = swap(waiting[0][2], "dp", 1)
        stack_got = [swap(stack, "band", key) for key in now_keys]
        got[0], got[1], core_got, stack, *stack_got = together(*got, core_got, stack, *stack_got)
        stacks.update(zip(now_keys, stack_got))
        if stage == 0:
            for blocks in kernel_groups:
                blocks.append(([1], core_got[None]))
        elif waiting:
            group, keys, _ = waiting.pop(0)
            kernel_groups[group].append(([key ^ 1 for key in keys], core_got))
        for group in range(groups):
            keys = [key ^ orders[group][stage] for key in held_keys[group]]
            kernel_groups[group].append((keys, got[group]))
            waiting.append((group, keys, got[group]))
            if not last:
                held[group] = jnp.concatenate([held[group], got[group]], axis=0)
                held_keys[group] = held_keys[group] + keys
    for group, keys, last_got in waiting:
        kernel_groups[group].append(([key ^ 1 for key in keys], swap(last_got, "dp", 1)))

    planes = plane_weights(spots, [stacks[key] for key in range(band_size)], weight_rows)
    got = [swap(plane, "dp", orders[half][0]) for half, plane in enumerate(planes)]
    embedded = embed_share(spots, patch_rows, kernel_groups, band_size)
    *embedded, first_got, last_got = together(*embedded, *got)
    held = [
        jnp.concatenate([plane[None], got[None]], axis=0)
        for plane, got in zip(planes, (first_got, last_got))
    ]
    held_keys = [[0, orders[half][0]] for half in range(2)]
    for stage in range(1, len(dp_steps) - 1):
        for half in range(2):
            step = orders[half][stage]
            held[half] = jnp.concatenate([held[half], swap(held[half], "dp", step)], axis=0)
            held_keys[half] = held_keys[half] + [key ^ step for key in held_keys[half]]
    got = [swap(held[half], "dp", orders[half][-1]) for half in range(2)]
    parts = [embedded[0]] + [swap(embedded[key], "band", key) for key in other_bands]
    held[0], held[1], got[0], got[1], *parts = together(*held, *got, *parts)
    weight_halves = []
    for half in range(2):
        blocks = [(held_keys[half], held[half])]
        blocks.append(([key ^ orders[half][-1] for key in held_keys[half]], got[half]))
        weight_halves.append(blocks + gather_core(blocks))

    valid_mask = jnp.arange(slot_count)[None, :] < counts[:, None]
    keep_col = valid_mask.reshape(row_total, 1)
    kept_flat = kept.reshape(row_total)
    pos_rows = jnp.take(pos_table, kept_flat, axis=0).astype(f32)
    base = embed_bias[0:1] + pos_rows
    tile_images = 2 if local_images % 2 == 0 else 1
    tile_rows = tile_images * slot_count
    image_spot = jnp.arange(tile_rows) // slot_count
    same_image = image_spot[:, None] == image_spot[None, :]
    mask = jnp.where(same_image[None] & valid_mask.reshape(-1, 1, tile_rows), 0.0, -1e30)
    cot = jnp.where(keep_col, cotangent.reshape(row_total, model_width), 0)
    (
        result,
        grad_embed,
        stash,
        sums,
    ) = block(
        parts,
        weight_halves,
        spots,
        base,
        cot,
        keep_col.astype(f32),
        mask.astype(f32),
        norm_gain.astype(f32),
        norm_bias.astype(f32),
        bias_in.astype(f32)[None],
        kept_flat[None],
    )

    small_share = row_total // device_count
    block_rows = weight_rows + [small_share]
    part_blocks = [[0, 9], [1], [2], [3], [4, 5, 6, 7], [8]]
    part_orders = [orders[0], orders[1], orders[1], orders[0], orders[0], orders[1]]
    weight_parts = [(order[0], numbers) for order, numbers in zip(part_orders, part_blocks)]
    grads = [grad_embed] + [swap(grad_embed, "band", key) for key in other_bands]
    weight_split = weight_grad(
        spots, dp_size, weight_parts, hidden, stash, swap(stash, "dp", 1)
    )
    mixed = together(*grads, *weight_split)
    grads, weight_split = list(mixed[:band_size]), mixed[band_size:]
    weight_keep, weight_send = list(weight_split[0::2]), list(weight_split[1::2])

    weight_got = [swap(weight_send[part], "dp", part_orders[part][0]) for part in range(2)]
    kernel_split = []
    for group in range(groups):
        *sends, keep = kernel_grad_part(
            spots,
            patch_rows,
            grads,
            group * group_bands,
            group_bands,
            bands_dev,
            dp_size,
            (),
        )
        core_got = [swap(send, "dp", 1) for send in sends]
        kernel_split += add_split(spots, keep, core_got, 1, orders[group][0], dp_steps)
    weight_got[0], weight_got[1], *kernel_split = together(*weight_got, *kernel_split)

    def cut_blocks(values, numbers):
        lead = values.shape[0]
        cuts = []
        first = 0
        for number in numbers:
            rows = block_rows[number]
            cut = values[:, first : first + rows * band_size]
            cuts.append(cut.reshape(lead, band_size, rows, model_width))
            first += rows * band_size
        return jnp.concatenate(cuts, axis=2)

    def over_band(by_band):
        sent = [
            lax.dynamic_index_in_dim(by_band, spot ^ key, 1, keepdims=False)
            for key in range(band_size)
        ]
        return [sent[0]] + [swap(sent[key], "band", key) for key in other_bands]

    def total(blocks):
        return sum(block_sum.astype(f32) for block_sum in blocks)

    def over_chips(sums):
        cut = [
            values if isinstance(values, tuple) else split_half(values, 0, order[0], order)
            for values, order in sums
        ]
        got = [None] * len(sums)
        for step in sorted({order[0] for _, order in sums}):
            here = [number for number, (_, order) in enumerate(sums) if order[0] == step]
            flat = [cut[number][0].reshape(-1, model_width) for number in here]
            moved = swap(jnp.concatenate(flat, axis=0) if len(flat) > 1 else flat[0], "dp", step)
            first = 0
            for number, rows in zip(here, flat):
                part = moved[first : first + rows.shape[0]]
                got[number] = part.reshape(cut[number][0].shape)
                first += rows.shape[0]
        return [
            (add_low(cut[number][1], got[number]), order[1:])
            for number, (_, order) in enumerate(sums)
        ]

    update = patch_grad(spots, grads, kernel_groups, pixel_count, 0, ())
    for stage in range(len(dp_steps)):
        last = stage == len(dp_steps) - 1
        got = [swap(kernel_split[2 * group], "dp", orders[group][stage]) for group in range(groups)]
        part = 2 + stage
        cuts = [
            cut_blocks(weight_keep[part], part_blocks[part]),
            cut_blocks(weight_send[part], part_blocks[part]),
        ]
        if stage == 0:
            cuts += [
                cut_blocks(add_low(weight_keep[early], weight_got[early]), part_blocks[early])
                for early in range(2)
            ]
        part_got = [None]
        if stage < 2:
            part_got = over_band(jnp.concatenate(cuts, axis=2))
        if stage == 0:
            got[0], got[1], update, *part_got = together(*got, update, *part_got)
        else:
            got[0], got[1], *part_got = together(*got, *part_got)
        if stage < 2:
            summed = total(part_got).astype(bf16)
            rows = [cut.shape[2] for cut in cuts]
            spots_in = [sum(rows[:number]) for number in range(len(rows))]
            summed = [summed[:, first : first + size] for first, size in zip(spots_in, rows)]
            weight_keep[part], weight_send[part] = summed[:2]
            if stage == 0:
                early = summed[2:]
        if not last:
            kernel_split = [
                part
                for group in range(groups)
                for part in add_split(
                    spots,
                    kernel_split[2 * group + 1],
                    [got[group]],
                    1,
                    orders[group][stage + 1],
                    orders[group][stage + 1 :],
                )
            ]
    sent = by_owner(
        spots,
        [
            kernel_split[2 * group + 1].reshape(group_bands, share, model_width)
            for group in range(groups)
        ],
        [got[group].reshape(group_bands, share, model_width) for group in range(groups)],
        band_size,
    )
    pieces = [sent[0]] + [swap(sent[key], "band", key) for key in other_bands]
    sums_left = over_chips(
        [(early[part], part_orders[part][1:]) for part in range(2)]
        + [
            ((weight_send[part], weight_keep[part]), part_orders[part])
            for part in range(2, len(part_blocks))
        ]
    )
    while any(order for _, order in sums_left[:2]):
        moved = over_chips([one for one in sums_left[:2] if one[1]])
        sums_left[:2] = [moved.pop(0) if one[1] else one for one in sums_left[:2]]
    weight_sums = [values for values, _ in sums_left]
    grad_patches = unflatten_rows([update], bands_dev, (sent[0],))
    mixed = together(*weight_sums, grad_patches, *pieces)
    count = len(part_blocks)
    weight_sums, grad_patches, pieces = list(mixed[:count]), mixed[count], mixed[count + 1 :]
    grad_gen_kernel, tail = states_grad(spots, band_states, gen_kernel, pieces, sums)
    mixed = together(*weight_sums, tail)
    weight_sums, tail = list(mixed[:-1]), mixed[-1]

    small = weight_sums[0][:, -small_share:]
    late = [(weight_sums[part], part_orders[part][1:]) for part in range(2, count)]
    small_steps = [("band", step) for step in bit_steps(band_size)]
    small_steps += [("dp", step) for step in turn(bit_steps(dp_size), 1)]

    def widen(values, number):
        return jnp.concatenate([values, swap(values, *small_steps[number])], axis=0)

    while any(order for _, order in late):
        late = over_chips(late)
    late = [values for values, _ in late]
    tail = total([tail] + [swap(tail, "band", key) for key in other_bands])
    tail_steps = bit_steps(dp_size)
    tail = tail + swap(tail, "dp", tail_steps[0])
    tail, *late = together(tail, *late)
    cuts = [cut_blocks(late[part - 2], part_blocks[part]) for part in range(4, count)]
    last_sum = total(over_band(jnp.concatenate(cuts, axis=2)))
    small = widen(small, 0)
    for number, step in enumerate(tail_steps[1:]):
        got = swap(tail, "dp", step)
        small = widen(small, number + 1)
        got, small = together(got, small)
        tail = tail + got
    for number in range(len(tail_steps), len(small_steps)):
        small = widen(small, number)
    own_grads = jnp.concatenate(
        [
            weight_sums[0][0, :-small_share].astype(f32),
            weight_sums[1][0].astype(f32),
            late[0][0].astype(f32),
            late[1][0].astype(f32),
            last_sum[0],
        ],
        axis=0,
    )
    small_order = (jnp.arange(dp_size) ^ spots[0])[:, None] * band_size
    small_order = (small_order + (jnp.arange(band_size) ^ spots[1])[None, :]).reshape(-1)
    small = small.reshape(2, dp_size // 2, band_size, small_share, model_width)
    small = small.transpose(1, 0, 2, 3, 4).reshape(-1, small_share, model_width)
    small = jnp.take(small, small_order, axis=0).reshape(row_total, model_width)
    own_blocks = []
    done = 0
    for rows in weight_rows:
        own_blocks.append(own_grads[done : done + rows])
        done += rows
    grad_qkv_own = jnp.concatenate(own_blocks[:3], axis=1)
    grad_out_own = own_blocks[3]
    grad_fc_in_own = jnp.concatenate(own_blocks[4:-1], axis=1)
    grad_fc_out_own = own_blocks[-1]
    grad_token, grad_attn, grad_gain_gen, grad_ff_first, grad_ff_second, grad_gen_bias = (
        generate_back(
            tail,
            gen_attn,
            gen_gain,
            gen_ff_in,
            gen_ff_out,
            gen_bias,
            gen_kept,
        )
    )

    small = small.astype(f32)
    sums_at = small.shape[0] - 16
    grad_pos_all = small[: pos_table.shape[0]]
    grad_gains = small[sums_at + 1 : sums_at + 3]
    grad_shifts = small[sums_at + 3 : sums_at + 5]
    grad_bias_all = small[sums_at + 8 : sums_at + 8 + hidden // model_width].reshape(-1)
    grad_patches = grad_patches.reshape(group_size, slot_count, bands_dev, pixel_count)
    return (
        result.reshape(local_images, slot_count, model_width),
        grad_patches,
        grad_token[0],
        grad_attn,
        grad_gain_gen,
        grad_ff_first,
        grad_ff_second,
        grad_gen_kernel,
        grad_gen_bias,
        grad_pos_all,
        grad_gains,
        grad_shifts,
        grad_qkv_own,
        grad_out_own,
        grad_fc_in_own,
        grad_bias_all,
        grad_fc_out_own,
    )


def solution(mesh):
    placed = (
        P("dp", None, "band", None),
        P(),
        P(),
        P(),
        P(),
        P(),
        P(None, ("dp", "band")),
        P(),
        P(),
        P(),
        P(),
        P(("dp", "band"), None),
        P(("dp", "band"), None),
        P(("dp", "band"), None),
        P(),
        P(("dp", "band"), None),
        P(),
        P(("dp", "band"), None),
        P(("dp", "band")),
        P(("dp", "band"), None, None),
    )
    return jax.shard_map(
        shards,
        mesh=mesh,
        in_specs=placed,
        out_specs=(
            P(("dp", "band"), None, None),
            P("dp", None, "band", None),
            P(),
            P(),
            P(),
            P(),
            P(),
            P(None, ("dp", "band")),
            P(),
            P(),
            P(),
            P(),
            P(("dp", "band"), None),
            P(("dp", "band"), None),
            P(("dp", "band"), None),
            P(),
            P(("dp", "band"), None),
        ),
        check_vma=False,
    )
```

```python
from functools import partial
import math

import jax
import jax.numpy as jnp
from jax import lax
from jax.experimental import pallas as pl
from jax.experimental.pallas import tpu as pltpu
from jax.sharding import PartitionSpec as P

HEADS = 12
HDIM = 64
GEN_HEADS = 4


def inner(left_arr, right_arr):
    return lax.dot_general(
        left_arr, right_arr, (((0,), (0,)), ((), ())), preferred_element_type=jnp.float32
    )


def times_transpose(left_arr, right_arr):
    return lax.dot_general(
        left_arr, right_arr, (((1,), (1,)), ((), ())), preferred_element_type=jnp.float32
    )


def bit_steps(size):
    steps = []
    step = 1
    while step < size:
        steps.append(step)
        step *= 2
    return steps


def swap(values, axis, step):
    size = lax.axis_size(axis)
    return lax.ppermute(values, axis, [(spot, spot ^ step) for spot in range(size)])


def turn(items, by):
    by = by % max(len(items), 1)
    return items[by:] + items[:by]


def gather_core(blocks):
    return [([key ^ 1 for key in keys], swap(block, "dp", 1)) for keys, block in blocks]


def place(blocks, axis, at):
    spot = lax.axis_index(axis)
    first = blocks[0][1]
    count = sum(len(keys) for keys, _ in blocks)
    shape = first.shape[1 : at + 1] + (count,) + first.shape[at + 1 :]
    whole = jnp.zeros(shape, first.dtype)
    for keys, block in blocks:
        for number, key in enumerate(keys):
            whole = lax.dynamic_update_index_in_dim(whole, block[number], spot ^ key, at)
    return whole


def add_low(left_arr, right_arr):
    return (left_arr.astype(jnp.float32) + right_arr.astype(jnp.float32)).astype(left_arr.dtype)


def split_half(values, at, step, left):
    left = sorted(left, reverse=True)
    shape = values.shape
    values = values.reshape(shape[:at] + (2,) * len(left) + shape[at + 1 :])
    dim = at + left.index(step)
    bit = (lax.axis_index("dp") // step) % 2
    rest = shape[:at] + (-1,) + shape[at + 1 :]
    send = lax.dynamic_index_in_dim(values, 1 - bit, dim, keepdims=False)
    keep = lax.dynamic_index_in_dim(values, bit, dim, keepdims=False)
    return send.reshape(rest), keep.reshape(rest)


def together(*arrays):
    return lax.optimization_barrier(arrays)


def column_blocks(matrix, width):
    return [matrix[:, spot : spot + width] for spot in range(0, matrix.shape[1], width)]


def run_kernel(body, args, in_specs, after=(), limit=60, **options):
    count = len(after)

    def whole(*refs):
        body(*refs[count:])

    return pl.pallas_call(
        whole,
        in_specs=[pl.BlockSpec(memory_space=pl.ANY)] * count + in_specs,
        compiler_params=pltpu.CompilerParams(vmem_limit_bytes=limit * 1024 * 1024),
        cost_estimate=pl.CostEstimate(flops=1000, bytes_accessed=1000, transcendentals=0),
        **options,
    )(*after, *args)


def dot_nn(left_arr, right_arr):
    return lax.dot_general(
        left_arr, right_arr, (((1,), (0,)), ((), ())), preferred_element_type=jnp.float32
    )


def norm_stats(values):
    center = values - jnp.mean(values, axis=-1, keepdims=True)
    spread = jnp.mean(center * center, axis=-1, keepdims=True)
    scale = lax.rsqrt(spread + 1e-06)
    return center * scale, scale


def norm_back(unit, scale, gain, grad):
    weighted = grad * gain
    first = jnp.mean(weighted, axis=-1, keepdims=True)
    second = jnp.mean(weighted * unit, axis=-1, keepdims=True)
    grad_values = (weighted - first - unit * second) * scale
    grad_gain = jnp.sum(grad * unit, axis=0, keepdims=True)
    grad_shift = jnp.sum(grad, axis=0, keepdims=True)
    return grad_values, grad_gain, grad_shift


def stash_spans(width, hidden):
    sizes = {
        "normed": width,
        "mixed": width,
        "normed_two": width,
        "act": hidden,
        "qkv_grad": 3 * width,
        "branch": width,
        "pre_grad": hidden,
        "cot": width,
        "small": width,
    }
    spans = {}
    first = 0
    for name, size in sizes.items():
        spans[name] = (first, size)
        first += size
    return spans


def block_body(part_count, tile_rows, ff_step, keys_lists, *refs):
    part_refs = refs[:part_count]
    weight_count = sum(len(keys_list) for keys_list in keys_lists)
    weight_refs = refs[part_count : part_count + weight_count]
    (
        spot_ref,
        base_ref,
        cot_ref,
        keep_ref,
        mask_ref,
        gain_ref,
        shift_ref,
        bias_ref,
        kept_ref,
        result_ref,
        embed_grad_ref,
        stash_hbm,
        sums_ref,
        qkv_w,
        out_w,
        fc_in_w,
        fc_out_w,
        qkv_ref,
        probs_ref,
        total_ref,
        back_ref,
        mixed_grad_ref,
        bias_grad_ref,
        stash_ref,
        sems,
        stash_sems,
    ) = refs[part_count + weight_count :]
    bf16 = jnp.bfloat16
    f32 = jnp.float32
    width = base_ref.shape[1]
    hidden = fc_in_w.shape[1]
    spans = stash_spans(width, hidden)
    views = {name: stash_ref.at[:, pl.ds(first, size)] for name, (first, size) in spans.items()}
    normed_ref = views["normed"]
    mixed_ref = views["mixed"]
    normed_two_ref = views["normed_two"]
    act_ref = views["act"]
    qkv_grad_ref = views["qkv_grad"]
    branch_ref = views["branch"]
    pre_grad_ref = views["pre_grad"]
    views["cot"][...] = cot_ref[...]
    leaving = []

    def leave(*names):
        for name in names:
            cols = pl.ds(*spans[name])
            copy = pltpu.make_async_copy(
                stash_ref.at[:, cols], stash_hbm.at[:, cols], stash_sems.at[len(leaving)]
            )
            copy.start()
            leaving.append(copy)

    leave("cot")
    share = width // sum(len(keys) for keys in keys_lists[0])
    targets = (
        [(qkv_w, column, share) for column in range(3)]
        + [(out_w, 0, share)]
        + [(fc_in_w, column, share) for column in range(hidden // width)]
        + [(fc_out_w, 0, share * hidden // width)]
    )
    copies = {}
    for number, (target_ref, column, rows) in enumerate(targets):
        half, first = (0, number * share) if number < 6 else (1, (number - 6) * share)
        half_refs = weight_refs[: len(keys_lists[0])] if half == 0 else weight_refs[len(keys_lists[0]) :]
        for keys, weight_ref in zip(keys_lists[half], half_refs):
            for index, key in enumerate(keys):
                at = pl.multiple_of(jnp.bitwise_xor(spot_ref[0], key) * rows, rows)
                copy = pltpu.make_async_copy(
                    weight_ref.at[index, pl.ds(first, rows), :],
                    target_ref.at[pl.ds(at, rows), pl.ds(column * width, width)],
                    sems.at[sum(len(some) for some in copies.values())],
                )
                copy.start()
                copies.setdefault(id(target_ref), []).append(copy)

    def arrive(target_ref):
        for copy in copies[id(target_ref)]:
            copy.wait()

    row_total, width = base_ref.shape
    tiles = row_total // tile_rows
    head_pairs = HEADS // 2
    lanes = 2 * HDIM

    start = base_ref[...]
    for part_ref in part_refs:
        start = start + part_ref[...].astype(f32)
    unit_one, scale_one = norm_stats(start)
    normed = (unit_one * gain_ref[0:1] + shift_ref[0:1]).astype(bf16)
    normed_ref[...] = normed
    arrive(qkv_w)
    for spot in range(3):
        cols = slice(spot * width, (spot + 1) * width)
        qkv_ref[:, cols] = dot_nn(normed, qkv_w[:, cols]).astype(bf16)

    low_lanes = lax.broadcasted_iota(jnp.int32, (tile_rows, lanes), 1) < HDIM

    def half(values, odd):
        keep = jnp.logical_not(low_lanes) if odd else low_lanes
        return jnp.where(keep, values, jnp.zeros_like(values))

    def head_slices(pair, tile):
        rows = pl.ds(tile * tile_rows, tile_rows)
        cols = [
            pl.ds(pl.multiple_of(which * width + pair * lanes, lanes), lanes) for which in range(3)
        ]
        return rows, cols

    def attend(pair, carry):
        for tile in range(tiles):
            rows, cols = head_slices(pair, tile)
            queries, keys_arr, values_arr = [qkv_ref[rows, col] for col in cols]
            mixed = jnp.zeros((tile_rows, lanes), f32)
            for odd in range(2):
                scores = times_transpose(half(queries, odd), keys_arr) * HDIM ** (-0.5)
                scores = scores + mask_ref[tile]
                exponent = jnp.exp(scores - jnp.max(scores, axis=-1, keepdims=True))
                probs = exponent * (1.0 / jnp.sum(exponent, axis=-1, keepdims=True))
                probs_ref[(pair * 2 + odd) * tiles + tile] = probs
                mixed = mixed + dot_nn(probs.astype(bf16), half(values_arr, odd))
            mixed_ref[rows, cols[0]] = mixed.astype(bf16)
        return carry

    lax.fori_loop(0, head_pairs, attend, 0, unroll=3)
    leave("normed", "mixed")
    arrive(out_w)
    middle = start + dot_nn(mixed_ref[...], out_w[...])
    unit_two, scale_two = norm_stats(middle)
    normed_two = (unit_two * gain_ref[1:2] + shift_ref[1:2]).astype(bf16)
    normed_two_ref[...] = normed_two
    total_ref[...] = middle
    back_ref[...] = jnp.zeros_like(back_ref)
    arrive(fc_in_w)
    arrive(fc_out_w)

    def feed(step, carry):
        cols = pl.ds(pl.multiple_of(step * ff_step, ff_step), ff_step)
        pre = dot_nn(normed_two_ref[...], fc_in_w[:, cols]) + bias_ref[:, cols]
        cdf = 0.5 * (1.0 + lax.erf(pre * 0.5**0.5))
        act = (pre * cdf).astype(bf16)
        act_ref[:, cols] = act
        slope = cdf + pre * (jnp.exp(-0.5 * pre * pre) * (2.0 * math.pi) ** (-0.5))
        pre_grad = slope * times_transpose(cot_ref[...], fc_out_w[cols, :])
        pre_grad = pre_grad.astype(bf16)
        pre_grad_ref[:, cols] = pre_grad
        bias_grad_ref[:, cols] = jnp.sum(pre_grad.astype(f32), axis=0, keepdims=True)
        total_ref[...] += dot_nn(act, fc_out_w[cols, :])
        back_ref[...] += times_transpose(pre_grad, fc_in_w[:, cols])
        return carry

    lax.fori_loop(0, fc_in_w.shape[1] // ff_step, feed, 0)
    leave("normed_two", "act", "pre_grad")
    result_ref[...] = (total_ref[...] * keep_ref[...]).astype(bf16)
    grad_norm, gain_two, shift_two = norm_back(unit_two, scale_two, gain_ref[1:2], back_ref[...])
    grad_middle = cot_ref[...].astype(f32) + grad_norm
    grad_branch = grad_middle.astype(bf16)
    branch_ref[...] = grad_branch
    mixed_grad_ref[...] = times_transpose(grad_branch, out_w[...]).astype(bf16)

    def attend_back(pair, carry):
        for tile in range(tiles):
            rows, cols = head_slices(pair, tile)
            queries, keys_arr, values_arr = [qkv_ref[rows, col] for col in cols]
            grad_mixed = mixed_grad_ref[rows, cols[0]]
            grads = [jnp.zeros((tile_rows, lanes), f32) for _ in range(3)]
            for odd in range(2):
                probs = probs_ref[(pair * 2 + odd) * tiles + tile]
                own_grad = half(grad_mixed, odd)
                grad_probs = times_transpose(own_grad, values_arr)
                grad_scores = probs * (
                    grad_probs - jnp.sum(grad_probs * probs, axis=-1, keepdims=True)
                )
                grad_scores = grad_scores.astype(bf16)
                grads[0] = grads[0] + dot_nn(grad_scores, half(keys_arr, odd))
                grads[1] = grads[1] + inner(grad_scores, half(queries, odd))
                grads[2] = grads[2] + inner(probs.astype(bf16), own_grad)
            for which, factor in enumerate((HDIM ** (-0.5), HDIM ** (-0.5), 1.0)):
                qkv_grad_ref[rows, cols[which]] = (grads[which] * factor).astype(bf16)
        return carry

    lax.fori_loop(0, head_pairs, attend_back, 0, unroll=3)
    leave("branch", "qkv_grad")
    back = jnp.zeros((row_total, width), f32)
    for spot in range(3):
        cols = slice(spot * width, (spot + 1) * width)
        back = back + times_transpose(qkv_grad_ref[:, cols], qkv_w[:, cols])
    grad_norm, gain_one, shift_one = norm_back(unit_one, scale_one, gain_ref[0:1], back)
    grad_start = grad_middle + grad_norm
    embed_grad_ref[...] = grad_start.astype(bf16)
    sums = jnp.concatenate(
        [jnp.sum(grad_start, axis=0, keepdims=True), gain_one, gain_two, shift_one, shift_two]
        + [jnp.zeros((3, width), f32)],
        axis=0,
    )
    sums_ref[...] = sums
    small_ref = views["small"]
    positions = small_ref.shape[0] - 16
    spots_at = lax.broadcasted_iota(jnp.int32, (positions, row_total), 0)
    one_hot = jnp.where(spots_at == kept_ref[...], 1.0, 0.0).astype(bf16)
    by_position = dot_nn(one_hot, grad_start.astype(bf16))
    cuts = [bias_grad_ref[:, spot : spot + width] for spot in range(0, hidden, width)]
    cuts.append(jnp.zeros((8 - len(cuts), width), f32))
    small_ref[...] = jnp.concatenate([by_position, sums, *cuts], axis=0).astype(bf16)
    leave("small")
    for copy in leaving:
        copy.wait()


def block(parts, weight_halves, spots, base, cot, keep, mask, gains, shifts, bias, kept):
    row_total, width = base.shape
    tile_rows = mask.shape[1]
    hidden = bias.shape[1]
    bf16 = jnp.bfloat16
    f32 = jnp.float32
    keys_lists = [[keys for keys, _ in blocks] for blocks in weight_halves]
    weight_args = [block for blocks in weight_halves for _, block in blocks]
    pieces = sum(len(keys) for keys in keys_lists[0])
    inside = pl.BlockSpec(memory_space=pltpu.VMEM)
    outside = pl.BlockSpec(memory_space=pl.ANY)
    rows = (row_total, width)
    shapes = [
        (rows, bf16),
        (rows, bf16),
        ((row_total, sum(stash_spans(width, hidden)["small"])), bf16),
        ((8, width), f32),
    ]
    return run_kernel(
        partial(block_body, len(parts), tile_rows, width, keys_lists),
        (*parts, *weight_args, spots, base, cot, keep, mask, gains, shifts, bias, kept),
        [inside] * len(parts)
        + [outside] * len(weight_args)
        + [pl.BlockSpec(memory_space=pltpu.SMEM)]
        + [inside] * 8,
        out_shape=[jax.ShapeDtypeStruct(shape, kind) for shape, kind in shapes],
        out_specs=[inside, inside, outside, inside],
        scratch_shapes=[
            pltpu.VMEM((width, 3 * width), bf16),
            pltpu.VMEM((width, width), bf16),
            pltpu.VMEM((width, hidden), bf16),
            pltpu.VMEM((hidden, width), bf16),
            pltpu.VMEM((row_total, 3 * width), bf16),
            pltpu.VMEM((HEADS * row_total // tile_rows, tile_rows, tile_rows), f32),
            pltpu.VMEM(rows, f32),
            pltpu.VMEM(rows, f32),
            pltpu.VMEM(rows, bf16),
            pltpu.VMEM((1, hidden), f32),
            pltpu.VMEM((row_total, sum(stash_spans(width, hidden)["small"])), bf16),
            pltpu.SemaphoreType.DMA(((5 + hidden // width) * pieces,)),
            pltpu.SemaphoreType.DMA((len(stash_spans(width, hidden)),)),
        ],
    )


def dot_full(left_arr, right_arr, left_dim=1, right_dim=0):
    return lax.dot_general(
        left_arr,
        right_arr,
        (((left_dim,), (right_dim,)), ((), ())),
        precision=lax.Precision.HIGH,
        preferred_element_type=jnp.float32,
    )


def head_part(values, head):
    size = values.shape[1] // GEN_HEADS
    lane = lax.broadcasted_iota(jnp.int32, values.shape, 1)
    inside = jnp.logical_and(lane >= head * size, lane < (head + 1) * size)
    return jnp.where(inside, values, 0.0)


def generate_body(
    waves_ref,
    token_ref,
    attn_hbm,
    gain_hbm,
    ff_in_hbm,
    ff_out_hbm,
    bias_w_hbm,
    columns_hbm,
    *refs,
):
    *kernel_refs, embed_bias_ref, low_ref, states_ref, rows_ref, weights_ref, pre_ref, scales_ref = refs[:-8]
    attn_ref, gain_ref, ff_in_ref, ff_out_ref, bias_w_ref, columns_ref, hold_ref, sems = refs[-8:]
    f32 = jnp.float32
    copies = [
        pltpu.make_async_copy(source, target, sems.at[number])
        for number, (source, target) in enumerate(
            (
                (attn_hbm, attn_ref),
                (gain_hbm, gain_ref),
                (ff_in_hbm, ff_in_ref),
                (ff_out_hbm, ff_out_ref),
                (columns_hbm, columns_ref),
                (bias_w_hbm, bias_w_ref),
            )
        )
    ]
    for copy in copies:
        copy.start()
    bands = waves_ref.shape[1]
    width = token_ref.shape[1]
    padded = rows_ref.shape[1]
    square = (bands, bands)
    diagonal = lax.broadcasted_iota(jnp.int32, square, 0) == lax.broadcasted_iota(
        jnp.int32, square, 1
    )
    waves = jnp.broadcast_to(waves_ref[...].astype(f32), square)
    column = jnp.sum(jnp.where(diagonal, waves, 0.0), axis=1, keepdims=True)
    lane = lax.broadcasted_iota(jnp.int32, (bands, width), 1)
    half_width = width // 2
    number = jnp.where(lane < half_width, lane, lane - half_width).astype(f32)
    angles = column * jnp.exp(number * (-math.log(10000.0) / half_width))
    wave = jnp.where(lane < half_width, jnp.sin(angles), jnp.cos(angles))
    sequence = jnp.concatenate(
        [wave, token_ref[...].astype(f32), jnp.zeros((padded - bands - 1, width), f32)], axis=0
    )
    rows_ref[0] = sequence
    copies[0].wait()
    copies[1].wait()
    for which in range(3):
        rows_ref[1 + which] = dot_full(sequence, attn_ref[which].astype(f32))
    queries = rows_ref[1]
    keys_arr = rows_ref[2]
    values_arr = rows_ref[3]
    key_spot = lax.broadcasted_iota(jnp.int32, (padded, padded), 1)
    mixed = jnp.zeros((padded, width), f32)
    for head in range(GEN_HEADS):
        scores = dot_full(head_part(queries, head), keys_arr, 1, 1)
        scores = scores * (1.0 / math.sqrt(width // GEN_HEADS))
        scores = jnp.where(key_spot <= bands, scores, -1e30)
        exponent = jnp.exp(scores - jnp.max(scores, axis=-1, keepdims=True))
        weights = exponent / jnp.sum(exponent, axis=-1, keepdims=True)
        weights_ref[head] = weights
        mixed = mixed + dot_full(weights, head_part(values_arr, head))
    rows_ref[4] = mixed
    unit_one, scale_one = norm_stats(sequence + dot_full(mixed, attn_ref[3].astype(f32)))
    rows_ref[5] = unit_one
    first = unit_one * gain_ref[0:1].astype(f32)
    copies[2].wait()
    pre = dot_full(first, ff_in_ref[...].astype(f32))
    pre_ref[...] = pre
    hidden = pre * (0.5 * (1.0 + lax.erf(pre * 0.5**0.5)))
    copies[3].wait()
    unit_two, scale_two = norm_stats(first + dot_full(hidden, ff_out_ref[...].astype(f32)))
    rows_ref[6] = unit_two
    states = unit_two * gain_ref[1:2].astype(f32)
    states_ref[...] = states
    scales_ref[0] = jnp.broadcast_to(scale_one, (padded, width))
    scales_ref[1] = jnp.broadcast_to(scale_two, (padded, width))
    low = states[:bands].astype(jnp.bfloat16)
    low_ref[...] = low
    features = hold_ref.shape[2]
    part_bands = kernel_refs[0].shape[1]
    copies[4].wait()
    for pixel in range(hold_ref.shape[0]):
        cols = slice(pixel * features, (pixel + 1) * features)
        hold_ref[pixel] = dot_nn(low, columns_ref[:, cols]).astype(jnp.bfloat16)
        for key, kernel_ref in enumerate(kernel_refs):
            first = 0
            if len(kernel_refs) > 1:
                first = jnp.bitwise_xor(lax.axis_index("band"), key) * part_bands
                first = pl.multiple_of(first, part_bands)
            kernel_ref[pixel] = hold_ref[pixel, pl.ds(first, part_bands), :]
    copies[5].wait()
    token_state = states[bands : bands + 8]
    embed_bias_ref[...] = dot_full(token_state, bias_w_ref[...].astype(f32))


def generate_fast(parts, wavelengths, token, gen_attn, gen_gain, ff_in, ff_out, gen_bias, columns):
    f32 = jnp.float32
    bf16 = jnp.bfloat16
    bands = wavelengths.shape[0]
    width = token.shape[0]
    padded = -(-(bands + 1) // 8) * 8
    features = gen_bias.shape[1]
    shapes = [
        ((8, features), f32),
        ((bands, width), bf16),
        ((padded, width), f32),
        ((7, padded, width), f32),
        ((GEN_HEADS, padded, padded), f32),
        ((padded, ff_in.shape[1]), f32),
        ((2, padded, width), f32),
    ]
    pixels = columns.shape[1] // features
    shapes = [((pixels, bands // parts, features), bf16)] * parts + shapes
    inside = pl.BlockSpec(memory_space=pltpu.VMEM)
    outside = pl.BlockSpec(memory_space=pl.ANY)
    weights = (gen_attn, gen_gain, ff_in, ff_out, gen_bias, columns)
    return run_kernel(
        generate_body,
        (wavelengths[None], token[None], *weights),
        out_shape=[jax.ShapeDtypeStruct(shape, kind) for shape, kind in shapes],
        in_specs=[inside] * 2 + [outside] * 6,
        out_specs=[inside] * len(shapes),
        scratch_shapes=[pltpu.VMEM(weight.shape, bf16) for weight in weights]
        + [
            pltpu.VMEM((pixels, bands, features), bf16),
            pltpu.SemaphoreType.DMA((6,)),
        ],
    )


def generate_back_body(
    tail_ref,
    attn_ref,
    gain_ref,
    ff_in_ref,
    ff_out_ref,
    bias_w_ref,
    states_ref,
    rows_ref,
    weights_ref,
    pre_ref,
    scales_ref,
    token_out,
    attn_out,
    gain_out,
    ff_in_out,
    ff_out_out,
    bias_out,
):
    f32 = jnp.float32
    padded, width = states_ref.shape
    features = bias_w_ref.shape[1]
    bands = padded - 8
    head_scale = 1.0 / math.sqrt(width // GEN_HEADS)
    cuts = [tail_ref[bands + spot : bands + spot + 1, :] for spot in range(features // width)]
    bias_grad = jnp.concatenate(cuts, axis=1)
    bias_grad = jnp.concatenate([bias_grad, jnp.zeros((7, features), f32)], axis=0)
    row_spot = lax.broadcasted_iota(jnp.int32, (padded - bands, width), 0)
    token_grad = dot_full(bias_grad, bias_w_ref[...].astype(f32), 1, 1)
    token_grad = jnp.where(row_spot == 0, token_grad[0:1], 0.0)
    grad_states = jnp.concatenate([tail_ref[:bands, :], token_grad], axis=0)
    token_state = states_ref[bands : bands + 8]
    first_row = lax.broadcasted_iota(jnp.int32, token_state.shape, 0) == 0
    bias_out[...] = dot_full(jnp.where(first_row, token_state, 0.0), bias_grad, 0, 0)
    unit_one = rows_ref[5]
    gain_one = gain_ref[0:1].astype(f32)
    gain_two = gain_ref[1:2].astype(f32)
    grad_two, gain_two_grad, _ = norm_back(rows_ref[6], scales_ref[1], gain_two, grad_states)
    pre = pre_ref[...]
    cdf = 0.5 * (1.0 + lax.erf(pre * 0.5**0.5))
    ff_out_out[...] = dot_full(pre * cdf, grad_two, 0, 0)
    slope = cdf + pre * (jnp.exp(-0.5 * pre * pre) * (2.0 * math.pi) ** (-0.5))
    grad_pre = slope * dot_full(grad_two, ff_out_ref[...].astype(f32), 1, 1)
    ff_in_out[...] = dot_full(unit_one * gain_one, grad_pre, 0, 0)
    grad_first = grad_two + dot_full(grad_pre, ff_in_ref[...].astype(f32), 1, 1)
    grad_one, gain_one_grad, _ = norm_back(unit_one, scales_ref[0], gain_one, grad_first)
    gain_out[...] = jnp.concatenate([gain_one_grad, gain_two_grad], axis=0)
    attn_out[3] = dot_full(rows_ref[4], grad_one, 0, 0)
    grad_mixed = dot_full(grad_one, attn_ref[3].astype(f32), 1, 1)
    sequence = rows_ref[0]
    queries = rows_ref[1]
    keys_arr = rows_ref[2]
    values_arr = rows_ref[3]
    grads = [jnp.zeros((padded, width), f32) for _ in range(3)]
    for head in range(GEN_HEADS):
        weights = weights_ref[head]
        own_grad = head_part(grad_mixed, head)
        grad_weights = dot_full(own_grad, values_arr, 1, 1)
        grad_scores = weights * (
            grad_weights - jnp.sum(grad_weights * weights, axis=-1, keepdims=True)
        )
        grad_scores = grad_scores * head_scale
        grads[0] = grads[0] + dot_full(grad_scores, head_part(keys_arr, head))
        grads[1] = grads[1] + dot_full(grad_scores, head_part(queries, head), 0, 0)
        grads[2] = grads[2] + dot_full(weights, own_grad, 0, 0)
    grad_sequence = grad_one
    for which in range(3):
        attn_out[which] = dot_full(sequence, grads[which], 0, 0)
        grad_sequence = grad_sequence + dot_full(
            grads[which], attn_ref[which].astype(f32), 1, 1
        )
    token_out[...] = grad_sequence[bands : bands + 1]


def generate_back(tail, gen_attn, gen_gain, ff_in, ff_out, gen_bias, kept_arrs):
    f32 = jnp.float32
    width = gen_gain.shape[1]
    shapes = [
        (1, width),
        gen_attn.shape,
        gen_gain.shape,
        ff_in.shape,
        ff_out.shape,
        gen_bias.shape,
    ]
    inside = pl.BlockSpec(memory_space=pltpu.VMEM)
    return run_kernel(
        generate_back_body,
        (tail, gen_attn, gen_gain, ff_in, ff_out, gen_bias, *kept_arrs),
        out_shape=[jax.ShapeDtypeStruct(shape, f32) for shape in shapes],
        in_specs=[inside] * (6 + len(kept_arrs)),
        out_specs=[inside] * len(shapes),
    )


def fill_kernel(keys_lists, piece_refs, spot, mat_ref, bands, pixels):
    for keys, piece_ref in zip(keys_lists, piece_refs):
        for number, key in enumerate(keys):
            share = piece_ref.shape[2]
            first = jnp.bitwise_xor(spot, key) * share
            for band in range(bands):
                rows = pl.ds(pl.multiple_of(band * pixels + first, share), share)
                mat_ref[rows, :] = piece_ref[number, band]


def fill_step(keys_lists, piece_refs, spot, mat_ref, band_step, group_steps):
    pixels = mat_ref.shape[0] // band_step
    step = pl.program_id(0)
    used = 0
    for group, keys_list in enumerate(keys_lists):
        group_refs = piece_refs[used : used + len(keys_list)]
        used += len(keys_list)

        @pl.when(step // group_steps == group)
        def _(keys_list=keys_list, group_refs=group_refs):
            fill_kernel(keys_list, group_refs, spot, mat_ref, band_step, pixels)


def embed_body(keys_lists, group_steps, band_step, *refs):
    spot_ref, patch_ref = refs[:2]
    count = sum(len(keys_list) for keys_list in keys_lists)
    piece_refs = refs[2 : 2 + count]
    *out_refs, mat_ref, total_ref = refs[2 + count :]
    step = pl.program_id(0)
    fill_step(keys_lists, piece_refs, spot_ref[0], mat_ref, band_step, group_steps)

    @pl.when(step == 0)
    def _():
        total_ref[...] = jnp.zeros_like(total_ref)

    total_ref[...] += dot_nn(patch_ref[...], mat_ref[...])

    @pl.when(step == pl.num_programs(0) - 1)
    def _():
        for key, out_ref in enumerate(out_refs):
            rows = out_ref.shape[0]
            first = pl.multiple_of(jnp.bitwise_xor(spot_ref[1], key) * rows, rows)
            out_ref[...] = total_ref[pl.ds(first, rows), :].astype(out_ref.dtype)


def group_band_count(kernel_groups):
    return min(block.shape[1] for blocks in kernel_groups for _, block in blocks)


def piece_specs(kernel_groups, band_step, first_group=0):
    group_steps = group_band_count(kernel_groups) // band_step
    specs = []
    arrays = []
    for group, blocks in enumerate(kernel_groups):
        for keys, block in blocks:
            whole = block.shape[1] > group_steps * band_step
            first = group * group_steps
            skip = first_group * group_steps

            def pick(step, first=first, whole=whole):
                here = jnp.clip(step - first, 0, group_steps - 1)
                return (0, here + first + skip if whole else here, 0, 0)

            specs.append(pl.BlockSpec((len(keys), band_step) + block.shape[2:], pick))
            arrays.append(block)
    keys_lists = [[keys for keys, _ in blocks] for blocks in kernel_groups]
    return specs, arrays, keys_lists, group_steps


def embed_share(spots, patch_rows, kernel_groups, owners):
    row_total = patch_rows.shape[0]
    blocks = kernel_groups[0]
    group_bands = group_band_count(kernel_groups)
    width = blocks[0][1].shape[3]
    pixels = sum(len(keys) for keys, _ in blocks) * blocks[0][1].shape[2]
    band_step = min(4, group_bands)
    depth = band_step * pixels
    specs, arrays, keys_lists, group_steps = piece_specs(kernel_groups, band_step)
    rows = row_total // owners
    return run_kernel(
        partial(embed_body, keys_lists, group_steps, band_step),
        [spots, patch_rows, *arrays],
        [
            pl.BlockSpec(memory_space=pltpu.SMEM),
            pl.BlockSpec((row_total, depth), lambda step: (0, step)),
        ]
        + specs,
        limit=63,
        grid=(group_steps * len(kernel_groups),),
        out_shape=[jax.ShapeDtypeStruct((rows, width), jnp.bfloat16)] * owners,
        out_specs=[pl.BlockSpec((rows, width), lambda step: (0, 0))] * owners,
        scratch_shapes=[
            pltpu.VMEM((depth, width), jnp.bfloat16),
            pltpu.VMEM((row_total, width), jnp.float32),
        ],
    )


def kernel_grad_body(dp_size, band_step, *refs):
    spot_ref, patch_ref = refs[:2]
    *grad_refs, send_ref, keep_ref, hold_ref = refs[2:]
    rows = grad_refs[0].shape[0]
    total = 0.0
    for key, grad_ref in enumerate(grad_refs):
        first = pl.multiple_of(jnp.bitwise_xor(spot_ref[1], key) * rows, rows)
        total = total + inner(patch_ref[pl.ds(first, rows), :], grad_ref[...])
    hold_ref[...] = total.astype(hold_ref.dtype)
    pixels = hold_ref.shape[0] // band_step
    share = pixels // dp_size
    core = lax.rem(spot_ref[0], 2)
    for band in range(band_step):
        for chip in range(dp_size // 2):
            base = band * pixels + chip * 2 * share
            kept = pl.multiple_of(base + core * share, share)
            keep_ref[band, chip] = hold_ref[pl.ds(kept, share), :]
            sent = pl.multiple_of(base + (1 - core) * share, share)
            send_ref[band, chip] = hold_ref[pl.ds(sent, share), :]


def kernel_grad_part(spots, patch_rows, grads, first_band, group_bands, bands_dev, dp_size, after):
    row_total = patch_rows.shape[0]
    width = grads[0].shape[1]
    band_step = min(4, group_bands)
    pixels = patch_rows.shape[1] // bands_dev
    depth = band_step * pixels
    offset = first_band // band_step
    share = pixels // dp_size
    chips = (dp_size // 2, share, width)
    steps = group_bands // band_step
    block = (band_step,) + chips
    return run_kernel(
        partial(kernel_grad_body, dp_size, band_step),
        (spots, patch_rows, *grads),
        after=after,
        limit=63,
        grid=(steps,),
        out_shape=[
            jax.ShapeDtypeStruct((bands,) + chips, jnp.bfloat16)
            for bands in (group_bands, group_bands)
        ],
        in_specs=[
            pl.BlockSpec(memory_space=pltpu.SMEM),
            pl.BlockSpec((row_total, depth), lambda step: (0, offset + step)),
        ]
        + [pl.BlockSpec(grad.shape, lambda step: (0, 0)) for grad in grads],
        out_specs=[
            pl.BlockSpec(block, lambda step: (step, 0, 0, 0)),
            pl.BlockSpec(block, lambda step: (step, 0, 0, 0)),
        ],
        scratch_shapes=[pltpu.VMEM((depth, width), jnp.bfloat16)],
    )


def patch_grad_body(keys_lists, grad_count, group_steps, band_step, *refs):
    spot_ref = refs[0]
    grad_refs = refs[1 : 1 + grad_count]
    out_ref, mat_ref = refs[-2:]
    piece_refs = refs[1 + grad_count : -2]
    fill_step(keys_lists, piece_refs, spot_ref[0], mat_ref, band_step, group_steps)
    for key, grad_ref in enumerate(grad_refs):
        rows = grad_ref.shape[0]
        first = pl.multiple_of(jnp.bitwise_xor(spot_ref[1], key) * rows, rows)
        out_ref[pl.ds(first, rows), :] = times_transpose(grad_ref[...], mat_ref[...]).astype(
            out_ref.dtype
        )


def patch_grad(spots, grads, kernel_groups, pixels, first_group, after):
    rows, width = grads[0].shape
    row_total = rows * len(grads)
    band_step = min(4, group_band_count(kernel_groups))
    depth = band_step * pixels
    specs, arrays, keys_lists, group_steps = piece_specs(kernel_groups, band_step, first_group)
    steps = group_steps * len(kernel_groups)
    return run_kernel(
        partial(patch_grad_body, keys_lists, len(grads), group_steps, band_step),
        [spots, *grads, *arrays],
        [pl.BlockSpec(memory_space=pltpu.SMEM)]
        + [pl.BlockSpec(grad.shape, lambda step: (0, 0)) for grad in grads]
        + specs,
        after=after,
        limit=63,
        grid=(steps,),
        out_shape=jax.ShapeDtypeStruct((row_total, steps * depth), jnp.bfloat16),
        out_specs=pl.BlockSpec((row_total, depth), lambda step: (0, step)),
        scratch_shapes=[pltpu.VMEM((depth, width), jnp.bfloat16)],
    )


def states_grad_body(batches, low_ref, columns_ref, *refs):
    *piece_refs, sums_ref, spot_ref, grad_ref, part_ref, hold_ref = refs
    pixels, bands, width = piece_refs[0].shape
    for number, piece_ref in enumerate(piece_refs):
        key, batch = divmod(number, batches)
        first = (jnp.bitwise_xor(spot_ref[1], key) * batches + batch) * bands
        hold_ref[:, pl.ds(pl.multiple_of(first, bands), bands), :] = piece_ref[...]
    total = 0.0
    for pixel in range(pixels):
        cols = slice(pixel * width, (pixel + 1) * width)
        grads = hold_ref[pixel]
        grad_ref[:, cols] = inner(low_ref[...], grads)
        total = total + times_transpose(grads, columns_ref[:, cols])
    bands, states = total.shape
    part_ref[:bands, :] = total
    rows = [sums_ref[0:1, spot : spot + states] for spot in range(0, width, states)]
    rows.append(jnp.zeros((part_ref.shape[0] - bands - len(rows), states), jnp.float32))
    part_ref[bands:, :] = jnp.concatenate(rows, axis=0)


def states_grad(spots, low, columns, pieces, sums):
    pixels, bands, width = pieces[0].shape
    tail_rows = low.shape[0] + -(-width // low.shape[1] // 8) * 8
    if bands % 16:
        blocks = [([key], piece[None]) for key, piece in enumerate(pieces)]
        whole = place(blocks, "band", 1).reshape(pixels, -1, width)
        grads = whole.transpose(1, 0, 2).reshape(low.shape[0], -1)
        rows = [times_transpose(grads, columns), sums[0].reshape(-1, low.shape[1])]
        tail = jnp.concatenate(rows, axis=0)
        tail = jnp.pad(tail, ((0, tail_rows - tail.shape[0]), (0, 0)))
        return inner(low, grads), tail
    inside = pl.BlockSpec(memory_space=pltpu.VMEM)
    return run_kernel(
        partial(states_grad_body, 1),
        (low, columns, *pieces, sums, spots),
        out_shape=[
            jax.ShapeDtypeStruct(columns.shape, jnp.float32),
            jax.ShapeDtypeStruct((tail_rows, low.shape[1]), jnp.float32),
        ],
        in_specs=[inside] * (3 + len(pieces)) + [pl.BlockSpec(memory_space=pltpu.SMEM)],
        out_specs=[inside, inside],
        scratch_shapes=[pltpu.VMEM((pixels, bands * len(pieces), width), jnp.bfloat16)],
    )


def flatten_body(in_ref, out_ref):
    out_ref[...] = in_ref[...].reshape(out_ref.shape)


def unflatten_body(*refs):
    *in_refs, out_ref = refs
    done = 0
    for in_ref in in_refs:
        part = in_ref[...]
        bands = part.shape[1] // out_ref.shape[2]
        out_ref[:, done : done + bands, :] = part.reshape(-1, bands, out_ref.shape[2])
        done += bands


def flatten_rows(cube, after):
    rows, bands, pixels = cube.shape
    step_rows = 64
    return run_kernel(
        flatten_body,
        (cube,),
        [pl.BlockSpec((step_rows, bands, pixels), lambda step: (step, 0, 0))],
        after=after,
        grid=(rows // step_rows,),
        out_shape=jax.ShapeDtypeStruct((rows, bands * pixels), cube.dtype),
        out_specs=pl.BlockSpec((step_rows, bands * pixels), lambda step: (step, 0)),
    )


def unflatten_rows(flats, bands, after):
    rows = flats[0].shape[0]
    pixels = sum(flat.shape[1] for flat in flats) // bands
    step_rows = 64
    return run_kernel(
        unflatten_body,
        flats,
        [pl.BlockSpec((step_rows, flat.shape[1]), lambda step: (step, 0)) for flat in flats],
        after=after,
        limit=63,
        grid=(rows // step_rows,),
        out_shape=jax.ShapeDtypeStruct((rows, bands, pixels), flats[0].dtype),
        out_specs=pl.BlockSpec((step_rows, bands, pixels), lambda step: (step, 0, 0)),
    )


def stack_body(*refs):
    *part_refs, out_ref, hold_ref = refs
    width = out_ref.shape[1]
    first = 0
    for part_ref in part_refs:
        rows = part_ref.shape[0]
        for spot in range(0, part_ref.shape[1], width):
            hold_ref[pl.ds(first, rows), :] = part_ref[:, spot : spot + width].astype(jnp.float32)
            first += rows
    out_ref[...] = hold_ref[...].astype(out_ref.dtype)


def stack_weights(shards_in):
    width = shards_in[-1].shape[1]
    if any(shard.shape[0] % 8 for shard in shards_in):
        return jnp.concatenate(
            [part for shard in shards_in for part in column_blocks(shard, width)], axis=0
        )
    row_total = sum(shard.size for shard in shards_in) // width
    inside = pl.BlockSpec(memory_space=pltpu.VMEM)
    return run_kernel(
        stack_body,
        shards_in,
        [inside] * len(shards_in),
        out_shape=jax.ShapeDtypeStruct((row_total, width), shards_in[0].dtype),
        out_specs=inside,
        scratch_shapes=[pltpu.VMEM((row_total, width), jnp.float32)],
    )


def plane_body(block_rows, spot_ref, *refs):
    *stack_refs, first_ref, last_ref, hold_ref = refs
    band_size = len(stack_refs)
    for key, stack_ref in enumerate(stack_refs):
        owner = jnp.bitwise_xor(spot_ref[1], key)
        values = stack_ref[...].astype(jnp.float32)
        done = 0
        for rows in block_rows:
            at = pl.multiple_of(done * band_size + owner * rows, 8)
            hold_ref[pl.ds(at, rows), :] = values[done : done + rows]
            done += rows
    half = first_ref.shape[0]
    first_ref[...] = hold_ref[:half, :].astype(first_ref.dtype)
    last_ref[...] = hold_ref[half:, :].astype(last_ref.dtype)


def plane_weights(spots, stacks, block_rows):
    row_total, width = stacks[0].shape
    band_size = len(stacks)
    half = row_total * band_size // 2
    if any(rows % 8 for rows in block_rows):
        whole = place([([key], stack[None]) for key, stack in enumerate(stacks)], "band", 0)
        parts = []
        done = 0
        for rows in block_rows:
            parts.append(whole[:, done : done + rows].reshape(-1, width))
            done += rows
        merged = jnp.concatenate(parts, axis=0)
        return merged[:half], merged[half:]
    inside = pl.BlockSpec(memory_space=pltpu.VMEM)
    return run_kernel(
        partial(plane_body, block_rows),
        (spots, *stacks),
        [pl.BlockSpec(memory_space=pltpu.SMEM)] + [inside] * band_size,
        out_shape=[jax.ShapeDtypeStruct((half, width), stacks[0].dtype)] * 2,
        out_specs=[inside] * 2,
        scratch_shapes=[pltpu.VMEM((row_total * band_size, width), jnp.float32)],
    )


def weight_grad_body(dp_size, parts, hidden, spot_ref, own_ref, other_ref, *refs):
    *out_refs, turned_ref, hold_ref, feed_ref, small_ref, sems = refs
    width = hold_ref.shape[2]
    row_total = own_ref.shape[0]
    spans = stash_spans(width, hidden)
    share = width // dp_size
    chips = dp_size // 2
    core = lax.rem(spot_ref[0], 2)
    copies = []

    def view(name, column=0, size=None):
        first, whole = spans[name]
        first = first + column * width
        return [ref[:, first : first + (size or whole)] for ref in (own_ref, other_ref)]

    def turn_rows(name, at):
        first, size = spans[name]
        for spot in range(0, size, width):
            for number, ref in enumerate((own_ref, other_ref)):
                cols = slice(number * row_total, (number + 1) * row_total)
                turned = ref[:, first + spot : first + spot + width].T
                turned_ref[at + spot : at + spot + width, cols] = turned

    def pick(at, rows):
        parts = []
        for chip in range(chips):
            first = at + (chip * 2 + core) * rows
            parts.append(turned_ref[pl.ds(pl.multiple_of(first, 16), rows), :])
        return jnp.concatenate(parts, axis=0)

    def send(source_ref, rows, number, stride=None):
        part = [number in numbers for _, numbers in parts].index(True)
        first_step, numbers = parts[part]
        first = share * numbers.index(number)
        step = first_step // 2
        bit = lax.rem(lax.div(spot_ref[0], first_step), 2)
        for index in range(chips // 2):
            for which in range(2):
                own_bit = bit if which == 0 else 1 - bit
                chip = index // step * 2 * step + own_bit * step + index % step
                at = chip * (stride or rows)
                copy = pltpu.make_async_copy(
                    source_ref.at[pl.ds(pl.multiple_of(at, 16), rows), :],
                    out_refs[part * 2 + which].at[index, pl.ds(first, rows), :],
                    sems.at[len(copies)],
                )
                copy.start()
                copies.append(copy)

    def product(left, names, column):
        right = view(names, column, width)
        total = dot_nn(left[:, :row_total], right[0])
        return total + dot_nn(left[:, row_total:], right[1])

    blocks = (
        [("normed", "qkv_grad", column) for column in range(3)]
        + [("mixed", "branch", 0)]
        + [("normed_two", "pre_grad", column) for column in range(hidden // width)]
    )
    turned_at = {"normed": 0, "mixed": width, "normed_two": 2 * width, "act": 3 * width}
    picked = {}
    for number, (left, right, column) in enumerate(blocks):
        if left not in picked:
            turn_rows(left, turned_at[left])
            picked = {left: pick(turned_at[left], share)}
        hold_ref[number] = product(picked[left], right, column).astype(hold_ref.dtype)
        send(hold_ref.at[number], share, number)
    small = sum(part.astype(jnp.float32) for part in view("small"))
    small_ref[...] = small.astype(small_ref.dtype)
    small_share = row_total // dp_size
    turn_rows("act", turned_at["act"])
    feed_rows = hidden // dp_size
    for chip in range(chips):
        at = turned_at["act"] + (chip * 2 + core) * feed_rows
        left = turned_ref[pl.ds(pl.multiple_of(at, 16), feed_rows), :]
        feed_ref[chip * feed_rows : (chip + 1) * feed_rows, :] = product(left, "cot", 0).astype(
            feed_ref.dtype
        )
    send(feed_ref, feed_rows, len(blocks))
    own_small = small_ref.at[pl.ds(pl.multiple_of(core * small_share, 16), (dp_size - 1) * small_share), :]
    send(own_small, small_share, len(blocks) + 1, 2 * small_share)
    for copy in copies:
        copy.wait()


def weight_grad(spots, dp_size, parts, hidden, own, other):
    row_total, columns = own.shape
    width = (columns - 2 * hidden) // 9
    bf16 = jnp.bfloat16
    blocks = 4 + hidden // width
    chips = dp_size // 2
    share = width // dp_size
    block_rows = [share] * blocks + [hidden // dp_size, row_total // dp_size]
    rows = [sum(block_rows[number] for number in numbers) for _, numbers in parts]
    inside = pl.BlockSpec(memory_space=pltpu.VMEM)
    outside = pl.BlockSpec(memory_space=pl.ANY)
    return run_kernel(
        partial(weight_grad_body, dp_size, parts, hidden),
        (spots, own, other),
        [pl.BlockSpec(memory_space=pltpu.SMEM), inside, inside],
        limit=63,
        out_shape=[
            jax.ShapeDtypeStruct((chips // 2, part_rows, width), bf16)
            for part_rows in rows
            for _ in range(2)
        ],
        out_specs=[outside] * (2 * len(parts)),
        scratch_shapes=[
            pltpu.VMEM((3 * width + hidden, 2 * row_total), bf16),
            pltpu.VMEM((blocks, chips * share, width), bf16),
            pltpu.VMEM((hidden // 2, width), bf16),
            pltpu.VMEM((row_total, width), bf16),
            pltpu.SemaphoreType.DMA(((blocks + 2) * chips,)),
        ],
    )


def add_split_body(step, part_steps, spot_ref, keep_ref, *refs):
    *got_refs, send_ref, held_ref = refs
    bit = lax.rem(lax.div(spot_ref[0], step), 2)
    for number, got_ref in enumerate(got_refs):

        @pl.when(pl.program_id(0) // part_steps == number)
        def _(got_ref=got_ref):
            for out_ref, which in ((send_ref, 1 - bit), (held_ref, bit)):
                values = keep_ref[:, which].astype(jnp.float32)
                values = values + got_ref[:, which].astype(jnp.float32)
                out_ref[...] = values.astype(out_ref.dtype)


def add_split(spots, keep, gots, at, step, left):
    left = sorted(left, reverse=True)
    place_of = left.index(step)
    shape = keep.shape
    width = shape[-1]
    outer = math.prod(shape[:at]) * 2**place_of
    part_outer = outer // len(gots)
    inner_rows = keep.size // (outer * 2 * width)
    rows_step = inner_rows
    while rows_step > 512 and rows_step % 32 == 0:
        rows_step //= 2
    outer_step = 1
    while part_outer % (2 * outer_step) == 0 and 2 * outer_step * rows_step <= 512:
        outer_step *= 2
    part_steps = part_outer // outer_step
    block_in = (outer_step, 2, rows_step, width)
    block_out = pl.BlockSpec((outer_step, rows_step, width), lambda first, rows: (first, rows, 0))

    def part_spec(number):
        def pick(first, rows):
            return (jnp.clip(first - number * part_steps, 0, part_steps - 1), 0, rows, 0)

        return pl.BlockSpec(block_in, pick)

    outs = run_kernel(
        partial(add_split_body, step, part_steps),
        (spots, keep.reshape((outer, 2, inner_rows, width)))
        + tuple(got.reshape((part_outer, 2, inner_rows, width)) for got in gots),
        [
            pl.BlockSpec(memory_space=pltpu.SMEM),
            pl.BlockSpec(block_in, lambda first, rows: (first, 0, rows, 0)),
        ]
        + [part_spec(number) for number in range(len(gots))],
        limit=63,
        grid=(outer // outer_step, inner_rows // rows_step),
        out_shape=[jax.ShapeDtypeStruct((outer, inner_rows, width), keep.dtype)] * 2,
        out_specs=[block_out] * 2,
    )
    rest = shape[:at] + (-1,) + shape[at + 1 :]
    return outs[0].reshape(rest), outs[1].reshape(rest)


def owners_body(groups, spot_ref, *refs):
    keep_refs = refs[:groups]
    got_refs = refs[groups : 2 * groups]
    *out_refs, hold_ref = refs[2 * groups :]
    pixels = out_refs[0].shape[0]
    for group, (keep_ref, got_ref) in enumerate(zip(keep_refs, got_refs)):
        bands = keep_ref.shape[0]
        hold_ref[...] = keep_ref[...].astype(jnp.float32) + got_ref[...].astype(jnp.float32)
        for key, out_ref in enumerate(out_refs):
            first = pl.multiple_of(jnp.bitwise_xor(spot_ref[1], key) * pixels, pixels)
            part = hold_ref[:, pl.ds(first, pixels), :]
            out_ref[:, group * bands : (group + 1) * bands, :] = jnp.swapaxes(part, 0, 1).astype(
                out_ref.dtype
            )


def by_owner(spots, keeps, gots, band_size):
    bands, share, width = keeps[0].shape
    pixels = share // band_size
    if pixels % 8:
        whole = jnp.concatenate([add_low(keep, got) for keep, got in zip(keeps, gots)], axis=0)
        whole = whole.reshape(-1, band_size, pixels, width).transpose(1, 2, 0, 3)
        return [
            lax.dynamic_index_in_dim(whole, spots[1] ^ key, 0, keepdims=False)
            for key in range(band_size)
        ]
    inside = pl.BlockSpec(memory_space=pltpu.VMEM)
    return run_kernel(
        partial(owners_body, len(keeps)),
        (spots, *keeps, *gots),
        [pl.BlockSpec(memory_space=pltpu.SMEM)] + [inside] * (2 * len(keeps)),
        limit=63,
        out_shape=[
            jax.ShapeDtypeStruct((pixels, bands * len(keeps), width), keeps[0].dtype)
        ]
        * band_size,
        out_specs=[inside] * band_size,
        scratch_shapes=[pltpu.VMEM((bands, share, width), jnp.float32)],
    )


def shards(
    patches,
    bias_token,
    gen_attn,
    gen_gain,
    gen_ff_in,
    gen_ff_out,
    gen_kernel,
    gen_bias,
    pos_table,
    norm_gain,
    norm_bias,
    w_qkv,
    w_out,
    w_fc1,
    bias_in,
    w_fc2,
    wavelengths,
    kept,
    counts,
    cotangent,
):
    group_size, slot_count, bands_dev, pixel_count = patches.shape
    dp_size = lax.axis_size("dp")
    band_size = lax.axis_size("band")
    device_count = dp_size * band_size
    local_images = group_size // band_size
    model_width = w_out.shape[1]
    row_total = local_images * slot_count
    own_pixels = pixel_count // device_count
    share = own_pixels * band_size
    groups = 2
    group_bands = bands_dev // groups
    f32 = jnp.float32
    bf16 = jnp.bfloat16
    spot = lax.axis_index("band")
    spots = jnp.stack([lax.axis_index("dp"), spot]).astype(jnp.int32)

    parts = band_size if bands_dev % 16 == 0 else 1
    outs = generate_fast(
        parts,
        wavelengths,
        bias_token,
        gen_attn,
        gen_gain,
        gen_ff_in,
        gen_ff_out,
        gen_bias,
        gen_kernel,
    )
    own_kernel = outs[:parts]
    embed_bias, band_states, *gen_kept = outs[parts:]
    hidden = w_fc1.shape[1]
    weight_rows = [w_qkv.shape[0]] * (4 + hidden // model_width) + [w_fc2.shape[0]]
    stack = stack_weights((w_qkv, w_out, w_fc1, w_fc2))
    patch_rows = flatten_rows(
        patches.reshape(group_size * slot_count, bands_dev, pixel_count), (band_states,)
    )
    other_bands = range(1, band_size)
    dp_steps = bit_steps(dp_size)[1:]
    orders = [turn(dp_steps, group) for group in range(groups)]

    if parts == 1:
        whole = own_kernel[0].reshape(own_pixels, band_size, bands_dev, model_width)
        own_kernel = [
            lax.dynamic_index_in_dim(whole, spot ^ key, 1, keepdims=False)
            for key in range(band_size)
        ]
    sent = [part.transpose(1, 0, 2) for part in own_kernel]
    got = [swap(sent[key], "band", key) for key in other_bands]
    *got, patch_rows, stack = together(*got, patch_rows, stack)
    piece = place(
        [([key], block[None]) for key, block in enumerate([sent[0]] + got)], "band", 1
    ).reshape(bands_dev, share, model_width)

    own_pieces = [piece[group * group_bands : (group + 1) * group_bands] for group in range(groups)]
    held = [own_piece[None] for own_piece in own_pieces]
    held_keys = [[0] for _ in range(groups)]
    kernel_groups = [[([0], piece[None])] for _ in range(groups)]
    waiting = []
    stacks = {0: stack}
    stack_keys = [band_size // 2] + [key for key in other_bands if key != band_size // 2]
    for stage in range(len(dp_steps)):
        last = stage == len(dp_steps) - 1
        now_keys = stack_keys if last else stack_keys[:1]
        stack_keys = stack_keys[len(now_keys) :]
        got = [swap(held[group], "dp", orders[group][stage]) for group in range(groups)]
        if stage == 0:
            core_got = swap(piece, "dp", 1)
        elif waiting:
            core_got = swap(waiting[0][2], "dp", 1)
        stack_got = [swap(stack, "band", key) for key in now_keys]
        got[0], got[1], core_got, stack, *stack_got = together(*got, core_got, stack, *stack_got)
        stacks.update(zip(now_keys, stack_got))
        if stage == 0:
            for blocks in kernel_groups:
                blocks.append(([1], core_got[None]))
        elif waiting:
            group, keys, _ = waiting.pop(0)
            kernel_groups[group].append(([key ^ 1 for key in keys], core_got))
        for group in range(groups):
            keys = [key ^ orders[group][stage] for key in held_keys[group]]
            kernel_groups[group].append((keys, got[group]))
            waiting.append((group, keys, got[group]))
            if not last:
                held[group] = jnp.concatenate([held[group], got[group]], axis=0)
                held_keys[group] = held_keys[group] + keys
    for group, keys, last_got in waiting:
        kernel_groups[group].append(([key ^ 1 for key in keys], swap(last_got, "dp", 1)))

    planes = plane_weights(spots, [stacks[key] for key in range(band_size)], weight_rows)
    got = [swap(plane, "dp", orders[half][0]) for half, plane in enumerate(planes)]
    embedded = embed_share(spots, patch_rows, kernel_groups, band_size)
    *embedded, first_got, last_got = together(*embedded, *got)
    held = [
        jnp.concatenate([plane[None], got[None]], axis=0)
        for plane, got in zip(planes, (first_got, last_got))
    ]
    held_keys = [[0, orders[half][0]] for half in range(2)]
    for stage in range(1, len(dp_steps) - 1):
        for half in range(2):
            step = orders[half][stage]
            held[half] = jnp.concatenate([held[half], swap(held[half], "dp", step)], axis=0)
            held_keys[half] = held_keys[half] + [key ^ step for key in held_keys[half]]
    got = [swap(held[half], "dp", orders[half][-1]) for half in range(2)]
    parts = [embedded[0]] + [swap(embedded[key], "band", key) for key in other_bands]
    held[0], held[1], got[0], got[1], *parts = together(*held, *got, *parts)
    weight_halves = []
    for half in range(2):
        blocks = [(held_keys[half], held[half])]
        blocks.append(([key ^ orders[half][-1] for key in held_keys[half]], got[half]))
        weight_halves.append(blocks + gather_core(blocks))

    valid_mask = jnp.arange(slot_count)[None, :] < counts[:, None]
    keep_col = valid_mask.reshape(row_total, 1)
    kept_flat = kept.reshape(row_total)
    pos_rows = jnp.take(pos_table, kept_flat, axis=0).astype(f32)
    base = embed_bias[0:1] + pos_rows
    tile_images = 2 if local_images % 2 == 0 else 1
    tile_rows = tile_images * slot_count
    image_spot = jnp.arange(tile_rows) // slot_count
    same_image = image_spot[:, None] == image_spot[None, :]
    mask = jnp.where(same_image[None] & valid_mask.reshape(-1, 1, tile_rows), 0.0, -1e30)
    cot = jnp.where(keep_col, cotangent.reshape(row_total, model_width), 0)
    (
        result,
        grad_embed,
        stash,
        sums,
    ) = block(
        parts,
        weight_halves,
        spots,
        base,
        cot,
        keep_col.astype(f32),
        mask.astype(f32),
        norm_gain.astype(f32),
        norm_bias.astype(f32),
        bias_in.astype(f32)[None],
        kept_flat[None],
    )

    small_share = row_total // device_count
    block_rows = weight_rows + [small_share]
    part_blocks = [[0, 9], [1], [2], [3], [4, 5, 6, 7], [8]]
    part_orders = [orders[0], orders[1], orders[1], orders[0], orders[0], orders[1]]
    weight_parts = [(order[0], numbers) for order, numbers in zip(part_orders, part_blocks)]
    grads = [grad_embed] + [swap(grad_embed, "band", key) for key in other_bands]
    weight_split = weight_grad(
        spots, dp_size, weight_parts, hidden, stash, swap(stash, "dp", 1)
    )
    mixed = together(*grads, *weight_split)
    grads, weight_split = list(mixed[:band_size]), mixed[band_size:]
    weight_keep, weight_send = list(weight_split[0::2]), list(weight_split[1::2])

    weight_got = [swap(weight_send[part], "dp", part_orders[part][0]) for part in range(2)]
    kernel_split = []
    for group in range(groups):
        *sends, keep = kernel_grad_part(
            spots,
            patch_rows,
            grads,
            group * group_bands,
            group_bands,
            bands_dev,
            dp_size,
            (),
        )
        core_got = [swap(send, "dp", 1) for send in sends]
        kernel_split += add_split(spots, keep, core_got, 1, orders[group][0], dp_steps)
    weight_got[0], weight_got[1], *kernel_split = together(*weight_got, *kernel_split)

    def cut_blocks(values, numbers):
        lead = values.shape[0]
        cuts = []
        first = 0
        for number in numbers:
            rows = block_rows[number]
            cut = values[:, first : first + rows * band_size]
            cuts.append(cut.reshape(lead, band_size, rows, model_width))
            first += rows * band_size
        return jnp.concatenate(cuts, axis=2)

    def over_band(by_band):
        sent = [
            lax.dynamic_index_in_dim(by_band, spot ^ key, 1, keepdims=False)
            for key in range(band_size)
        ]
        return [sent[0]] + [swap(sent[key], "band", key) for key in other_bands]

    def total(blocks):
        return sum(block_sum.astype(f32) for block_sum in blocks)

    def over_chips(sums):
        cut = [
            values if isinstance(values, tuple) else split_half(values, 0, order[0], order)
            for values, order in sums
        ]
        got = [None] * len(sums)
        for step in sorted({order[0] for _, order in sums}):
            here = [number for number, (_, order) in enumerate(sums) if order[0] == step]
            flat = [cut[number][0].reshape(-1, model_width) for number in here]
            moved = swap(jnp.concatenate(flat, axis=0) if len(flat) > 1 else flat[0], "dp", step)
            first = 0
            for number, rows in zip(here, flat):
                part = moved[first : first + rows.shape[0]]
                got[number] = part.reshape(cut[number][0].shape)
                first += rows.shape[0]
        return [
            (add_low(cut[number][1], got[number]), order[1:])
            for number, (_, order) in enumerate(sums)
        ]

    update = patch_grad(spots, grads, kernel_groups, pixel_count, 0, ())
    for stage in range(len(dp_steps)):
        last = stage == len(dp_steps) - 1
        got = [swap(kernel_split[2 * group], "dp", orders[group][stage]) for group in range(groups)]
        part = 2 + stage
        cuts = [
            cut_blocks(weight_keep[part], part_blocks[part]),
            cut_blocks(weight_send[part], part_blocks[part]),
        ]
        if stage == 0:
            cuts += [
                cut_blocks(add_low(weight_keep[early], weight_got[early]), part_blocks[early])
                for early in range(2)
            ]
        part_got = [None]
        if stage < 2:
            part_got = over_band(jnp.concatenate(cuts, axis=2))
        if stage == 0:
            got[0], got[1], update, *part_got = together(*got, update, *part_got)
        else:
            got[0], got[1], *part_got = together(*got, *part_got)
        if stage < 2:
            summed = total(part_got).astype(bf16)
            rows = [cut.shape[2] for cut in cuts]
            spots_in = [sum(rows[:number]) for number in range(len(rows))]
            summed = [summed[:, first : first + size] for first, size in zip(spots_in, rows)]
            weight_keep[part], weight_send[part] = summed[:2]
            if stage == 0:
                early = summed[2:]
        if not last:
            kernel_split = [
                part
                for group in range(groups)
                for part in add_split(
                    spots,
                    kernel_split[2 * group + 1],
                    [got[group]],
                    1,
                    orders[group][stage + 1],
                    orders[group][stage + 1 :],
                )
            ]
    sent = by_owner(
        spots,
        [
            kernel_split[2 * group + 1].reshape(group_bands, share, model_width)
            for group in range(groups)
        ],
        [got[group].reshape(group_bands, share, model_width) for group in range(groups)],
        band_size,
    )
    pieces = [sent[0]] + [swap(sent[key], "band", key) for key in other_bands]
    sums_left = over_chips(
        [(early[part], part_orders[part][1:]) for part in range(2)]
        + [
            ((weight_send[part], weight_keep[part]), part_orders[part])
            for part in range(2, len(part_blocks))
        ]
    )
    while any(order for _, order in sums_left[:2]):
        moved = over_chips([one for one in sums_left[:2] if one[1]])
        sums_left[:2] = [moved.pop(0) if one[1] else one for one in sums_left[:2]]
    weight_sums = [values for values, _ in sums_left]
    grad_patches = unflatten_rows([update], bands_dev, (sent[0],))
    mixed = together(*weight_sums, grad_patches, *pieces)
    count = len(part_blocks)
    weight_sums, grad_patches, pieces = list(mixed[:count]), mixed[count], mixed[count + 1 :]
    grad_gen_kernel, tail = states_grad(spots, band_states, gen_kernel, pieces, sums)
    mixed = together(*weight_sums, tail)
    weight_sums, tail = list(mixed[:-1]), mixed[-1]

    small = weight_sums[0][:, -small_share:]
    late = [(weight_sums[part], part_orders[part][1:]) for part in range(2, count)]
    small_steps = [("band", step) for step in bit_steps(band_size)]
    small_steps += [("dp", step) for step in turn(bit_steps(dp_size), 1)]

    def widen(values, number):
        return jnp.concatenate([values, swap(values, *small_steps[number])], axis=0)

    while any(order for _, order in late):
        late = over_chips(late)
    late = [values for values, _ in late]
    tail = total([tail] + [swap(tail, "band", key) for key in other_bands])
    tail_steps = bit_steps(dp_size)
    tail = tail + swap(tail, "dp", tail_steps[0])
    tail, *late = together(tail, *late)
    cuts = [cut_blocks(late[part - 2], part_blocks[part]) for part in range(4, count)]
    last_sum = total(over_band(jnp.concatenate(cuts, axis=2)))
    small = widen(small, 0)
    for number, step in enumerate(tail_steps[1:]):
        got = swap(tail, "dp", step)
        small = widen(small, number + 1)
        got, small = together(got, small)
        tail = tail + got
    for number in range(len(tail_steps), len(small_steps)):
        small = widen(small, number)
    own_grads = jnp.concatenate(
        [
            weight_sums[0][0, :-small_share].astype(f32),
            weight_sums[1][0].astype(f32),
            late[0][0].astype(f32),
            late[1][0].astype(f32),
            last_sum[0],
        ],
        axis=0,
    )
    small_order = (jnp.arange(dp_size) ^ spots[0])[:, None] * band_size
    small_order = (small_order + (jnp.arange(band_size) ^ spots[1])[None, :]).reshape(-1)
    small = small.reshape(2, dp_size // 2, band_size, small_share, model_width)
    small = small.transpose(1, 0, 2, 3, 4).reshape(-1, small_share, model_width)
    small = jnp.take(small, small_order, axis=0).reshape(row_total, model_width)
    own_blocks = []
    done = 0
    for rows in weight_rows:
        own_blocks.append(own_grads[done : done + rows])
        done += rows
    grad_qkv_own = jnp.concatenate(own_blocks[:3], axis=1)
    grad_out_own = own_blocks[3]
    grad_fc_in_own = jnp.concatenate(own_blocks[4:-1], axis=1)
    grad_fc_out_own = own_blocks[-1]
    grad_token, grad_attn, grad_gain_gen, grad_ff_first, grad_ff_second, grad_gen_bias = (
        generate_back(
            tail,
            gen_attn,
            gen_gain,
            gen_ff_in,
            gen_ff_out,
            gen_bias,
            gen_kept,
        )
    )

    small = small.astype(f32)
    sums_at = small.shape[0] - 16
    grad_pos_all = small[: pos_table.shape[0]]
    grad_gains = small[sums_at + 1 : sums_at + 3]
    grad_shifts = small[sums_at + 3 : sums_at + 5]
    grad_bias_all = small[sums_at + 8 : sums_at + 8 + hidden // model_width].reshape(-1)
    grad_patches = grad_patches.reshape(group_size, slot_count, bands_dev, pixel_count)
    return (
        result.reshape(local_images, slot_count, model_width),
        grad_patches,
        grad_token[0],
        grad_attn,
        grad_gain_gen,
        grad_ff_first,
        grad_ff_second,
        grad_gen_kernel,
        grad_gen_bias,
        grad_pos_all,
        grad_gains,
        grad_shifts,
        grad_qkv_own,
        grad_out_own,
        grad_fc_in_own,
        grad_bias_all,
        grad_fc_out_own,
    )


def solution(mesh):
    placed = (
        P("dp", None, "band", None),
        P(),
        P(),
        P(),
        P(),
        P(),
        P(None, ("dp", "band")),
        P(),
        P(),
        P(),
        P(),
        P(("dp", "band"), None),
        P(("dp", "band"), None),
        P(("dp", "band"), None),
        P(),
        P(("dp", "band"), None),
        P(),
        P(("dp", "band"), None),
        P(("dp", "band")),
        P(("dp", "band"), None, None),
    )
    return jax.shard_map(
        shards,
        mesh=mesh,
        in_specs=placed,
        out_specs=(
            P(("dp", "band"), None, None),
            P("dp", None, "band", None),
            P(),
            P(),
            P(),
            P(),
            P(),
            P(None, ("dp", "band")),
            P(),
            P(),
            P(),
            P(),
            P(("dp", "band"), None),
            P(("dp", "band"), None),
            P(("dp", "band"), None),
            P(),
            P(("dp", "band"), None),
        ),
        check_vma=False,
    )
```

```python
from functools import partial
import math

import jax
import jax.numpy as jnp
from jax import lax
from jax.experimental import pallas as pl
from jax.experimental.pallas import tpu as pltpu
from jax.sharding import PartitionSpec as P

HEADS = 12
HDIM = 64
GEN_HEADS = 4


def inner(left_arr, right_arr):
    return lax.dot_general(
        left_arr, right_arr, (((0,), (0,)), ((), ())), preferred_element_type=jnp.float32
    )


def times_transpose(left_arr, right_arr):
    return lax.dot_general(
        left_arr, right_arr, (((1,), (1,)), ((), ())), preferred_element_type=jnp.float32
    )


def bit_steps(size):
    steps = []
    step = 1
    while step < size:
        steps.append(step)
        step *= 2
    return steps


def swap(values, axis, step):
    size = lax.axis_size(axis)
    return lax.ppermute(values, axis, [(spot, spot ^ step) for spot in range(size)])


def turn(items, by):
    by = by % max(len(items), 1)
    return items[by:] + items[:by]


def gather_core(blocks):
    return [([key ^ 1 for key in keys], swap(block, "dp", 1)) for keys, block in blocks]


def place(blocks, axis, at):
    spot = lax.axis_index(axis)
    first = blocks[0][1]
    count = sum(len(keys) for keys, _ in blocks)
    shape = first.shape[1 : at + 1] + (count,) + first.shape[at + 1 :]
    whole = jnp.zeros(shape, first.dtype)
    for keys, block in blocks:
        for number, key in enumerate(keys):
            whole = lax.dynamic_update_index_in_dim(whole, block[number], spot ^ key, at)
    return whole


def add_low(left_arr, right_arr):
    return (left_arr.astype(jnp.float32) + right_arr.astype(jnp.float32)).astype(left_arr.dtype)


def split_half(values, at, step, left):
    left = sorted(left, reverse=True)
    shape = values.shape
    values = values.reshape(shape[:at] + (2,) * len(left) + shape[at + 1 :])
    dim = at + left.index(step)
    bit = (lax.axis_index("dp") // step) % 2
    rest = shape[:at] + (-1,) + shape[at + 1 :]
    send = lax.dynamic_index_in_dim(values, 1 - bit, dim, keepdims=False)
    keep = lax.dynamic_index_in_dim(values, bit, dim, keepdims=False)
    return send.reshape(rest), keep.reshape(rest)


def together(*arrays):
    return lax.optimization_barrier(arrays)


def column_blocks(matrix, width):
    return [matrix[:, spot : spot + width] for spot in range(0, matrix.shape[1], width)]


def run_kernel(body, args, in_specs, after=(), limit=60, **options):
    count = len(after)

    def whole(*refs):
        body(*refs[count:])

    return pl.pallas_call(
        whole,
        in_specs=[pl.BlockSpec(memory_space=pl.ANY)] * count + in_specs,
        compiler_params=pltpu.CompilerParams(vmem_limit_bytes=limit * 1024 * 1024),
        cost_estimate=pl.CostEstimate(flops=1000, bytes_accessed=1000, transcendentals=0),
        **options,
    )(*after, *args)


def dot_nn(left_arr, right_arr):
    return lax.dot_general(
        left_arr, right_arr, (((1,), (0,)), ((), ())), preferred_element_type=jnp.float32
    )


def norm_stats(values):
    center = values - jnp.mean(values, axis=-1, keepdims=True)
    spread = jnp.mean(center * center, axis=-1, keepdims=True)
    scale = lax.rsqrt(spread + 1e-06)
    return center * scale, scale


def norm_back(unit, scale, gain, grad):
    weighted = grad * gain
    first = jnp.mean(weighted, axis=-1, keepdims=True)
    second = jnp.mean(weighted * unit, axis=-1, keepdims=True)
    grad_values = (weighted - first - unit * second) * scale
    grad_gain = jnp.sum(grad * unit, axis=0, keepdims=True)
    grad_shift = jnp.sum(grad, axis=0, keepdims=True)
    return grad_values, grad_gain, grad_shift


def stash_spans(width, hidden):
    sizes = {
        "normed": width,
        "mixed": width,
        "normed_two": width,
        "act": hidden,
        "qkv_grad": 3 * width,
        "branch": width,
        "pre_grad": hidden,
        "cot": width,
        "small": width,
    }
    spans = {}
    first = 0
    for name, size in sizes.items():
        spans[name] = (first, size)
        first += size
    return spans


def block_body(part_count, tile_rows, ff_step, keys_lists, *refs):
    part_refs = refs[:part_count]
    weight_count = sum(len(keys_list) for keys_list in keys_lists)
    weight_refs = refs[part_count : part_count + weight_count]
    (
        spot_ref,
        base_ref,
        cot_ref,
        keep_ref,
        mask_ref,
        gain_ref,
        shift_ref,
        bias_ref,
        kept_ref,
        result_ref,
        embed_grad_ref,
        stash_hbm,
        sums_ref,
        qkv_w,
        out_w,
        fc_in_w,
        fc_out_w,
        qkv_ref,
        probs_ref,
        total_ref,
        back_ref,
        mixed_grad_ref,
        bias_grad_ref,
        stash_ref,
        sems,
        stash_sems,
    ) = refs[part_count + weight_count :]
    bf16 = jnp.bfloat16
    f32 = jnp.float32
    width = base_ref.shape[1]
    hidden = fc_in_w.shape[1]
    spans = stash_spans(width, hidden)
    views = {name: stash_ref.at[:, pl.ds(first, size)] for name, (first, size) in spans.items()}
    normed_ref = views["normed"]
    mixed_ref = views["mixed"]
    normed_two_ref = views["normed_two"]
    act_ref = views["act"]
    qkv_grad_ref = views["qkv_grad"]
    branch_ref = views["branch"]
    pre_grad_ref = views["pre_grad"]
    views["cot"][...] = cot_ref[...]
    leaving = []

    def leave(*names):
        for name in names:
            cols = pl.ds(*spans[name])
            copy = pltpu.make_async_copy(
                stash_ref.at[:, cols], stash_hbm.at[:, cols], stash_sems.at[len(leaving)]
            )
            copy.start()
            leaving.append(copy)

    leave("cot")
    share = width // sum(len(keys) for keys in keys_lists[0])
    targets = (
        [(qkv_w, column, share) for column in range(3)]
        + [(out_w, 0, share)]
        + [(fc_in_w, column, share) for column in range(hidden // width)]
        + [(fc_out_w, 0, share * hidden // width)]
    )
    copies = {}
    for number, (target_ref, column, rows) in enumerate(targets):
        half, first = (0, number * share) if number < 6 else (1, (number - 6) * share)
        half_refs = weight_refs[: len(keys_lists[0])] if half == 0 else weight_refs[len(keys_lists[0]) :]
        for keys, weight_ref in zip(keys_lists[half], half_refs):
            for index, key in enumerate(keys):
                at = pl.multiple_of(jnp.bitwise_xor(spot_ref[0], key) * rows, rows)
                copy = pltpu.make_async_copy(
                    weight_ref.at[index, pl.ds(first, rows), :],
                    target_ref.at[pl.ds(at, rows), pl.ds(column * width, width)],
                    sems.at[sum(len(some) for some in copies.values())],
                )
                copy.start()
                copies.setdefault(id(target_ref), []).append(copy)

    def arrive(target_ref):
        for copy in copies[id(target_ref)]:
            copy.wait()

    row_total, width = base_ref.shape
    tiles = row_total // tile_rows
    head_pairs = HEADS // 2
    lanes = 2 * HDIM

    start = base_ref[...]
    for part_ref in part_refs:
        start = start + part_ref[...].astype(f32)
    unit_one, scale_one = norm_stats(start)
    normed = (unit_one * gain_ref[0:1] + shift_ref[0:1]).astype(bf16)
    normed_ref[...] = normed
    arrive(qkv_w)
    for spot in range(3):
        cols = slice(spot * width, (spot + 1) * width)
        qkv_ref[:, cols] = dot_nn(normed, qkv_w[:, cols]).astype(bf16)

    low_lanes = lax.broadcasted_iota(jnp.int32, (tile_rows, lanes), 1) < HDIM

    def half(values, odd):
        keep = jnp.logical_not(low_lanes) if odd else low_lanes
        return jnp.where(keep, values, jnp.zeros_like(values))

    def head_slices(pair, tile):
        rows = pl.ds(tile * tile_rows, tile_rows)
        cols = [
            pl.ds(pl.multiple_of(which * width + pair * lanes, lanes), lanes) for which in range(3)
        ]
        return rows, cols

    def attend(pair, carry):
        for tile in range(tiles):
            rows, cols = head_slices(pair, tile)
            queries, keys_arr, values_arr = [qkv_ref[rows, col] for col in cols]
            mixed = jnp.zeros((tile_rows, lanes), f32)
            for odd in range(2):
                scores = times_transpose(half(queries, odd), keys_arr) * HDIM ** (-0.5)
                scores = scores + mask_ref[tile]
                exponent = jnp.exp(scores - jnp.max(scores, axis=-1, keepdims=True))
                probs = exponent * (1.0 / jnp.sum(exponent, axis=-1, keepdims=True))
                probs_ref[(pair * 2 + odd) * tiles + tile] = probs
                mixed = mixed + dot_nn(probs.astype(bf16), half(values_arr, odd))
            mixed_ref[rows, cols[0]] = mixed.astype(bf16)
        return carry

    lax.fori_loop(0, head_pairs, attend, 0, unroll=3)
    leave("normed", "mixed")
    arrive(out_w)
    middle = start + dot_nn(mixed_ref[...], out_w[...])
    unit_two, scale_two = norm_stats(middle)
    normed_two = (unit_two * gain_ref[1:2] + shift_ref[1:2]).astype(bf16)
    normed_two_ref[...] = normed_two
    total_ref[...] = middle
    back_ref[...] = jnp.zeros_like(back_ref)
    arrive(fc_in_w)
    arrive(fc_out_w)

    def feed(step, carry):
        cols = pl.ds(pl.multiple_of(step * ff_step, ff_step), ff_step)
        pre = dot_nn(normed_two_ref[...], fc_in_w[:, cols]) + bias_ref[:, cols]
        cdf = 0.5 * (1.0 + lax.erf(pre * 0.5**0.5))
        act = (pre * cdf).astype(bf16)
        act_ref[:, cols] = act
        slope = cdf + pre * (jnp.exp(-0.5 * pre * pre) * (2.0 * math.pi) ** (-0.5))
        pre_grad = slope * times_transpose(cot_ref[...], fc_out_w[cols, :])
        pre_grad = pre_grad.astype(bf16)
        pre_grad_ref[:, cols] = pre_grad
        bias_grad_ref[:, cols] = jnp.sum(pre_grad.astype(f32), axis=0, keepdims=True)
        total_ref[...] += dot_nn(act, fc_out_w[cols, :])
        back_ref[...] += times_transpose(pre_grad, fc_in_w[:, cols])
        return carry

    lax.fori_loop(0, fc_in_w.shape[1] // ff_step, feed, 0)
    leave("normed_two", "act", "pre_grad")
    result_ref[...] = (total_ref[...] * keep_ref[...]).astype(bf16)
    grad_norm, gain_two, shift_two = norm_back(unit_two, scale_two, gain_ref[1:2], back_ref[...])
    grad_middle = cot_ref[...].astype(f32) + grad_norm
    grad_branch = grad_middle.astype(bf16)
    branch_ref[...] = grad_branch
    mixed_grad_ref[...] = times_transpose(grad_branch, out_w[...]).astype(bf16)

    def attend_back(pair, carry):
        for tile in range(tiles):
            rows, cols = head_slices(pair, tile)
            queries, keys_arr, values_arr = [qkv_ref[rows, col] for col in cols]
            grad_mixed = mixed_grad_ref[rows, cols[0]]
            grads = [jnp.zeros((tile_rows, lanes), f32) for _ in range(3)]
            for odd in range(2):
                probs = probs_ref[(pair * 2 + odd) * tiles + tile]
                own_grad = half(grad_mixed, odd)
                grad_probs = times_transpose(own_grad, values_arr)
                grad_scores = probs * (
                    grad_probs - jnp.sum(grad_probs * probs, axis=-1, keepdims=True)
                )
                grad_scores = grad_scores.astype(bf16)
                grads[0] = grads[0] + dot_nn(grad_scores, half(keys_arr, odd))
                grads[1] = grads[1] + inner(grad_scores, half(queries, odd))
                grads[2] = grads[2] + inner(probs.astype(bf16), own_grad)
            for which, factor in enumerate((HDIM ** (-0.5), HDIM ** (-0.5), 1.0)):
                qkv_grad_ref[rows, cols[which]] = (grads[which] * factor).astype(bf16)
        return carry

    lax.fori_loop(0, head_pairs, attend_back, 0, unroll=3)
    leave("branch", "qkv_grad")
    back = jnp.zeros((row_total, width), f32)
    for spot in range(3):
        cols = slice(spot * width, (spot + 1) * width)
        back = back + times_transpose(qkv_grad_ref[:, cols], qkv_w[:, cols])
    grad_norm, gain_one, shift_one = norm_back(unit_one, scale_one, gain_ref[0:1], back)
    grad_start = grad_middle + grad_norm
    embed_grad_ref[...] = grad_start.astype(bf16)
    sums = jnp.concatenate(
        [jnp.sum(grad_start, axis=0, keepdims=True), gain_one, gain_two, shift_one, shift_two]
        + [jnp.zeros((3, width), f32)],
        axis=0,
    )
    sums_ref[...] = sums
    small_ref = views["small"]
    positions = small_ref.shape[0] - 16
    spots_at = lax.broadcasted_iota(jnp.int32, (positions, row_total), 0)
    one_hot = jnp.where(spots_at == kept_ref[...], 1.0, 0.0).astype(bf16)
    by_position = dot_nn(one_hot, grad_start.astype(bf16))
    cuts = [bias_grad_ref[:, spot : spot + width] for spot in range(0, hidden, width)]
    cuts.append(jnp.zeros((8 - len(cuts), width), f32))
    small_ref[...] = jnp.concatenate([by_position, sums, *cuts], axis=0).astype(bf16)
    leave("small")
    for copy in leaving:
        copy.wait()


def block(parts, weight_halves, spots, base, cot, keep, mask, gains, shifts, bias, kept):
    row_total, width = base.shape
    tile_rows = mask.shape[1]
    hidden = bias.shape[1]
    bf16 = jnp.bfloat16
    f32 = jnp.float32
    keys_lists = [[keys for keys, _ in blocks] for blocks in weight_halves]
    weight_args = [block for blocks in weight_halves for _, block in blocks]
    pieces = sum(len(keys) for keys in keys_lists[0])
    inside = pl.BlockSpec(memory_space=pltpu.VMEM)
    outside = pl.BlockSpec(memory_space=pl.ANY)
    rows = (row_total, width)
    shapes = [
        (rows, bf16),
        (rows, bf16),
        ((row_total, sum(stash_spans(width, hidden)["small"])), bf16),
        ((8, width), f32),
    ]
    return run_kernel(
        partial(block_body, len(parts), tile_rows, width, keys_lists),
        (*parts, *weight_args, spots, base, cot, keep, mask, gains, shifts, bias, kept),
        [inside] * len(parts)
        + [outside] * len(weight_args)
        + [pl.BlockSpec(memory_space=pltpu.SMEM)]
        + [inside] * 8,
        out_shape=[jax.ShapeDtypeStruct(shape, kind) for shape, kind in shapes],
        out_specs=[inside, inside, outside, inside],
        scratch_shapes=[
            pltpu.VMEM((width, 3 * width), bf16),
            pltpu.VMEM((width, width), bf16),
            pltpu.VMEM((width, hidden), bf16),
            pltpu.VMEM((hidden, width), bf16),
            pltpu.VMEM((row_total, 3 * width), bf16),
            pltpu.VMEM((HEADS * row_total // tile_rows, tile_rows, tile_rows), f32),
            pltpu.VMEM(rows, f32),
            pltpu.VMEM(rows, f32),
            pltpu.VMEM(rows, bf16),
            pltpu.VMEM((1, hidden), f32),
            pltpu.VMEM((row_total, sum(stash_spans(width, hidden)["small"])), bf16),
            pltpu.SemaphoreType.DMA(((5 + hidden // width) * pieces,)),
            pltpu.SemaphoreType.DMA((len(stash_spans(width, hidden)),)),
        ],
    )


def dot_full(left_arr, right_arr, left_dim=1, right_dim=0):
    return lax.dot_general(
        left_arr,
        right_arr,
        (((left_dim,), (right_dim,)), ((), ())),
        precision=lax.Precision.HIGH,
        preferred_element_type=jnp.float32,
    )


def head_part(values, head):
    size = values.shape[1] // GEN_HEADS
    lane = lax.broadcasted_iota(jnp.int32, values.shape, 1)
    inside = jnp.logical_and(lane >= head * size, lane < (head + 1) * size)
    return jnp.where(inside, values, 0.0)


def generate_body(
    waves_ref,
    token_ref,
    attn_hbm,
    gain_hbm,
    ff_in_hbm,
    ff_out_hbm,
    bias_w_hbm,
    columns_hbm,
    *refs,
):
    *kernel_refs, embed_bias_ref, low_ref, states_ref, rows_ref, weights_ref, pre_ref, scales_ref = refs[:-8]
    attn_ref, gain_ref, ff_in_ref, ff_out_ref, bias_w_ref, columns_ref, hold_ref, sems = refs[-8:]
    f32 = jnp.float32
    copies = [
        pltpu.make_async_copy(source, target, sems.at[number])
        for number, (source, target) in enumerate(
            (
                (attn_hbm, attn_ref),
                (gain_hbm, gain_ref),
                (ff_in_hbm, ff_in_ref),
                (ff_out_hbm, ff_out_ref),
                (columns_hbm, columns_ref),
                (bias_w_hbm, bias_w_ref),
            )
        )
    ]
    for copy in copies:
        copy.start()
    bands = waves_ref.shape[1]
    width = token_ref.shape[1]
    padded = rows_ref.shape[1]
    square = (bands, bands)
    diagonal = lax.broadcasted_iota(jnp.int32, square, 0) == lax.broadcasted_iota(
        jnp.int32, square, 1
    )
    waves = jnp.broadcast_to(waves_ref[...].astype(f32), square)
    column = jnp.sum(jnp.where(diagonal, waves, 0.0), axis=1, keepdims=True)
    lane = lax.broadcasted_iota(jnp.int32, (bands, width), 1)
    half_width = width // 2
    number = jnp.where(lane < half_width, lane, lane - half_width).astype(f32)
    angles = column * jnp.exp(number * (-math.log(10000.0) / half_width))
    wave = jnp.where(lane < half_width, jnp.sin(angles), jnp.cos(angles))
    sequence = jnp.concatenate(
        [wave, token_ref[...].astype(f32), jnp.zeros((padded - bands - 1, width), f32)], axis=0
    )
    rows_ref[0] = sequence
    copies[0].wait()
    copies[1].wait()
    for which in range(3):
        rows_ref[1 + which] = dot_full(sequence, attn_ref[which].astype(f32))
    queries = rows_ref[1]
    keys_arr = rows_ref[2]
    values_arr = rows_ref[3]
    key_spot = lax.broadcasted_iota(jnp.int32, (padded, padded), 1)
    mixed = jnp.zeros((padded, width), f32)
    for head in range(GEN_HEADS):
        scores = dot_full(head_part(queries, head), keys_arr, 1, 1)
        scores = scores * (1.0 / math.sqrt(width // GEN_HEADS))
        scores = jnp.where(key_spot <= bands, scores, -1e30)
        exponent = jnp.exp(scores - jnp.max(scores, axis=-1, keepdims=True))
        weights = exponent / jnp.sum(exponent, axis=-1, keepdims=True)
        weights_ref[head] = weights
        mixed = mixed + dot_full(weights, head_part(values_arr, head))
    rows_ref[4] = mixed
    unit_one, scale_one = norm_stats(sequence + dot_full(mixed, attn_ref[3].astype(f32)))
    rows_ref[5] = unit_one
    first = unit_one * gain_ref[0:1].astype(f32)
    copies[2].wait()
    pre = dot_full(first, ff_in_ref[...].astype(f32))
    pre_ref[...] = pre
    hidden = pre * (0.5 * (1.0 + lax.erf(pre * 0.5**0.5)))
    copies[3].wait()
    unit_two, scale_two = norm_stats(first + dot_full(hidden, ff_out_ref[...].astype(f32)))
    rows_ref[6] = unit_two
    states = unit_two * gain_ref[1:2].astype(f32)
    states_ref[...] = states
    scales_ref[0] = jnp.broadcast_to(scale_one, (padded, width))
    scales_ref[1] = jnp.broadcast_to(scale_two, (padded, width))
    low = states[:bands].astype(jnp.bfloat16)
    low_ref[...] = low
    features = hold_ref.shape[2]
    part_bands = kernel_refs[0].shape[1]
    copies[4].wait()
    for pixel in range(hold_ref.shape[0]):
        cols = slice(pixel * features, (pixel + 1) * features)
        hold_ref[pixel] = dot_nn(low, columns_ref[:, cols]).astype(jnp.bfloat16)
        for key, kernel_ref in enumerate(kernel_refs):
            first = 0
            if len(kernel_refs) > 1:
                first = jnp.bitwise_xor(lax.axis_index("band"), key) * part_bands
                first = pl.multiple_of(first, part_bands)
            kernel_ref[pixel] = hold_ref[pixel, pl.ds(first, part_bands), :]
    copies[5].wait()
    token_state = states[bands : bands + 8]
    embed_bias_ref[...] = dot_full(token_state, bias_w_ref[...].astype(f32))


def generate_fast(parts, wavelengths, token, gen_attn, gen_gain, ff_in, ff_out, gen_bias, columns):
    f32 = jnp.float32
    bf16 = jnp.bfloat16
    bands = wavelengths.shape[0]
    width = token.shape[0]
    padded = -(-(bands + 1) // 8) * 8
    features = gen_bias.shape[1]
    shapes = [
        ((8, features), f32),
        ((bands, width), bf16),
        ((padded, width), f32),
        ((7, padded, width), f32),
        ((GEN_HEADS, padded, padded), f32),
        ((padded, ff_in.shape[1]), f32),
        ((2, padded, width), f32),
    ]
    pixels = columns.shape[1] // features
    shapes = [((pixels, bands // parts, features), bf16)] * parts + shapes
    inside = pl.BlockSpec(memory_space=pltpu.VMEM)
    outside = pl.BlockSpec(memory_space=pl.ANY)
    weights = (gen_attn, gen_gain, ff_in, ff_out, gen_bias, columns)
    return run_kernel(
        generate_body,
        (wavelengths[None], token[None], *weights),
        out_shape=[jax.ShapeDtypeStruct(shape, kind) for shape, kind in shapes],
        in_specs=[inside] * 2 + [outside] * 6,
        out_specs=[inside] * len(shapes),
        scratch_shapes=[pltpu.VMEM(weight.shape, bf16) for weight in weights]
        + [
            pltpu.VMEM((pixels, bands, features), bf16),
            pltpu.SemaphoreType.DMA((6,)),
        ],
    )


def generate_back_body(
    tail_ref,
    attn_ref,
    gain_ref,
    ff_in_ref,
    ff_out_ref,
    bias_w_ref,
    states_ref,
    rows_ref,
    weights_ref,
    pre_ref,
    scales_ref,
    token_out,
    attn_out,
    gain_out,
    ff_in_out,
    ff_out_out,
    bias_out,
):
    f32 = jnp.float32
    padded, width = states_ref.shape
    features = bias_w_ref.shape[1]
    bands = padded - 8
    head_scale = 1.0 / math.sqrt(width // GEN_HEADS)
    cuts = [tail_ref[bands + spot : bands + spot + 1, :] for spot in range(features // width)]
    bias_grad = jnp.concatenate(cuts, axis=1)
    bias_grad = jnp.concatenate([bias_grad, jnp.zeros((7, features), f32)], axis=0)
    row_spot = lax.broadcasted_iota(jnp.int32, (padded - bands, width), 0)
    token_grad = dot_full(bias_grad, bias_w_ref[...].astype(f32), 1, 1)
    token_grad = jnp.where(row_spot == 0, token_grad[0:1], 0.0)
    grad_states = jnp.concatenate([tail_ref[:bands, :], token_grad], axis=0)
    token_state = states_ref[bands : bands + 8]
    first_row = lax.broadcasted_iota(jnp.int32, token_state.shape, 0) == 0
    bias_out[...] = dot_full(jnp.where(first_row, token_state, 0.0), bias_grad, 0, 0)
    unit_one = rows_ref[5]
    gain_one = gain_ref[0:1].astype(f32)
    gain_two = gain_ref[1:2].astype(f32)
    grad_two, gain_two_grad, _ = norm_back(rows_ref[6], scales_ref[1], gain_two, grad_states)
    pre = pre_ref[...]
    cdf = 0.5 * (1.0 + lax.erf(pre * 0.5**0.5))
    ff_out_out[...] = dot_full(pre * cdf, grad_two, 0, 0)
    slope = cdf + pre * (jnp.exp(-0.5 * pre * pre) * (2.0 * math.pi) ** (-0.5))
    grad_pre = slope * dot_full(grad_two, ff_out_ref[...].astype(f32), 1, 1)
    ff_in_out[...] = dot_full(unit_one * gain_one, grad_pre, 0, 0)
    grad_first = grad_two + dot_full(grad_pre, ff_in_ref[...].astype(f32), 1, 1)
    grad_one, gain_one_grad, _ = norm_back(unit_one, scales_ref[0], gain_one, grad_first)
    gain_out[...] = jnp.concatenate([gain_one_grad, gain_two_grad], axis=0)
    attn_out[3] = dot_full(rows_ref[4], grad_one, 0, 0)
    grad_mixed = dot_full(grad_one, attn_ref[3].astype(f32), 1, 1)
    sequence = rows_ref[0]
    queries = rows_ref[1]
    keys_arr = rows_ref[2]
    values_arr = rows_ref[3]
    grads = [jnp.zeros((padded, width), f32) for _ in range(3)]
    for head in range(GEN_HEADS):
        weights = weights_ref[head]
        own_grad = head_part(grad_mixed, head)
        grad_weights = dot_full(own_grad, values_arr, 1, 1)
        grad_scores = weights * (
            grad_weights - jnp.sum(grad_weights * weights, axis=-1, keepdims=True)
        )
        grad_scores = grad_scores * head_scale
        grads[0] = grads[0] + dot_full(grad_scores, head_part(keys_arr, head))
        grads[1] = grads[1] + dot_full(grad_scores, head_part(queries, head), 0, 0)
        grads[2] = grads[2] + dot_full(weights, own_grad, 0, 0)
    grad_sequence = grad_one
    for which in range(3):
        attn_out[which] = dot_full(sequence, grads[which], 0, 0)
        grad_sequence = grad_sequence + dot_full(
            grads[which], attn_ref[which].astype(f32), 1, 1
        )
    token_out[...] = grad_sequence[bands : bands + 1]


def generate_back(tail, gen_attn, gen_gain, ff_in, ff_out, gen_bias, kept_arrs):
    f32 = jnp.float32
    width = gen_gain.shape[1]
    shapes = [
        (1, width),
        gen_attn.shape,
        gen_gain.shape,
        ff_in.shape,
        ff_out.shape,
        gen_bias.shape,
    ]
    inside = pl.BlockSpec(memory_space=pltpu.VMEM)
    return run_kernel(
        generate_back_body,
        (tail, gen_attn, gen_gain, ff_in, ff_out, gen_bias, *kept_arrs),
        out_shape=[jax.ShapeDtypeStruct(shape, f32) for shape in shapes],
        in_specs=[inside] * (6 + len(kept_arrs)),
        out_specs=[inside] * len(shapes),
    )


def fill_kernel(keys_lists, piece_refs, spot, mat_ref, bands, pixels):
    for keys, piece_ref in zip(keys_lists, piece_refs):
        for number, key in enumerate(keys):
            share = piece_ref.shape[2]
            first = jnp.bitwise_xor(spot, key) * share
            for band in range(bands):
                rows = pl.ds(pl.multiple_of(band * pixels + first, share), share)
                mat_ref[rows, :] = piece_ref[number, band]


def fill_step(keys_lists, piece_refs, spot, mat_ref, band_step, group_steps):
    pixels = mat_ref.shape[0] // band_step
    step = pl.program_id(0)
    used = 0
    for group, keys_list in enumerate(keys_lists):
        group_refs = piece_refs[used : used + len(keys_list)]
        used += len(keys_list)

        @pl.when(step // group_steps == group)
        def _(keys_list=keys_list, group_refs=group_refs):
            fill_kernel(keys_list, group_refs, spot, mat_ref, band_step, pixels)


def embed_body(keys_lists, group_steps, band_step, *refs):
    spot_ref, patch_ref = refs[:2]
    count = sum(len(keys_list) for keys_list in keys_lists)
    piece_refs = refs[2 : 2 + count]
    *out_refs, mat_ref, total_ref = refs[2 + count :]
    step = pl.program_id(0)
    fill_step(keys_lists, piece_refs, spot_ref[0], mat_ref, band_step, group_steps)

    @pl.when(step == 0)
    def _():
        total_ref[...] = jnp.zeros_like(total_ref)

    total_ref[...] += dot_nn(patch_ref[...], mat_ref[...])

    @pl.when(step == pl.num_programs(0) - 1)
    def _():
        for key, out_ref in enumerate(out_refs):
            rows = out_ref.shape[0]
            first = pl.multiple_of(jnp.bitwise_xor(spot_ref[1], key) * rows, rows)
            out_ref[...] = total_ref[pl.ds(first, rows), :].astype(out_ref.dtype)


def group_band_count(kernel_groups):
    return min(block.shape[1] for blocks in kernel_groups for _, block in blocks)


def piece_specs(kernel_groups, band_step, first_group=0):
    group_steps = group_band_count(kernel_groups) // band_step
    specs = []
    arrays = []
    for group, blocks in enumerate(kernel_groups):
        for keys, block in blocks:
            whole = block.shape[1] > group_steps * band_step
            first = group * group_steps
            skip = first_group * group_steps

            def pick(step, first=first, whole=whole):
                here = jnp.clip(step - first, 0, group_steps - 1)
                return (0, here + first + skip if whole else here, 0, 0)

            specs.append(pl.BlockSpec((len(keys), band_step) + block.shape[2:], pick))
            arrays.append(block)
    keys_lists = [[keys for keys, _ in blocks] for blocks in kernel_groups]
    return specs, arrays, keys_lists, group_steps


def embed_share(spots, patch_rows, kernel_groups, owners):
    row_total = patch_rows.shape[0]
    blocks = kernel_groups[0]
    group_bands = group_band_count(kernel_groups)
    width = blocks[0][1].shape[3]
    pixels = sum(len(keys) for keys, _ in blocks) * blocks[0][1].shape[2]
    band_step = min(4, group_bands)
    depth = band_step * pixels
    specs, arrays, keys_lists, group_steps = piece_specs(kernel_groups, band_step)
    rows = row_total // owners
    return run_kernel(
        partial(embed_body, keys_lists, group_steps, band_step),
        [spots, patch_rows, *arrays],
        [
            pl.BlockSpec(memory_space=pltpu.SMEM),
            pl.BlockSpec((row_total, depth), lambda step: (0, step)),
        ]
        + specs,
        limit=63,
        grid=(group_steps * len(kernel_groups),),
        out_shape=[jax.ShapeDtypeStruct((rows, width), jnp.bfloat16)] * owners,
        out_specs=[pl.BlockSpec((rows, width), lambda step: (0, 0))] * owners,
        scratch_shapes=[
            pltpu.VMEM((depth, width), jnp.bfloat16),
            pltpu.VMEM((row_total, width), jnp.float32),
        ],
    )


def kernel_grad_body(dp_size, band_step, *refs):
    spot_ref, patch_ref = refs[:2]
    *grad_refs, send_ref, keep_ref, hold_ref = refs[2:]
    rows = grad_refs[0].shape[0]
    total = 0.0
    for key, grad_ref in enumerate(grad_refs):
        first = pl.multiple_of(jnp.bitwise_xor(spot_ref[1], key) * rows, rows)
        total = total + inner(patch_ref[pl.ds(first, rows), :], grad_ref[...])
    hold_ref[...] = total.astype(hold_ref.dtype)
    pixels = hold_ref.shape[0] // band_step
    share = pixels // dp_size
    core = lax.rem(spot_ref[0], 2)
    for band in range(band_step):
        for chip in range(dp_size // 2):
            base = band * pixels + chip * 2 * share
            kept = pl.multiple_of(base + core * share, share)
            keep_ref[band, chip] = hold_ref[pl.ds(kept, share), :]
            sent = pl.multiple_of(base + (1 - core) * share, share)
            send_ref[band, chip] = hold_ref[pl.ds(sent, share), :]


def kernel_grad_part(spots, patch_rows, grads, first_band, group_bands, bands_dev, dp_size, after):
    row_total = patch_rows.shape[0]
    width = grads[0].shape[1]
    band_step = min(4, group_bands)
    pixels = patch_rows.shape[1] // bands_dev
    depth = band_step * pixels
    offset = first_band // band_step
    share = pixels // dp_size
    chips = (dp_size // 2, share, width)
    steps = group_bands // band_step
    block = (band_step,) + chips
    return run_kernel(
        partial(kernel_grad_body, dp_size, band_step),
        (spots, patch_rows, *grads),
        after=after,
        limit=63,
        grid=(steps,),
        out_shape=[
            jax.ShapeDtypeStruct((bands,) + chips, jnp.bfloat16)
            for bands in (group_bands, group_bands)
        ],
        in_specs=[
            pl.BlockSpec(memory_space=pltpu.SMEM),
            pl.BlockSpec((row_total, depth), lambda step: (0, offset + step)),
        ]
        + [pl.BlockSpec(grad.shape, lambda step: (0, 0)) for grad in grads],
        out_specs=[
            pl.BlockSpec(block, lambda step: (step, 0, 0, 0)),
            pl.BlockSpec(block, lambda step: (step, 0, 0, 0)),
        ],
        scratch_shapes=[pltpu.VMEM((depth, width), jnp.bfloat16)],
    )


def patch_grad_body(keys_lists, grad_count, group_steps, band_step, *refs):
    spot_ref = refs[0]
    grad_refs = refs[1 : 1 + grad_count]
    out_ref, mat_ref = refs[-2:]
    piece_refs = refs[1 + grad_count : -2]
    fill_step(keys_lists, piece_refs, spot_ref[0], mat_ref, band_step, group_steps)
    for key, grad_ref in enumerate(grad_refs):
        rows = grad_ref.shape[0]
        first = pl.multiple_of(jnp.bitwise_xor(spot_ref[1], key) * rows, rows)
        out_ref[pl.ds(first, rows), :] = times_transpose(grad_ref[...], mat_ref[...]).astype(
            out_ref.dtype
        )


def patch_grad(spots, grads, kernel_groups, pixels, first_group, after):
    rows, width = grads[0].shape
    row_total = rows * len(grads)
    band_step = min(4, group_band_count(kernel_groups))
    depth = band_step * pixels
    specs, arrays, keys_lists, group_steps = piece_specs(kernel_groups, band_step, first_group)
    steps = group_steps * len(kernel_groups)
    return run_kernel(
        partial(patch_grad_body, keys_lists, len(grads), group_steps, band_step),
        [spots, *grads, *arrays],
        [pl.BlockSpec(memory_space=pltpu.SMEM)]
        + [pl.BlockSpec(grad.shape, lambda step: (0, 0)) for grad in grads]
        + specs,
        after=after,
        limit=63,
        grid=(steps,),
        out_shape=jax.ShapeDtypeStruct((row_total, steps * depth), jnp.bfloat16),
        out_specs=pl.BlockSpec((row_total, depth), lambda step: (0, step)),
        scratch_shapes=[pltpu.VMEM((depth, width), jnp.bfloat16)],
    )


def states_grad_body(batches, low_ref, columns_ref, *refs):
    *piece_refs, sums_ref, spot_ref, grad_ref, part_ref, hold_ref = refs
    pixels, bands, width = piece_refs[0].shape
    for number, piece_ref in enumerate(piece_refs):
        key, batch = divmod(number, batches)
        first = (jnp.bitwise_xor(spot_ref[1], key) * batches + batch) * bands
        hold_ref[:, pl.ds(pl.multiple_of(first, bands), bands), :] = piece_ref[...]
    total = 0.0
    for pixel in range(pixels):
        cols = slice(pixel * width, (pixel + 1) * width)
        grads = hold_ref[pixel]
        grad_ref[:, cols] = inner(low_ref[...], grads)
        total = total + times_transpose(grads, columns_ref[:, cols])
    bands, states = total.shape
    part_ref[:bands, :] = total
    rows = [sums_ref[0:1, spot : spot + states] for spot in range(0, width, states)]
    rows.append(jnp.zeros((part_ref.shape[0] - bands - len(rows), states), jnp.float32))
    part_ref[bands:, :] = jnp.concatenate(rows, axis=0)


def states_grad(spots, low, columns, pieces, sums):
    pixels, bands, width = pieces[0].shape
    tail_rows = low.shape[0] + -(-width // low.shape[1] // 8) * 8
    if bands % 16:
        blocks = [([key], piece[None]) for key, piece in enumerate(pieces)]
        whole = place(blocks, "band", 1).reshape(pixels, -1, width)
        grads = whole.transpose(1, 0, 2).reshape(low.shape[0], -1)
        rows = [times_transpose(grads, columns), sums[0].reshape(-1, low.shape[1])]
        tail = jnp.concatenate(rows, axis=0)
        tail = jnp.pad(tail, ((0, tail_rows - tail.shape[0]), (0, 0)))
        return inner(low, grads), tail
    inside = pl.BlockSpec(memory_space=pltpu.VMEM)
    return run_kernel(
        partial(states_grad_body, 1),
        (low, columns, *pieces, sums, spots),
        out_shape=[
            jax.ShapeDtypeStruct(columns.shape, jnp.float32),
            jax.ShapeDtypeStruct((tail_rows, low.shape[1]), jnp.float32),
        ],
        in_specs=[inside] * (3 + len(pieces)) + [pl.BlockSpec(memory_space=pltpu.SMEM)],
        out_specs=[inside, inside],
        scratch_shapes=[pltpu.VMEM((pixels, bands * len(pieces), width), jnp.bfloat16)],
    )


def flatten_body(in_ref, out_ref):
    out_ref[...] = in_ref[...].reshape(out_ref.shape)


def unflatten_body(*refs):
    *in_refs, out_ref = refs
    done = 0
    for in_ref in in_refs:
        part = in_ref[...]
        bands = part.shape[1] // out_ref.shape[2]
        out_ref[:, done : done + bands, :] = part.reshape(-1, bands, out_ref.shape[2])
        done += bands


def flatten_rows(cube, after):
    rows, bands, pixels = cube.shape
    step_rows = 64
    return run_kernel(
        flatten_body,
        (cube,),
        [pl.BlockSpec((step_rows, bands, pixels), lambda step: (step, 0, 0))],
        after=after,
        grid=(rows // step_rows,),
        out_shape=jax.ShapeDtypeStruct((rows, bands * pixels), cube.dtype),
        out_specs=pl.BlockSpec((step_rows, bands * pixels), lambda step: (step, 0)),
    )


def unflatten_rows(flats, bands, after):
    rows = flats[0].shape[0]
    pixels = sum(flat.shape[1] for flat in flats) // bands
    step_rows = 64
    return run_kernel(
        unflatten_body,
        flats,
        [pl.BlockSpec((step_rows, flat.shape[1]), lambda step: (step, 0)) for flat in flats],
        after=after,
        limit=63,
        grid=(rows // step_rows,),
        out_shape=jax.ShapeDtypeStruct((rows, bands, pixels), flats[0].dtype),
        out_specs=pl.BlockSpec((step_rows, bands, pixels), lambda step: (step, 0, 0)),
    )


def stack_body(*refs):
    *part_refs, out_ref, hold_ref = refs
    width = out_ref.shape[1]
    first = 0
    for part_ref in part_refs:
        rows = part_ref.shape[0]
        for spot in range(0, part_ref.shape[1], width):
            hold_ref[pl.ds(first, rows), :] = part_ref[:, spot : spot + width].astype(jnp.float32)
            first += rows
    out_ref[...] = hold_ref[...].astype(out_ref.dtype)


def stack_weights(shards_in):
    width = shards_in[-1].shape[1]
    if any(shard.shape[0] % 8 for shard in shards_in):
        return jnp.concatenate(
            [part for shard in shards_in for part in column_blocks(shard, width)], axis=0
        )
    row_total = sum(shard.size for shard in shards_in) // width
    inside = pl.BlockSpec(memory_space=pltpu.VMEM)
    return run_kernel(
        stack_body,
        shards_in,
        [inside] * len(shards_in),
        out_shape=jax.ShapeDtypeStruct((row_total, width), shards_in[0].dtype),
        out_specs=inside,
        scratch_shapes=[pltpu.VMEM((row_total, width), jnp.float32)],
    )


def plane_body(block_rows, spot_ref, *refs):
    *stack_refs, first_ref, last_ref, hold_ref = refs
    band_size = len(stack_refs)
    for key, stack_ref in enumerate(stack_refs):
        owner = jnp.bitwise_xor(spot_ref[1], key)
        values = stack_ref[...].astype(jnp.float32)
        done = 0
        for rows in block_rows:
            at = pl.multiple_of(done * band_size + owner * rows, 8)
            hold_ref[pl.ds(at, rows), :] = values[done : done + rows]
            done += rows
    half = first_ref.shape[0]
    first_ref[...] = hold_ref[:half, :].astype(first_ref.dtype)
    last_ref[...] = hold_ref[half:, :].astype(last_ref.dtype)


def plane_weights(spots, stacks, block_rows):
    row_total, width = stacks[0].shape
    band_size = len(stacks)
    half = row_total * band_size // 2
    if any(rows % 8 for rows in block_rows):
        whole = place([([key], stack[None]) for key, stack in enumerate(stacks)], "band", 0)
        parts = []
        done = 0
        for rows in block_rows:
            parts.append(whole[:, done : done + rows].reshape(-1, width))
            done += rows
        merged = jnp.concatenate(parts, axis=0)
        return merged[:half], merged[half:]
    inside = pl.BlockSpec(memory_space=pltpu.VMEM)
    return run_kernel(
        partial(plane_body, block_rows),
        (spots, *stacks),
        [pl.BlockSpec(memory_space=pltpu.SMEM)] + [inside] * band_size,
        out_shape=[jax.ShapeDtypeStruct((half, width), stacks[0].dtype)] * 2,
        out_specs=[inside] * 2,
        scratch_shapes=[pltpu.VMEM((row_total * band_size, width), jnp.float32)],
    )


def weight_grad_body(dp_size, parts, hidden, spot_ref, own_ref, other_ref, *refs):
    *out_refs, turned_ref, hold_ref, feed_ref, small_ref, sems = refs
    width = hold_ref.shape[2]
    row_total = own_ref.shape[0]
    spans = stash_spans(width, hidden)
    share = width // dp_size
    chips = dp_size // 2
    core = lax.rem(spot_ref[0], 2)
    copies = []

    def view(name, column=0, size=None):
        first, whole = spans[name]
        first = first + column * width
        return [ref[:, first : first + (size or whole)] for ref in (own_ref, other_ref)]

    def turn_rows(name, at):
        first, size = spans[name]
        for spot in range(0, size, width):
            for number, ref in enumerate((own_ref, other_ref)):
                cols = slice(number * row_total, (number + 1) * row_total)
                turned = ref[:, first + spot : first + spot + width].T
                turned_ref[at + spot : at + spot + width, cols] = turned

    def pick(at, rows):
        parts = []
        for chip in range(chips):
            first = at + (chip * 2 + core) * rows
            parts.append(turned_ref[pl.ds(pl.multiple_of(first, 16), rows), :])
        return jnp.concatenate(parts, axis=0)

    def send(source_ref, rows, number, stride=None):
        part = [number in numbers for _, numbers in parts].index(True)
        first_step, numbers = parts[part]
        first = share * numbers.index(number)
        step = first_step // 2
        bit = lax.rem(lax.div(spot_ref[0], first_step), 2)
        for index in range(chips // 2):
            for which in range(2):
                own_bit = bit if which == 0 else 1 - bit
                chip = index // step * 2 * step + own_bit * step + index % step
                at = chip * (stride or rows)
                copy = pltpu.make_async_copy(
                    source_ref.at[pl.ds(pl.multiple_of(at, 16), rows), :],
                    out_refs[part * 2 + which].at[index, pl.ds(first, rows), :],
                    sems.at[len(copies)],
                )
                copy.start()
                copies.append(copy)

    def product(left, names, column):
        right = view(names, column, width)
        total = dot_nn(left[:, :row_total], right[0])
        return total + dot_nn(left[:, row_total:], right[1])

    blocks = (
        [("normed", "qkv_grad", column) for column in range(3)]
        + [("mixed", "branch", 0)]
        + [("normed_two", "pre_grad", column) for column in range(hidden // width)]
    )
    turned_at = {"normed": 0, "mixed": width, "normed_two": 2 * width, "act": 3 * width}
    picked = {}
    for number, (left, right, column) in enumerate(blocks):
        if left not in picked:
            turn_rows(left, turned_at[left])
            picked = {left: pick(turned_at[left], share)}
        hold_ref[number] = product(picked[left], right, column).astype(hold_ref.dtype)
        send(hold_ref.at[number], share, number)
    small = sum(part.astype(jnp.float32) for part in view("small"))
    small_ref[...] = small.astype(small_ref.dtype)
    small_share = row_total // dp_size
    turn_rows("act", turned_at["act"])
    feed_rows = hidden // dp_size
    for chip in range(chips):
        at = turned_at["act"] + (chip * 2 + core) * feed_rows
        left = turned_ref[pl.ds(pl.multiple_of(at, 16), feed_rows), :]
        feed_ref[chip * feed_rows : (chip + 1) * feed_rows, :] = product(left, "cot", 0).astype(
            feed_ref.dtype
        )
    send(feed_ref, feed_rows, len(blocks))
    own_small = small_ref.at[pl.ds(pl.multiple_of(core * small_share, 16), (dp_size - 1) * small_share), :]
    send(own_small, small_share, len(blocks) + 1, 2 * small_share)
    for copy in copies:
        copy.wait()


def weight_grad(spots, dp_size, parts, hidden, own, other):
    row_total, columns = own.shape
    width = (columns - 2 * hidden) // 9
    bf16 = jnp.bfloat16
    blocks = 4 + hidden // width
    chips = dp_size // 2
    share = width // dp_size
    block_rows = [share] * blocks + [hidden // dp_size, row_total // dp_size]
    rows = [sum(block_rows[number] for number in numbers) for _, numbers in parts]
    inside = pl.BlockSpec(memory_space=pltpu.VMEM)
    outside = pl.BlockSpec(memory_space=pl.ANY)
    return run_kernel(
        partial(weight_grad_body, dp_size, parts, hidden),
        (spots, own, other),
        [pl.BlockSpec(memory_space=pltpu.SMEM), inside, inside],
        limit=63,
        out_shape=[
            jax.ShapeDtypeStruct((chips // 2, part_rows, width), bf16)
            for part_rows in rows
            for _ in range(2)
        ],
        out_specs=[outside] * (2 * len(parts)),
        scratch_shapes=[
            pltpu.VMEM((3 * width + hidden, 2 * row_total), bf16),
            pltpu.VMEM((blocks, chips * share, width), bf16),
            pltpu.VMEM((hidden // 2, width), bf16),
            pltpu.VMEM((row_total, width), bf16),
            pltpu.SemaphoreType.DMA(((blocks + 2) * chips,)),
        ],
    )


def add_split_body(step, part_steps, spot_ref, keep_ref, *refs):
    *got_refs, send_ref, held_ref = refs
    bit = lax.rem(lax.div(spot_ref[0], step), 2)
    for number, got_ref in enumerate(got_refs):

        @pl.when(pl.program_id(0) // part_steps == number)
        def _(got_ref=got_ref):
            for out_ref, which in ((send_ref, 1 - bit), (held_ref, bit)):
                values = keep_ref[:, which].astype(jnp.float32)
                values = values + got_ref[:, which].astype(jnp.float32)
                out_ref[...] = values.astype(out_ref.dtype)


def add_split(spots, keep, gots, at, step, left):
    left = sorted(left, reverse=True)
    place_of = left.index(step)
    shape = keep.shape
    width = shape[-1]
    outer = math.prod(shape[:at]) * 2**place_of
    part_outer = outer // len(gots)
    inner_rows = keep.size // (outer * 2 * width)
    rows_most = max(part_outer * inner_rows // 2, 16)
    rows_step = inner_rows
    while rows_step > rows_most and rows_step % 32 == 0:
        rows_step //= 2
    outer_step = 1
    while part_outer % (2 * outer_step) == 0 and 2 * outer_step * rows_step <= rows_most:
        outer_step *= 2
    part_steps = part_outer // outer_step
    block_in = (outer_step, 2, rows_step, width)
    block_out = pl.BlockSpec((outer_step, rows_step, width), lambda first, rows: (first, rows, 0))

    def part_spec(number):
        def pick(first, rows):
            return (jnp.clip(first - number * part_steps, 0, part_steps - 1), 0, rows, 0)

        return pl.BlockSpec(block_in, pick)

    outs = run_kernel(
        partial(add_split_body, step, part_steps),
        (spots, keep.reshape((outer, 2, inner_rows, width)))
        + tuple(got.reshape((part_outer, 2, inner_rows, width)) for got in gots),
        [
            pl.BlockSpec(memory_space=pltpu.SMEM),
            pl.BlockSpec(block_in, lambda first, rows: (first, 0, rows, 0)),
        ]
        + [part_spec(number) for number in range(len(gots))],
        limit=63,
        grid=(outer // outer_step, inner_rows // rows_step),
        out_shape=[jax.ShapeDtypeStruct((outer, inner_rows, width), keep.dtype)] * 2,
        out_specs=[block_out] * 2,
    )
    rest = shape[:at] + (-1,) + shape[at + 1 :]
    return outs[0].reshape(rest), outs[1].reshape(rest)


def owners_body(groups, spot_ref, *refs):
    keep_refs = refs[:groups]
    got_refs = refs[groups : 2 * groups]
    *out_refs, hold_ref = refs[2 * groups :]
    pixels = out_refs[0].shape[0]
    for group, (keep_ref, got_ref) in enumerate(zip(keep_refs, got_refs)):
        bands = keep_ref.shape[0]
        hold_ref[...] = keep_ref[...].astype(jnp.float32) + got_ref[...].astype(jnp.float32)
        for key, out_ref in enumerate(out_refs):
            first = pl.multiple_of(jnp.bitwise_xor(spot_ref[1], key) * pixels, pixels)
            part = hold_ref[:, pl.ds(first, pixels), :]
            out_ref[:, group * bands : (group + 1) * bands, :] = jnp.swapaxes(part, 0, 1).astype(
                out_ref.dtype
            )


def by_owner(spots, keeps, gots, band_size):
    bands, share, width = keeps[0].shape
    pixels = share // band_size
    if pixels % 8:
        whole = jnp.concatenate([add_low(keep, got) for keep, got in zip(keeps, gots)], axis=0)
        whole = whole.reshape(-1, band_size, pixels, width).transpose(1, 2, 0, 3)
        return [
            lax.dynamic_index_in_dim(whole, spots[1] ^ key, 0, keepdims=False)
            for key in range(band_size)
        ]
    inside = pl.BlockSpec(memory_space=pltpu.VMEM)
    return run_kernel(
        partial(owners_body, len(keeps)),
        (spots, *keeps, *gots),
        [pl.BlockSpec(memory_space=pltpu.SMEM)] + [inside] * (2 * len(keeps)),
        limit=63,
        out_shape=[
            jax.ShapeDtypeStruct((pixels, bands * len(keeps), width), keeps[0].dtype)
        ]
        * band_size,
        out_specs=[inside] * band_size,
        scratch_shapes=[pltpu.VMEM((bands, share, width), jnp.float32)],
    )


def shards(
    patches,
    bias_token,
    gen_attn,
    gen_gain,
    gen_ff_in,
    gen_ff_out,
    gen_kernel,
    gen_bias,
    pos_table,
    norm_gain,
    norm_bias,
    w_qkv,
    w_out,
    w_fc1,
    bias_in,
    w_fc2,
    wavelengths,
    kept,
    counts,
    cotangent,
):
    group_size, slot_count, bands_dev, pixel_count = patches.shape
    dp_size = lax.axis_size("dp")
    band_size = lax.axis_size("band")
    device_count = dp_size * band_size
    local_images = group_size // band_size
    model_width = w_out.shape[1]
    row_total = local_images * slot_count
    own_pixels = pixel_count // device_count
    share = own_pixels * band_size
    groups = 2
    group_bands = bands_dev // groups
    f32 = jnp.float32
    bf16 = jnp.bfloat16
    spot = lax.axis_index("band")
    spots = jnp.stack([lax.axis_index("dp"), spot]).astype(jnp.int32)

    parts = band_size if bands_dev % 16 == 0 else 1
    outs = generate_fast(
        parts,
        wavelengths,
        bias_token,
        gen_attn,
        gen_gain,
        gen_ff_in,
        gen_ff_out,
        gen_bias,
        gen_kernel,
    )
    own_kernel = outs[:parts]
    embed_bias, band_states, *gen_kept = outs[parts:]
    hidden = w_fc1.shape[1]
    weight_rows = [w_qkv.shape[0]] * (4 + hidden // model_width) + [w_fc2.shape[0]]
    stack = stack_weights((w_qkv, w_out, w_fc1, w_fc2))
    patch_rows = flatten_rows(
        patches.reshape(group_size * slot_count, bands_dev, pixel_count), (band_states,)
    )
    other_bands = range(1, band_size)
    dp_steps = bit_steps(dp_size)[1:]
    orders = [turn(dp_steps, group) for group in range(groups)]

    if parts == 1:
        whole = own_kernel[0].reshape(own_pixels, band_size, bands_dev, model_width)
        own_kernel = [
            lax.dynamic_index_in_dim(whole, spot ^ key, 1, keepdims=False)
            for key in range(band_size)
        ]
    sent = [part.transpose(1, 0, 2) for part in own_kernel]
    got = [swap(sent[key], "band", key) for key in other_bands]
    *got, patch_rows, stack = together(*got, patch_rows, stack)
    piece = place(
        [([key], block[None]) for key, block in enumerate([sent[0]] + got)], "band", 1
    ).reshape(bands_dev, share, model_width)

    own_pieces = [piece[group * group_bands : (group + 1) * group_bands] for group in range(groups)]
    held = [own_piece[None] for own_piece in own_pieces]
    held_keys = [[0] for _ in range(groups)]
    kernel_groups = [[([0], piece[None])] for _ in range(groups)]
    waiting = []
    stacks = {0: stack}
    stack_keys = [band_size // 2] + [key for key in other_bands if key != band_size // 2]
    for stage in range(len(dp_steps)):
        last = stage == len(dp_steps) - 1
        now_keys = stack_keys if last else stack_keys[:1]
        stack_keys = stack_keys[len(now_keys) :]
        got = [swap(held[group], "dp", orders[group][stage]) for group in range(groups)]
        if stage == 0:
            core_got = swap(piece, "dp", 1)
        elif waiting:
            core_got = swap(waiting[0][2], "dp", 1)
        stack_got = [swap(stack, "band", key) for key in now_keys]
        got[0], got[1], core_got, stack, *stack_got = together(*got, core_got, stack, *stack_got)
        stacks.update(zip(now_keys, stack_got))
        if stage == 0:
            for blocks in kernel_groups:
                blocks.append(([1], core_got[None]))
        elif waiting:
            group, keys, _ = waiting.pop(0)
            kernel_groups[group].append(([key ^ 1 for key in keys], core_got))
        for group in range(groups):
            keys = [key ^ orders[group][stage] for key in held_keys[group]]
            kernel_groups[group].append((keys, got[group]))
            waiting.append((group, keys, got[group]))
            if not last:
                held[group] = jnp.concatenate([held[group], got[group]], axis=0)
                held_keys[group] = held_keys[group] + keys
    for group, keys, last_got in waiting:
        kernel_groups[group].append(([key ^ 1 for key in keys], swap(last_got, "dp", 1)))

    planes = plane_weights(spots, [stacks[key] for key in range(band_size)], weight_rows)
    got = [swap(plane, "dp", orders[half][0]) for half, plane in enumerate(planes)]
    embedded = embed_share(spots, patch_rows, kernel_groups, band_size)
    *embedded, first_got, last_got = together(*embedded, *got)
    held = [
        jnp.concatenate([plane[None], got[None]], axis=0)
        for plane, got in zip(planes, (first_got, last_got))
    ]
    held_keys = [[0, orders[half][0]] for half in range(2)]
    for stage in range(1, len(dp_steps) - 1):
        for half in range(2):
            step = orders[half][stage]
            held[half] = jnp.concatenate([held[half], swap(held[half], "dp", step)], axis=0)
            held_keys[half] = held_keys[half] + [key ^ step for key in held_keys[half]]
    got = [swap(held[half], "dp", orders[half][-1]) for half in range(2)]
    parts = [embedded[0]] + [swap(embedded[key], "band", key) for key in other_bands]
    held[0], held[1], got[0], got[1], *parts = together(*held, *got, *parts)
    weight_halves = []
    for half in range(2):
        blocks = [(held_keys[half], held[half])]
        blocks.append(([key ^ orders[half][-1] for key in held_keys[half]], got[half]))
        weight_halves.append(blocks + gather_core(blocks))

    valid_mask = jnp.arange(slot_count)[None, :] < counts[:, None]
    keep_col = valid_mask.reshape(row_total, 1)
    kept_flat = kept.reshape(row_total)
    pos_rows = jnp.take(pos_table, kept_flat, axis=0).astype(f32)
    base = embed_bias[0:1] + pos_rows
    tile_images = 2 if local_images % 2 == 0 else 1
    tile_rows = tile_images * slot_count
    image_spot = jnp.arange(tile_rows) // slot_count
    same_image = image_spot[:, None] == image_spot[None, :]
    mask = jnp.where(same_image[None] & valid_mask.reshape(-1, 1, tile_rows), 0.0, -1e30)
    cot = jnp.where(keep_col, cotangent.reshape(row_total, model_width), 0)
    (
        result,
        grad_embed,
        stash,
        sums,
    ) = block(
        parts,
        weight_halves,
        spots,
        base,
        cot,
        keep_col.astype(f32),
        mask.astype(f32),
        norm_gain.astype(f32),
        norm_bias.astype(f32),
        bias_in.astype(f32)[None],
        kept_flat[None],
    )

    small_share = row_total // device_count
    block_rows = weight_rows + [small_share]
    part_blocks = [[0, 9], [1], [2], [3], [4, 5, 6, 7], [8]]
    part_orders = [orders[0], orders[1], orders[1], orders[0], orders[0], orders[1]]
    weight_parts = [(order[0], numbers) for order, numbers in zip(part_orders, part_blocks)]
    grads = [grad_embed] + [swap(grad_embed, "band", key) for key in other_bands]
    weight_split = weight_grad(
        spots, dp_size, weight_parts, hidden, stash, swap(stash, "dp", 1)
    )
    mixed = together(*grads, *weight_split)
    grads, weight_split = list(mixed[:band_size]), mixed[band_size:]
    weight_keep, weight_send = list(weight_split[0::2]), list(weight_split[1::2])

    weight_got = [swap(weight_send[part], "dp", part_orders[part][0]) for part in range(2)]
    kernel_split = []
    for group in range(groups):
        *sends, keep = kernel_grad_part(
            spots,
            patch_rows,
            grads,
            group * group_bands,
            group_bands,
            bands_dev,
            dp_size,
            (),
        )
        core_got = [swap(send, "dp", 1) for send in sends]
        kernel_split += add_split(spots, keep, core_got, 1, orders[group][0], dp_steps)
    weight_got[0], weight_got[1], *kernel_split = together(*weight_got, *kernel_split)

    def cut_blocks(values, numbers):
        lead = values.shape[0]
        cuts = []
        first = 0
        for number in numbers:
            rows = block_rows[number]
            cut = values[:, first : first + rows * band_size]
            cuts.append(cut.reshape(lead, band_size, rows, model_width))
            first += rows * band_size
        return jnp.concatenate(cuts, axis=2)

    def over_band(by_band):
        sent = [
            lax.dynamic_index_in_dim(by_band, spot ^ key, 1, keepdims=False)
            for key in range(band_size)
        ]
        return [sent[0]] + [swap(sent[key], "band", key) for key in other_bands]

    def total(blocks):
        return sum(block_sum.astype(f32) for block_sum in blocks)

    def over_chips(sums):
        cut = [
            values if isinstance(values, tuple) else split_half(values, 0, order[0], order)
            for values, order in sums
        ]
        got = [None] * len(sums)
        for step in sorted({order[0] for _, order in sums}):
            here = [number for number, (_, order) in enumerate(sums) if order[0] == step]
            flat = [cut[number][0].reshape(-1, model_width) for number in here]
            moved = swap(jnp.concatenate(flat, axis=0) if len(flat) > 1 else flat[0], "dp", step)
            first = 0
            for number, rows in zip(here, flat):
                part = moved[first : first + rows.shape[0]]
                got[number] = part.reshape(cut[number][0].shape)
                first += rows.shape[0]
        return [
            (add_low(cut[number][1], got[number]), order[1:])
            for number, (_, order) in enumerate(sums)
        ]

    update = patch_grad(spots, grads, kernel_groups, pixel_count, 0, ())
    for stage in range(len(dp_steps)):
        last = stage == len(dp_steps) - 1
        got = [swap(kernel_split[2 * group], "dp", orders[group][stage]) for group in range(groups)]
        part = 2 + stage
        cuts = [
            cut_blocks(weight_keep[part], part_blocks[part]),
            cut_blocks(weight_send[part], part_blocks[part]),
        ]
        if stage == 0:
            cuts += [
                cut_blocks(add_low(weight_keep[early], weight_got[early]), part_blocks[early])
                for early in range(2)
            ]
        part_got = [None]
        if stage < 2:
            part_got = over_band(jnp.concatenate(cuts, axis=2))
        if stage == 0:
            got[0], got[1], update, *part_got = together(*got, update, *part_got)
        else:
            got[0], got[1], *part_got = together(*got, *part_got)
        if stage < 2:
            summed = total(part_got).astype(bf16)
            rows = [cut.shape[2] for cut in cuts]
            spots_in = [sum(rows[:number]) for number in range(len(rows))]
            summed = [summed[:, first : first + size] for first, size in zip(spots_in, rows)]
            weight_keep[part], weight_send[part] = summed[:2]
            if stage == 0:
                early = summed[2:]
        if not last:
            kernel_split = [
                part
                for group in range(groups)
                for part in add_split(
                    spots,
                    kernel_split[2 * group + 1],
                    [got[group]],
                    1,
                    orders[group][stage + 1],
                    orders[group][stage + 1 :],
                )
            ]
    sent = by_owner(
        spots,
        [
            kernel_split[2 * group + 1].reshape(group_bands, share, model_width)
            for group in range(groups)
        ],
        [got[group].reshape(group_bands, share, model_width) for group in range(groups)],
        band_size,
    )
    pieces = [sent[0]] + [swap(sent[key], "band", key) for key in other_bands]
    sums_left = over_chips(
        [(early[part], part_orders[part][1:]) for part in range(2)]
        + [
            ((weight_send[part], weight_keep[part]), part_orders[part])
            for part in range(2, len(part_blocks))
        ]
    )
    while any(order for _, order in sums_left[:2]):
        moved = over_chips([one for one in sums_left[:2] if one[1]])
        sums_left[:2] = [moved.pop(0) if one[1] else one for one in sums_left[:2]]
    weight_sums = [values for values, _ in sums_left]
    grad_patches = unflatten_rows([update], bands_dev, (sent[0],))
    mixed = together(*weight_sums, grad_patches, *pieces)
    count = len(part_blocks)
    weight_sums, grad_patches, pieces = list(mixed[:count]), mixed[count], mixed[count + 1 :]
    grad_gen_kernel, tail = states_grad(spots, band_states, gen_kernel, pieces, sums)
    mixed = together(*weight_sums, tail)
    weight_sums, tail = list(mixed[:-1]), mixed[-1]

    small = weight_sums[0][:, -small_share:]
    late = [(weight_sums[part], part_orders[part][1:]) for part in range(2, count)]
    small_steps = [("band", step) for step in bit_steps(band_size)]
    small_steps += [("dp", step) for step in turn(bit_steps(dp_size), 1)]

    def widen(values, number):
        return jnp.concatenate([values, swap(values, *small_steps[number])], axis=0)

    while any(order for _, order in late):
        late = over_chips(late)
    late = [values for values, _ in late]
    tail = total([tail] + [swap(tail, "band", key) for key in other_bands])
    tail_steps = bit_steps(dp_size)
    tail = tail + swap(tail, "dp", tail_steps[0])
    tail, *late = together(tail, *late)
    cuts = [cut_blocks(late[part - 2], part_blocks[part]) for part in range(4, count)]
    last_sum = total(over_band(jnp.concatenate(cuts, axis=2)))
    small = widen(small, 0)
    for number, step in enumerate(tail_steps[1:]):
        got = swap(tail, "dp", step)
        small = widen(small, number + 1)
        got, small = together(got, small)
        tail = tail + got
    for number in range(len(tail_steps), len(small_steps)):
        small = widen(small, number)
    own_grads = jnp.concatenate(
        [
            weight_sums[0][0, :-small_share].astype(f32),
            weight_sums[1][0].astype(f32),
            late[0][0].astype(f32),
            late[1][0].astype(f32),
            last_sum[0],
        ],
        axis=0,
    )
    small_order = (jnp.arange(dp_size) ^ spots[0])[:, None] * band_size
    small_order = (small_order + (jnp.arange(band_size) ^ spots[1])[None, :]).reshape(-1)
    small = small.reshape(2, dp_size // 2, band_size, small_share, model_width)
    small = small.transpose(1, 0, 2, 3, 4).reshape(-1, small_share, model_width)
    small = jnp.take(small, small_order, axis=0).reshape(row_total, model_width)
    own_blocks = []
    done = 0
    for rows in weight_rows:
        own_blocks.append(own_grads[done : done + rows])
        done += rows
    grad_qkv_own = jnp.concatenate(own_blocks[:3], axis=1)
    grad_out_own = own_blocks[3]
    grad_fc_in_own = jnp.concatenate(own_blocks[4:-1], axis=1)
    grad_fc_out_own = own_blocks[-1]
    grad_token, grad_attn, grad_gain_gen, grad_ff_first, grad_ff_second, grad_gen_bias = (
        generate_back(
            tail,
            gen_attn,
            gen_gain,
            gen_ff_in,
            gen_ff_out,
            gen_bias,
            gen_kept,
        )
    )

    small = small.astype(f32)
    sums_at = small.shape[0] - 16
    grad_pos_all = small[: pos_table.shape[0]]
    grad_gains = small[sums_at + 1 : sums_at + 3]
    grad_shifts = small[sums_at + 3 : sums_at + 5]
    grad_bias_all = small[sums_at + 8 : sums_at + 8 + hidden // model_width].reshape(-1)
    grad_patches = grad_patches.reshape(group_size, slot_count, bands_dev, pixel_count)
    return (
        result.reshape(local_images, slot_count, model_width),
        grad_patches,
        grad_token[0],
        grad_attn,
        grad_gain_gen,
        grad_ff_first,
        grad_ff_second,
        grad_gen_kernel,
        grad_gen_bias,
        grad_pos_all,
        grad_gains,
        grad_shifts,
        grad_qkv_own,
        grad_out_own,
        grad_fc_in_own,
        grad_bias_all,
        grad_fc_out_own,
    )


def solution(mesh):
    placed = (
        P("dp", None, "band", None),
        P(),
        P(),
        P(),
        P(),
        P(),
        P(None, ("dp", "band")),
        P(),
        P(),
        P(),
        P(),
        P(("dp", "band"), None),
        P(("dp", "band"), None),
        P(("dp", "band"), None),
        P(),
        P(("dp", "band"), None),
        P(),
        P(("dp", "band"), None),
        P(("dp", "band")),
        P(("dp", "band"), None, None),
    )
    return jax.shard_map(
        shards,
        mesh=mesh,
        in_specs=placed,
        out_specs=(
            P(("dp", "band"), None, None),
            P("dp", None, "band", None),
            P(),
            P(),
            P(),
            P(),
            P(),
            P(None, ("dp", "band")),
            P(),
            P(),
            P(),
            P(),
            P(("dp", "band"), None),
            P(("dp", "band"), None),
            P(("dp", "band"), None),
            P(),
            P(("dp", "band"), None),
        ),
        check_vma=False,
    )
```
